32 devices in a mesh: dp: 8 (over y, x, core), text: 4 (over z).
Axes of the slice: x: 2, y: 2, z: 4, core: 2. Of those that a mesh axis runs over, the one named last changes fastest.
Arguments:
- latents: float32 [16, 1024, 64], P('dp', 'text'), may hold values from -6 to 6
- noise_field: float32 [16, 1024, 64], P('dp', 'text'), may hold values from -6 to 6
- timesteps: int32 [16], P('dp'), may hold values from 0 to 255
- text_tokens: bfloat16 [16, 128, 768], P('dp', 'text'), may hold values from -6 to 6
- text_lengths: int32 [16], P('dp'), may hold values from 4 to 128, as said below
- negatives: int32 [16, 15], P('dp'), may hold values from 0 to 15, as said below
- assignment: int32 [256], replicated, may hold values from 0 to 255, as said below
- end_weights: float32 [1536, 2, 64], P(('dp', 'text')), as said below
- time_table: float32 [256, 1536], P(('dp', 'text')), may hold values from -0.375 to 0.375
- square_slots: float32 [256, 192, 192], P(('dp', 'text')), as said below
- cross_weights: float32 [1536, 2, 1536], P(('dp', 'text')), as said below
- key_value: float32 [768, 3072], P(('dp', 'text')), may hold values from -0.21875 to 0.21875
- gate_up: float32 [1536, 12288], P(('dp', 'text')), may hold values from -0.15625 to 0.15625
- down_weight: float32 [6144, 1536], P(('dp', 'text')), may hold values from -0.078125 to 0.078125
- norm_gains: float32 [1536, 3], P(('dp', 'text')), as said below
- first_ends: float32 [1536, 2, 64], P(('dp', 'text')), may hold values from -4.7683716e-07 to 4.7683716e-07
- second_ends: float32 [1536, 2, 64], P(('dp', 'text')), may hold values from 5.504055e-16 to 2.201622e-15
- first_table: float32 [256, 1536], P(('dp', 'text')), may hold values from -2.2351742e-08 to 2.2351742e-08
- second_table: float32 [256, 1536], P(('dp', 'text')), may hold values from 1.100811e-18 to 4.403244e-18
- first_cross: float32 [1536, 2, 1536], P(('dp', 'text')), may hold values from -1.7881393e-07 to 1.7881393e-07
- second_cross: float32 [1536, 2, 1536], P(('dp', 'text')), may hold values from 6.6048665e-17 to 2.6419466e-16
- first_key_value: float32 [768, 3072], P(('dp', 'text')), may hold values from -4.7683716e-07 to 4.7683716e-07
- second_key_value: float32 [768, 3072], P(('dp', 'text')), may hold values from 5.504055e-16 to 2.201622e-15
- first_gate_up: float32 [1536, 12288], P(('dp', 'text')), may hold values from -8.940697e-08 to 8.940697e-08
- second_gate_up: float32 [1536, 12288], P(('dp', 'text')), may hold values from 1.6512166e-17 to 6.6048665e-17
- first_down: float32 [6144, 1536], P(('dp', 'text')), may hold values from -1.4901161e-07 to 1.4901161e-07
- second_down: float32 [6144, 1536], P(('dp', 'text')), may hold values from 4.4032442e-17 to 1.7612977e-16
- first_gains: float32 [1536, 3], P(('dp', 'text')), may hold values from -1.9073486e-06 to 1.9073486e-06
- second_gains: float32 [1536, 3], P(('dp', 'text')), may hold values from 8.806488e-15 to 3.5225952e-14
- left_stats: float32 [256, 192, 192], P(('dp', 'text')), as said below
- right_stats: float32 [256, 192, 192], P(('dp', 'text')), as said below
- left_roots: float32 [256, 192, 192], P(('dp', 'text')), as said below
- right_roots: float32 [256, 192, 192], P(('dp', 'text')), as said below
Outputs:
- loss_sum: float32 [], replicated
- gradient_norm: float32 [], replicated
- new_first_ends: float32 [1536, 2, 64], P(('dp', 'text'))
- new_second_ends: float32 [1536, 2, 64], P(('dp', 'text'))
- new_end_weights: float32 [1536, 2, 64], P(('dp', 'text'))
- new_first_table: float32 [256, 1536], P(('dp', 'text'))
- new_second_table: float32 [256, 1536], P(('dp', 'text'))
- new_time_table: float32 [256, 1536], P(('dp', 'text'))
- new_first_cross: float32 [1536, 2, 1536], P(('dp', 'text'))
- renewed_cross_moment: float32 [1536, 2, 1536], P(('dp', 'text'))
- new_cross_weights: float32 [1536, 2, 1536], P(('dp', 'text'))
- new_first_key_value: float32 [768, 3072], P(('dp', 'text'))
- new_second_key_value: float32 [768, 3072], P(('dp', 'text'))
- new_key_value: float32 [768, 3072], P(('dp', 'text'))
- new_first_gate_up: float32 [1536, 12288], P(('dp', 'text'))
- new_second_gate_up: float32 [1536, 12288], P(('dp', 'text'))
- new_gate_up: float32 [1536, 12288], P(('dp', 'text'))
- new_first_down: float32 [6144, 1536], P(('dp', 'text'))
- new_second_down: float32 [6144, 1536], P(('dp', 'text'))
- new_down_weight: float32 [6144, 1536], P(('dp', 'text'))
- new_first_gains: float32 [1536, 3], P(('dp', 'text'))
- new_second_gains: float32 [1536, 3], P(('dp', 'text'))
- new_norm_gains: float32 [1536, 3], P(('dp', 'text'))
- clipped_slots: float32 [256, 192, 192], P(('dp', 'text'))
- new_left_stats: float32 [256, 192, 192], P(('dp', 'text'))
- new_right_stats: float32 [256, 192, 192], P(('dp', 'text'))
- new_square_slots: float32 [256, 192, 192], P(('dp', 'text'))
The draws below stay inside these ranges and needn't reach their ends.
Inputs may be any that keep to these rules, and one draw needn't show every extreme that they name: `text_lengths`: in each aligned block of 2 items one item's prompt reaches the last text shard; some item has length 128. negatives[i, :] never holds i; repeats may occur. `assignment`: A permutation of the block numbers. `end_weights`: normal entries, fan-in scaled. `square_slots`: normal entries. `cross_weights`: normal entries. `norm_gains`: Positive. `left_stats`: Diagonal, positive on the diagonal. `right_stats`: Diagonal, positive on the diagonal. `left_roots`: Symmetric. `right_roots`: Symmetric.
All inputs are finite; a program needn't handle non-finite values.
Results may differ from the reference program's by a relative error of at most 0.02.
The reference program's roundings to bfloat16 on the way count: a program that leaves them out, or rounds other values in their place, can miss the bound.
Values may be sent and summed in bfloat16 or wider, within the bound.
A program may use at most 448 MiB of HBM per device.

```python
import math
import jax
import jax.numpy as jnp
from jax import lax

D = 1536
HEADS = 24
HD = 64
FF = 6144
DIN = 64
DT = 768
FRAMES = 1024
TXT = 128
ITEMS_DEV = 2
NTIME = 256
NNEG = 15
STEP = 10
ITEMS = 16
BLK = 192
NBLK = 256
PARAMS = 45421056
N_TEXT = 4


def block_order(key):
    return jax.random.permutation(key, NBLK).astype(jnp.int32)


def draw_assignment(key, part):
    return block_order(key)


def draw_square_slots(key, part):
    order = block_order(key)
    key = jax.random.fold_in(key, 11)
    matrix_index = order // (NBLK // 4)
    factor = jnp.where(matrix_index == 3, 0.5 * math.sqrt(FRAMES / D), D ** (-0.5)).astype(jnp.float32)
    values = jax.random.truncated_normal(key, -4.0, 4.0, (NBLK, BLK, BLK), jnp.float32)
    return values * factor[:, None, None]


def draw_text_lengths(key, part):
    key = jax.random.fold_in(key, 3)
    key_one, key_two, key_three, key_four = jax.random.split(key, 4)
    lengths = jax.random.randint(key_one, (ITEMS,), 4, TXT + 1)
    groups = ITEMS // ITEMS_DEV
    chosen = jax.random.randint(key_two, (groups,), 0, ITEMS_DEV)
    long_low = TXT - TXT // N_TEXT + 1
    long_lengths = jax.random.randint(key_three, (ITEMS,), long_low, TXT + 1)
    marked = jnp.zeros((ITEMS,), jnp.int32).at[jnp.arange(groups, dtype=jnp.int32) * ITEMS_DEV + chosen].set(1)
    lengths = jnp.where(marked == 1, long_lengths, lengths)
    fullest = jax.random.randint(key_four, (), 0, ITEMS)
    lengths = jnp.where(jnp.arange(ITEMS, dtype=jnp.int32) == fullest, TXT, lengths)
    return lengths.astype(jnp.int32)


def draw_negatives(key, part):
    key = jax.random.fold_in(key, 5)
    offsets = jax.random.randint(key, (ITEMS, NNEG), 1, ITEMS)
    return ((jnp.arange(ITEMS, dtype=jnp.int32)[:, None] + offsets) % ITEMS).astype(jnp.int32)


def draw_end_weights(key, part):
    key = jax.random.fold_in(key, 7)
    factor = jnp.array([DIN ** (-0.5), D ** (-0.5)], jnp.float32)
    return jax.random.truncated_normal(key, -4.0, 4.0, (D, 2, DIN), jnp.float32) * factor[None, :, None]


def draw_cross_weights(key, part):
    key = jax.random.fold_in(key, 9)
    factor = jnp.array([D ** (-0.5), 0.5 * math.sqrt(TXT / D)], jnp.float32)
    return jax.random.truncated_normal(key, -4.0, 4.0, (D, 2, D), jnp.float32) * factor[None, :, None]


def draw_norm_gains(key, part):
    key = jax.random.fold_in(key, 13)
    ramp = jnp.arange(D, dtype=jnp.float32)[:, None] / D
    return (0.6 + 1.2 * ramp) * jax.random.uniform(key, (D, 3), jnp.float32, 0.85, 1.15)


def stat_draw(key):
    base_level = 2.5e-08 * BLK / PARAMS
    diagonal = base_level * jnp.exp(jax.random.uniform(key, (NBLK, BLK), jnp.float32, 0.0, math.log(4.0)))
    return diagonal[:, :, None] * jnp.eye(BLK, dtype=jnp.float32)[None]


def root_draw(key):
    base_level = 2.5e-08 * BLK / PARAMS
    factor = (2.0 * base_level) ** (-0.25)
    entries = jax.random.uniform(key, (NBLK, BLK, BLK), jnp.float32, -1.0, 1.0)
    symmetric = 0.4 * (entries + jnp.swapaxes(entries, 1, 2)) / math.sqrt(BLK)
    return factor * (jnp.eye(BLK, dtype=jnp.float32)[None] + symmetric)


def draw_left_stats(key, part):
    key = jax.random.fold_in(key, 17)
    return stat_draw(key)


def draw_right_stats(key, part):
    key = jax.random.fold_in(key, 19)
    return stat_draw(key)


def draw_left_roots(key, part):
    key = jax.random.fold_in(key, 23)
    return root_draw(key)


def draw_right_roots(key, part):
    key = jax.random.fold_in(key, 29)
    return root_draw(key)


def set_ends(values, stream_key, smallest, top_value):
    longest = values.shape.index(max(values.shape))
    spots = []
    for shift in (0, 1):
        where = [jax.random.randint(jax.random.fold_in(stream_key, axis), (), 0, length) for axis, length in enumerate(values.shape)]
        where[longest] = (where[longest] + shift) % values.shape[longest]
        spots.append(tuple(where))
    return values.at[spots[0]].set(smallest).at[spots[1]].set(top_value)


def levels(own_key, extent, cuts, low, top_value):
    level = 1.0
    for axis_at, parts in cuts:
        steps = jax.random.uniform(jax.random.fold_in(jax.random.fold_in(own_key, 6), axis_at), (parts,), jnp.float32, low / len(cuts), top_value / len(cuts))
        level = level * jnp.repeat(jnp.exp(steps), extent[axis_at] // parts).reshape((-1,) + (1,) * (len(extent) - 1 - axis_at))
    return level


def centred(key, dims, deviation, limit, cuts=(), held_as=jnp.bfloat16):
    result = deviation * jax.random.normal(key, dims, jnp.float32)
    if cuts:
        result = result * levels(key, dims, cuts, -0.22, 0.18)
    return jnp.clip(result, -limit, limit).astype(held_as)


def setup_inputs(seed: int = 0) -> dict:
    arg_keys = jax.random.split(jax.random.key(seed), 34)
    return {
        "latents": centred(arg_keys[0], (ITEMS, FRAMES, DIN), 1.0, 6.0, ((0, 8), (1, 4)), jnp.float32),
        "noise_field": centred(arg_keys[1], (ITEMS, FRAMES, DIN), 1.0, 6.0, ((0, 8), (1, 4)), jnp.float32),
        "timesteps": set_ends(jax.random.randint(arg_keys[2], (ITEMS,), 0, NTIME), jax.random.fold_in(arg_keys[2], 1), 0, NTIME - 1).astype(jnp.int32),
        "text_tokens": centred(arg_keys[3], (ITEMS, TXT, DT), 1.0, 6.0, ((0, 8), (1, 4))),
        "text_lengths": draw_text_lengths(jax.random.fold_in(arg_keys[33], 71), 0),
        "negatives": draw_negatives(jax.random.fold_in(arg_keys[33], 71), 0),
        "assignment": draw_assignment(jax.random.fold_in(arg_keys[33], 71), 0),
        "end_weights": draw_end_weights(jax.random.fold_in(arg_keys[33], 71), 0),
        "time_table": centred(arg_keys[8], (NTIME, D), NTIME ** -0.5, 0.375, ((0, 32),), jnp.float32),
        "square_slots": draw_square_slots(jax.random.fold_in(arg_keys[33], 71), 0),
        "cross_weights": draw_cross_weights(jax.random.fold_in(arg_keys[33], 71), 0),
        "key_value": centred(arg_keys[11], (DT, 2 * D), DT ** -0.5, 0.21875, ((0, 32),), jnp.float32),
        "gate_up": centred(arg_keys[12], (D, 2 * FF), D ** -0.5, 0.15625, ((0, 32),), jnp.float32),
        "down_weight": centred(arg_keys[13], (FF, D), FF ** -0.5, 0.078125, ((0, 32),), jnp.float32),
        "norm_gains": draw_norm_gains(jax.random.fold_in(arg_keys[33], 71), 0),
        "first_ends": centred(arg_keys[15], (D, 2, DIN), (0.000555 / PARAMS ** 0.5), 4.76837158203125e-07, ((0, 32),), jnp.float32),
        "second_ends": jnp.clip(jnp.exp(math.log(2.201622012547007e-15) - 1.3862944 * jax.random.uniform(arg_keys[16], (D, 2, DIN), jnp.float32) ** levels(arg_keys[16], (D, 2, DIN), ((0, 32),), -0.2, 0.2)), 5.504055031367518e-16, 2.201622012547007e-15),
        "first_table": centred(arg_keys[17], (NTIME, D), (0.0000248 / PARAMS ** 0.5), 2.2351741790771484e-08, ((0, 32),), jnp.float32),
        "second_table": jnp.clip(jnp.exp(math.log(4.4032441144295204e-18) - 1.3862944 * jax.random.uniform(arg_keys[18], (NTIME, D), jnp.float32) ** levels(arg_keys[18], (NTIME, D), ((0, 32),), -0.2, 0.2)), 1.1008110286073801e-18, 4.4032441144295204e-18),
        "first_cross": centred(arg_keys[19], (D, 2, D), (0.000192 / PARAMS ** 0.5), 1.7881393432617188e-07, ((0, 32),), jnp.float32),
        "second_cross": jnp.clip(jnp.exp(math.log(2.641946584462998e-16) - 1.3862944 * jax.random.uniform(arg_keys[20], (D, 2, D), jnp.float32) ** levels(arg_keys[20], (D, 2, D), ((0, 32),), -0.2, 0.2)), 6.604866461157495e-17, 2.641946584462998e-16),
        "first_key_value": centred(arg_keys[21], (DT, 2 * D), (0.000555 / PARAMS ** 0.5), 4.76837158203125e-07, ((0, 32),), jnp.float32),
        "second_key_value": jnp.clip(jnp.exp(math.log(2.201622012547007e-15) - 1.3862944 * jax.random.uniform(arg_keys[22], (DT, 2 * D), jnp.float32) ** levels(arg_keys[22], (DT, 2 * D), ((0, 32),), -0.2, 0.2)), 5.504055031367518e-16, 2.201622012547007e-15),
        "first_gate_up": centred(arg_keys[23], (D, 2 * FF), (0.0000961 / PARAMS ** 0.5), 8.940696716308594e-08, ((0, 32),), jnp.float32),
        "second_gate_up": jnp.clip(jnp.exp(math.log(6.604866461157495e-17) - 1.3862944 * jax.random.uniform(arg_keys[24], (D, 2 * FF), jnp.float32) ** levels(arg_keys[24], (D, 2 * FF), ((0, 32),), -0.2, 0.2)), 1.6512166152893738e-17, 6.604866461157495e-17),
        "first_down": centred(arg_keys[25], (FF, D), (0.000157 / PARAMS ** 0.5), 1.4901161193847656e-07, ((0, 32),), jnp.float32),
        "second_down": jnp.clip(jnp.exp(math.log(1.7612976788590327e-16) - 1.3862944 * jax.random.uniform(arg_keys[26], (FF, D), jnp.float32) ** levels(arg_keys[26], (FF, D), ((0, 32),), -0.2, 0.2)), 4.4032441971475817e-17, 1.7612976788590327e-16),
        "first_gains": centred(arg_keys[27], (D, 3), (0.00222 / PARAMS ** 0.5), 1.9073486328125e-06, ((0, 32),), jnp.float32),
        "second_gains": jnp.clip(jnp.exp(math.log(3.5225952200752114e-14) - 1.3862944 * jax.random.uniform(arg_keys[28], (D, 3), jnp.float32) ** levels(arg_keys[28], (D, 3), ((0, 32),), -0.2, 0.2)), 8.806488050188029e-15, 3.5225952200752114e-14),
        "left_stats": draw_left_stats(jax.random.fold_in(arg_keys[33], 71), 0),
        "right_stats": draw_right_stats(jax.random.fold_in(arg_keys[33], 71), 0),
        "left_roots": draw_left_roots(jax.random.fold_in(arg_keys[33], 71), 0),
        "right_roots": draw_right_roots(jax.random.fold_in(arg_keys[33], 71), 0),
    }


@jax.custom_vjp
def low(v):
    return lax.optimization_barrier(v.astype(jnp.bfloat16)).astype(jnp.float32)

@jax.custom_vjp
def low_back(v):
    return v

def low_keep(v):
    return (low(v), None)

def low_pass(kept, grad):
    return (grad,)

def back_keep(v):
    return (v, None)

def back_low(kept, grad):
    return (low(grad),)
low.defvjp(low_keep, low_pass)
low_back.defvjp(back_keep, back_low)
BEST_PRECISION = lax.Precision.HIGHEST
NORM_EPS = 1e-05
POOL_EPS = 1e-06
SCORE_SCALE = 0.125
CONTRAST_TEMP = 0.02
CONTRAST_WEIGHT = 0.1
CLIP_NORM = 0.005
BETA_FIRST = 0.9
BETA_SECOND = 0.999
ADAM_EPS = 1e-08
WEIGHT_DECAY = 0.01
ADAM_RATES = (0.02, 0.05, 0.0, 0.1, 0.02, 0.02, 0.02, 1.0)
STAT_DECAY = 0.999
SHAMPOO_RATE = 0.01
MASK_VALUE = -1000000000.0

def matmul(left_side, right_side):
    return jnp.dot(left_side, right_side, precision=BEST_PRECISION)

def layer_norm(inputs, gain_row):
    center = inputs - lax.optimization_barrier(jnp.mean(inputs, -1, keepdims=True))
    return center * lax.rsqrt(lax.optimization_barrier(jnp.mean(center * center, -1, keepdims=True)) + NORM_EPS) * gain_row

def time_features(timesteps):
    halfway = NTIME // 2
    frequency = jnp.exp(jnp.arange(halfway, dtype=jnp.float32) * (math.log(64.0) / halfway))
    moment = (timesteps.astype(jnp.float32) + 0.5) / NTIME
    phase = 2.0 * math.pi * moment[:, None] * frequency[None, :]
    return jnp.concatenate([jnp.cos(phase), jnp.sin(phase)], 1)

def rope_tables(positions_count, offset):
    halfway = HD // 2
    frequency = jnp.exp(jnp.arange(halfway, dtype=jnp.float32) * (-2.0 * math.log(10000.0) / HD))
    positions = (jnp.arange(positions_count, dtype=jnp.int32) + offset).astype(jnp.float32)
    angles = positions[:, None] * frequency[None, :]
    return (jnp.concatenate([jnp.cos(angles)] * 2, -1), jnp.concatenate([jnp.sin(angles)] * 2, -1))

def rotate(values, cosine_table, sine_table):
    halfway = HD // 2
    turned = jnp.concatenate([-values[..., halfway:], values[..., :halfway]], -1)
    return values * cosine_table[:, None, :] + turned * sine_table[:, None, :]

def to_matrices(blocks):
    per_side = D // BLK
    return blocks.reshape(4, per_side, per_side, BLK, BLK).transpose(0, 1, 3, 2, 4).reshape(4, D, D)

def normalize(vectors):
    return vectors * lax.rsqrt(lax.optimization_barrier(jnp.sum(vectors * vectors, -1, keepdims=True)) + POOL_EPS)

def contrast_loss(pooled_audio, pooled_text, negatives):
    audio_unit_vectors = normalize(pooled_audio)
    text_unit_vectors = normalize(pooled_text)
    positive_pairs = lax.optimization_barrier(jnp.sum(audio_unit_vectors * text_unit_vectors, -1)) / CONTRAST_TEMP
    negative_pairs = jnp.einsum('ux,uax->ua', audio_unit_vectors, text_unit_vectors[negatives], precision=BEST_PRECISION) / CONTRAST_TEMP
    scores = jnp.concatenate([positive_pairs[:, None], negative_pairs], 1)
    peak_score = lax.optimization_barrier(jnp.max(scores, -1, keepdims=True))
    logsum = peak_score[:, 0] + jnp.log(lax.optimization_barrier(jnp.sum(jnp.exp(scores - peak_score), -1)))
    return jnp.sum(logsum - positive_pairs)

def attend(queries, all_keys, values, key_bias):
    scores = low_back(jnp.einsum('fhd,khd->hfk', queries, all_keys, precision=BEST_PRECISION) * SCORE_SCALE) + key_bias
    peak_score = lax.optimization_barrier(jnp.max(scores, -1, keepdims=True))
    weights = jnp.exp(scores - peak_score)
    attention = weights / lax.optimization_barrier(jnp.sum(weights, -1, keepdims=True))
    mixture = jnp.einsum('hfk,khd->fhd', low(attention), values, precision=BEST_PRECISION)
    return low(low_back(mixture.reshape(queries.shape[0], D)))

def forward(pieces, latents, noise_field, timesteps, text_float, text_lengths, negatives, assignment):
    end_weights, time_table, square_slots, cross_weights, key_value, gate_up, down_weight, norm_gains = pieces
    weight_in = low(end_weights[:, 0, :])
    weight_out = low(end_weights[:, 1, :])
    blocks = jnp.zeros_like(square_slots).at[assignment].set(square_slots)
    squares = low(to_matrices(blocks))
    cross_query = low(cross_weights[:, 0, :])
    cross_out = low(cross_weights[:, 1, :])
    pair_weight = low(key_value)
    gate_weight = low(gate_up)
    down_low = low(down_weight)
    gain_values = low(norm_gains)
    embeds = matmul(low(time_features(timesteps)), low(time_table))
    cosine_table, sine_table = rope_tables(FRAMES, 1)
    valid_keys = jnp.arange(TXT, dtype=jnp.int32)[None, :] < text_lengths[:, None]

    def one_item(running, inputs):
        clean_item, noise_item, step_index, tokens, valid_row, embed_row = inputs
        angles = (step_index.astype(jnp.float32) + 0.5) * (0.5 * math.pi / NTIME)
        signal = jnp.cos(angles)
        spread = jnp.sin(angles)
        noised = low(signal * clean_item + spread * noise_item)
        residual = low_back(matmul(noised, weight_in.T))
        normed = low(layer_norm(residual, gain_values[:, 0]))
        timing = low(layer_norm(embed_row[None, :], gain_values[:, 0]))
        queries = low_back(matmul(normed, squares[0]))
        key_rows = low_back(matmul(normed, squares[1]))
        value_rows = low(low_back(matmul(normed, squares[2])))
        rot_queries = low(rotate(queries.reshape(FRAMES, HEADS, HD), cosine_table, sine_table))
        rot_keys = low(rotate(key_rows.reshape(FRAMES, HEADS, HD), cosine_table, sine_table))
        time_key = low(matmul(timing, squares[1])).reshape(1, HEADS, HD)
        time_value = low(matmul(timing, squares[2])).reshape(1, HEADS, HD)
        all_keys = jnp.concatenate([time_key, rot_keys], 0)
        all_values = jnp.concatenate([time_value, value_rows.reshape(FRAMES, HEADS, HD)], 0)
        mixture = attend(rot_queries, all_keys, all_values, jnp.zeros((FRAMES + 1,), jnp.float32))
        after_self = residual + low_back(matmul(mixture, squares[3]))
        normed_two = low(layer_norm(after_self, gain_values[:, 1]))
        cross_queries = low(low_back(matmul(normed_two, cross_query))).reshape(FRAMES, HEADS, HD)
        projected = low(low_back(matmul(tokens, pair_weight)))
        key_bias = jnp.where(valid_row, 0.0, MASK_VALUE).astype(jnp.float32)
        cross_mixture = attend(cross_queries, projected[:, :D].reshape(TXT, HEADS, HD), projected[:, D:].reshape(TXT, HEADS, HD), key_bias)
        after_cross = after_self + low_back(matmul(cross_mixture, cross_out))
        normed_three = low(layer_norm(after_cross, gain_values[:, 2]))
        gate_values = low_back(matmul(normed_three, gate_weight))
        hidden = low(jax.nn.silu(gate_values[:, :FF]) * gate_values[:, FF:])
        output_rows = after_cross + low_back(matmul(hidden, down_low))
        predicted = low_back(matmul(low(output_rows), weight_out))
        errors = predicted - (signal * noise_item - spread * clean_item)
        pooled_audio = lax.optimization_barrier(jnp.mean(output_rows, 0))
        valid_float = valid_row.astype(jnp.float32)
        pooled_text = lax.optimization_barrier(jnp.sum(projected[:, :D] * valid_float[:, None], 0)) / jnp.sum(valid_float)
        return (running + jnp.sum(errors * errors), (pooled_audio, pooled_text))
    squared, pooled = lax.scan(jax.checkpoint(one_item), jnp.zeros((), jnp.float32), (latents, noise_field, timesteps, text_float, valid_keys, embeds))
    pooled_audio, pooled_text = pooled
    contrast = contrast_loss(pooled_audio, pooled_text, negatives)
    mse_scale = 1.0 / (ITEMS * FRAMES * DIN)
    return squared * mse_scale + CONTRAST_WEIGHT * contrast / ITEMS

def adam_update(weight, first_moment, second_moment, gradient, rate):
    first_moment = BETA_FIRST * first_moment + (1.0 - BETA_FIRST) * gradient
    second_moment = BETA_SECOND * second_moment + (1.0 - BETA_SECOND) * gradient * gradient
    corrected = first_moment / (1.0 - BETA_FIRST ** STEP)
    scaled = second_moment / (1.0 - BETA_SECOND ** STEP)
    weight = weight - rate * (corrected / (jnp.sqrt(scaled) + ADAM_EPS) + WEIGHT_DECAY * weight)
    return (first_moment, second_moment, weight)

def shampoo_update(slots_now, gradient, left_stat, right_stat, left_root, right_root):
    left_stat = STAT_DECAY * left_stat + (1.0 - STAT_DECAY) * jnp.einsum('sij,skj->sik', gradient, gradient, precision=BEST_PRECISION)
    right_stat = STAT_DECAY * right_stat + (1.0 - STAT_DECAY) * jnp.einsum('sji,sjk->sik', gradient, gradient, precision=BEST_PRECISION)
    inner = jnp.einsum('sij,sjk->sik', gradient, right_root, precision=BEST_PRECISION)
    direction = jnp.einsum('sij,sjk->sik', left_root, inner, precision=BEST_PRECISION)
    return (left_stat, right_stat, slots_now - SHAMPOO_RATE * (direction + WEIGHT_DECAY * slots_now))

def reference(latents, noise_field, timesteps, text_tokens, text_lengths, negatives, assignment, end_weights, time_table, square_slots, cross_weights, key_value, gate_up, down_weight, norm_gains, first_ends, second_ends, first_table, second_table, first_cross, second_cross, first_key_value, second_key_value, first_gate_up, second_gate_up, first_down, second_down, first_gains, second_gains, left_stats, right_stats, left_roots, right_roots):
    text_float = text_tokens.astype(jnp.float32)
    masters = (end_weights, time_table, square_slots, cross_weights, key_value, gate_up, down_weight, norm_gains)

    def loss_of(*pieces):
        return forward(pieces, latents, noise_field, timesteps, text_float, text_lengths, negatives, assignment)
    loss_sum, pullback = jax.vjp(loss_of, *masters)
    gradients = pullback(jnp.ones((), jnp.float32))
    square_sum = jnp.zeros((), jnp.float32)
    for member in gradients:
        square_sum = square_sum + jnp.sum(member * member)
    gradient_norm = jnp.sqrt(square_sum)
    factor = CLIP_NORM / jnp.maximum(gradient_norm, CLIP_NORM)
    clipped = [factor * member for member in gradients]
    firsts = (first_ends, first_table, None, first_cross, first_key_value, first_gate_up, first_down, first_gains)
    seconds = (second_ends, second_table, None, second_cross, second_key_value, second_gate_up, second_down, second_gains)
    results = [loss_sum, gradient_norm]
    for index_value in (0, 1, 3, 4, 5, 6, 7):
        results.extend(adam_update(masters[index_value], firsts[index_value], seconds[index_value], clipped[index_value], ADAM_RATES[index_value]))
    left_new, right_new, slots_new = shampoo_update(square_slots, clipped[2], left_stats, right_stats, left_roots, right_roots)
    results.extend([clipped[2], left_new, right_new, slots_new])
    return tuple(results)
```

```python
from functools import partial
import math

import jax
import jax.numpy as jnp
from jax import lax
from jax.experimental import pallas as pl
from jax.experimental.pallas import tpu as pltpu
from jax.sharding import Mesh, PartitionSpec as P

D = 1536
HEADS = 24
HD = 64
FF = 6144
DIN = 64
DT = 768
FRAMES = 1024
NTIME = 256
STEP = 10
BLK = 192


BEST_PRECISION = lax.Precision.HIGHEST
NORM_EPS = 1e-05
POOL_EPS = 1e-06
SCORE_SCALE = 0.125
CONTRAST_TEMP = 0.02
CONTRAST_WEIGHT = 0.1
CLIP_NORM = 0.005
BETA_FIRST = 0.9
BETA_SECOND = 0.999
ADAM_EPS = 1e-08
WEIGHT_DECAY = 0.01
ADAM_RATES = (0.02, 0.05, 0.0, 0.1, 0.02, 0.02, 0.02, 1.0)
STAT_DECAY = 0.999
SHAMPOO_RATE = 0.01
MASK_VALUE = -1000000000.0


def layer_stats(inputs):
    center = inputs - jnp.mean(inputs, -1, keepdims=True)
    inverse = lax.rsqrt(jnp.mean(center * center, -1, keepdims=True) + NORM_EPS)
    return (center * inverse, inverse)


def layer_back(grad_out, normed, inverse, gain_row):
    scaled = grad_out * gain_row
    grad_in = inverse * (
        scaled
        - jnp.mean(scaled, -1, keepdims=True)
        - normed * jnp.mean(scaled * normed, -1, keepdims=True)
    )
    return (grad_in, jnp.sum(grad_out * normed, 0))


def time_features(timesteps):
    halfway = NTIME // 2
    frequency = jnp.exp(jnp.arange(halfway, dtype=jnp.float32) * (math.log(64.0) / halfway))
    moment = (timesteps.astype(jnp.float32) + 0.5) / NTIME
    phase = 2.0 * math.pi * moment[:, None] * frequency[None, :]
    return jnp.concatenate([jnp.cos(phase), jnp.sin(phase)], 1)


def rope_tables(positions_count, offset):
    halfway = HD // 2
    frequency = jnp.exp(jnp.arange(halfway, dtype=jnp.float32) * (-2.0 * math.log(10000.0) / HD))
    positions = (jnp.arange(positions_count, dtype=jnp.int32) + offset).astype(jnp.float32)
    angles = positions[:, None] * frequency[None, :]
    return (jnp.concatenate([jnp.cos(angles)] * 2, -1), jnp.concatenate([jnp.sin(angles)] * 2, -1))


def rotate(values, cosine_table, sine_table):
    halfway = HD // 2
    turned = jnp.concatenate([-values[..., halfway:], values[..., :halfway]], -1)
    return values * cosine_table[:, None, :] + turned * sine_table[:, None, :]


def rotate_back(gradient, cosine_table, sine_table):
    halfway = HD // 2
    product = gradient * sine_table[:, None, :]
    return gradient * cosine_table[:, None, :] + jnp.concatenate(
        [product[..., halfway:], -product[..., :halfway]], -1
    )


def to_matrices(blocks):
    per_side = D // BLK
    return blocks.reshape(4, per_side, per_side, BLK, BLK).transpose(0, 1, 3, 2, 4).reshape(4, D, D)


def to_blocks(matrices):
    per_side = D // BLK
    return (
        matrices.reshape(4, per_side, BLK, per_side, BLK)
        .transpose(0, 1, 3, 2, 4)
        .reshape(4 * per_side * per_side, BLK, BLK)
    )


def normalize(vectors):
    return vectors * lax.rsqrt(jnp.sum(vectors * vectors, -1, keepdims=True) + POOL_EPS)


def contrast_loss(pooled_audio, pooled_text, negatives):
    audio_unit_vectors = normalize(pooled_audio)
    text_unit_vectors = normalize(pooled_text)
    positive_pairs = jnp.sum(audio_unit_vectors * text_unit_vectors, -1) / CONTRAST_TEMP
    negative_pairs = (
        jnp.einsum(
            "ux,uax->ua", audio_unit_vectors, text_unit_vectors[negatives], precision=BEST_PRECISION
        )
        / CONTRAST_TEMP
    )
    scores = jnp.concatenate([positive_pairs[:, None], negative_pairs], 1)
    peak_score = jnp.max(scores, -1, keepdims=True)
    logsum = peak_score[:, 0] + jnp.log(jnp.sum(jnp.exp(scores - peak_score), -1))
    return jnp.sum(logsum - positive_pairs)


def item_scores(one_query, one_key, one_bias):
    scores = jnp.einsum("fhd,khd->hfk", one_query, one_key, preferred_element_type=jnp.float32)
    return scores * SCORE_SCALE + one_bias


def attend_forward(queries, all_keys, values, key_bias):

    def single(pieces):
        one_query, one_key, one_value, one_bias = pieces
        scores = item_scores(one_query, one_key, one_bias)
        peak_score = jnp.max(scores, -1, keepdims=True)
        weights = jnp.exp(scores - peak_score)
        row_total = jnp.sum(weights, -1, keepdims=True)
        mixture = jnp.einsum(
            "hfk,khd->fhd",
            (weights / row_total).astype(jnp.bfloat16),
            one_value,
            preferred_element_type=jnp.float32,
        )
        return (mixture.astype(jnp.bfloat16), peak_score + jnp.log(row_total))

    return lax.map(single, (queries, all_keys, values, key_bias))


def attend_backward(queries, all_keys, values, key_bias, logsums, grad_mixture):

    def single(pieces):
        one_query, one_key, one_value, one_bias, one_logsum, grad_rows = pieces
        attention = jnp.exp(item_scores(one_query, one_key, one_bias) - one_logsum)
        grad_attention = jnp.einsum(
            "fhd,khd->hfk", grad_rows, one_value, preferred_element_type=jnp.float32
        )
        grad_value = jnp.einsum(
            "hfk,fhd->khd",
            attention.astype(jnp.bfloat16),
            grad_rows,
            preferred_element_type=jnp.float32,
        )
        grad_scores = attention * (
            grad_attention - jnp.sum(attention * grad_attention, -1, keepdims=True)
        )
        grad_scores = grad_scores.astype(jnp.bfloat16)
        grad_query = (
            jnp.einsum("hfk,khd->fhd", grad_scores, one_key, preferred_element_type=jnp.float32)
            * SCORE_SCALE
        )
        grad_key = (
            jnp.einsum("hfk,fhd->khd", grad_scores, one_query, preferred_element_type=jnp.float32)
            * SCORE_SCALE
        )
        return (grad_query, grad_key, grad_value)

    return lax.map(single, (queries, all_keys, values, key_bias, logsums, grad_mixture))


def feed_forward(rows_in, gate_matrix, down_matrix):
    width = down_matrix.shape[0]
    gate_values = jnp.dot(rows_in, gate_matrix, preferred_element_type=jnp.float32)
    gate_part = gate_values[:, :width]
    up_part = gate_values[:, width:]
    sigmoid = jax.nn.sigmoid(gate_part)
    silu_value = gate_part * sigmoid
    hidden = (silu_value * up_part).astype(jnp.bfloat16)
    partial_out = jnp.dot(hidden, down_matrix, preferred_element_type=jnp.float32)
    return (partial_out, (hidden, gate_part, up_part, sigmoid, silu_value))


def feed_back(rows_in, gate_matrix, down_matrix, kept, grad_low):
    hidden, gate_part, up_part, sigmoid, silu_value = kept
    grad_down = jnp.einsum("rf,rd->fd", hidden, grad_low, preferred_element_type=jnp.float32)
    grad_hidden = jnp.einsum("rd,fd->rf", grad_low, down_matrix, preferred_element_type=jnp.float32)
    grad_gate = grad_hidden * up_part * sigmoid * (1.0 + gate_part * (1.0 - sigmoid))
    grad_pair = jnp.concatenate([grad_gate, grad_hidden * silu_value], 1).astype(jnp.bfloat16)
    grad_gate_up = jnp.einsum("rd,rg->dg", rows_in, grad_pair, preferred_element_type=jnp.float32)
    grad_rows = jnp.einsum("rg,dg->rd", grad_pair, gate_matrix, preferred_element_type=jnp.float32)
    return (grad_rows, grad_gate_up, grad_down)


def adam_update(weight, first_moment, second_moment, gradient, rate):
    first_moment = BETA_FIRST * first_moment + (1.0 - BETA_FIRST) * gradient
    second_moment = BETA_SECOND * second_moment + (1.0 - BETA_SECOND) * gradient * gradient
    corrected = first_moment / (1.0 - BETA_FIRST**STEP)
    scaled = second_moment / (1.0 - BETA_SECOND**STEP)
    weight = weight - rate * (corrected / (jnp.sqrt(scaled) + ADAM_EPS) + WEIGHT_DECAY * weight)
    return (first_moment, second_moment, weight)


def shampoo_update(slots_now, gradient, left_stat, right_stat, left_root, right_root):
    left_stat = STAT_DECAY * left_stat + (1.0 - STAT_DECAY) * jnp.einsum(
        "sij,skj->sik", gradient, gradient, precision=BEST_PRECISION
    )
    right_stat = STAT_DECAY * right_stat + (1.0 - STAT_DECAY) * jnp.einsum(
        "sji,sjk->sik", gradient, gradient, precision=BEST_PRECISION
    )
    inner = jnp.einsum("sij,sjk->sik", gradient, right_root, precision=BEST_PRECISION)
    direction = jnp.einsum("sij,sjk->sik", left_root, inner, precision=BEST_PRECISION)
    return (
        left_stat,
        right_stat,
        slots_now - SHAMPOO_RATE * (direction + WEIGHT_DECAY * slots_now),
    )


def shards(
    latents,
    noise_field,
    timesteps,
    text_tokens,
    text_lengths,
    negatives,
    assignment,
    end_weights,
    time_table,
    square_slots,
    cross_weights,
    key_value,
    gate_up,
    down_weight,
    norm_gains,
    first_ends,
    second_ends,
    first_table,
    second_table,
    first_cross,
    second_cross,
    first_key_value,
    second_key_value,
    first_gate_up,
    second_gate_up,
    first_down,
    second_down,
    first_gains,
    second_gains,
    left_stats,
    right_stats,
    left_roots,
    right_roots,
):
    text_index = lax.axis_index("text")
    group_index = lax.axis_index("dp")
    group_count = lax.axis_size("dp")
    text_count_axis = lax.axis_size("text")
    piece_width = FF // (group_count * text_count_axis)
    low_ends = end_weights.astype(jnp.bfloat16)
    low_table = time_table.astype(jnp.bfloat16)
    low_slots = square_slots.astype(jnp.bfloat16)
    low_cross = cross_weights.astype(jnp.bfloat16)
    low_pairs = key_value.astype(jnp.bfloat16)
    low_gains = norm_gains.astype(jnp.bfloat16)
    low_gate = gate_up.astype(jnp.bfloat16)
    low_down = down_weight.astype(jnp.bfloat16)
    group_set = (
        lax.all_gather(low_ends, "text", axis=0, tiled=True),
        lax.all_gather(low_table, "text", axis=0, tiled=True),
        lax.all_gather(low_slots, "text", axis=0, tiled=True),
        lax.all_gather(low_cross, "text", axis=0, tiled=True),
        lax.all_gather(low_pairs, "text", axis=0, tiled=True),
        lax.all_gather(low_gains, "text", axis=0, tiled=True),
        lax.all_gather(low_gate, "text", axis=0, tiled=True),
    )
    gate_group = group_set[6].reshape(
        group_set[6].shape[0], 2, group_count, text_count_axis, piece_width
    )
    gate_columns = lax.dynamic_index_in_dim(gate_group, text_index, 3, keepdims=False)
    full_set = (
        lax.all_gather(group_set[0], "dp", axis=0, tiled=True),
        lax.all_gather(group_set[1], "dp", axis=0, tiled=True),
        lax.all_gather(group_set[2], "dp", axis=0, tiled=True),
        lax.all_gather(group_set[3], "dp", axis=0, tiled=True),
        lax.all_gather(group_set[4], "dp", axis=0, tiled=True),
        lax.all_gather(group_set[5], "dp", axis=0, tiled=True),
        lax.all_gather(gate_columns, "dp", axis=0, tiled=True),
        lax.all_gather(low_down, "dp", axis=0, tiled=True),
    )
    ends_full, table_full, slots_full, cross_full, pairs_full, gains_full = full_set[:6]
    gate_full = full_set[6].reshape(D, 2 * group_count * piece_width)
    down_full = full_set[7]
    item_count = latents.shape[0]
    frames_dev = latents.shape[1]
    tokens_dev = text_tokens.shape[1]
    row_count = item_count * frames_dev
    items_total = item_count * group_count
    mse_scale = 1.0 / (items_total * FRAMES * DIN)
    weight_in = ends_full[:, 0, :]
    weight_out = ends_full[:, 1, :]
    gain_values = gains_full.astype(jnp.float32)
    inverse_order = (
        jnp.zeros_like(assignment)
        .at[assignment]
        .set(jnp.arange(assignment.shape[0], dtype=jnp.int32))
    )
    squares = to_matrices(slots_full[inverse_order])
    projection = jnp.concatenate([squares[0], squares[1], squares[2]], 1)
    cosine_table, sine_table = rope_tables(frames_dev, 1 + text_index * frames_dev)
    angles = (timesteps.astype(jnp.float32) + 0.5) * (0.5 * math.pi / NTIME)
    signal = jnp.cos(angles)[:, None, None]
    spread = jnp.sin(angles)[:, None, None]
    noised = (signal * latents + spread * noise_field).astype(jnp.bfloat16).reshape(row_count, DIN)
    residual = jnp.einsum("rc,dc->rd", noised, weight_in, preferred_element_type=jnp.float32)
    normed_one, inverse_one = layer_stats(residual)
    input_one = (normed_one * gain_values[:, 0]).astype(jnp.bfloat16)
    features = time_features(timesteps).astype(jnp.bfloat16)
    embeds = jnp.dot(features, table_full, preferred_element_type=jnp.float32)
    normed_time, inverse_time = layer_stats(embeds)
    input_time = (normed_time * gain_values[:, 0]).astype(jnp.bfloat16)
    joined_rows = jnp.dot(input_one, projection, preferred_element_type=jnp.float32)
    head_shape = (item_count, frames_dev, HEADS, HD)
    rot_queries = rotate(joined_rows[:, :D].reshape(head_shape), cosine_table, sine_table).astype(
        jnp.bfloat16
    )
    rot_keys = rotate(
        joined_rows[:, D : 2 * D].reshape(head_shape), cosine_table, sine_table
    ).astype(jnp.bfloat16)
    value_rows = joined_rows[:, 2 * D :].astype(jnp.bfloat16).reshape(item_count, frames_dev, D)
    time_pair = jnp.dot(input_time, projection[:, D:], preferred_element_type=jnp.float32).astype(
        jnp.bfloat16
    )
    keys_all, values_all = (
        lax.all_gather(rot_keys.reshape(item_count, frames_dev, D), "text", axis=1, tiled=True),
        lax.all_gather(value_rows, "text", axis=1, tiled=True),
    )
    key_count = keys_all.shape[1] + 1
    all_keys = jnp.concatenate([time_pair[:, None, :D], keys_all], 1).reshape(
        item_count, key_count, HEADS, HD
    )
    all_values = jnp.concatenate([time_pair[:, None, D:], values_all], 1).reshape(
        item_count, key_count, HEADS, HD
    )
    self_bias = jnp.zeros((item_count, key_count), jnp.float32)
    mixed_self, logsum_self = attend_forward(rot_queries, all_keys, all_values, self_bias)
    mixed_flat = mixed_self.reshape(row_count, D)
    after_self = residual + jnp.dot(mixed_flat, squares[3], preferred_element_type=jnp.float32)
    normed_two, inverse_two = layer_stats(after_self)
    input_two = (normed_two * gain_values[:, 1]).astype(jnp.bfloat16)
    cross_queries = jnp.dot(
        input_two, cross_full[:, 0, :], preferred_element_type=jnp.float32
    ).astype(jnp.bfloat16)
    cross_heads = cross_queries.reshape(head_shape)
    projected = jnp.dot(
        text_tokens.reshape(item_count * tokens_dev, DT),
        pairs_full,
        preferred_element_type=jnp.float32,
    )
    projected = projected.astype(jnp.bfloat16).reshape(item_count, tokens_dev, 2 * D)
    text_all = lax.all_gather(projected, "text", axis=1, tiled=True)
    text_count = text_all.shape[1]
    valid_keys = jnp.arange(text_count, dtype=jnp.int32)[None, :] < text_lengths[:, None]
    cross_bias = jnp.where(valid_keys, 0.0, MASK_VALUE).astype(jnp.float32)
    text_keys = text_all[:, :, :D].reshape(item_count, text_count, HEADS, HD)
    text_values = text_all[:, :, D:].reshape(item_count, text_count, HEADS, HD)
    mixed_cross, logsum_cross = attend_forward(cross_heads, text_keys, text_values, cross_bias)
    cross_flat = mixed_cross.reshape(row_count, D)
    after_cross = after_self + jnp.dot(
        cross_flat, cross_full[:, 1, :], preferred_element_type=jnp.float32
    )
    normed_three, inverse_three = layer_stats(after_cross)
    input_three = (normed_three * gain_values[:, 2]).astype(jnp.bfloat16)
    feed_rows = lax.all_gather(
        input_three.reshape(item_count, frames_dev, D), "text", axis=1, tiled=True
    ).reshape(-1, D)
    feed_out, feed_kept = feed_forward(feed_rows, gate_full, down_full)
    down_out = (
        lax.psum_scatter(
            feed_out.reshape(item_count, -1, D).astype(jnp.bfloat16),
            "text",
            scatter_dimension=1,
            tiled=True,
        )
        .astype(jnp.float32)
        .reshape(row_count, D)
    )
    output_rows = after_cross + down_out
    output_low = output_rows.astype(jnp.bfloat16)
    predicted = jnp.dot(output_low, weight_out, preferred_element_type=jnp.float32).reshape(
        latents.shape
    )
    errors = predicted - (signal * noise_field - spread * latents)
    lengths_float = text_lengths.astype(jnp.float32)
    own_valid = (text_index * tokens_dev + jnp.arange(tokens_dev, dtype=jnp.int32))[
        None, :
    ] < text_lengths[:, None]
    own_mask = own_valid.astype(jnp.float32)
    audio_part = jnp.sum(output_rows.reshape(item_count, frames_dev, D), 1)
    text_part = (
        jnp.sum(projected[:, :, :D].astype(jnp.float32) * own_mask[:, :, None], 1)
        / lengths_float[:, None]
    )
    pooled_set = (
        lax.all_gather(audio_part, ("dp", "text"), axis=0, tiled=True),
        lax.all_gather(text_part, ("dp", "text"), axis=0, tiled=True),
        lax.all_gather(negatives.astype(jnp.float32), ("dp", "text"), axis=0, tiled=True),
    )
    audio_pooled = (
        jnp.sum(pooled_set[0].reshape(group_count, text_count_axis, item_count, D), 1).reshape(
            -1, D
        )
        / FRAMES
    )
    text_pooled = jnp.sum(
        pooled_set[1].reshape(group_count, text_count_axis, item_count, D), 1
    ).reshape(-1, D)
    negative_rows = pooled_set[2].reshape(group_count, text_count_axis, item_count, -1)[:, 0]
    negative_rows = negative_rows.reshape(items_total, -1).astype(jnp.int32)
    contrast_value, contrast_back = jax.vjp(
        partial(contrast_loss, negatives=negative_rows), audio_pooled, text_pooled
    )
    grad_audio_all, grad_text_all = contrast_back(jnp.float32(CONTRAST_WEIGHT / items_total))
    grad_audio = lax.dynamic_slice_in_dim(grad_audio_all, group_index * item_count, item_count, 0)
    grad_text = lax.dynamic_slice_in_dim(grad_text_all, group_index * item_count, item_count, 0)
    grad_predicted = (2.0 * mse_scale * errors).astype(jnp.bfloat16).reshape(row_count, DIN)
    grad_out_weight = jnp.einsum(
        "rd,rc->dc", output_low, grad_predicted, preferred_element_type=jnp.float32
    )
    grad_output = jnp.einsum(
        "rc,dc->rd", grad_predicted, weight_out, preferred_element_type=jnp.float32
    )
    grad_output = (
        grad_output.reshape(item_count, frames_dev, D) + grad_audio[:, None, :] / FRAMES
    ).reshape(row_count, D)
    grad_down_in = grad_output.astype(jnp.bfloat16)
    grad_feed_rows = lax.all_gather(
        grad_down_in.reshape(item_count, frames_dev, D), "text", axis=1, tiled=True
    ).reshape(-1, D)
    grad_feed_in, grad_gate_up, grad_down = feed_back(
        feed_rows, gate_full, down_full, feed_kept, grad_feed_rows
    )
    grad_input_three = (
        lax.psum_scatter(
            grad_feed_in.reshape(item_count, -1, D).astype(jnp.bfloat16),
            "text",
            scatter_dimension=1,
            tiled=True,
        )
        .astype(jnp.float32)
        .reshape(row_count, D)
    )
    grad_after_cross, gain_three = layer_back(
        grad_input_three, normed_three, inverse_three, gain_values[:, 2]
    )
    grad_after_cross = grad_after_cross + grad_output
    grad_cross_in = grad_after_cross.astype(jnp.bfloat16)
    grad_cross_out = jnp.einsum(
        "rd,re->de", cross_flat, grad_cross_in, preferred_element_type=jnp.float32
    )
    grad_mixed_cross = jnp.einsum(
        "re,de->rd", grad_cross_in, cross_full[:, 1, :], preferred_element_type=jnp.float32
    )
    grad_mixed_cross = grad_mixed_cross.astype(jnp.bfloat16).reshape(head_shape)
    grad_cq, grad_text_keys, grad_text_values = attend_backward(
        cross_heads, text_keys, text_values, cross_bias, logsum_cross, grad_mixed_cross
    )
    grad_cq_low = grad_cq.reshape(row_count, D).astype(jnp.bfloat16)
    grad_cross_query = jnp.einsum(
        "rd,re->de", input_two, grad_cq_low, preferred_element_type=jnp.float32
    )
    grad_input_two = jnp.einsum(
        "re,de->rd", grad_cq_low, cross_full[:, 0, :], preferred_element_type=jnp.float32
    )
    grad_pairs = jnp.concatenate(
        [
            grad_text_keys.reshape(item_count, text_count, D),
            grad_text_values.reshape(item_count, text_count, D),
        ],
        2,
    )
    grad_own_pairs = lax.psum_scatter(
        grad_pairs.astype(jnp.bfloat16), "text", scatter_dimension=1, tiled=True
    ).astype(jnp.float32)
    pooled_grad = own_mask[:, :, None] * (grad_text[:, None, :] / lengths_float[:, None, None])
    grad_own_pairs = grad_own_pairs + jnp.concatenate([pooled_grad, jnp.zeros_like(pooled_grad)], 2)
    grad_own_pairs = grad_own_pairs.astype(jnp.bfloat16).reshape(item_count * tokens_dev, 2 * D)
    grad_textside = jnp.einsum(
        "tc,tk->ck",
        text_tokens.reshape(item_count * tokens_dev, DT),
        grad_own_pairs,
        preferred_element_type=jnp.float32,
    )
    grad_after_self, gain_two = layer_back(
        grad_input_two, normed_two, inverse_two, gain_values[:, 1]
    )
    grad_after_self = grad_after_self + grad_after_cross
    grad_self_in = grad_after_self.astype(jnp.bfloat16)
    grad_attn_out = jnp.einsum(
        "rd,re->de", mixed_flat, grad_self_in, preferred_element_type=jnp.float32
    )
    grad_mixed_self = jnp.einsum(
        "re,de->rd", grad_self_in, squares[3], preferred_element_type=jnp.float32
    )
    grad_mixed_self = grad_mixed_self.astype(jnp.bfloat16).reshape(head_shape)
    grad_rot_queries, grad_keys, value_gradients = attend_backward(
        rot_queries, all_keys, all_values, self_bias, logsum_self, grad_mixed_self
    )
    grad_keys_own, grad_values_own = (
        lax.psum_scatter(
            grad_keys[:, 1:].reshape(item_count, key_count - 1, D).astype(jnp.bfloat16),
            "text",
            scatter_dimension=1,
            tiled=True,
        ).astype(jnp.float32),
        lax.psum_scatter(
            value_gradients[:, 1:].reshape(item_count, key_count - 1, D).astype(jnp.bfloat16),
            "text",
            scatter_dimension=1,
            tiled=True,
        ).astype(jnp.float32),
    )
    grad_queries = (
        rotate_back(grad_rot_queries, cosine_table, sine_table)
        .astype(jnp.bfloat16)
        .reshape(row_count, D)
    )
    grad_key_rows = rotate_back(grad_keys_own.reshape(head_shape), cosine_table, sine_table)
    grad_key_rows = grad_key_rows.astype(jnp.bfloat16).reshape(row_count, D)
    grad_joined = jnp.concatenate(
        [grad_queries, grad_key_rows, grad_values_own.astype(jnp.bfloat16).reshape(row_count, D)], 1
    )
    grad_projection = jnp.einsum(
        "rd,rk->dk", input_one, grad_joined, preferred_element_type=jnp.float32
    )
    grad_input_one = jnp.einsum(
        "rk,dk->rd", grad_joined, projection, preferred_element_type=jnp.float32
    )
    grad_time_pair = jnp.concatenate(
        [grad_keys[:, 0].reshape(item_count, D), value_gradients[:, 0].reshape(item_count, D)], 1
    )
    time_rows = jnp.dot(input_time.astype(jnp.float32).T, grad_time_pair, precision=BEST_PRECISION)
    grad_projection = grad_projection + jnp.concatenate(
        [jnp.zeros((D, D), jnp.float32), time_rows], 1
    )
    grad_input_time = jnp.einsum(
        "ik,dk->id", grad_time_pair, projection[:, D:].astype(jnp.float32), precision=BEST_PRECISION
    )
    grad_residual, gain_one = layer_back(grad_input_one, normed_one, inverse_one, gain_values[:, 0])
    grad_residual = (grad_residual + grad_after_self).astype(jnp.bfloat16)
    grad_embeds, gain_time = layer_back(
        grad_input_time, normed_time, inverse_time, gain_values[:, 0]
    )
    grad_in_weight = jnp.einsum(
        "rd,rc->dc", grad_residual, noised, preferred_element_type=jnp.float32
    )
    grad_table = jnp.dot(features.astype(jnp.float32).T, grad_embeds, precision=BEST_PRECISION)
    grad_gains = jnp.stack([gain_one + gain_time, gain_two, gain_three], 1)
    grad_ends = jnp.stack([grad_in_weight, grad_out_weight], 1)
    grad_cross = jnp.stack([grad_cross_query, grad_cross_out], 1)
    grad_squares = jnp.stack(
        [
            grad_projection[:, :D],
            grad_projection[:, D : 2 * D],
            grad_projection[:, 2 * D :],
            grad_attn_out,
        ],
        0,
    )
    grad_slots = jnp.take(to_blocks(grad_squares), assignment, axis=0)
    gate_pieces = grad_gate_up.reshape(D, 2, group_count, piece_width)
    group_grads = (
        lax.psum_scatter(
            grad_ends.astype(jnp.bfloat16), "dp", scatter_dimension=0, tiled=True
        ).astype(jnp.float32),
        lax.psum_scatter(
            grad_table.astype(jnp.bfloat16), "dp", scatter_dimension=0, tiled=True
        ).astype(jnp.float32),
        lax.psum_scatter(
            grad_slots.astype(jnp.bfloat16), "dp", scatter_dimension=0, tiled=True
        ).astype(jnp.float32),
        lax.psum_scatter(
            grad_cross.astype(jnp.bfloat16), "dp", scatter_dimension=0, tiled=True
        ).astype(jnp.float32),
        lax.psum_scatter(
            grad_textside.astype(jnp.bfloat16), "dp", scatter_dimension=0, tiled=True
        ).astype(jnp.float32),
        lax.psum_scatter(
            grad_gains.astype(jnp.bfloat16), "dp", scatter_dimension=0, tiled=True
        ).astype(jnp.float32),
        lax.psum_scatter(
            gate_pieces.astype(jnp.bfloat16), "dp", scatter_dimension=0, tiled=True
        ).astype(jnp.float32),
        lax.psum_scatter(
            grad_down.astype(jnp.bfloat16), "dp", scatter_dimension=0, tiled=True
        ).astype(jnp.float32),
    )
    placing = (jnp.arange(text_count_axis, dtype=jnp.int32) == text_index).astype(jnp.float32)
    spread_gate = group_grads[6][:, :, :, None, :] * placing[None, None, None, :, None]
    spread_gate = spread_gate.reshape(spread_gate.shape[0], 2 * FF)
    owned = (
        lax.psum_scatter(
            group_grads[0].astype(jnp.bfloat16), "text", scatter_dimension=0, tiled=True
        ).astype(jnp.float32),
        lax.psum_scatter(
            group_grads[1].astype(jnp.bfloat16), "text", scatter_dimension=0, tiled=True
        ).astype(jnp.float32),
        lax.psum_scatter(
            group_grads[2].astype(jnp.bfloat16), "text", scatter_dimension=0, tiled=True
        ).astype(jnp.float32),
        lax.psum_scatter(
            group_grads[3].astype(jnp.bfloat16), "text", scatter_dimension=0, tiled=True
        ).astype(jnp.float32),
        lax.psum_scatter(
            group_grads[4].astype(jnp.bfloat16), "text", scatter_dimension=0, tiled=True
        ).astype(jnp.float32),
        lax.psum_scatter(
            group_grads[5].astype(jnp.bfloat16), "text", scatter_dimension=0, tiled=True
        ).astype(jnp.float32),
        lax.psum_scatter(
            spread_gate.astype(jnp.bfloat16), "text", scatter_dimension=0, tiled=True
        ).astype(jnp.float32),
    )
    reduced = (owned[0], owned[1], owned[2], owned[3], owned[4], owned[6], group_grads[7], owned[5])
    square_sum = jnp.zeros((), jnp.float32)
    for member in reduced:
        square_sum = square_sum + jnp.sum(member * member)
    loss_part = jnp.sum(errors * errors) * mse_scale
    totals = lax.psum((square_sum, loss_part), ("dp", "text"))
    loss_total = totals[1] + CONTRAST_WEIGHT * contrast_value / items_total
    gradient_norm = jnp.sqrt(totals[0])
    masters = (
        end_weights,
        time_table,
        square_slots,
        cross_weights,
        key_value,
        gate_up,
        down_weight,
        norm_gains,
    )
    firsts = (
        first_ends,
        first_table,
        None,
        first_cross,
        first_key_value,
        first_gate_up,
        first_down,
        first_gains,
    )
    seconds = (
        second_ends,
        second_table,
        None,
        second_cross,
        second_key_value,
        second_gate_up,
        second_down,
        second_gains,
    )
    return finish(
        loss_total,
        gradient_norm,
        reduced,
        masters,
        firsts,
        seconds,
        (left_stats, right_stats, left_roots, right_roots),
    )


def swap(values, axis, bit=1):
    return lax.ppermute(values, axis, [(i, i ^ bit) for i in range(lax.axis_size(axis))])


def pick(values, position, axis=0):
    return lax.dynamic_index_in_dim(values, position, axis, keepdims=False)


def grow(values, axis):
    bit = 1
    while bit < lax.axis_size(axis):
        values = jnp.concatenate([values, swap(values, axis, bit)], 0)
        bit *= 2
    return values


def own_quarters(values, core, line):
    pair = jnp.concatenate([values, swap(values, "c")], 0)
    pieces = []
    for offset in range(4):
        target = line ^ offset
        piece = pick(pair, ((target // 2) ^ core) * 2 + target % 2)
        pieces.append(swap(piece, "z", offset) if offset else piece)
    return jnp.concatenate(pieces, 0)


def gather_pieces(block, first, second):
    base = grow(block[None], "z")
    near = swap(base, first)
    across = swap(base, second)
    far = swap(near, second)
    return (base, near, across, far) if first == "x" else (base, across, near, far)


def place_kernel(spot, *refs):
    sources, target = refs[:4], refs[4]
    quadrant = pl.program_id(0)
    pair = target.shape[1] == 2
    for index_value, source in enumerate(sources):

        @pl.when(quadrant == index_value)
        def store():
            if pair:
                target[0, spot[2], 0] = source[0, 0]
                target[0, 1 - spot[2], 0] = source[0, 1]
            else:
                target[0, 0, 0] = source[0, 0]


def place(pieces, spot):
    lines, cores, height, width = pieces[0].shape

    def source_map(index_value):
        def at(quadrant, line, where):
            return (jnp.clip((quadrant - index_value) * lines + line, 0, lines - 1), 0, 0, 0)

        return at

    placed = pl.pallas_call(
        place_kernel,
        grid_spec=pltpu.PrefetchScalarGridSpec(
            num_scalar_prefetch=1,
            grid=(4, lines),
            in_specs=[
                pl.BlockSpec((1, cores, height, width), source_map(index_value))
                for index_value in range(4)
            ],
            out_specs=pl.BlockSpec(
                (1, cores, 1, height, width),
                lambda quadrant, line, where: (where[0] ^ quadrant, 0, where[1] ^ line, 0, 0),
            ),
        ),
        out_shape=jax.ShapeDtypeStruct((4, cores, lines, height, width), pieces[0].dtype),
        cost_estimate=pl.CostEstimate(
            flops=0, bytes_accessed=16 * lines * cores * height * width, transcendentals=0
        ),
    )(spot, *pieces)
    return placed.reshape(4 * cores * lines * height, width)


def half_block(tile, is_right, to_right):
    wide = tile.astype(jnp.float32)
    turned = pltpu.roll(wide, BLK, 1)
    return jnp.where(is_right == to_right, wide, turned)


def assemble_kernel(left_at, right_at, left_half, right_half, left, right, target):
    step = pl.program_id(0)
    left_tile = half_block(left[0], left_half[step], 0)
    right_tile = half_block(right[0], right_half[step], 1)
    lane = lax.broadcasted_iota(jnp.int32, left_tile.shape, 1)
    target[...] = jnp.where(lane < BLK, left_tile, right_tile).astype(target.dtype)


def assemble(pairs, places, rights, rows, columns):
    steps = places.shape[0] // 2
    across = columns // (2 * BLK)
    return pl.pallas_call(
        assemble_kernel,
        grid_spec=pltpu.PrefetchScalarGridSpec(
            num_scalar_prefetch=4,
            grid=(steps,),
            in_specs=[
                pl.BlockSpec((1, BLK, 2 * BLK), lambda step, a, b, c, d: (a[step], 0, 0)),
                pl.BlockSpec((1, BLK, 2 * BLK), lambda step, a, b, c, d: (b[step], 0, 0)),
            ],
            out_specs=pl.BlockSpec(
                (BLK, 2 * BLK), lambda step, a, b, c, d: (step // across, step % across)
            ),
        ),
        out_shape=jax.ShapeDtypeStruct((rows, columns), pairs.dtype),
        cost_estimate=pl.CostEstimate(flops=0, bytes_accessed=6 * rows * columns, transcendentals=0),
    )(places[0::2], places[1::2], rights[0::2], rights[1::2], pairs, pairs)


def collect_kernel(left_at, right_at, left_half, right_half, left, right, target):
    step = pl.program_id(0)
    left_tile = half_block(left[...], left_half[step] % 2, 0)
    right_tile = half_block(right[...], right_half[step] % 2, 1)
    left_tile = jnp.where(left_half[step] < 2, left_tile, 0.0)
    right_tile = jnp.where(right_half[step] < 2, right_tile, 0.0)
    lane = lax.broadcasted_iota(jnp.int32, left_tile.shape, 1)
    target[0] = jnp.where(lane < BLK, left_tile, right_tile).astype(target.dtype)


def collect(matrix, places, halves):
    steps = places.shape[0] // 2
    across = matrix.shape[1] // (2 * BLK)
    return pl.pallas_call(
        collect_kernel,
        grid_spec=pltpu.PrefetchScalarGridSpec(
            num_scalar_prefetch=4,
            grid=(steps,),
            in_specs=[
                pl.BlockSpec(
                    (BLK, 2 * BLK), lambda step, a, b, c, d: (a[step] // across, a[step] % across)
                ),
                pl.BlockSpec(
                    (BLK, 2 * BLK), lambda step, a, b, c, d: (b[step] // across, b[step] % across)
                ),
            ],
            out_specs=pl.BlockSpec((1, BLK, 2 * BLK), lambda step, a, b, c, d: (step, 0, 0)),
        ),
        out_shape=jax.ShapeDtypeStruct((steps, BLK, 2 * BLK), matrix.dtype),
        cost_estimate=pl.CostEstimate(
            flops=0, bytes_accessed=6 * matrix.size, transcendentals=0
        ),
    )(places[0::2], places[1::2], halves[0::2], halves[1::2], matrix, matrix)


def low_sum(*terms):
    total = terms[0].astype(jnp.float32)
    for term in terms[1:]:
        total = total + term.astype(jnp.float32)
    return total


def reduce_quads(quads, first, line, line_axis):
    mine, near_x, near_y, far = quads
    if first == "y":
        from_far = swap(far, "y")
        from_side = swap(near_y, "y")
        onward = low_sum(near_x, from_far).astype(jnp.bfloat16)
        from_onward = swap(onward, "x")
    else:
        from_far = swap(far, "x")
        from_side = swap(near_x, "x")
        onward = low_sum(near_y, from_far).astype(jnp.bfloat16)
        from_onward = swap(onward, "y")
    return reduce_line((mine, from_side, from_onward), line, line_axis)


def reduce_line(terms, line, line_axis):
    def part(index_value):
        return low_sum(*[pick(term, index_value, line_axis) for term in terms])

    far_send = jnp.stack(
        [part((line ^ 2) & 2), part(((line ^ 2) & 2) + 1)], 0
    ).astype(jnp.bfloat16)
    received = swap(far_send, "z", 2)
    near_send = part(line ^ 1) + pick(received, (line ^ 1) % 2).astype(jnp.float32)
    last = swap(near_send.astype(jnp.bfloat16), "z", 1)
    return part(line) + low_sum(pick(received, line % 2), last)


def reduce_small(values, row, column, line):
    for axis, me in (("y", row), ("x", column)):
        received = swap(pick(values, 1 - me).astype(jnp.bfloat16), axis)
        values = pick(values, me) + received.astype(jnp.float32)
    return reduce_line((values,), line, 0)


def on_both(partial_sum):
    low = partial_sum.astype(jnp.bfloat16)
    return low_sum(low, swap(low, "c"))


def tdot(left, right):
    return lax.dot_general(left, right, (((0,), (0,)), ((), ())), preferred_element_type=jnp.float32)


def dot_back(left, right):
    return lax.dot_general(left, right, (((1,), (1,)), ((), ())), preferred_element_type=jnp.float32)


def item_per_chip(
    latents,
    noise_field,
    timesteps,
    text_tokens,
    text_lengths,
    negatives,
    assignment,
    end_weights,
    time_table,
    square_slots,
    cross_weights,
    key_value,
    gate_up,
    down_weight,
    norm_gains,
    first_ends,
    second_ends,
    first_table,
    second_table,
    first_cross,
    second_cross,
    first_key_value,
    second_key_value,
    first_gate_up,
    second_gate_up,
    first_down,
    second_down,
    first_gains,
    second_gains,
    left_stats,
    right_stats,
    left_roots,
    right_roots,
):
    bf16, f32 = jnp.bfloat16, jnp.float32
    row, column = lax.axis_index("y"), lax.axis_index("x")
    core, line = lax.axis_index("c"), lax.axis_index("z")
    plane = 2 * row + column
    item = 4 * plane + line
    spot = jnp.stack([plane, line, core]).astype(jnp.int32)
    quads = range(4)
    half = D // 2
    heads = HEADS // 2
    items_total = 16
    mse_scale = 1.0 / (items_total * FRAMES * DIN)

    pack = jnp.concatenate(
        [
            end_weights.reshape(4, D),
            time_table,
            jnp.pad(norm_gains.reshape(1, 144), ((0, 3), (0, D - 144))),
        ],
        0,
    ).astype(bf16)
    packs = pack[None]
    for axis in ("c", "z", "x", "y"):
        packs = grow(packs, axis)
    owner = jnp.arange(32, dtype=jnp.int32)
    packs = packs[
        ((owner // 4) % 2 ^ core) + 2 * (owner % 4 ^ line) + 8 * (owner // 8 ^ plane)
    ]
    ends_full = packs[:, :4].reshape(D, 2, DIN)
    table_full = packs[:, 4:12].reshape(NTIME, D)
    gain_values = packs[:, 12, :144].reshape(D, 3).astype(f32)
    weight_in, weight_out = ends_full[:, 0, :], ends_full[:, 1, :]

    low_slots = square_slots.astype(bf16).reshape(4, 2, BLK, BLK)
    low_pairs = jnp.concatenate([low_slots[:, 0], low_slots[:, 1]], 2)
    slot_pieces = []
    for color, (first, second) in enumerate((("x", "y"), ("y", "x"))):
        pieces = gather_pieces(low_pairs[2 * color : 2 * color + 2], first, second)
        slot_pieces.append(jnp.concatenate(pieces, 0))
    own_pairs = jnp.concatenate(slot_pieces, 0).reshape(64, BLK, 2 * BLK)
    all_pairs = jnp.concatenate([own_pairs, swap(own_pairs, "c")], 0)
    inverse_order = (
        jnp.zeros_like(assignment)
        .at[assignment]
        .set(jnp.arange(assignment.shape[0], dtype=jnp.int32))
    )

    def pair_place(slot):
        device, inner = slot // 8, slot % 8
        place_value = ((device // 4) % 2 ^ core) * 2 + inner // 4
        place_value = (place_value * 4 + (device // 8 ^ plane)) * 4 + (device % 4 ^ line)
        return place_value * 2 + (inner // 2) % 2, inner % 2

    def grid_blocks(matrix, rows, columns):
        return (matrix * 64 + rows * 8 + columns).reshape(-1)

    eight, four = jnp.arange(8, dtype=jnp.int32), jnp.arange(4, dtype=jnp.int32)
    joined_blocks = grid_blocks(
        jnp.arange(3, dtype=jnp.int32)[None, :, None],
        eight[:, None, None],
        (4 * core + four)[None, None, :],
    )
    out_blocks = grid_blocks(3, (4 * core + four)[:, None], eight[None, :])
    places, rights = pair_place(inverse_order[joined_blocks])
    projection = assemble(all_pairs, places, rights, D, 3 * half)
    places, rights = pair_place(inverse_order[out_blocks])
    weight_mix = assemble(all_pairs, places, rights, half, D)

    low_cross = cross_weights.astype(bf16)
    query_both = jnp.stack(
        [
            lax.dynamic_slice_in_dim(low_cross[:, 0, :], core * half, half, 1),
            swap(
                lax.dynamic_slice_in_dim(low_cross[:, 0, :], (1 - core) * half, half, 1), "c"
            ),
        ],
        0,
    )
    cross_query = place(gather_pieces(query_both, "x", "y"), spot)
    out_own = place(gather_pieces(low_cross[None, :, 1, :], "y", "x"), spot)
    out_own = out_own.reshape(2, 2, 1, 4 * 48, D)
    out_kept = pick(out_own, core)
    out_other = swap(pick(out_own, 1 - core), "c")
    cross_out = jnp.where(
        core == 0,
        jnp.concatenate([out_kept, out_other], 1),
        jnp.concatenate([out_other, out_kept], 1),
    ).reshape(half, D)
    low_kv = key_value.astype(bf16)
    kv_weights = []
    for color, (first, second) in enumerate((("x", "y"), ("y", "x"))):
        own = lax.dynamic_slice_in_dim(low_kv, color * D + core * half, half, 1)
        other = lax.dynamic_slice_in_dim(low_kv, color * D + (1 - core) * half, half, 1)
        pieces = gather_pieces(jnp.stack([own, swap(other, "c")], 0), first, second)
        stacked = jnp.stack(pieces, 0)
        stacked = stacked[plane ^ four][:, line ^ four]
        stacked = stacked[:, :, core ^ four[:2]]
        kv_weights.append(stacked.transpose(0, 2, 1, 3, 4).reshape(DT, half))
    kv_own = jnp.concatenate(kv_weights, 1)

    low_gate = gate_up.astype(bf16)

    def unit_columns(which, side):
        return jnp.concatenate(
            [
                lax.dynamic_slice_in_dim(
                    low_gate, which * FF + quadrant * 1536 + side * 768, 768, 1
                )
                for quadrant in quads
            ],
            1,
        )

    gate_sides = []
    for which, (first, second) in enumerate((("x", "y"), ("y", "x"))):
        block = jnp.stack(
            [unit_columns(which, core), swap(unit_columns(which, 1 - core), "c")], 0
        )
        gate_sides.append(place(gather_pieces(block, first, second), spot))
    gate_weight, up_weight = gate_sides
    low_down = down_weight.astype(bf16)
    down_sides = []
    for which, (first, second) in enumerate((("x", "y"), ("y", "x"))):
        block = low_down[None, :, which * half : (which + 1) * half]
        down_sides.append(place(gather_pieces(block, first, second), spot))

    meta = jnp.concatenate([timesteps[:, None], text_lengths[:, None], negatives], 1)
    metas = meta
    for axis in ("c", "x", "y"):
        metas = grow(metas, axis)
    base = 4 * plane + 2 * core
    relative = jnp.arange(items_total, dtype=jnp.int32)
    metas = metas[(item ^ base) ^ relative]
    timestep, text_length = metas[0, 0], metas[0, 1]
    negative_rows = metas[:, 2:]
    frames = own_quarters(jnp.concatenate([latents, noise_field], 2), core, line)
    clean, noise = frames[:, :DIN], frames[:, DIN:]
    tokens = own_quarters(text_tokens, core, line)
    quarter = line ^ four
    frame_positions = (
        (quarter[:, None] * 256 + jnp.arange(256, dtype=jnp.int32)[None, :]).reshape(-1) + 1
    )
    token_slots = (
        quarter[:, None] * 32 + jnp.arange(32, dtype=jnp.int32)[None, :]
    ).reshape(-1)
    halfway = HD // 2
    frequency = jnp.exp(jnp.arange(halfway, dtype=f32) * (-2.0 * math.log(10000.0) / HD))
    turn = frame_positions.astype(f32)[:, None] * frequency[None, :]
    cosine_table = jnp.concatenate([jnp.cos(turn)] * 2, -1)
    sine_table = jnp.concatenate([jnp.sin(turn)] * 2, -1)
    angle = (timestep.astype(f32) + 0.5) * (0.5 * math.pi / NTIME)
    signal, spread = jnp.cos(angle), jnp.sin(angle)
    noised = (signal * clean + spread * noise).astype(bf16)
    target = signal * noise - spread * clean

    residual = dot_back(noised, weight_in)
    normed_one, inverse_one = layer_stats(residual)
    input_one = (normed_one * gain_values[:, 0]).astype(bf16)
    features = time_features(timestep[None]).astype(bf16)
    embeds = jnp.dot(features, table_full, preferred_element_type=f32)
    normed_time, inverse_time = layer_stats(embeds)
    input_time = (normed_time * gain_values[:, 0]).astype(bf16)
    joined_rows = jnp.dot(input_one, projection, preferred_element_type=f32)
    head_shape = (FRAMES, heads, HD)
    rot_queries = rotate(
        joined_rows[:, :half].reshape(head_shape), cosine_table, sine_table
    ).astype(bf16)
    rot_keys = rotate(
        joined_rows[:, half : 2 * half].reshape(head_shape), cosine_table, sine_table
    ).astype(bf16)
    value_rows = joined_rows[:, 2 * half :].astype(bf16)
    time_pair = jnp.dot(input_time, projection[:, half:], preferred_element_type=f32).astype(bf16)
    all_keys = jnp.concatenate([time_pair[:, :half].reshape(1, heads, HD), rot_keys], 0)
    all_values = jnp.concatenate([time_pair[:, half:], value_rows], 0).reshape(-1, heads, HD)
    self_bias = jnp.zeros((1, FRAMES + 1), f32)
    mixed_self, logsum_self = attend_forward(
        rot_queries[None], all_keys[None], all_values[None], self_bias
    )
    mixed_flat = mixed_self.reshape(FRAMES, half)
    after_self = residual + on_both(jnp.dot(mixed_flat, weight_mix, preferred_element_type=f32))
    normed_two, inverse_two = layer_stats(after_self)
    input_two = (normed_two * gain_values[:, 1]).astype(bf16)
    cross_queries = jnp.dot(input_two, cross_query, preferred_element_type=f32).astype(bf16)
    cross_heads = cross_queries.reshape(head_shape)
    projected = jnp.dot(tokens, kv_own, preferred_element_type=f32).astype(bf16)
    valid = token_slots < text_length
    cross_bias = jnp.where(valid, 0.0, MASK_VALUE).astype(f32)[None]
    text_keys = projected[:, :half].reshape(1, -1, heads, HD)
    text_values = projected[:, half:].reshape(1, -1, heads, HD)
    mixed_cross, logsum_cross = attend_forward(
        cross_heads[None], text_keys, text_values, cross_bias
    )
    cross_flat = mixed_cross.reshape(FRAMES, half)
    after_cross = after_self + on_both(jnp.dot(cross_flat, cross_out, preferred_element_type=f32))
    normed_three, inverse_three = layer_stats(after_cross)
    input_three = (normed_three * gain_values[:, 2]).astype(bf16)
    gate_part = jnp.dot(input_three, gate_weight, preferred_element_type=f32)
    up_part = jnp.dot(input_three, up_weight, preferred_element_type=f32)
    sigmoid = jax.nn.sigmoid(gate_part)
    silu_value = gate_part * sigmoid
    hidden = (silu_value * up_part).astype(bf16)
    down_out = jnp.concatenate(
        [on_both(jnp.dot(hidden, side, preferred_element_type=f32)) for side in down_sides], 1
    )
    output_rows = after_cross + down_out
    output_low = output_rows.astype(bf16)
    predicted = jnp.dot(output_low, weight_out, preferred_element_type=f32)
    errors = predicted - target

    length_float = text_length.astype(f32)
    mask = valid.astype(f32)[:, None]
    text_half = jnp.sum(projected[:, :half].astype(f32) * mask, 0) / length_float
    text_rest = swap(text_half, "c")
    text_pool = jnp.where(
        core == 0,
        jnp.concatenate([text_half, text_rest]),
        jnp.concatenate([text_rest, text_half]),
    )
    pools = jnp.stack([jnp.sum(output_rows, 0) / FRAMES, text_pool], 0)[None]
    for axis in ("z", "x", "y"):
        pools = grow(pools, axis)
    inverse_pools = lax.rsqrt(jnp.sum(pools * pools, -1, keepdims=True) + POOL_EPS)
    units = pools * inverse_pools
    audio_units, text_units = units[:, 0], units[:, 1]
    similar = (
        lax.dot_general(
            audio_units, text_units, (((1,), (1,)), ((), ())), precision=BEST_PRECISION
        )
        / CONTRAST_TEMP
    )
    same = jnp.eye(items_total, dtype=f32)
    counts = same + jnp.sum(
        (negative_rows[:, None, :] == (item ^ relative)[None, :, None]).astype(f32), -1
    )
    peak = jnp.max(jnp.where(counts > 0, similar, -jnp.inf), -1, keepdims=True)
    powers = jnp.where(counts > 0, counts * jnp.exp(similar - peak), 0.0)
    totals_row = jnp.sum(powers, -1, keepdims=True)
    contrast_own = peak[0, 0] + jnp.log(totals_row[0, 0]) - similar[0, 0]
    grad_similar = (powers / totals_row - same) * (
        CONTRAST_WEIGHT / items_total / CONTRAST_TEMP
    )
    grad_audio_unit = jnp.sum(grad_similar[0][:, None] * text_units, 0)
    grad_text_unit = jnp.sum(grad_similar[:, 0][:, None] * audio_units, 0)

    def unit_back(gradient, unit, inverse):
        return inverse * (gradient - unit * jnp.sum(unit * gradient))

    grad_audio = unit_back(grad_audio_unit, audio_units[0], inverse_pools[0, 0])
    grad_text = unit_back(grad_text_unit, text_units[0], inverse_pools[0, 1])

    grad_predicted = (2.0 * mse_scale * errors).astype(bf16)
    grad_out_weight = tdot(output_low, grad_predicted)
    grad_output = dot_back(grad_predicted, weight_out) + grad_audio[None, :] / FRAMES
    grad_low = grad_output.astype(bf16)
    reduced_down = []

    def columns_of(values, quadrant, width):
        return lax.dynamic_slice_in_dim(values, (plane ^ quadrant) * width, width, 1)

    for which, first in enumerate(("y", "x")):
        parts = [
            tdot(
                columns_of(hidden, quadrant, 768), grad_low[:, which * half : (which + 1) * half]
            )
            .astype(bf16)
            .reshape(4, 192, half)
            for quadrant in quads
        ]
        reduced_down.append(reduce_quads(parts, first, line, 0))
    grad_down = jnp.concatenate(reduced_down, 1)
    grad_hidden = dot_back(grad_low[:, :half], down_sides[0]) + dot_back(
        grad_low[:, half:], down_sides[1]
    )
    grad_gate = (grad_hidden * up_part * sigmoid * (1.0 + gate_part * (1.0 - sigmoid))).astype(bf16)
    grad_up = (grad_hidden * silu_value).astype(bf16)
    reduced_gate = []
    for gradient, first in ((grad_gate, "y"), (grad_up, "x")):
        parts = [
            tdot(columns_of(input_three, quadrant, 384), gradient)
            .astype(bf16)
            .reshape(2, 4, 48, FF // 2)
            for quadrant in quads
        ]
        both_rows = reduce_quads(parts, first, line, 1)
        other = swap(pick(both_rows, 1 - core).astype(bf16), "c").astype(f32)
        reduced_gate.append((pick(both_rows, core), other))
    gate_columns = []
    for mine, other in reduced_gate:
        sides = (jnp.where(core == 0, mine, other), jnp.where(core == 0, other, mine))
        for quadrant in quads:
            for side in sides:
                gate_columns.append(side[:, quadrant * 768 : (quadrant + 1) * 768])
    grad_gate_up = jnp.concatenate(gate_columns, 1)
    grad_input_three = on_both(dot_back(grad_gate, gate_weight) + dot_back(grad_up, up_weight))
    grad_after_cross, gain_three = layer_back(
        grad_input_three, normed_three, inverse_three, gain_values[:, 2]
    )
    grad_after_cross = grad_after_cross + grad_output
    grad_cross_in = grad_after_cross.astype(bf16)
    cross_rows = tdot(cross_flat, grad_cross_in).astype(bf16).reshape(2, 2, 192, D)
    cross_kept = pick(cross_rows, core, 1)
    cross_received = swap(pick(cross_rows, 1 - core, 1), "c")
    cross_pair = jnp.stack([cross_kept, cross_received], 0)
    parts = [
        pick(pick(cross_pair, row ^ (quadrant // 2) ^ core), column ^ (quadrant % 2)).reshape(
            4, 48, D
        )
        for quadrant in quads
    ]
    grad_cross_out = reduce_quads(parts, "x", line, 0)
    grad_mixed_cross = dot_back(grad_cross_in, cross_out).astype(bf16).reshape(head_shape)
    grad_cq, grad_text_keys, grad_text_values = attend_backward(
        cross_heads[None],
        text_keys,
        text_values,
        cross_bias,
        logsum_cross,
        grad_mixed_cross[None],
    )
    grad_cq_low = grad_cq.reshape(FRAMES, half).astype(bf16)
    parts = [
        tdot(columns_of(input_two, quadrant, 384), grad_cq_low).astype(bf16).reshape(2, 4, 48, half)
        for quadrant in quads
    ]
    both_rows = reduce_quads(parts, "y", line, 1)
    query_other = swap(pick(both_rows, 1 - core).astype(bf16), "c").astype(f32)
    query_mine = pick(both_rows, core)
    grad_cross_query = jnp.where(
        core == 0,
        jnp.concatenate([query_mine, query_other], 1),
        jnp.concatenate([query_other, query_mine], 1),
    )
    grad_cross = jnp.stack([grad_cross_query, grad_cross_out], 1)
    grad_input_two = on_both(dot_back(grad_cq_low, cross_query))
    text_half_grad = lax.dynamic_slice_in_dim(grad_text, core * half, half, 0)
    grad_pair_keys = (
        grad_text_keys.reshape(-1, half) + mask * (text_half_grad[None, :] / length_float)
    ).astype(bf16)
    grad_pair_values = grad_text_values.reshape(-1, half).astype(bf16)
    kv_columns = []
    for gradient, first in ((grad_pair_keys, "y"), (grad_pair_values, "x")):
        parts = [
            tdot(columns_of(tokens, quadrant, 192), gradient).astype(bf16).reshape(2, 4, 24, half)
            for quadrant in quads
        ]
        both_rows = reduce_quads(parts, first, line, 1)
        other = swap(pick(both_rows, 1 - core).astype(bf16), "c").astype(f32)
        mine = pick(both_rows, core)
        kv_columns.append(jnp.where(core == 0, mine, other))
        kv_columns.append(jnp.where(core == 0, other, mine))
    grad_key_value = jnp.concatenate(kv_columns, 1)
    grad_after_self, gain_two = layer_back(
        grad_input_two, normed_two, inverse_two, gain_values[:, 1]
    )
    grad_after_self = grad_after_self + grad_after_cross
    grad_self_in = grad_after_self.astype(bf16)
    grad_mix = tdot(mixed_flat, grad_self_in).astype(bf16)
    grad_mixed_self = dot_back(grad_self_in, weight_mix).astype(bf16).reshape(head_shape)
    grad_rot_queries, grad_keys, grad_values = attend_backward(
        rot_queries[None],
        all_keys[None],
        all_values[None],
        self_bias,
        logsum_self,
        grad_mixed_self[None],
    )
    grad_queries = rotate_back(grad_rot_queries[0], cosine_table, sine_table)
    grad_key_rows = rotate_back(grad_keys[0, 1:], cosine_table, sine_table)
    grad_joined = jnp.concatenate(
        [
            grad_queries.astype(bf16).reshape(FRAMES, half),
            grad_key_rows.astype(bf16).reshape(FRAMES, half),
            grad_values[0, 1:].astype(bf16).reshape(FRAMES, half),
        ],
        1,
    )
    grad_time_pair = jnp.concatenate(
        [grad_keys[0, 0].reshape(1, half), grad_values[0, 0].reshape(1, half)], 1
    )
    grad_projection = tdot(input_one, grad_joined)
    time_rows = input_time.astype(f32).reshape(D, 1) * grad_time_pair
    grad_projection = jnp.concatenate(
        [
            grad_projection[:, :half].astype(bf16),
            (grad_projection[:, half:] + time_rows).astype(bf16),
            jnp.concatenate([grad_mix[:, :half], grad_mix[:, half:]], 0),
        ],
        1,
    )

    position = jnp.arange(256, dtype=jnp.int32)
    owner_core = core ^ (position // 128)
    owner_plane = plane ^ ((position // 16) % 4)
    owner_line = (position // 4) % 4
    inner = ((position // 64) % 2) * 4 + position % 4
    block = assignment[owner_plane * 64 + owner_core * 32 + owner_line * 8 + inner]
    matrix, block_row, block_column = block // 64, (block // 8) % 8, block % 8
    is_out = matrix == 3
    out_pair = block_column // 2
    tile_row = jnp.where(is_out, block_row % 4 + 4 * (out_pair // 2), block_row)
    tile_column = jnp.where(is_out, 6 + out_pair % 2, matrix * 2 + (block_column % 4) // 2)
    held = jnp.where(is_out, block_row // 4, block_column // 4) == core
    collected = collect(
        grad_projection,
        jnp.where(held, tile_row * 8 + tile_column, 0),
        jnp.where(held, block_column % 2, 2 + block_column % 2),
    ).reshape(2, 2, 4, 4, 2, BLK, 2 * BLK)
    slot_sums = low_sum(collected[0], swap(collected[1], "c")).astype(bf16)
    slot_colors = [
        reduce_quads([slot_sums[color, quadrant] for quadrant in quads], first, line, 0)
        for color, first in enumerate(("y", "x"))
    ]
    slot_rows = jnp.concatenate(slot_colors, 0)
    grad_slots = jnp.stack([slot_rows[:, :, :BLK], slot_rows[:, :, BLK:]], 1).reshape(8, BLK, BLK)

    partial_one = dot_back(grad_joined, projection)
    partial_time = jnp.dot(
        grad_time_pair, projection[:, half:].astype(f32).T, precision=BEST_PRECISION
    )
    grad_input_one = on_both(partial_one)
    grad_input_time = partial_time + swap(partial_time, "c")
    grad_residual, gain_one = layer_back(grad_input_one, normed_one, inverse_one, gain_values[:, 0])
    grad_residual = (grad_residual + grad_after_self).astype(bf16)
    grad_embeds, gain_time = layer_back(
        grad_input_time, normed_time, inverse_time, gain_values[:, 0]
    )
    grad_in_weight = tdot(grad_residual, noised)
    grad_table = features.astype(f32).reshape(NTIME, 1) * grad_embeds
    grad_gains = jnp.stack([gain_one + gain_time, gain_two, gain_three], 1)
    grad_ends = jnp.stack([grad_in_weight, grad_out_weight], 1)

    def own_rows(values, width):
        return pick(values.reshape(2, 2, 2, 4, -1, width), core, 2)

    small = jnp.concatenate(
        [
            own_rows(grad_ends.reshape(-1, D), D),
            own_rows(grad_table, D),
            jnp.pad(
                own_rows(grad_gains.reshape(32, 144), 144),
                ((0, 0), (0, 0), (0, 0), (0, 3), (0, D - 144)),
            ),
        ],
        3,
    )
    small = reduce_small(small, row, column, line)
    grad_ends = small[:4].reshape(48, 2, DIN)
    grad_table = small[4:12]
    grad_gains = small[12, :144].reshape(48, 3)

    reduced = (
        grad_ends,
        grad_table,
        grad_slots,
        grad_cross,
        grad_key_value,
        grad_gate_up,
        grad_down,
        grad_gains,
    )
    square_sum = jnp.zeros((), f32)
    for member in reduced:
        square_sum = square_sum + jnp.sum(member * member)
    loss_part = jnp.where(
        core == 0,
        jnp.sum(errors * errors) * mse_scale + contrast_own * (CONTRAST_WEIGHT / items_total),
        0.0,
    )
    loss_total, norm_square = all_sum(loss_part, square_sum)
    return finish(
        loss_total,
        jnp.sqrt(norm_square),
        reduced,
        (
            end_weights,
            time_table,
            square_slots,
            cross_weights,
            key_value,
            gate_up,
            down_weight,
            norm_gains,
        ),
        (
            first_ends,
            first_table,
            None,
            first_cross,
            first_key_value,
            first_gate_up,
            first_down,
            first_gains,
        ),
        (
            second_ends,
            second_table,
            None,
            second_cross,
            second_key_value,
            second_gate_up,
            second_down,
            second_gains,
        ),
        (left_stats, right_stats, left_roots, right_roots),
    )


def all_sum(*values):
    total = jnp.stack(values)
    for axis in ("c", "z", "x", "y"):
        bit = 1
        while bit < lax.axis_size(axis):
            total = total + swap(total, axis, bit)
            bit *= 2
    return total[0], total[1]


def finish(loss_total, gradient_norm, reduced, masters, firsts, seconds, statistics):
    factor = CLIP_NORM / jnp.maximum(gradient_norm, CLIP_NORM)
    results = [loss_total, gradient_norm]
    for index_value in (0, 1, 3, 4, 5, 6, 7):
        results.extend(
            adam_update(
                masters[index_value],
                firsts[index_value],
                seconds[index_value],
                factor * reduced[index_value],
                ADAM_RATES[index_value],
            )
        )
    clipped_slots = factor * reduced[2]
    left_new, right_new, slots_new = shampoo_update(masters[2], clipped_slots, *statistics)
    results.extend([clipped_slots, left_new, right_new, slots_new])
    return tuple(results)


def solution(mesh):
    lines = mesh.shape["text"]
    chips = mesh.devices.size // 2
    if mesh.shape["dp"] == 8 and lines == 4 and 2 * mesh.shape["dp"] == chips:
        mesh = Mesh(mesh.devices.reshape(2, 2, 2, lines), ("y", "x", "c", "z"))
        dp, text, body = ("y", "x", "c"), ("z",), item_per_chip
    else:
        dp, text, body = ("dp",), ("text",), shards
    own = dp + text
    in_specs = (
        P(dp, text, None),
        P(dp, text, None),
        P(dp),
        P(dp, text, None),
        P(dp),
        P(dp, None),
        P(),
    ) + (P(own),) * 26
    out_specs = (P(), P()) + (P(own),) * 25
    return jax.shard_map(body, mesh=mesh, in_specs=in_specs, out_specs=out_specs, check_vma=False)
```

```python
from functools import partial
import math

import jax
import jax.numpy as jnp
from jax import lax
from jax.experimental import pallas as pl
from jax.experimental.pallas import tpu as pltpu
from jax.sharding import Mesh, PartitionSpec as P

D = 1536
HEADS = 24
HD = 64
FF = 6144
DIN = 64
DT = 768
FRAMES = 1024
NTIME = 256
STEP = 10
BLK = 192


BEST_PRECISION = lax.Precision.HIGHEST
NORM_EPS = 1e-05
POOL_EPS = 1e-06
SCORE_SCALE = 0.125
CONTRAST_TEMP = 0.02
CONTRAST_WEIGHT = 0.1
CLIP_NORM = 0.005
BETA_FIRST = 0.9
BETA_SECOND = 0.999
ADAM_EPS = 1e-08
WEIGHT_DECAY = 0.01
ADAM_RATES = (0.02, 0.05, 0.0, 0.1, 0.02, 0.02, 0.02, 1.0)
STAT_DECAY = 0.999
SHAMPOO_RATE = 0.01
MASK_VALUE = -1000000000.0


def layer_stats(inputs):
    center = inputs - jnp.mean(inputs, -1, keepdims=True)
    inverse = lax.rsqrt(jnp.mean(center * center, -1, keepdims=True) + NORM_EPS)
    return (center * inverse, inverse)


def layer_back(grad_out, normed, inverse, gain_row):
    scaled = grad_out * gain_row
    grad_in = inverse * (
        scaled
        - jnp.mean(scaled, -1, keepdims=True)
        - normed * jnp.mean(scaled * normed, -1, keepdims=True)
    )
    return (grad_in, jnp.sum(grad_out * normed, 0))


def time_features(timesteps):
    halfway = NTIME // 2
    frequency = jnp.exp(jnp.arange(halfway, dtype=jnp.float32) * (math.log(64.0) / halfway))
    moment = (timesteps.astype(jnp.float32) + 0.5) / NTIME
    phase = 2.0 * math.pi * moment[:, None] * frequency[None, :]
    return jnp.concatenate([jnp.cos(phase), jnp.sin(phase)], 1)


def rope_tables(positions_count, offset):
    halfway = HD // 2
    frequency = jnp.exp(jnp.arange(halfway, dtype=jnp.float32) * (-2.0 * math.log(10000.0) / HD))
    positions = (jnp.arange(positions_count, dtype=jnp.int32) + offset).astype(jnp.float32)
    angles = positions[:, None] * frequency[None, :]
    return (jnp.concatenate([jnp.cos(angles)] * 2, -1), jnp.concatenate([jnp.sin(angles)] * 2, -1))


def rotate(values, cosine_table, sine_table):
    halfway = HD // 2
    turned = jnp.concatenate([-values[..., halfway:], values[..., :halfway]], -1)
    return values * cosine_table[:, None, :] + turned * sine_table[:, None, :]


def rotate_back(gradient, cosine_table, sine_table):
    halfway = HD // 2
    product = gradient * sine_table[:, None, :]
    return gradient * cosine_table[:, None, :] + jnp.concatenate(
        [product[..., halfway:], -product[..., :halfway]], -1
    )


def to_matrices(blocks):
    per_side = D // BLK
    return blocks.reshape(4, per_side, per_side, BLK, BLK).transpose(0, 1, 3, 2, 4).reshape(4, D, D)


def to_blocks(matrices):
    per_side = D // BLK
    return (
        matrices.reshape(4, per_side, BLK, per_side, BLK)
        .transpose(0, 1, 3, 2, 4)
        .reshape(4 * per_side * per_side, BLK, BLK)
    )


def normalize(vectors):
    return vectors * lax.rsqrt(jnp.sum(vectors * vectors, -1, keepdims=True) + POOL_EPS)


def contrast_loss(pooled_audio, pooled_text, negatives):
    audio_unit_vectors = normalize(pooled_audio)
    text_unit_vectors = normalize(pooled_text)
    positive_pairs = jnp.sum(audio_unit_vectors * text_unit_vectors, -1) / CONTRAST_TEMP
    negative_pairs = (
        jnp.einsum(
            "ux,uax->ua", audio_unit_vectors, text_unit_vectors[negatives], precision=BEST_PRECISION
        )
        / CONTRAST_TEMP
    )
    scores = jnp.concatenate([positive_pairs[:, None], negative_pairs], 1)
    peak_score = jnp.max(scores, -1, keepdims=True)
    logsum = peak_score[:, 0] + jnp.log(jnp.sum(jnp.exp(scores - peak_score), -1))
    return jnp.sum(logsum - positive_pairs)


def item_scores(one_query, one_key, one_bias):
    scores = jnp.einsum("fhd,khd->hfk", one_query, one_key, preferred_element_type=jnp.float32)
    return scores * SCORE_SCALE + one_bias


def attend_forward(queries, all_keys, values, key_bias):

    def single(pieces):
        one_query, one_key, one_value, one_bias = pieces
        scores = item_scores(one_query, one_key, one_bias)
        peak_score = jnp.max(scores, -1, keepdims=True)
        weights = jnp.exp(scores - peak_score)
        row_total = jnp.sum(weights, -1, keepdims=True)
        mixture = jnp.einsum(
            "hfk,khd->fhd",
            (weights / row_total).astype(jnp.bfloat16),
            one_value,
            preferred_element_type=jnp.float32,
        )
        return (mixture.astype(jnp.bfloat16), peak_score + jnp.log(row_total))

    return lax.map(single, (queries, all_keys, values, key_bias))


def attend_backward(queries, all_keys, values, key_bias, logsums, grad_mixture):

    def single(pieces):
        one_query, one_key, one_value, one_bias, one_logsum, grad_rows = pieces
        attention = jnp.exp(item_scores(one_query, one_key, one_bias) - one_logsum)
        grad_attention = jnp.einsum(
            "fhd,khd->hfk", grad_rows, one_value, preferred_element_type=jnp.float32
        )
        grad_value = jnp.einsum(
            "hfk,fhd->khd",
            attention.astype(jnp.bfloat16),
            grad_rows,
            preferred_element_type=jnp.float32,
        )
        grad_scores = attention * (
            grad_attention - jnp.sum(attention * grad_attention, -1, keepdims=True)
        )
        grad_scores = grad_scores.astype(jnp.bfloat16)
        grad_query = (
            jnp.einsum("hfk,khd->fhd", grad_scores, one_key, preferred_element_type=jnp.float32)
            * SCORE_SCALE
        )
        grad_key = (
            jnp.einsum("hfk,fhd->khd", grad_scores, one_query, preferred_element_type=jnp.float32)
            * SCORE_SCALE
        )
        return (grad_query, grad_key, grad_value)

    return lax.map(single, (queries, all_keys, values, key_bias, logsums, grad_mixture))


def feed_forward(rows_in, gate_matrix, down_matrix):
    width = down_matrix.shape[0]
    gate_values = jnp.dot(rows_in, gate_matrix, preferred_element_type=jnp.float32)
    gate_part = gate_values[:, :width]
    up_part = gate_values[:, width:]
    sigmoid = jax.nn.sigmoid(gate_part)
    silu_value = gate_part * sigmoid
    hidden = (silu_value * up_part).astype(jnp.bfloat16)
    partial_out = jnp.dot(hidden, down_matrix, preferred_element_type=jnp.float32)
    return (partial_out, (hidden, gate_part, up_part, sigmoid, silu_value))


def feed_back(rows_in, gate_matrix, down_matrix, kept, grad_low):
    hidden, gate_part, up_part, sigmoid, silu_value = kept
    grad_down = jnp.einsum("rf,rd->fd", hidden, grad_low, preferred_element_type=jnp.float32)
    grad_hidden = jnp.einsum("rd,fd->rf", grad_low, down_matrix, preferred_element_type=jnp.float32)
    grad_gate = grad_hidden * up_part * sigmoid * (1.0 + gate_part * (1.0 - sigmoid))
    grad_pair = jnp.concatenate([grad_gate, grad_hidden * silu_value], 1).astype(jnp.bfloat16)
    grad_gate_up = jnp.einsum("rd,rg->dg", rows_in, grad_pair, preferred_element_type=jnp.float32)
    grad_rows = jnp.einsum("rg,dg->rd", grad_pair, gate_matrix, preferred_element_type=jnp.float32)
    return (grad_rows, grad_gate_up, grad_down)


def adam_update(weight, first_moment, second_moment, gradient, rate):
    first_moment = BETA_FIRST * first_moment + (1.0 - BETA_FIRST) * gradient
    second_moment = BETA_SECOND * second_moment + (1.0 - BETA_SECOND) * gradient * gradient
    corrected = first_moment / (1.0 - BETA_FIRST**STEP)
    scaled = second_moment / (1.0 - BETA_SECOND**STEP)
    weight = weight - rate * (corrected / (jnp.sqrt(scaled) + ADAM_EPS) + WEIGHT_DECAY * weight)
    return (first_moment, second_moment, weight)


def shampoo_update(slots_now, gradient, left_stat, right_stat, left_root, right_root):
    left_stat = STAT_DECAY * left_stat + (1.0 - STAT_DECAY) * jnp.einsum(
        "sij,skj->sik", gradient, gradient, precision=BEST_PRECISION
    )
    right_stat = STAT_DECAY * right_stat + (1.0 - STAT_DECAY) * jnp.einsum(
        "sji,sjk->sik", gradient, gradient, precision=BEST_PRECISION
    )
    inner = jnp.einsum("sij,sjk->sik", gradient, right_root, precision=BEST_PRECISION)
    direction = jnp.einsum("sij,sjk->sik", left_root, inner, precision=BEST_PRECISION)
    return (
        left_stat,
        right_stat,
        slots_now - SHAMPOO_RATE * (direction + WEIGHT_DECAY * slots_now),
    )


def shards(
    latents,
    noise_field,
    timesteps,
    text_tokens,
    text_lengths,
    negatives,
    assignment,
    end_weights,
    time_table,
    square_slots,
    cross_weights,
    key_value,
    gate_up,
    down_weight,
    norm_gains,
    first_ends,
    second_ends,
    first_table,
    second_table,
    first_cross,
    second_cross,
    first_key_value,
    second_key_value,
    first_gate_up,
    second_gate_up,
    first_down,
    second_down,
    first_gains,
    second_gains,
    left_stats,
    right_stats,
    left_roots,
    right_roots,
):
    text_index = lax.axis_index("text")
    group_index = lax.axis_index("dp")
    group_count = lax.axis_size("dp")
    text_count_axis = lax.axis_size("text")
    piece_width = FF // (group_count * text_count_axis)
    low_ends = end_weights.astype(jnp.bfloat16)
    low_table = time_table.astype(jnp.bfloat16)
    low_slots = square_slots.astype(jnp.bfloat16)
    low_cross = cross_weights.astype(jnp.bfloat16)
    low_pairs = key_value.astype(jnp.bfloat16)
    low_gains = norm_gains.astype(jnp.bfloat16)
    low_gate = gate_up.astype(jnp.bfloat16)
    low_down = down_weight.astype(jnp.bfloat16)
    group_set = (
        lax.all_gather(low_ends, "text", axis=0, tiled=True),
        lax.all_gather(low_table, "text", axis=0, tiled=True),
        lax.all_gather(low_slots, "text", axis=0, tiled=True),
        lax.all_gather(low_cross, "text", axis=0, tiled=True),
        lax.all_gather(low_pairs, "text", axis=0, tiled=True),
        lax.all_gather(low_gains, "text", axis=0, tiled=True),
        lax.all_gather(low_gate, "text", axis=0, tiled=True),
    )
    gate_group = group_set[6].reshape(
        group_set[6].shape[0], 2, group_count, text_count_axis, piece_width
    )
    gate_columns = lax.dynamic_index_in_dim(gate_group, text_index, 3, keepdims=False)
    full_set = (
        lax.all_gather(group_set[0], "dp", axis=0, tiled=True),
        lax.all_gather(group_set[1], "dp", axis=0, tiled=True),
        lax.all_gather(group_set[2], "dp", axis=0, tiled=True),
        lax.all_gather(group_set[3], "dp", axis=0, tiled=True),
        lax.all_gather(group_set[4], "dp", axis=0, tiled=True),
        lax.all_gather(group_set[5], "dp", axis=0, tiled=True),
        lax.all_gather(gate_columns, "dp", axis=0, tiled=True),
        lax.all_gather(low_down, "dp", axis=0, tiled=True),
    )
    ends_full, table_full, slots_full, cross_full, pairs_full, gains_full = full_set[:6]
    gate_full = full_set[6].reshape(D, 2 * group_count * piece_width)
    down_full = full_set[7]
    item_count = latents.shape[0]
    frames_dev = latents.shape[1]
    tokens_dev = text_tokens.shape[1]
    row_count = item_count * frames_dev
    items_total = item_count * group_count
    mse_scale = 1.0 / (items_total * FRAMES * DIN)
    weight_in = ends_full[:, 0, :]
    weight_out = ends_full[:, 1, :]
    gain_values = gains_full.astype(jnp.float32)
    inverse_order = (
        jnp.zeros_like(assignment)
        .at[assignment]
        .set(jnp.arange(assignment.shape[0], dtype=jnp.int32))
    )
    squares = to_matrices(slots_full[inverse_order])
    projection = jnp.concatenate([squares[0], squares[1], squares[2]], 1)
    cosine_table, sine_table = rope_tables(frames_dev, 1 + text_index * frames_dev)
    angles = (timesteps.astype(jnp.float32) + 0.5) * (0.5 * math.pi / NTIME)
    signal = jnp.cos(angles)[:, None, None]
    spread = jnp.sin(angles)[:, None, None]
    noised = (signal * latents + spread * noise_field).astype(jnp.bfloat16).reshape(row_count, DIN)
    residual = jnp.einsum("rc,dc->rd", noised, weight_in, preferred_element_type=jnp.float32)
    normed_one, inverse_one = layer_stats(residual)
    input_one = (normed_one * gain_values[:, 0]).astype(jnp.bfloat16)
    features = time_features(timesteps).astype(jnp.bfloat16)
    embeds = jnp.dot(features, table_full, preferred_element_type=jnp.float32)
    normed_time, inverse_time = layer_stats(embeds)
    input_time = (normed_time * gain_values[:, 0]).astype(jnp.bfloat16)
    joined_rows = jnp.dot(input_one, projection, preferred_element_type=jnp.float32)
    head_shape = (item_count, frames_dev, HEADS, HD)
    rot_queries = rotate(joined_rows[:, :D].reshape(head_shape), cosine_table, sine_table).astype(
        jnp.bfloat16
    )
    rot_keys = rotate(
        joined_rows[:, D : 2 * D].reshape(head_shape), cosine_table, sine_table
    ).astype(jnp.bfloat16)
    value_rows = joined_rows[:, 2 * D :].astype(jnp.bfloat16).reshape(item_count, frames_dev, D)
    time_pair = jnp.dot(input_time, projection[:, D:], preferred_element_type=jnp.float32).astype(
        jnp.bfloat16
    )
    keys_all, values_all = (
        lax.all_gather(rot_keys.reshape(item_count, frames_dev, D), "text", axis=1, tiled=True),
        lax.all_gather(value_rows, "text", axis=1, tiled=True),
    )
    key_count = keys_all.shape[1] + 1
    all_keys = jnp.concatenate([time_pair[:, None, :D], keys_all], 1).reshape(
        item_count, key_count, HEADS, HD
    )
    all_values = jnp.concatenate([time_pair[:, None, D:], values_all], 1).reshape(
        item_count, key_count, HEADS, HD
    )
    self_bias = jnp.zeros((item_count, key_count), jnp.float32)
    mixed_self, logsum_self = attend_forward(rot_queries, all_keys, all_values, self_bias)
    mixed_flat = mixed_self.reshape(row_count, D)
    after_self = residual + jnp.dot(mixed_flat, squares[3], preferred_element_type=jnp.float32)
    normed_two, inverse_two = layer_stats(after_self)
    input_two = (normed_two * gain_values[:, 1]).astype(jnp.bfloat16)
    cross_queries = jnp.dot(
        input_two, cross_full[:, 0, :], preferred_element_type=jnp.float32
    ).astype(jnp.bfloat16)
    cross_heads = cross_queries.reshape(head_shape)
    projected = jnp.dot(
        text_tokens.reshape(item_count * tokens_dev, DT),
        pairs_full,
        preferred_element_type=jnp.float32,
    )
    projected = projected.astype(jnp.bfloat16).reshape(item_count, tokens_dev, 2 * D)
    text_all = lax.all_gather(projected, "text", axis=1, tiled=True)
    text_count = text_all.shape[1]
    valid_keys = jnp.arange(text_count, dtype=jnp.int32)[None, :] < text_lengths[:, None]
    cross_bias = jnp.where(valid_keys, 0.0, MASK_VALUE).astype(jnp.float32)
    text_keys = text_all[:, :, :D].reshape(item_count, text_count, HEADS, HD)
    text_values = text_all[:, :, D:].reshape(item_count, text_count, HEADS, HD)
    mixed_cross, logsum_cross = attend_forward(cross_heads, text_keys, text_values, cross_bias)
    cross_flat = mixed_cross.reshape(row_count, D)
    after_cross = after_self + jnp.dot(
        cross_flat, cross_full[:, 1, :], preferred_element_type=jnp.float32
    )
    normed_three, inverse_three = layer_stats(after_cross)
    input_three = (normed_three * gain_values[:, 2]).astype(jnp.bfloat16)
    feed_rows = lax.all_gather(
        input_three.reshape(item_count, frames_dev, D), "text", axis=1, tiled=True
    ).reshape(-1, D)
    feed_out, feed_kept = feed_forward(feed_rows, gate_full, down_full)
    down_out = (
        lax.psum_scatter(
            feed_out.reshape(item_count, -1, D).astype(jnp.bfloat16),
            "text",
            scatter_dimension=1,
            tiled=True,
        )
        .astype(jnp.float32)
        .reshape(row_count, D)
    )
    output_rows = after_cross + down_out
    output_low = output_rows.astype(jnp.bfloat16)
    predicted = jnp.dot(output_low, weight_out, preferred_element_type=jnp.float32).reshape(
        latents.shape
    )
    errors = predicted - (signal * noise_field - spread * latents)
    lengths_float = text_lengths.astype(jnp.float32)
    own_valid = (text_index * tokens_dev + jnp.arange(tokens_dev, dtype=jnp.int32))[
        None, :
    ] < text_lengths[:, None]
    own_mask = own_valid.astype(jnp.float32)
    audio_part = jnp.sum(output_rows.reshape(item_count, frames_dev, D), 1)
    text_part = (
        jnp.sum(projected[:, :, :D].astype(jnp.float32) * own_mask[:, :, None], 1)
        / lengths_float[:, None]
    )
    pooled_set = (
        lax.all_gather(audio_part, ("dp", "text"), axis=0, tiled=True),
        lax.all_gather(text_part, ("dp", "text"), axis=0, tiled=True),
        lax.all_gather(negatives.astype(jnp.float32), ("dp", "text"), axis=0, tiled=True),
    )
    audio_pooled = (
        jnp.sum(pooled_set[0].reshape(group_count, text_count_axis, item_count, D), 1).reshape(
            -1, D
        )
        / FRAMES
    )
    text_pooled = jnp.sum(
        pooled_set[1].reshape(group_count, text_count_axis, item_count, D), 1
    ).reshape(-1, D)
    negative_rows = pooled_set[2].reshape(group_count, text_count_axis, item_count, -1)[:, 0]
    negative_rows = negative_rows.reshape(items_total, -1).astype(jnp.int32)
    contrast_value, contrast_back = jax.vjp(
        partial(contrast_loss, negatives=negative_rows), audio_pooled, text_pooled
    )
    grad_audio_all, grad_text_all = contrast_back(jnp.float32(CONTRAST_WEIGHT / items_total))
    grad_audio = lax.dynamic_slice_in_dim(grad_audio_all, group_index * item_count, item_count, 0)
    grad_text = lax.dynamic_slice_in_dim(grad_text_all, group_index * item_count, item_count, 0)
    grad_predicted = (2.0 * mse_scale * errors).astype(jnp.bfloat16).reshape(row_count, DIN)
    grad_out_weight = jnp.einsum(
        "rd,rc->dc", output_low, grad_predicted, preferred_element_type=jnp.float32
    )
    grad_output = jnp.einsum(
        "rc,dc->rd", grad_predicted, weight_out, preferred_element_type=jnp.float32
    )
    grad_output = (
        grad_output.reshape(item_count, frames_dev, D) + grad_audio[:, None, :] / FRAMES
    ).reshape(row_count, D)
    grad_down_in = grad_output.astype(jnp.bfloat16)
    grad_feed_rows = lax.all_gather(
        grad_down_in.reshape(item_count, frames_dev, D), "text", axis=1, tiled=True
    ).reshape(-1, D)
    grad_feed_in, grad_gate_up, grad_down = feed_back(
        feed_rows, gate_full, down_full, feed_kept, grad_feed_rows
    )
    grad_input_three = (
        lax.psum_scatter(
            grad_feed_in.reshape(item_count, -1, D).astype(jnp.bfloat16),
            "text",
            scatter_dimension=1,
            tiled=True,
        )
        .astype(jnp.float32)
        .reshape(row_count, D)
    )
    grad_after_cross, gain_three = layer_back(
        grad_input_three, normed_three, inverse_three, gain_values[:, 2]
    )
    grad_after_cross = grad_after_cross + grad_output
    grad_cross_in = grad_after_cross.astype(jnp.bfloat16)
    grad_cross_out = jnp.einsum(
        "rd,re->de", cross_flat, grad_cross_in, preferred_element_type=jnp.float32
    )
    grad_mixed_cross = jnp.einsum(
        "re,de->rd", grad_cross_in, cross_full[:, 1, :], preferred_element_type=jnp.float32
    )
    grad_mixed_cross = grad_mixed_cross.astype(jnp.bfloat16).reshape(head_shape)
    grad_cq, grad_text_keys, grad_text_values = attend_backward(
        cross_heads, text_keys, text_values, cross_bias, logsum_cross, grad_mixed_cross
    )
    grad_cq_low = grad_cq.reshape(row_count, D).astype(jnp.bfloat16)
    grad_cross_query = jnp.einsum(
        "rd,re->de", input_two, grad_cq_low, preferred_element_type=jnp.float32
    )
    grad_input_two = jnp.einsum(
        "re,de->rd", grad_cq_low, cross_full[:, 0, :], preferred_element_type=jnp.float32
    )
    grad_pairs = jnp.concatenate(
        [
            grad_text_keys.reshape(item_count, text_count, D),
            grad_text_values.reshape(item_count, text_count, D),
        ],
        2,
    )
    grad_own_pairs = lax.psum_scatter(
        grad_pairs.astype(jnp.bfloat16), "text", scatter_dimension=1, tiled=True
    ).astype(jnp.float32)
    pooled_grad = own_mask[:, :, None] * (grad_text[:, None, :] / lengths_float[:, None, None])
    grad_own_pairs = grad_own_pairs + jnp.concatenate([pooled_grad, jnp.zeros_like(pooled_grad)], 2)
    grad_own_pairs = grad_own_pairs.astype(jnp.bfloat16).reshape(item_count * tokens_dev, 2 * D)
    grad_textside = jnp.einsum(
        "tc,tk->ck",
        text_tokens.reshape(item_count * tokens_dev, DT),
        grad_own_pairs,
        preferred_element_type=jnp.float32,
    )
    grad_after_self, gain_two = layer_back(
        grad_input_two, normed_two, inverse_two, gain_values[:, 1]
    )
    grad_after_self = grad_after_self + grad_after_cross
    grad_self_in = grad_after_self.astype(jnp.bfloat16)
    grad_attn_out = jnp.einsum(
        "rd,re->de", mixed_flat, grad_self_in, preferred_element_type=jnp.float32
    )
    grad_mixed_self = jnp.einsum(
        "re,de->rd", grad_self_in, squares[3], preferred_element_type=jnp.float32
    )
    grad_mixed_self = grad_mixed_self.astype(jnp.bfloat16).reshape(head_shape)
    grad_rot_queries, grad_keys, value_gradients = attend_backward(
        rot_queries, all_keys, all_values, self_bias, logsum_self, grad_mixed_self
    )
    grad_keys_own, grad_values_own = (
        lax.psum_scatter(
            grad_keys[:, 1:].reshape(item_count, key_count - 1, D).astype(jnp.bfloat16),
            "text",
            scatter_dimension=1,
            tiled=True,
        ).astype(jnp.float32),
        lax.psum_scatter(
            value_gradients[:, 1:].reshape(item_count, key_count - 1, D).astype(jnp.bfloat16),
            "text",
            scatter_dimension=1,
            tiled=True,
        ).astype(jnp.float32),
    )
    grad_queries = (
        rotate_back(grad_rot_queries, cosine_table, sine_table)
        .astype(jnp.bfloat16)
        .reshape(row_count, D)
    )
    grad_key_rows = rotate_back(grad_keys_own.reshape(head_shape), cosine_table, sine_table)
    grad_key_rows = grad_key_rows.astype(jnp.bfloat16).reshape(row_count, D)
    grad_joined = jnp.concatenate(
        [grad_queries, grad_key_rows, grad_values_own.astype(jnp.bfloat16).reshape(row_count, D)], 1
    )
    grad_projection = jnp.einsum(
        "rd,rk->dk", input_one, grad_joined, preferred_element_type=jnp.float32
    )
    grad_input_one = jnp.einsum(
        "rk,dk->rd", grad_joined, projection, preferred_element_type=jnp.float32
    )
    grad_time_pair = jnp.concatenate(
        [grad_keys[:, 0].reshape(item_count, D), value_gradients[:, 0].reshape(item_count, D)], 1
    )
    time_rows = jnp.dot(input_time.astype(jnp.float32).T, grad_time_pair, precision=BEST_PRECISION)
    grad_projection = grad_projection + jnp.concatenate(
        [jnp.zeros((D, D), jnp.float32), time_rows], 1
    )
    grad_input_time = jnp.einsum(
        "ik,dk->id", grad_time_pair, projection[:, D:].astype(jnp.float32), precision=BEST_PRECISION
    )
    grad_residual, gain_one = layer_back(grad_input_one, normed_one, inverse_one, gain_values[:, 0])
    grad_residual = (grad_residual + grad_after_self).astype(jnp.bfloat16)
    grad_embeds, gain_time = layer_back(
        grad_input_time, normed_time, inverse_time, gain_values[:, 0]
    )
    grad_in_weight = jnp.einsum(
        "rd,rc->dc", grad_residual, noised, preferred_element_type=jnp.float32
    )
    grad_table = jnp.dot(features.astype(jnp.float32).T, grad_embeds, precision=BEST_PRECISION)
    grad_gains = jnp.stack([gain_one + gain_time, gain_two, gain_three], 1)
    grad_ends = jnp.stack([grad_in_weight, grad_out_weight], 1)
    grad_cross = jnp.stack([grad_cross_query, grad_cross_out], 1)
    grad_squares = jnp.stack(
        [
            grad_projection[:, :D],
            grad_projection[:, D : 2 * D],
            grad_projection[:, 2 * D :],
            grad_attn_out,
        ],
        0,
    )
    grad_slots = jnp.take(to_blocks(grad_squares), assignment, axis=0)
    gate_pieces = grad_gate_up.reshape(D, 2, group_count, piece_width)
    group_grads = (
        lax.psum_scatter(
            grad_ends.astype(jnp.bfloat16), "dp", scatter_dimension=0, tiled=True
        ).astype(jnp.float32),
        lax.psum_scatter(
            grad_table.astype(jnp.bfloat16), "dp", scatter_dimension=0, tiled=True
        ).astype(jnp.float32),
        lax.psum_scatter(
            grad_slots.astype(jnp.bfloat16), "dp", scatter_dimension=0, tiled=True
        ).astype(jnp.float32),
        lax.psum_scatter(
            grad_cross.astype(jnp.bfloat16), "dp", scatter_dimension=0, tiled=True
        ).astype(jnp.float32),
        lax.psum_scatter(
            grad_textside.astype(jnp.bfloat16), "dp", scatter_dimension=0, tiled=True
        ).astype(jnp.float32),
        lax.psum_scatter(
            grad_gains.astype(jnp.bfloat16), "dp", scatter_dimension=0, tiled=True
        ).astype(jnp.float32),
        lax.psum_scatter(
            gate_pieces.astype(jnp.bfloat16), "dp", scatter_dimension=0, tiled=True
        ).astype(jnp.float32),
        lax.psum_scatter(
            grad_down.astype(jnp.bfloat16), "dp", scatter_dimension=0, tiled=True
        ).astype(jnp.float32),
    )
    placing = (jnp.arange(text_count_axis, dtype=jnp.int32) == text_index).astype(jnp.float32)
    spread_gate = group_grads[6][:, :, :, None, :] * placing[None, None, None, :, None]
    spread_gate = spread_gate.reshape(spread_gate.shape[0], 2 * FF)
    owned = (
        lax.psum_scatter(
            group_grads[0].astype(jnp.bfloat16), "text", scatter_dimension=0, tiled=True
        ).astype(jnp.float32),
        lax.psum_scatter(
            group_grads[1].astype(jnp.bfloat16), "text", scatter_dimension=0, tiled=True
        ).astype(jnp.float32),
        lax.psum_scatter(
            group_grads[2].astype(jnp.bfloat16), "text", scatter_dimension=0, tiled=True
        ).astype(jnp.float32),
        lax.psum_scatter(
            group_grads[3].astype(jnp.bfloat16), "text", scatter_dimension=0, tiled=True
        ).astype(jnp.float32),
        lax.psum_scatter(
            group_grads[4].astype(jnp.bfloat16), "text", scatter_dimension=0, tiled=True
        ).astype(jnp.float32),
        lax.psum_scatter(
            group_grads[5].astype(jnp.bfloat16), "text", scatter_dimension=0, tiled=True
        ).astype(jnp.float32),
        lax.psum_scatter(
            spread_gate.astype(jnp.bfloat16), "text", scatter_dimension=0, tiled=True
        ).astype(jnp.float32),
    )
    reduced = (owned[0], owned[1], owned[2], owned[3], owned[4], owned[6], group_grads[7], owned[5])
    square_sum = jnp.zeros((), jnp.float32)
    for member in reduced:
        square_sum = square_sum + jnp.sum(member * member)
    loss_part = jnp.sum(errors * errors) * mse_scale
    totals = lax.psum((square_sum, loss_part), ("dp", "text"))
    loss_total = totals[1] + CONTRAST_WEIGHT * contrast_value / items_total
    gradient_norm = jnp.sqrt(totals[0])
    masters = (
        end_weights,
        time_table,
        square_slots,
        cross_weights,
        key_value,
        gate_up,
        down_weight,
        norm_gains,
    )
    firsts = (
        first_ends,
        first_table,
        None,
        first_cross,
        first_key_value,
        first_gate_up,
        first_down,
        first_gains,
    )
    seconds = (
        second_ends,
        second_table,
        None,
        second_cross,
        second_key_value,
        second_gate_up,
        second_down,
        second_gains,
    )
    return finish(
        loss_total,
        gradient_norm,
        reduced,
        masters,
        firsts,
        seconds,
        (left_stats, right_stats, left_roots, right_roots),
    )


def swap(values, axis, bit=1):
    return lax.ppermute(values, axis, [(i, i ^ bit) for i in range(lax.axis_size(axis))])


def pick(values, position, axis=0):
    return lax.dynamic_index_in_dim(values, position, axis, keepdims=False)


def grow(values, axis):
    bit = 1
    while bit < lax.axis_size(axis):
        values = jnp.concatenate([values, swap(values, axis, bit)], 0)
        bit *= 2
    return values


def own_quarters(values, core, line):
    pair = jnp.concatenate([values, swap(values, "c")], 0)
    pieces = []
    for offset in range(4):
        target = line ^ offset
        piece = pick(pair, ((target // 2) ^ core) * 2 + target % 2)
        pieces.append(swap(piece, "z", offset) if offset else piece)
    return jnp.concatenate(pieces, 0)


def low_sum(*terms):
    total = terms[0].astype(jnp.float32)
    for term in terms[1:]:
        total = total + term.astype(jnp.float32)
    return total


def on_both(partial_sum):
    low = partial_sum.astype(jnp.bfloat16)
    return low_sum(low, swap(low, "c"))


def tdot(left, right):
    return lax.dot_general(left, right, (((0,), (0,)), ((), ())), preferred_element_type=jnp.float32)


def dot_back(left, right):
    return lax.dot_general(left, right, (((1,), (1,)), ((), ())), preferred_element_type=jnp.float32)


MESH_ID = pl.DeviceIdType.MESH
TILE = 256


def anywhere(count):
    return [pl.BlockSpec(memory_space=pl.ANY)] * count


def coordinates():
    return tuple(lax.axis_index(axis) for axis in ("y", "x", "c", "z"))


def chip_peers(me):
    row, column, core, line = me
    beside = {
        "c": (row, column, 1 - core, line),
        "x": (row, 1 - column, core, line),
        "y": (1 - row, column, core, line),
    }
    for offset in (1, 2, 3):
        beside[offset] = (row, column, core, line ^ offset)
    return beside


def greet(peers):
    barrier = pltpu.get_barrier_semaphore()
    for peer in peers.values():
        pl.semaphore_signal(barrier, inc=1, device_id=peer, device_id_type=MESH_ID)
    pl.semaphore_wait(barrier, len(peers))


def send(source, target, send_sem, recv_sem, peer):
    return pltpu.make_async_remote_copy(
        src_ref=source,
        dst_ref=target,
        send_sem=send_sem,
        recv_sem=recv_sem,
        device_id=peer,
        device_id_type=MESH_ID,
    )


def gather_kernel(arrays, groups, *refs):
    count = len(arrays)
    inputs = sum(2 if kind == "cols" else 1 for kind, _, _ in arrays)
    sources, bufs = list(refs[:inputs]), refs[inputs : inputs + count]
    send_sem, recv_sem, core_send, core_recv, local_sem = refs[inputs + count :]
    me = coordinates()
    row, column, core, line = me
    plane = 2 * row + column
    peers = chip_peers(me)
    greet(peers)
    local, cross = [], []
    for index_value, (kind, _, _) in enumerate(arrays):
        spot = bufs[index_value].at[plane, 0 if kind == "one" else core, line]
        copy = pltpu.make_async_copy(sources.pop(0), spot, local_sem.at[index_value])
        copy.start()
        local.append(copy)
        cross.append(None)
        if kind == "cols":
            cross[-1] = send(
                sources.pop(0),
                spot,
                core_send.at[index_value],
                core_recv.at[index_value],
                peers["c"],
            )
            cross[-1].start()
    whole = slice(None)
    flat = [unit for group in groups for unit in group]
    ready = set()

    def move(number, slot, planes, lines, peer):
        array, _, rows, columns = flat[number]
        cores = {"cols": whole, "one": 0}.get(arrays[array][0], core)
        view = bufs[array].at[planes, cores, lines, rows, columns]
        return send(view, view, send_sem.at[number, slot], recv_sem.at[number, slot], peer)

    def line_copies(number):
        return [move(number, o - 1, plane, line, peers[o]) for o in (1, 2, 3)]

    def near_copy(number):
        axis = "y" if flat[number][1] else "x"
        return move(number, 3, plane, whole, peers[axis])

    def side_copy(number):
        axis = "x" if flat[number][1] else "y"
        return move(number, 4, plane, whole, peers[axis])

    def far_copy(number):
        color = flat[number][1]
        return move(number, 5, plane ^ (2 if color else 1), whole, peers["x" if color else "y"])

    def core_copy(number):
        array, _, rows, columns = flat[number]
        kind = arrays[array][0]
        if kind not in ("both", "half"):
            return None
        planes = whole if kind == "both" else pl.ds(2 * (1 - core), 2)
        view = bufs[array].at[planes, core, whole, rows, columns]
        return send(view, view, send_sem.at[number, 6], recv_sem.at[number, 6], peers["c"])

    def start_line(number):
        array = flat[number][0]
        if array not in ready:
            ready.add(array)
            local[array].wait()
            if cross[array] is not None:
                cross[array].wait()
        for copy in line_copies(number):
            copy.start()

    def start_near(number):
        for copy in line_copies(number):
            copy.wait_recv()
        near_copy(number).start()
        side_copy(number).start()

    def start_far(number):
        near_copy(number).wait_recv()
        far_copy(number).start()

    def close(number):
        side_copy(number).wait_recv()
        far_copy(number).wait_recv()
        last = core_copy(number)
        if last is not None:
            last.start()
        for copy in line_copies(number) + [near_copy(number), side_copy(number), far_copy(number)]:
            copy.wait_send()

    stages = (start_line, start_near, start_far, close)
    numbers, at = [], 0
    for group in groups:
        numbers.append(range(at, at + len(group)))
        at += len(group)
    for step in range(len(groups) + 3):
        for lag, stage in enumerate(stages):
            if 0 <= step - lag < len(groups):
                for number in numbers[step - lag]:
                    stage(number)
    for number in range(len(flat)):
        last = core_copy(number)
        if last is not None:
            last.wait()


def gather_weights(arrays, groups, sources, collective_id):
    units = sum(len(group) for group in groups)
    dma = pltpu.SemaphoreType.DMA
    return pl.pallas_call(
        partial(gather_kernel, arrays, groups),
        out_shape=[
            jax.ShapeDtypeStruct((4, 1 if kind == "one" else 2, 4) + shape, dtype)
            for kind, shape, dtype in arrays
        ],
        in_specs=anywhere(len(sources)),
        out_specs=anywhere(len(arrays)),
        scratch_shapes=[
            dma((units, 7)),
            dma((units, 7)),
            dma((len(arrays),)),
            dma((len(arrays),)),
            dma((len(arrays),)),
        ],
        compiler_params=pltpu.CompilerParams(collective_id=collective_id, has_side_effects=True),
    )(*sources)


def reduce_kernel(arrays, groups, *refs):
    count = len(arrays)
    flat = [unit for group in groups for unit in group]
    total = len(flat)
    sources = refs[:count]
    outputs = sum(2 if kind == "cols" else 1 for kind, _ in arrays)
    targets, at = [], count
    for kind, _ in arrays:
        width = 2 if kind == "cols" else 1
        targets.append(refs[at : at + width])
        at += width
    scratch = refs[at:]
    sides, onwards, mines, from_ons, from_lines, from_cores = (
        scratch[index_value * total : (index_value + 1) * total] for index_value in range(6)
    )
    send_sem, recv_sem, load_sem = scratch[6 * total :]
    me = coordinates()
    row, column, core, line = me
    plane = 2 * row + column
    peers = chip_peers(me)
    greet(peers)
    whole = slice(None)

    def source(number, planes):
        array, _, rows, columns = flat[number]
        return sources[array].at[planes, whole, whole, rows, columns]

    def first_copy(number, slot):
        bit, axis = (1, "x") if flat[number][1] else (2, "y")
        return send(
            source(number, plane ^ (3 if slot else bit)),
            sides[number].at[slot],
            send_sem.at[number, slot],
            recv_sem.at[number, slot],
            peers[axis],
        )

    def load_onward(number):
        off = 2 if flat[number][1] else 1
        return pltpu.make_async_copy(
            source(number, plane ^ off), onwards[number], load_sem.at[number, 0]
        )

    def load_mine(number):
        return pltpu.make_async_copy(source(number, plane), mines[number], load_sem.at[number, 1])

    def onward_copy(number):
        axis = "y" if flat[number][1] else "x"
        return send(
            onwards[number],
            from_ons[number],
            send_sem.at[number, 2],
            recv_sem.at[number, 2],
            peers[axis],
        )

    def line_copies(number):
        return [
            send(
                mines[number].at[whole, line ^ offset],
                from_lines[number].at[offset - 1],
                send_sem.at[number, 2 + offset],
                recv_sem.at[number, 2 + offset],
                peers[offset],
            )
            for offset in (1, 2, 3)
        ]

    def core_copy(number):
        return send(
            mines[number].at[1 - core, line],
            from_cores[number],
            send_sem.at[number, 6],
            recv_sem.at[number, 6],
            peers["c"],
        )

    def is_cols(number):
        return arrays[flat[number][0]][0] == "cols"

    def add_into(target, *terms):
        cores, lines, height, _ = target.shape

        def body(step, carry):
            side = step // (lines * (height // 16))
            rest = step % (lines * (height // 16))
            at_line = rest // (height // 16)
            rows = pl.ds(pl.multiple_of((rest % (height // 16)) * 16, 16), 16)
            value = target[side, at_line, rows].astype(jnp.float32)
            for term in terms:
                value = value + term[side, at_line, rows].astype(jnp.float32)
            target[side, at_line, rows] = value.astype(target.dtype)
            return carry

        lax.fori_loop(0, cores * lines * (height // 16), body, 0)

    def stage_one(number):
        first_copy(number, 1).start()
        first_copy(number, 0).start()
        load_onward(number).start()
        load_mine(number).start()

    def stage_two(number):
        first_copy(number, 1).wait_recv()
        load_onward(number).wait()
        add_into(onwards[number], sides[number].at[1])
        onward_copy(number).start()

    def stage_three(number):
        first_copy(number, 0).wait_recv()
        load_mine(number).wait()
        onward_copy(number).wait_recv()
        add_into(mines[number], sides[number].at[0], from_ons[number])
        for copy in line_copies(number):
            copy.start()

    def stage_four(number):
        for copy in line_copies(number):
            copy.wait_recv()
        array, _, rows, columns = flat[number]
        mine, pieces = mines[number], from_lines[number]
        for side in range(mine.shape[0]):
            value = mine[side, line].astype(jnp.float32)
            for offset in range(3):
                value = value + pieces[offset, side].astype(jnp.float32)
            mine[side, line] = value.astype(mine.dtype)
        if is_cols(number):
            core_copy(number).start()
            targets[array][0][rows, columns] = mine[core, line]
        else:
            targets[array][0][rows, columns] = mine[0, line]

    def stage_five(number):
        if is_cols(number):
            core_copy(number).wait()
            array, _, rows, columns = flat[number]
            targets[array][1][rows, columns] = from_cores[number][...]
        first_copy(number, 0).wait_send()
        first_copy(number, 1).wait_send()
        onward_copy(number).wait_send()
        for copy in line_copies(number):
            copy.wait_send()

    stages = (stage_one, stage_two, stage_three, stage_four, stage_five)
    numbers, at = [], 0
    for group in groups:
        numbers.append(range(at, at + len(group)))
        at += len(group)
    for step in range(len(groups) + 4):
        for lag, stage in enumerate(stages):
            if 0 <= step - lag < len(groups):
                for number in numbers[step - lag]:
                    stage(number)


def extent(sel, size):
    return size if isinstance(sel, slice) else sel.size


def reduce_gradients(arrays, groups, sources, collective_id):
    flat = [unit for group in groups for unit in group]
    vmem, dma, low = pltpu.VMEM, pltpu.SemaphoreType.DMA, jnp.bfloat16
    shapes = []
    for array, _, rows, columns in flat:
        kind, (height, width) = arrays[array]
        shapes.append((2 if kind == "cols" else 1, extent(rows, height), extent(columns, width)))
    scratch = [vmem((2, c, 4, h, w), low) for c, h, w in shapes]
    for _ in range(3):
        scratch += [vmem((c, 4, h, w), low) for c, h, w in shapes]
    scratch += [vmem((3, c, h, w), low) for c, h, w in shapes]
    scratch += [vmem((h, w) if c == 2 else (16, 128), low) for c, h, w in shapes]
    out_shape = []
    for kind, shape in arrays:
        out_shape += [jax.ShapeDtypeStruct(shape, low)] * (2 if kind == "cols" else 1)
    return pl.pallas_call(
        partial(reduce_kernel, arrays, groups),
        out_shape=out_shape,
        in_specs=anywhere(len(sources)),
        out_specs=[pl.BlockSpec(memory_space=pltpu.VMEM)] * len(out_shape),
        scratch_shapes=scratch
        + [dma((len(flat), 7)), dma((len(flat), 7)), dma((len(flat), 2))],
        compiler_params=pltpu.CompilerParams(
            collective_id=collective_id, has_side_effects=True, vmem_limit_bytes=60 * 2**20
        ),
    )(*sources)


def turned(values, cosine, sine):
    lane = lax.broadcasted_iota(jnp.int32, values.shape, 1)
    halfway = HD // 2
    partner = jnp.where(
        lane % HD < halfway,
        pltpu.roll(values, 128 - halfway, 1),
        pltpu.roll(values, halfway, 1),
    )
    return values * cosine + partner * sine


def join_kernel(rows, times, weights, cosine, sine, joined, joined_time):
    is_turned = pl.program_id(0) < 6

    def body(step, carry):
        at = pl.ds(pl.multiple_of(step * TILE, TILE), TILE)
        values = jnp.dot(rows[at, :], weights[...], preferred_element_type=jnp.float32)

        @pl.when(is_turned)
        def turn():
            for side in (0, 128):
                joined[at, side : side + 128] = turned(
                    values[:, side : side + 128], cosine[at, :], sine[at, :]
                ).astype(joined.dtype)

        @pl.when(jnp.logical_not(is_turned))
        def keep():
            joined[at, :] = values.astype(joined.dtype)

        return carry

    lax.fori_loop(0, rows.shape[0] // TILE, body, 0)
    joined_time[...] = jnp.dot(
        times[...], weights[...], preferred_element_type=jnp.float32
    ).astype(joined_time.dtype)


def join(rows, times, weights, cosine, sine):
    width = weights.shape[1]

    def fixed(array):
        return pl.BlockSpec(array.shape, lambda step: (0, 0))

    return pl.pallas_call(
        join_kernel,
        grid=(width // 256,),
        in_specs=[
            fixed(rows),
            fixed(times),
            pl.BlockSpec((D, 256), lambda step: (0, step)),
            fixed(cosine),
            fixed(sine),
        ],
        out_specs=[
            pl.BlockSpec((rows.shape[0], 256), lambda step: (0, step)),
            pl.BlockSpec((times.shape[0], 256), lambda step: (0, step)),
        ],
        out_shape=[
            jax.ShapeDtypeStruct((rows.shape[0], width), jnp.bfloat16),
            jax.ShapeDtypeStruct((times.shape[0], width), jnp.bfloat16),
        ],
        compiler_params=pltpu.CompilerParams(vmem_limit_bytes=48 * 2**20),
        cost_estimate=pl.CostEstimate(
            flops=2 * rows.shape[0] * D * width,
            bytes_accessed=2 * (rows.size + weights.size + rows.shape[0] * width),
            transcendentals=0,
        ),
    )(rows, times, weights, cosine, sine)


def head_lanes(shape, head):
    return lax.broadcasted_iota(jnp.int32, shape, 1) // HD == head


def attend_kernel(timed, queries, keys, values, first, second, mixed, logsum):
    def body(step, carry):
        at = pl.ds(pl.multiple_of(step * TILE, TILE), TILE)
        rows = queries[at, :]
        total = jnp.zeros(rows.shape, jnp.float32)
        sums = jnp.zeros(rows.shape, jnp.float32)
        for head in range(2):
            own = head_lanes(rows.shape, head)
            query = jnp.where(own, rows, jnp.zeros_like(rows))
            scores = dot_back(query, keys[...]) * SCORE_SCALE
            if timed:
                extra = (
                    jnp.sum(
                        query.astype(jnp.float32) * first[0:1, :].astype(jnp.float32),
                        -1,
                        keepdims=True,
                    )
                    * SCORE_SCALE
                )
                peak = jnp.maximum(jnp.max(scores, -1, keepdims=True), extra)
            else:
                scores = scores + first[0:1, :]
                peak = jnp.max(scores, -1, keepdims=True)
            powers = jnp.exp(scores - peak)
            row_total = jnp.sum(powers, -1, keepdims=True)
            mixture = jnp.dot(
                powers.astype(jnp.bfloat16), values[...], preferred_element_type=jnp.float32
            )
            if timed:
                power = jnp.exp(extra - peak)
                row_total = row_total + power
                mixture = mixture + power * second[0:1, :].astype(jnp.float32)
            total = jnp.where(own, mixture / row_total, total)
            sums = jnp.where(own, peak + jnp.log(row_total), sums)
        mixed[at, :] = total.astype(mixed.dtype)
        logsum[at, :] = sums
        return carry

    lax.fori_loop(0, queries.shape[0] // TILE, body, 0)


def lane_block(array, offset):
    return pl.BlockSpec((array.shape[0], 128), lambda pair: (0, pair + offset))


def attend(queries, keys, values, extras, offsets, timed):
    rows, count, pairs = queries.shape[0], keys.shape[0], HEADS // 4
    extra_specs = (
        [lane_block(extras[0], offsets[1]), lane_block(extras[1], offsets[2])]
        if timed
        else [pl.BlockSpec(extra.shape, lambda pair: (0, 0)) for extra in extras]
    )
    return pl.pallas_call(
        partial(attend_kernel, timed),
        grid=(pairs,),
        in_specs=[
            lane_block(queries, offsets[0]),
            lane_block(keys, offsets[1]),
            lane_block(values, offsets[2]),
        ]
        + extra_specs,
        out_specs=[pl.BlockSpec((rows, 128), lambda pair: (0, pair))] * 2,
        out_shape=[
            jax.ShapeDtypeStruct((rows, 128 * pairs), jnp.bfloat16),
            jax.ShapeDtypeStruct((rows, 128 * pairs), jnp.float32),
        ],
        compiler_params=pltpu.CompilerParams(vmem_limit_bytes=48 * 2**20),
        cost_estimate=pl.CostEstimate(
            flops=pairs * 2 * rows * count * 128 * 4,
            bytes_accessed=pairs * 128 * (rows * 10 + count * 4),
            transcendentals=pairs * 2 * rows * count,
        ),
    )(queries, keys, values, *extras)


def attend_back_kernel(timed, *refs):
    queries, keys, values, first, second, mixed, logsum, gradient = refs[:8]
    if timed:
        cosine, sine, out_q, out_k, out_v, out_first, out_second, sum_k, sum_v = refs[8:]
    else:
        out_q, out_k, out_v, sum_k, sum_v = refs[8:]
    sum_k[...] = jnp.zeros_like(sum_k)
    sum_v[...] = jnp.zeros_like(sum_v)
    if timed:
        out_first[...] = jnp.zeros_like(out_first)
        out_second[...] = jnp.zeros_like(out_second)

    def body(step, carry):
        at = pl.ds(pl.multiple_of(step * TILE, TILE), TILE)
        rows, grad = queries[at, :], gradient[at, :]
        product = grad.astype(jnp.float32) * mixed[at, :].astype(jnp.float32)
        sums = logsum[at, :]
        sums_row = sums.T
        grad_query = jnp.zeros(rows.shape, jnp.float32)
        for head in range(2):
            own = head_lanes(rows.shape, head)
            query = jnp.where(own, rows, jnp.zeros_like(rows))
            grad_own = jnp.where(own, grad, jnp.zeros_like(grad))
            inner = jnp.sum(jnp.where(own, product, 0.0), -1, keepdims=True)
            inner_row = jnp.broadcast_to(inner, rows.shape).T[0:1, :]
            scores = dot_back(keys[...], query) * SCORE_SCALE
            if not timed:
                scores = scores + second[:, 0:1]
            attention = jnp.exp(scores - sums_row[head * HD : head * HD + 1, :])
            grad_attention = dot_back(values[...], grad_own)
            sum_v[...] += jnp.dot(
                attention.astype(jnp.bfloat16), grad_own, preferred_element_type=jnp.float32
            )
            grad_scores = (attention * (grad_attention - inner_row)).astype(jnp.bfloat16)
            sum_k[...] += jnp.dot(grad_scores, query, preferred_element_type=jnp.float32)
            key_own = jnp.where(
                head_lanes(keys.shape, head), keys[...], jnp.zeros(keys.shape, keys.dtype)
            )
            grad_query = grad_query + tdot(grad_scores, key_own)
            if timed:
                key_time = jnp.where(
                    own[0:1, :], first[0:1, :].astype(jnp.float32), jnp.zeros((1, 128), jnp.float32)
                )
                wide_query, wide_grad = query.astype(jnp.float32), grad_own.astype(jnp.float32)
                score = jnp.sum(wide_query * key_time, -1, keepdims=True) * SCORE_SCALE
                power = jnp.exp(score - sums[:, head * HD : head * HD + 1])
                back = jnp.sum(
                    wide_grad * second[0:1, :].astype(jnp.float32), -1, keepdims=True
                )
                grad_score = (power * (back - inner)).astype(jnp.bfloat16).astype(jnp.float32)
                grad_query = grad_query + grad_score * key_time
                out_first[0:1, :] += SCORE_SCALE * jnp.sum(
                    grad_score * wide_query, 0, keepdims=True
                )
                out_second[0:1, :] += jnp.sum(
                    power.astype(jnp.bfloat16).astype(jnp.float32) * wide_grad, 0, keepdims=True
                )
        grad_query = grad_query * SCORE_SCALE
        if timed:
            grad_query = turned(grad_query, cosine[at, :], -sine[at, :])
        out_q[at, :] = grad_query.astype(out_q.dtype)
        return carry

    lax.fori_loop(0, queries.shape[0] // TILE, body, 0)
    grad_key = sum_k[...] * SCORE_SCALE
    if timed:
        grad_key = turned(grad_key, cosine[...], -sine[...])
    out_k[...] = grad_key.astype(out_k.dtype)
    out_v[...] = sum_v[...].astype(out_v.dtype)


def attend_back(queries, keys, values, extras, offsets, mixed, logsum, gradient, tables):
    timed = tables is not None
    rows, count, pairs = queries.shape[0], keys.shape[0], HEADS // 4
    extra_specs = (
        [lane_block(extras[0], offsets[1]), lane_block(extras[1], offsets[2])]
        if timed
        else [pl.BlockSpec(extra.shape, lambda pair: (0, 0)) for extra in extras]
    )
    low = jnp.bfloat16 if timed else jnp.float32

    def out(height, dtype):
        return (
            jax.ShapeDtypeStruct((height, 128 * pairs), dtype),
            pl.BlockSpec((height, 128), lambda pair: (0, pair)),
        )

    outs = [out(rows, jnp.bfloat16), out(count, low), out(count, low)]
    operands = [queries, keys, values, *extras, mixed, logsum, gradient]
    specs = (
        [
            lane_block(queries, offsets[0]),
            lane_block(keys, offsets[1]),
            lane_block(values, offsets[2]),
        ]
        + extra_specs
        + [lane_block(mixed, 0), lane_block(logsum, 0), lane_block(gradient, 0)]
    )
    if timed:
        outs += [out(8, jnp.float32), out(8, jnp.float32)]
        operands += list(tables)
        specs += [pl.BlockSpec(table.shape, lambda pair: (0, 0)) for table in tables]
    return pl.pallas_call(
        partial(attend_back_kernel, timed),
        grid=(pairs,),
        in_specs=specs,
        out_specs=[spec for _, spec in outs],
        out_shape=[shape for shape, _ in outs],
        scratch_shapes=[pltpu.VMEM((count, 128), jnp.float32)] * 2,
        compiler_params=pltpu.CompilerParams(vmem_limit_bytes=48 * 2**20),
        cost_estimate=pl.CostEstimate(
            flops=pairs * 2 * rows * count * 128 * 10,
            bytes_accessed=pairs * 128 * (rows * 16 + count * 8),
            transcendentals=pairs * 2 * rows * count,
        ),
    )(*operands)


def lane_moves():
    source = lax.broadcasted_iota(jnp.int32, (6, 2 * BLK, 2 * BLK), 1)
    target = lax.broadcasted_iota(jnp.int32, (6, 2 * BLK, 2 * BLK), 2)
    code = lax.broadcasted_iota(jnp.int32, (6, 2 * BLK, 2 * BLK), 0)
    to_right, taken = code // 3, code % 3
    moves = (target // BLK == to_right) & (taken < 2)
    moves = moves & (source == target + (taken - to_right) * BLK)
    return moves.astype(jnp.bfloat16)


def pair_kernel(left_at, right_at, left_half, right_half, left, right, moves, target):
    step = pl.program_id(0)
    tile_shape = (BLK, 2 * BLK)
    total = jnp.dot(
        left[...].reshape(tile_shape), moves[left_half[step]], preferred_element_type=jnp.float32
    )
    total = total + jnp.dot(
        right[...].reshape(tile_shape),
        moves[3 + right_half[step]],
        preferred_element_type=jnp.float32,
    )
    target[...] = total.astype(target.dtype).reshape(target.shape)


def pair_up(blocks, places, halves, moves, source_spec, target_spec, shape):
    steps = places.shape[0] // 2
    return pl.pallas_call(
        pair_kernel,
        grid_spec=pltpu.PrefetchScalarGridSpec(
            num_scalar_prefetch=4,
            grid=(steps,),
            in_specs=[
                source_spec(lambda step, a, b, c, d: a[step]),
                source_spec(lambda step, a, b, c, d: b[step]),
                pl.BlockSpec(moves.shape, lambda step, a, b, c, d: (0, 0, 0)),
            ],
            out_specs=target_spec,
        ),
        out_shape=jax.ShapeDtypeStruct(shape, blocks.dtype),
        cost_estimate=pl.CostEstimate(
            flops=8 * steps * BLK**3, bytes_accessed=12 * steps * BLK * BLK, transcendentals=0
        ),
    )(places[0::2], places[1::2], halves[0::2], halves[1::2], blocks, blocks, moves)


def stacked_spec(where):
    return pl.BlockSpec((1, BLK, 2 * BLK), lambda *at: (where(*at), 0, 0))


def tiled_spec(across):
    def spec(where):
        return pl.BlockSpec(
            (BLK, 2 * BLK), lambda *at: (where(*at) // across, where(*at) % across)
        )

    return spec


def assemble(pairs, slots, moves, rows, columns):
    across = columns // (2 * BLK)
    return pair_up(
        pairs,
        slots // 2,
        slots % 2,
        moves,
        stacked_spec,
        pl.BlockSpec((BLK, 2 * BLK), lambda step, *_: (step // across, step % across)),
        (rows, columns),
    )


def collect(matrix, places, halves, moves):
    return pair_up(
        matrix,
        places,
        halves,
        moves,
        tiled_spec(matrix.shape[1] // (2 * BLK)),
        pl.BlockSpec((1, BLK, 2 * BLK), lambda step, *_: (step, 0, 0)),
        (places.shape[0] // 2, BLK, 2 * BLK),
    )


def item_per_chip(
    latents,
    noise_field,
    timesteps,
    text_tokens,
    text_lengths,
    negatives,
    assignment,
    end_weights,
    time_table,
    square_slots,
    cross_weights,
    key_value,
    gate_up,
    down_weight,
    norm_gains,
    first_ends,
    second_ends,
    first_table,
    second_table,
    first_cross,
    second_cross,
    first_key_value,
    second_key_value,
    first_gate_up,
    second_gate_up,
    first_down,
    second_down,
    first_gains,
    second_gains,
    left_stats,
    right_stats,
    left_roots,
    right_roots,
):
    bf16, f32 = jnp.bfloat16, jnp.float32
    row, column = lax.axis_index("y"), lax.axis_index("x")
    core, line = lax.axis_index("c"), lax.axis_index("z")
    plane = 2 * row + column
    item = 4 * plane + line
    quads = range(4)
    half = D // 2
    items_total = 16
    mse_scale = 1.0 / (items_total * FRAMES * DIN)

    pack = jnp.concatenate(
        [
            end_weights.reshape(4, D),
            time_table,
            jnp.pad(norm_gains.reshape(1, 144), ((0, 3), (0, D - 144))),
        ],
        0,
    ).astype(bf16)
    low_slots = square_slots.astype(bf16).reshape(4, 2, BLK, BLK)
    low_pairs = jnp.concatenate([low_slots[:, 0], low_slots[:, 1]], 2).reshape(4 * BLK, 2 * BLK)
    low_cross = cross_weights.astype(bf16)
    low_kv = key_value.astype(bf16)
    low_gate = gate_up.astype(bf16)
    low_down = down_weight.astype(bf16)

    def head_columns(array, which, side):
        return lax.dynamic_slice_in_dim(array, which * D + side * half, half, 1)

    def unit_columns(which, side):
        return jnp.concatenate(
            [
                lax.dynamic_slice_in_dim(
                    low_gate, which * FF + quadrant * 1536 + side * 768, 768, 1
                )
                for quadrant in quads
            ],
            1,
        )

    def kv_block(which, side):
        return head_columns(low_kv, which, side).reshape(16, 1152)

    arrays = (
        ("cols", (16, D), bf16),
        ("both", (4 * BLK, 2 * BLK), bf16),
        ("cols", (48, half), bf16),
        ("half", (48, D), bf16),
        ("cols", (16, 1152), bf16),
        ("cols", (16, 1152), bf16),
        ("cols", (48, FF // 2), bf16),
        ("cols", (48, FF // 2), bf16),
        ("one", (192, D), bf16),
    )
    whole = slice(None)
    groups = [((0, 0, whole, whole), (5, 1, whole, whole))]
    groups += [
        ((1, 0, pl.ds(step * 192, 192), whole), (1, 1, pl.ds(384 + step * 192, 192), whole))
        for step in range(2)
    ]
    groups += [((2, 0, whole, whole), (3, 1, whole, whole), (4, 0, whole, whole))]
    groups += [
        ((6, 0, whole, pl.ds(step * 768, 768)), (7, 1, whole, pl.ds(step * 768, 768)))
        for step in range(4)
    ]
    groups += [
        ((8, 0, whole, pl.ds(step * 384, 384)), (8, 1, whole, pl.ds(half + step * 384, 384)))
        for step in range(2)
    ]
    packs, all_pairs, cross_query, cross_out, keys_own, values_own, gate_weight, up_weight, down = (
        gather_weights(
            arrays,
            groups,
            (
                pack,
                pack,
                low_pairs,
                head_columns(low_cross[:, 0, :], 0, core),
                head_columns(low_cross[:, 0, :], 0, 1 - core),
                low_cross[:, 1, :],
                kv_block(0, core),
                kv_block(0, 1 - core),
                kv_block(1, core),
                kv_block(1, 1 - core),
                unit_columns(0, core),
                unit_columns(0, 1 - core),
                unit_columns(1, core),
                unit_columns(1, 1 - core),
                low_down,
            ),
            1,
        )
    )
    packs = packs.reshape(32, 16, D)
    ends_full = packs[:, :4].reshape(D, 2, DIN)
    table_full = packs[:, 4:12].reshape(NTIME, D)
    gain_values = packs[:, 12, :144].reshape(D, 3).astype(f32)
    weight_in, weight_out = ends_full[:, 0, :], ends_full[:, 1, :]
    all_pairs = all_pairs.reshape(128, BLK, 2 * BLK)
    inverse_order = (
        jnp.zeros_like(assignment)
        .at[assignment]
        .set(jnp.arange(assignment.shape[0], dtype=jnp.int32))
    )

    def grid_blocks(matrix, rows, columns):
        return (matrix * 64 + rows * 8 + columns).reshape(-1)

    eight, four = jnp.arange(8, dtype=jnp.int32), jnp.arange(4, dtype=jnp.int32)
    joined_blocks = grid_blocks(
        jnp.arange(3, dtype=jnp.int32)[None, :, None],
        eight[:, None, None],
        (4 * core + four)[None, None, :],
    )
    out_blocks = grid_blocks(3, (4 * core + four)[:, None], eight[None, :])
    moves = lane_moves()
    projection = assemble(all_pairs, inverse_order[joined_blocks], moves, D, 3 * half)
    weight_mix = assemble(all_pairs, inverse_order[out_blocks], moves, half, D)
    cross_query = cross_query.reshape(D, half)
    cross_out = lax.dynamic_slice_in_dim(cross_out.reshape(D, D), core * half, half, 0)
    kv_own = jnp.concatenate(
        [keys_own.reshape(DT, half), values_own.reshape(DT, half)], 1
    )
    gate_weight, up_weight = gate_weight.reshape(D, FF // 2), up_weight.reshape(D, FF // 2)
    down = down.reshape(FF // 2, D)

    meta = jnp.concatenate([timesteps[:, None], text_lengths[:, None], negatives], 1)
    metas = meta
    for axis in ("c", "x", "y"):
        metas = grow(metas, axis)
    base = 4 * plane + 2 * core
    relative = jnp.arange(items_total, dtype=jnp.int32)
    metas = metas[(item ^ base) ^ relative]
    timestep, text_length = metas[0, 0], metas[0, 1]
    negative_rows = metas[:, 2:]
    frames = own_quarters(jnp.concatenate([latents, noise_field], 2), core, line)
    clean, noise = frames[:, :DIN], frames[:, DIN:]
    tokens = own_quarters(text_tokens, core, line)
    quarter = line ^ four
    frame_positions = (
        (quarter[:, None] * 256 + jnp.arange(256, dtype=jnp.int32)[None, :]).reshape(-1) + 1
    )
    token_slots = (
        quarter[:, None] * 32 + jnp.arange(32, dtype=jnp.int32)[None, :]
    ).reshape(-1)
    halfway = HD // 2
    frequency = jnp.exp(jnp.arange(halfway, dtype=f32) * (-2.0 * math.log(10000.0) / HD))
    turn = frame_positions.astype(f32)[:, None] * frequency[None, :]
    cosine_table = jnp.concatenate([jnp.cos(turn)] * 4, -1)
    sine_table = jnp.concatenate([-jnp.sin(turn), jnp.sin(turn)] * 2, -1)
    angle = (timestep.astype(f32) + 0.5) * (0.5 * math.pi / NTIME)
    signal, spread = jnp.cos(angle), jnp.sin(angle)
    noised = (signal * clean + spread * noise).astype(bf16)
    target = signal * noise - spread * clean

    residual = dot_back(noised, weight_in)
    normed_one, inverse_one = layer_stats(residual)
    input_one = (normed_one * gain_values[:, 0]).astype(bf16)
    features = time_features(timestep[None]).astype(bf16)
    embeds = jnp.dot(features, table_full, preferred_element_type=f32)
    normed_time, inverse_time = layer_stats(embeds)
    input_time = (normed_time * gain_values[:, 0]).astype(bf16)
    time_block = jnp.pad(input_time, ((0, 15), (0, 0)))
    joined, joined_time = join(input_one, time_block, projection, cosine_table, sine_table)
    pairs = half // 128
    self_offsets = (0, pairs, 2 * pairs)
    mixed_flat, logsum_self = attend(
        joined, joined, joined, (joined_time, joined_time), self_offsets, True
    )
    after_self = residual + on_both(jnp.dot(mixed_flat, weight_mix, preferred_element_type=f32))
    normed_two, inverse_two = layer_stats(after_self)
    input_two = (normed_two * gain_values[:, 1]).astype(bf16)
    cross_queries = jnp.dot(input_two, cross_query, preferred_element_type=f32).astype(bf16)
    projected = jnp.dot(tokens, kv_own, preferred_element_type=f32).astype(bf16)
    valid = token_slots < text_length
    cross_bias = jnp.where(valid, 0.0, MASK_VALUE).astype(f32)[None]
    text_biases = (
        jnp.broadcast_to(cross_bias, (8, 128)),
        jnp.broadcast_to(cross_bias.T, (128, 128)),
    )
    cross_offsets = (0, 0, pairs)
    cross_flat, logsum_cross = attend(
        cross_queries, projected, projected, text_biases, cross_offsets, False
    )
    after_cross = after_self + on_both(jnp.dot(cross_flat, cross_out, preferred_element_type=f32))
    normed_three, inverse_three = layer_stats(after_cross)
    input_three = (normed_three * gain_values[:, 2]).astype(bf16)
    gate_part = jnp.dot(input_three, gate_weight, preferred_element_type=f32)
    up_part = jnp.dot(input_three, up_weight, preferred_element_type=f32)
    sigmoid = jax.nn.sigmoid(gate_part)
    silu_value = gate_part * sigmoid
    hidden = (silu_value * up_part).astype(bf16)
    down_out = on_both(jnp.dot(hidden, down, preferred_element_type=f32))
    output_rows = after_cross + down_out
    output_low = output_rows.astype(bf16)
    predicted = jnp.dot(output_low, weight_out, preferred_element_type=f32)
    errors = predicted - target

    length_float = text_length.astype(f32)
    mask = valid.astype(f32)[:, None]
    text_half = jnp.sum(projected[:, :half].astype(f32) * mask, 0) / length_float
    text_rest = swap(text_half, "c")
    text_pool = jnp.where(
        core == 0,
        jnp.concatenate([text_half, text_rest]),
        jnp.concatenate([text_rest, text_half]),
    )
    pools = jnp.stack([jnp.sum(output_rows, 0) / FRAMES, text_pool], 0)[None]
    for axis in ("z", "x", "y"):
        pools = grow(pools, axis)
    inverse_pools = lax.rsqrt(jnp.sum(pools * pools, -1, keepdims=True) + POOL_EPS)
    units = pools * inverse_pools
    audio_units, text_units = units[:, 0], units[:, 1]
    similar = (
        lax.dot_general(
            audio_units, text_units, (((1,), (1,)), ((), ())), precision=BEST_PRECISION
        )
        / CONTRAST_TEMP
    )
    same = jnp.eye(items_total, dtype=f32)
    counts = same + jnp.sum(
        (negative_rows[:, None, :] == (item ^ relative)[None, :, None]).astype(f32), -1
    )
    peak = jnp.max(jnp.where(counts > 0, similar, -jnp.inf), -1, keepdims=True)
    powers = jnp.where(counts > 0, counts * jnp.exp(similar - peak), 0.0)
    totals_row = jnp.sum(powers, -1, keepdims=True)
    contrast_own = peak[0, 0] + jnp.log(totals_row[0, 0]) - similar[0, 0]
    grad_similar = (powers / totals_row - same) * (
        CONTRAST_WEIGHT / items_total / CONTRAST_TEMP
    )
    grad_audio_unit = jnp.sum(grad_similar[0][:, None] * text_units, 0)
    grad_text_unit = jnp.sum(grad_similar[:, 0][:, None] * audio_units, 0)

    def unit_back(gradient, unit, inverse):
        return inverse * (gradient - unit * jnp.sum(unit * gradient))

    grad_audio = unit_back(grad_audio_unit, audio_units[0], inverse_pools[0, 0])
    grad_text = unit_back(grad_text_unit, text_units[0], inverse_pools[0, 1])

    grad_predicted = (2.0 * mse_scale * errors).astype(bf16)
    grad_out_weight = tdot(output_low, grad_predicted)
    grad_output = dot_back(grad_predicted, weight_out) + grad_audio[None, :] / FRAMES
    grad_low = grad_output.astype(bf16)
    grad_down = tdot(hidden, grad_low).astype(bf16)
    grad_hidden = dot_back(grad_low, down)
    grad_gate = (grad_hidden * up_part * sigmoid * (1.0 + gate_part * (1.0 - sigmoid))).astype(bf16)
    grad_up = (grad_hidden * silu_value).astype(bf16)
    grad_gate_weight = tdot(input_three, grad_gate).astype(bf16)
    grad_up_weight = tdot(input_three, grad_up).astype(bf16)
    feed_arrays = (("cols", (48, FF // 2)), ("cols", (48, FF // 2)), ("one", (192, D)))
    feed_groups = [
        ((2, 0, whole, pl.ds(step * 384, 384)), (2, 1, whole, pl.ds(half + step * 384, 384)))
        for step in range(2)
    ]
    feed_groups += [
        ((0, 0, whole, pl.ds(step * 768, 768)), (1, 1, whole, pl.ds(step * 768, 768)))
        for step in range(4)
    ]
    feed_sums = reduce_gradients(
        feed_arrays,
        feed_groups,
        (
            grad_gate_weight.reshape(4, 2, 4, 48, FF // 2),
            grad_up_weight.reshape(4, 2, 4, 48, FF // 2),
            grad_down.reshape(4, 1, 4, 192, D),
        ),
        2,
    )
    gate_columns = []
    for mine, other in ((feed_sums[0], feed_sums[1]), (feed_sums[2], feed_sums[3])):
        sides = (jnp.where(core == 0, mine, other), jnp.where(core == 0, other, mine))
        for quadrant in quads:
            for side in sides:
                gate_columns.append(side[:, quadrant * 768 : (quadrant + 1) * 768])
    grad_gate_up = jnp.concatenate(gate_columns, 1).astype(f32)
    grad_down = feed_sums[4].astype(f32)
    grad_input_three = on_both(dot_back(grad_gate, gate_weight) + dot_back(grad_up, up_weight))
    grad_after_cross, gain_three = layer_back(
        grad_input_three, normed_three, inverse_three, gain_values[:, 2]
    )
    grad_after_cross = grad_after_cross + grad_output
    grad_cross_in = grad_after_cross.astype(bf16)
    cross_rows = tdot(cross_flat, grad_cross_in).astype(bf16).reshape(2, 2, 192, D)
    cross_kept = pick(cross_rows, core, 1)
    cross_received = swap(pick(cross_rows, 1 - core, 1), "c")
    cross_pair = jnp.stack([cross_kept, cross_received], 0)
    out_rows = jnp.where(core == 0, cross_pair, cross_pair[::-1]).reshape(4, 1, 4, 48, D)
    grad_mixed_cross = dot_back(grad_cross_in, cross_out).astype(bf16)
    grad_cq, grad_text_keys, grad_text_values = attend_back(
        cross_queries,
        projected,
        projected,
        text_biases,
        cross_offsets,
        cross_flat,
        logsum_cross,
        grad_mixed_cross,
        None,
    )
    grad_query_weight = tdot(input_two, grad_cq).astype(bf16).reshape(4, 2, 4, 48, half)
    grad_input_two = on_both(dot_back(grad_cq, cross_query))
    text_half_grad = lax.dynamic_slice_in_dim(grad_text, core * half, half, 0)
    grad_pair_keys = (
        grad_text_keys + mask * (text_half_grad[None, :] / length_float)
    ).astype(bf16)
    kv_sources = [
        tdot(tokens, gradient.astype(bf16)).astype(bf16).reshape(4, 2, 4, 16, 1152)
        for gradient in (grad_pair_keys, grad_text_values)
    ]
    grad_after_self, gain_two = layer_back(
        grad_input_two, normed_two, inverse_two, gain_values[:, 1]
    )
    grad_after_self = grad_after_self + grad_after_cross
    grad_self_in = grad_after_self.astype(bf16)
    grad_mix = tdot(mixed_flat, grad_self_in).astype(bf16)
    grad_mixed_self = dot_back(grad_self_in, weight_mix).astype(bf16)
    grad_queries, grad_keys, grad_values, grad_time_keys, grad_time_values = attend_back(
        joined,
        joined,
        joined,
        (joined_time, joined_time),
        self_offsets,
        mixed_flat,
        logsum_self,
        grad_mixed_self,
        (cosine_table, sine_table),
    )
    grad_joined = jnp.concatenate([grad_queries, grad_keys, grad_values], 1)
    grad_time_pair = jnp.concatenate([grad_time_keys[:1], grad_time_values[:1]], 1)
    time_row = jnp.concatenate([jnp.zeros((1, half), f32), grad_time_pair], 1)
    grad_projection = (
        tdot(input_one, grad_joined) + input_time.astype(f32).reshape(D, 1) * time_row
    ).astype(bf16)
    grad_squares = jnp.concatenate(
        [grad_projection, jnp.concatenate([grad_mix[:, :half], grad_mix[:, half:]], 0)], 1
    )

    position = jnp.arange(256, dtype=jnp.int32)
    owner_core = core ^ (position // 128)
    block = assignment[
        (position // 32) % 4 * 64 + owner_core * 32 + (position // 8) % 4 * 8 + position % 8
    ]
    matrix, block_row, block_column = block // 64, (block // 8) % 8, block % 8
    is_out = matrix == 3
    out_pair = block_column // 2
    tile_row = jnp.where(is_out, block_row % 4 + 4 * (out_pair // 2), block_row)
    tile_column = jnp.where(is_out, 6 + out_pair % 2, matrix * 2 + (block_column % 4) // 2)
    held = jnp.where(is_out, block_row // 4, block_column // 4) == core
    collected = collect(
        grad_squares,
        jnp.where(held, tile_row * 8 + tile_column, 0),
        jnp.where(held, block_column % 2, 2),
        moves,
    ).reshape(2, 4, 1, 4, 4 * BLK, 2 * BLK)
    slot_sums = low_sum(collected[0], swap(collected[1], "c")).astype(bf16)

    partial_one = dot_back(grad_joined, projection)
    partial_time = jnp.dot(
        grad_time_pair, projection[:, half:].astype(f32).T, precision=BEST_PRECISION
    )
    grad_input_one = on_both(partial_one)
    grad_input_time = partial_time + swap(partial_time, "c")
    grad_residual, gain_one = layer_back(grad_input_one, normed_one, inverse_one, gain_values[:, 0])
    grad_residual = (grad_residual + grad_after_self).astype(bf16)
    grad_embeds, gain_time = layer_back(
        grad_input_time, normed_time, inverse_time, gain_values[:, 0]
    )
    grad_in_weight = tdot(grad_residual, noised)
    grad_table = features.astype(f32).reshape(NTIME, 1) * grad_embeds
    grad_gains = jnp.stack([gain_one + gain_time, gain_two, gain_three], 1)
    grad_ends = jnp.stack([grad_in_weight, grad_out_weight], 1)

    def own_rows(values, width):
        return pick(values.reshape(2, 2, 2, 4, -1, width), core, 2)

    small = jnp.concatenate(
        [
            own_rows(grad_ends.reshape(-1, D), D),
            own_rows(grad_table, D),
            jnp.pad(
                own_rows(grad_gains.reshape(32, 144), 144),
                ((0, 0), (0, 0), (0, 0), (0, 3), (0, D - 144)),
            ),
        ],
        3,
    )
    rest_arrays = (
        ("one", (4 * BLK, 2 * BLK)),
        ("cols", (48, half)),
        ("one", (48, D)),
        ("cols", (16, 1152)),
        ("cols", (16, 1152)),
        ("one", (16, D)),
    )
    rest_groups = [
        ((1, 0, whole, whole), (2, 1, whole, whole), (3, 0, whole, whole), (4, 1, whole, whole))
    ]
    rest_groups += [
        ((0, 0, pl.ds(step * 192, 192), whole), (0, 1, pl.ds(384 + step * 192, 192), whole))
        for step in range(2)
    ]
    rest_groups += [((5, 0, whole, whole),)]
    rest_sums = reduce_gradients(
        rest_arrays,
        rest_groups,
        (
            slot_sums,
            grad_query_weight,
            out_rows,
            kv_sources[0],
            kv_sources[1],
            small.astype(bf16).reshape(4, 1, 4, 16, D),
        ),
        3,
    )
    slot_rows, query_mine, query_other, grad_cross_out, *kv_sums, small = (
        value.astype(f32) for value in rest_sums
    )
    slot_rows = slot_rows.reshape(4, BLK, 2 * BLK)
    grad_slots = jnp.stack([slot_rows[:, :, :BLK], slot_rows[:, :, BLK:]], 1).reshape(8, BLK, BLK)
    grad_cross_query = jnp.where(
        core == 0,
        jnp.concatenate([query_mine, query_other], 1),
        jnp.concatenate([query_other, query_mine], 1),
    )
    grad_cross = jnp.stack([grad_cross_query, grad_cross_out], 1)
    kv_columns = []
    for mine, other in (kv_sums[:2], kv_sums[2:]):
        mine, other = mine.reshape(24, half), other.reshape(24, half)
        kv_columns.append(jnp.where(core == 0, mine, other))
        kv_columns.append(jnp.where(core == 0, other, mine))
    grad_key_value = jnp.concatenate(kv_columns, 1)
    grad_ends = small[:4].reshape(48, 2, DIN)
    grad_table = small[4:12]
    grad_gains = small[12, :144].reshape(48, 3)

    reduced = (
        grad_ends,
        grad_table,
        grad_slots,
        grad_cross,
        grad_key_value,
        grad_gate_up,
        grad_down,
        grad_gains,
    )
    square_sum = jnp.zeros((), f32)
    for member in reduced:
        square_sum = square_sum + jnp.sum(member * member)
    loss_part = jnp.where(
        core == 0,
        jnp.sum(errors * errors) * mse_scale + contrast_own * (CONTRAST_WEIGHT / items_total),
        0.0,
    )
    loss_total, norm_square = all_sum(loss_part, square_sum)
    return finish(
        loss_total,
        jnp.sqrt(norm_square),
        reduced,
        (
            end_weights,
            time_table,
            square_slots,
            cross_weights,
            key_value,
            gate_up,
            down_weight,
            norm_gains,
        ),
        (
            first_ends,
            first_table,
            None,
            first_cross,
            first_key_value,
            first_gate_up,
            first_down,
            first_gains,
        ),
        (
            second_ends,
            second_table,
            None,
            second_cross,
            second_key_value,
            second_gate_up,
            second_down,
            second_gains,
        ),
        (left_stats, right_stats, left_roots, right_roots),
    )


def all_sum(*values):
    total = jnp.stack(values)
    for axis in ("c", "z", "x", "y"):
        bit = 1
        while bit < lax.axis_size(axis):
            total = total + swap(total, axis, bit)
            bit *= 2
    return total[0], total[1]


def finish(loss_total, gradient_norm, reduced, masters, firsts, seconds, statistics):
    factor = CLIP_NORM / jnp.maximum(gradient_norm, CLIP_NORM)
    results = [loss_total, gradient_norm]
    for index_value in (0, 1, 3, 4, 5, 6, 7):
        results.extend(
            adam_update(
                masters[index_value],
                firsts[index_value],
                seconds[index_value],
                factor * reduced[index_value],
                ADAM_RATES[index_value],
            )
        )
    clipped_slots = factor * reduced[2]
    left_new, right_new, slots_new = shampoo_update(masters[2], clipped_slots, *statistics)
    results.extend([clipped_slots, left_new, right_new, slots_new])
    return tuple(results)


def solution(mesh):
    lines = mesh.shape["text"]
    chips = mesh.devices.size // 2
    if mesh.shape["dp"] == 8 and lines == 4 and 2 * mesh.shape["dp"] == chips:
        mesh = Mesh(mesh.devices.reshape(2, 2, 2, lines), ("y", "x", "c", "z"))
        dp, text, body = ("y", "x", "c"), ("z",), item_per_chip
    else:
        dp, text, body = ("dp",), ("text",), shards
    own = dp + text
    in_specs = (
        P(dp, text, None),
        P(dp, text, None),
        P(dp),
        P(dp, text, None),
        P(dp),
        P(dp, None),
        P(),
    ) + (P(own),) * 26
    out_specs = (P(), P()) + (P(own),) * 25
    return jax.shard_map(body, mesh=mesh, in_specs=in_specs, out_specs=out_specs, check_vma=False)
```

```python
from functools import partial
import math

import jax
import jax.numpy as jnp
from jax import lax
from jax.experimental import pallas as pl
from jax.experimental.pallas import tpu as pltpu
from jax.sharding import Mesh, PartitionSpec as P

D = 1536
HEADS = 24
HD = 64
FF = 6144
DIN = 64
DT = 768
FRAMES = 1024
NTIME = 256
STEP = 10
BLK = 192


BEST_PRECISION = lax.Precision.HIGHEST
NORM_EPS = 1e-05
POOL_EPS = 1e-06
SCORE_SCALE = 0.125
CONTRAST_TEMP = 0.02
CONTRAST_WEIGHT = 0.1
CLIP_NORM = 0.005
BETA_FIRST = 0.9
BETA_SECOND = 0.999
ADAM_EPS = 1e-08
WEIGHT_DECAY = 0.01
ADAM_RATES = (0.02, 0.05, 0.0, 0.1, 0.02, 0.02, 0.02, 1.0)
STAT_DECAY = 0.999
SHAMPOO_RATE = 0.01
MASK_VALUE = -1000000000.0


def layer_stats(inputs):
    center = inputs - jnp.mean(inputs, -1, keepdims=True)
    inverse = lax.rsqrt(jnp.mean(center * center, -1, keepdims=True) + NORM_EPS)
    return (center * inverse, inverse)


def layer_back(grad_out, normed, inverse, gain_row):
    scaled = grad_out * gain_row
    grad_in = inverse * (
        scaled
        - jnp.mean(scaled, -1, keepdims=True)
        - normed * jnp.mean(scaled * normed, -1, keepdims=True)
    )
    return (grad_in, jnp.sum(grad_out * normed, 0))


def time_features(timesteps):
    halfway = NTIME // 2
    frequency = jnp.exp(jnp.arange(halfway, dtype=jnp.float32) * (math.log(64.0) / halfway))
    moment = (timesteps.astype(jnp.float32) + 0.5) / NTIME
    phase = 2.0 * math.pi * moment[:, None] * frequency[None, :]
    return jnp.concatenate([jnp.cos(phase), jnp.sin(phase)], 1)


def rope_tables(positions_count, offset):
    halfway = HD // 2
    frequency = jnp.exp(jnp.arange(halfway, dtype=jnp.float32) * (-2.0 * math.log(10000.0) / HD))
    positions = (jnp.arange(positions_count, dtype=jnp.int32) + offset).astype(jnp.float32)
    angles = positions[:, None] * frequency[None, :]
    return (jnp.concatenate([jnp.cos(angles)] * 2, -1), jnp.concatenate([jnp.sin(angles)] * 2, -1))


def rotate(values, cosine_table, sine_table):
    halfway = HD // 2
    turned = jnp.concatenate([-values[..., halfway:], values[..., :halfway]], -1)
    return values * cosine_table[:, None, :] + turned * sine_table[:, None, :]


def rotate_back(gradient, cosine_table, sine_table):
    halfway = HD // 2
    product = gradient * sine_table[:, None, :]
    return gradient * cosine_table[:, None, :] + jnp.concatenate(
        [product[..., halfway:], -product[..., :halfway]], -1
    )


def to_matrices(blocks):
    per_side = D // BLK
    return blocks.reshape(4, per_side, per_side, BLK, BLK).transpose(0, 1, 3, 2, 4).reshape(4, D, D)


def to_blocks(matrices):
    per_side = D // BLK
    return (
        matrices.reshape(4, per_side, BLK, per_side, BLK)
        .transpose(0, 1, 3, 2, 4)
        .reshape(4 * per_side * per_side, BLK, BLK)
    )


def normalize(vectors):
    return vectors * lax.rsqrt(jnp.sum(vectors * vectors, -1, keepdims=True) + POOL_EPS)


def contrast_loss(pooled_audio, pooled_text, negatives):
    audio_unit_vectors = normalize(pooled_audio)
    text_unit_vectors = normalize(pooled_text)
    positive_pairs = jnp.sum(audio_unit_vectors * text_unit_vectors, -1) / CONTRAST_TEMP
    negative_pairs = (
        jnp.einsum(
            "ux,uax->ua", audio_unit_vectors, text_unit_vectors[negatives], precision=BEST_PRECISION
        )
        / CONTRAST_TEMP
    )
    scores = jnp.concatenate([positive_pairs[:, None], negative_pairs], 1)
    peak_score = jnp.max(scores, -1, keepdims=True)
    logsum = peak_score[:, 0] + jnp.log(jnp.sum(jnp.exp(scores - peak_score), -1))
    return jnp.sum(logsum - positive_pairs)


def item_scores(one_query, one_key, one_bias):
    scores = jnp.einsum("fhd,khd->hfk", one_query, one_key, preferred_element_type=jnp.float32)
    return scores * SCORE_SCALE + one_bias


def attend_forward(queries, all_keys, values, key_bias):

    def single(pieces):
        one_query, one_key, one_value, one_bias = pieces
        scores = item_scores(one_query, one_key, one_bias)
        peak_score = jnp.max(scores, -1, keepdims=True)
        weights = jnp.exp(scores - peak_score)
        row_total = jnp.sum(weights, -1, keepdims=True)
        mixture = jnp.einsum(
            "hfk,khd->fhd",
            (weights / row_total).astype(jnp.bfloat16),
            one_value,
            preferred_element_type=jnp.float32,
        )
        return (mixture.astype(jnp.bfloat16), peak_score + jnp.log(row_total))

    return lax.map(single, (queries, all_keys, values, key_bias))


def attend_backward(queries, all_keys, values, key_bias, logsums, grad_mixture):

    def single(pieces):
        one_query, one_key, one_value, one_bias, one_logsum, grad_rows = pieces
        attention = jnp.exp(item_scores(one_query, one_key, one_bias) - one_logsum)
        grad_attention = jnp.einsum(
            "fhd,khd->hfk", grad_rows, one_value, preferred_element_type=jnp.float32
        )
        grad_value = jnp.einsum(
            "hfk,fhd->khd",
            attention.astype(jnp.bfloat16),
            grad_rows,
            preferred_element_type=jnp.float32,
        )
        grad_scores = attention * (
            grad_attention - jnp.sum(attention * grad_attention, -1, keepdims=True)
        )
        grad_scores = grad_scores.astype(jnp.bfloat16)
        grad_query = (
            jnp.einsum("hfk,khd->fhd", grad_scores, one_key, preferred_element_type=jnp.float32)
            * SCORE_SCALE
        )
        grad_key = (
            jnp.einsum("hfk,fhd->khd", grad_scores, one_query, preferred_element_type=jnp.float32)
            * SCORE_SCALE
        )
        return (grad_query, grad_key, grad_value)

    return lax.map(single, (queries, all_keys, values, key_bias, logsums, grad_mixture))


def feed_forward(rows_in, gate_matrix, down_matrix):
    width = down_matrix.shape[0]
    gate_values = jnp.dot(rows_in, gate_matrix, preferred_element_type=jnp.float32)
    gate_part = gate_values[:, :width]
    up_part = gate_values[:, width:]
    sigmoid = jax.nn.sigmoid(gate_part)
    silu_value = gate_part * sigmoid
    hidden = (silu_value * up_part).astype(jnp.bfloat16)
    partial_out = jnp.dot(hidden, down_matrix, preferred_element_type=jnp.float32)
    return (partial_out, (hidden, gate_part, up_part, sigmoid, silu_value))


def feed_back(rows_in, gate_matrix, down_matrix, kept, grad_low):
    hidden, gate_part, up_part, sigmoid, silu_value = kept
    grad_down = jnp.einsum("rf,rd->fd", hidden, grad_low, preferred_element_type=jnp.float32)
    grad_hidden = jnp.einsum("rd,fd->rf", grad_low, down_matrix, preferred_element_type=jnp.float32)
    grad_gate = grad_hidden * up_part * sigmoid * (1.0 + gate_part * (1.0 - sigmoid))
    grad_pair = jnp.concatenate([grad_gate, grad_hidden * silu_value], 1).astype(jnp.bfloat16)
    grad_gate_up = jnp.einsum("rd,rg->dg", rows_in, grad_pair, preferred_element_type=jnp.float32)
    grad_rows = jnp.einsum("rg,dg->rd", grad_pair, gate_matrix, preferred_element_type=jnp.float32)
    return (grad_rows, grad_gate_up, grad_down)


def adam_update(weight, first_moment, second_moment, gradient, rate):
    first_moment = BETA_FIRST * first_moment + (1.0 - BETA_FIRST) * gradient
    second_moment = BETA_SECOND * second_moment + (1.0 - BETA_SECOND) * gradient * gradient
    corrected = first_moment / (1.0 - BETA_FIRST**STEP)
    scaled = second_moment / (1.0 - BETA_SECOND**STEP)
    weight = weight - rate * (corrected / (jnp.sqrt(scaled) + ADAM_EPS) + WEIGHT_DECAY * weight)
    return (first_moment, second_moment, weight)


def shampoo_update(slots_now, gradient, left_stat, right_stat, left_root, right_root):
    left_stat = STAT_DECAY * left_stat + (1.0 - STAT_DECAY) * jnp.einsum(
        "sij,skj->sik", gradient, gradient, precision=BEST_PRECISION
    )
    right_stat = STAT_DECAY * right_stat + (1.0 - STAT_DECAY) * jnp.einsum(
        "sji,sjk->sik", gradient, gradient, precision=BEST_PRECISION
    )
    inner = jnp.einsum("sij,sjk->sik", gradient, right_root, precision=BEST_PRECISION)
    direction = jnp.einsum("sij,sjk->sik", left_root, inner, precision=BEST_PRECISION)
    return (
        left_stat,
        right_stat,
        slots_now - SHAMPOO_RATE * (direction + WEIGHT_DECAY * slots_now),
    )


def shards(
    latents,
    noise_field,
    timesteps,
    text_tokens,
    text_lengths,
    negatives,
    assignment,
    end_weights,
    time_table,
    square_slots,
    cross_weights,
    key_value,
    gate_up,
    down_weight,
    norm_gains,
    first_ends,
    second_ends,
    first_table,
    second_table,
    first_cross,
    second_cross,
    first_key_value,
    second_key_value,
    first_gate_up,
    second_gate_up,
    first_down,
    second_down,
    first_gains,
    second_gains,
    left_stats,
    right_stats,
    left_roots,
    right_roots,
):
    text_index = lax.axis_index("text")
    group_index = lax.axis_index("dp")
    group_count = lax.axis_size("dp")
    text_count_axis = lax.axis_size("text")
    piece_width = FF // (group_count * text_count_axis)
    low_ends = end_weights.astype(jnp.bfloat16)
    low_table = time_table.astype(jnp.bfloat16)
    low_slots = square_slots.astype(jnp.bfloat16)
    low_cross = cross_weights.astype(jnp.bfloat16)
    low_pairs = key_value.astype(jnp.bfloat16)
    low_gains = norm_gains.astype(jnp.bfloat16)
    low_gate = gate_up.astype(jnp.bfloat16)
    low_down = down_weight.astype(jnp.bfloat16)
    group_set = (
        lax.all_gather(low_ends, "text", axis=0, tiled=True),
        lax.all_gather(low_table, "text", axis=0, tiled=True),
        lax.all_gather(low_slots, "text", axis=0, tiled=True),
        lax.all_gather(low_cross, "text", axis=0, tiled=True),
        lax.all_gather(low_pairs, "text", axis=0, tiled=True),
        lax.all_gather(low_gains, "text", axis=0, tiled=True),
        lax.all_gather(low_gate, "text", axis=0, tiled=True),
    )
    gate_group = group_set[6].reshape(
        group_set[6].shape[0], 2, group_count, text_count_axis, piece_width
    )
    gate_columns = lax.dynamic_index_in_dim(gate_group, text_index, 3, keepdims=False)
    full_set = (
        lax.all_gather(group_set[0], "dp", axis=0, tiled=True),
        lax.all_gather(group_set[1], "dp", axis=0, tiled=True),
        lax.all_gather(group_set[2], "dp", axis=0, tiled=True),
        lax.all_gather(group_set[3], "dp", axis=0, tiled=True),
        lax.all_gather(group_set[4], "dp", axis=0, tiled=True),
        lax.all_gather(group_set[5], "dp", axis=0, tiled=True),
        lax.all_gather(gate_columns, "dp", axis=0, tiled=True),
        lax.all_gather(low_down, "dp", axis=0, tiled=True),
    )
    ends_full, table_full, slots_full, cross_full, pairs_full, gains_full = full_set[:6]
    gate_full = full_set[6].reshape(D, 2 * group_count * piece_width)
    down_full = full_set[7]
    item_count = latents.shape[0]
    frames_dev = latents.shape[1]
    tokens_dev = text_tokens.shape[1]
    row_count = item_count * frames_dev
    items_total = item_count * group_count
    mse_scale = 1.0 / (items_total * FRAMES * DIN)
    weight_in = ends_full[:, 0, :]
    weight_out = ends_full[:, 1, :]
    gain_values = gains_full.astype(jnp.float32)
    inverse_order = (
        jnp.zeros_like(assignment)
        .at[assignment]
        .set(jnp.arange(assignment.shape[0], dtype=jnp.int32))
    )
    squares = to_matrices(slots_full[inverse_order])
    projection = jnp.concatenate([squares[0], squares[1], squares[2]], 1)
    cosine_table, sine_table = rope_tables(frames_dev, 1 + text_index * frames_dev)
    angles = (timesteps.astype(jnp.float32) + 0.5) * (0.5 * math.pi / NTIME)
    signal = jnp.cos(angles)[:, None, None]
    spread = jnp.sin(angles)[:, None, None]
    noised = (signal * latents + spread * noise_field).astype(jnp.bfloat16).reshape(row_count, DIN)
    residual = jnp.einsum("rc,dc->rd", noised, weight_in, preferred_element_type=jnp.float32)
    normed_one, inverse_one = layer_stats(residual)
    input_one = (normed_one * gain_values[:, 0]).astype(jnp.bfloat16)
    features = time_features(timesteps).astype(jnp.bfloat16)
    embeds = jnp.dot(features, table_full, preferred_element_type=jnp.float32)
    normed_time, inverse_time = layer_stats(embeds)
    input_time = (normed_time * gain_values[:, 0]).astype(jnp.bfloat16)
    joined_rows = jnp.dot(input_one, projection, preferred_element_type=jnp.float32)
    head_shape = (item_count, frames_dev, HEADS, HD)
    rot_queries = rotate(joined_rows[:, :D].reshape(head_shape), cosine_table, sine_table).astype(
        jnp.bfloat16
    )
    rot_keys = rotate(
        joined_rows[:, D : 2 * D].reshape(head_shape), cosine_table, sine_table
    ).astype(jnp.bfloat16)
    value_rows = joined_rows[:, 2 * D :].astype(jnp.bfloat16).reshape(item_count, frames_dev, D)
    time_pair = jnp.dot(input_time, projection[:, D:], preferred_element_type=jnp.float32).astype(
        jnp.bfloat16
    )
    keys_all, values_all = (
        lax.all_gather(rot_keys.reshape(item_count, frames_dev, D), "text", axis=1, tiled=True),
        lax.all_gather(value_rows, "text", axis=1, tiled=True),
    )
    key_count = keys_all.shape[1] + 1
    all_keys = jnp.concatenate([time_pair[:, None, :D], keys_all], 1).reshape(
        item_count, key_count, HEADS, HD
    )
    all_values = jnp.concatenate([time_pair[:, None, D:], values_all], 1).reshape(
        item_count, key_count, HEADS, HD
    )
    self_bias = jnp.zeros((item_count, key_count), jnp.float32)
    mixed_self, logsum_self = attend_forward(rot_queries, all_keys, all_values, self_bias)
    mixed_flat = mixed_self.reshape(row_count, D)
    after_self = residual + jnp.dot(mixed_flat, squares[3], preferred_element_type=jnp.float32)
    normed_two, inverse_two = layer_stats(after_self)
    input_two = (normed_two * gain_values[:, 1]).astype(jnp.bfloat16)
    cross_queries = jnp.dot(
        input_two, cross_full[:, 0, :], preferred_element_type=jnp.float32
    ).astype(jnp.bfloat16)
    cross_heads = cross_queries.reshape(head_shape)
    projected = jnp.dot(
        text_tokens.reshape(item_count * tokens_dev, DT),
        pairs_full,
        preferred_element_type=jnp.float32,
    )
    projected = projected.astype(jnp.bfloat16).reshape(item_count, tokens_dev, 2 * D)
    text_all = lax.all_gather(projected, "text", axis=1, tiled=True)
    text_count = text_all.shape[1]
    valid_keys = jnp.arange(text_count, dtype=jnp.int32)[None, :] < text_lengths[:, None]
    cross_bias = jnp.where(valid_keys, 0.0, MASK_VALUE).astype(jnp.float32)
    text_keys = text_all[:, :, :D].reshape(item_count, text_count, HEADS, HD)
    text_values = text_all[:, :, D:].reshape(item_count, text_count, HEADS, HD)
    mixed_cross, logsum_cross = attend_forward(cross_heads, text_keys, text_values, cross_bias)
    cross_flat = mixed_cross.reshape(row_count, D)
    after_cross = after_self + jnp.dot(
        cross_flat, cross_full[:, 1, :], preferred_element_type=jnp.float32
    )
    normed_three, inverse_three = layer_stats(after_cross)
    input_three = (normed_three * gain_values[:, 2]).astype(jnp.bfloat16)
    feed_rows = lax.all_gather(
        input_three.reshape(item_count, frames_dev, D), "text", axis=1, tiled=True
    ).reshape(-1, D)
    feed_out, feed_kept = feed_forward(feed_rows, gate_full, down_full)
    down_out = (
        lax.psum_scatter(
            feed_out.reshape(item_count, -1, D).astype(jnp.bfloat16),
            "text",
            scatter_dimension=1,
            tiled=True,
        )
        .astype(jnp.float32)
        .reshape(row_count, D)
    )
    output_rows = after_cross + down_out
    output_low = output_rows.astype(jnp.bfloat16)
    predicted = jnp.dot(output_low, weight_out, preferred_element_type=jnp.float32).reshape(
        latents.shape
    )
    errors = predicted - (signal * noise_field - spread * latents)
    lengths_float = text_lengths.astype(jnp.float32)
    own_valid = (text_index * tokens_dev + jnp.arange(tokens_dev, dtype=jnp.int32))[
        None, :
    ] < text_lengths[:, None]
    own_mask = own_valid.astype(jnp.float32)
    audio_part = jnp.sum(output_rows.reshape(item_count, frames_dev, D), 1)
    text_part = (
        jnp.sum(projected[:, :, :D].astype(jnp.float32) * own_mask[:, :, None], 1)
        / lengths_float[:, None]
    )
    pooled_set = (
        lax.all_gather(audio_part, ("dp", "text"), axis=0, tiled=True),
        lax.all_gather(text_part, ("dp", "text"), axis=0, tiled=True),
        lax.all_gather(negatives.astype(jnp.float32), ("dp", "text"), axis=0, tiled=True),
    )
    audio_pooled = (
        jnp.sum(pooled_set[0].reshape(group_count, text_count_axis, item_count, D), 1).reshape(
            -1, D
        )
        / FRAMES
    )
    text_pooled = jnp.sum(
        pooled_set[1].reshape(group_count, text_count_axis, item_count, D), 1
    ).reshape(-1, D)
    negative_rows = pooled_set[2].reshape(group_count, text_count_axis, item_count, -1)[:, 0]
    negative_rows = negative_rows.reshape(items_total, -1).astype(jnp.int32)
    contrast_value, contrast_back = jax.vjp(
        partial(contrast_loss, negatives=negative_rows), audio_pooled, text_pooled
    )
    grad_audio_all, grad_text_all = contrast_back(jnp.float32(CONTRAST_WEIGHT / items_total))
    grad_audio = lax.dynamic_slice_in_dim(grad_audio_all, group_index * item_count, item_count, 0)
    grad_text = lax.dynamic_slice_in_dim(grad_text_all, group_index * item_count, item_count, 0)
    grad_predicted = (2.0 * mse_scale * errors).astype(jnp.bfloat16).reshape(row_count, DIN)
    grad_out_weight = jnp.einsum(
        "rd,rc->dc", output_low, grad_predicted, preferred_element_type=jnp.float32
    )
    grad_output = jnp.einsum(
        "rc,dc->rd", grad_predicted, weight_out, preferred_element_type=jnp.float32
    )
    grad_output = (
        grad_output.reshape(item_count, frames_dev, D) + grad_audio[:, None, :] / FRAMES
    ).reshape(row_count, D)
    grad_down_in = grad_output.astype(jnp.bfloat16)
    grad_feed_rows = lax.all_gather(
        grad_down_in.reshape(item_count, frames_dev, D), "text", axis=1, tiled=True
    ).reshape(-1, D)
    grad_feed_in, grad_gate_up, grad_down = feed_back(
        feed_rows, gate_full, down_full, feed_kept, grad_feed_rows
    )
    grad_input_three = (
        lax.psum_scatter(
            grad_feed_in.reshape(item_count, -1, D).astype(jnp.bfloat16),
            "text",
            scatter_dimension=1,
            tiled=True,
        )
        .astype(jnp.float32)
        .reshape(row_count, D)
    )
    grad_after_cross, gain_three = layer_back(
        grad_input_three, normed_three, inverse_three, gain_values[:, 2]
    )
    grad_after_cross = grad_after_cross + grad_output
    grad_cross_in = grad_after_cross.astype(jnp.bfloat16)
    grad_cross_out = jnp.einsum(
        "rd,re->de", cross_flat, grad_cross_in, preferred_element_type=jnp.float32
    )
    grad_mixed_cross = jnp.einsum(
        "re,de->rd", grad_cross_in, cross_full[:, 1, :], preferred_element_type=jnp.float32
    )
    grad_mixed_cross = grad_mixed_cross.astype(jnp.bfloat16).reshape(head_shape)
    grad_cq, grad_text_keys, grad_text_values = attend_backward(
        cross_heads, text_keys, text_values, cross_bias, logsum_cross, grad_mixed_cross
    )
    grad_cq_low = grad_cq.reshape(row_count, D).astype(jnp.bfloat16)
    grad_cross_query = jnp.einsum(
        "rd,re->de", input_two, grad_cq_low, preferred_element_type=jnp.float32
    )
    grad_input_two = jnp.einsum(
        "re,de->rd", grad_cq_low, cross_full[:, 0, :], preferred_element_type=jnp.float32
    )
    grad_pairs = jnp.concatenate(
        [
            grad_text_keys.reshape(item_count, text_count, D),
            grad_text_values.reshape(item_count, text_count, D),
        ],
        2,
    )
    grad_own_pairs = lax.psum_scatter(
        grad_pairs.astype(jnp.bfloat16), "text", scatter_dimension=1, tiled=True
    ).astype(jnp.float32)
    pooled_grad = own_mask[:, :, None] * (grad_text[:, None, :] / lengths_float[:, None, None])
    grad_own_pairs = grad_own_pairs + jnp.concatenate([pooled_grad, jnp.zeros_like(pooled_grad)], 2)
    grad_own_pairs = grad_own_pairs.astype(jnp.bfloat16).reshape(item_count * tokens_dev, 2 * D)
    grad_textside = jnp.einsum(
        "tc,tk->ck",
        text_tokens.reshape(item_count * tokens_dev, DT),
        grad_own_pairs,
        preferred_element_type=jnp.float32,
    )
    grad_after_self, gain_two = layer_back(
        grad_input_two, normed_two, inverse_two, gain_values[:, 1]
    )
    grad_after_self = grad_after_self + grad_after_cross
    grad_self_in = grad_after_self.astype(jnp.bfloat16)
    grad_attn_out = jnp.einsum(
        "rd,re->de", mixed_flat, grad_self_in, preferred_element_type=jnp.float32
    )
    grad_mixed_self = jnp.einsum(
        "re,de->rd", grad_self_in, squares[3], preferred_element_type=jnp.float32
    )
    grad_mixed_self = grad_mixed_self.astype(jnp.bfloat16).reshape(head_shape)
    grad_rot_queries, grad_keys, value_gradients = attend_backward(
        rot_queries, all_keys, all_values, self_bias, logsum_self, grad_mixed_self
    )
    grad_keys_own, grad_values_own = (
        lax.psum_scatter(
            grad_keys[:, 1:].reshape(item_count, key_count - 1, D).astype(jnp.bfloat16),
            "text",
            scatter_dimension=1,
            tiled=True,
        ).astype(jnp.float32),
        lax.psum_scatter(
            value_gradients[:, 1:].reshape(item_count, key_count - 1, D).astype(jnp.bfloat16),
            "text",
            scatter_dimension=1,
            tiled=True,
        ).astype(jnp.float32),
    )
    grad_queries = (
        rotate_back(grad_rot_queries, cosine_table, sine_table)
        .astype(jnp.bfloat16)
        .reshape(row_count, D)
    )
    grad_key_rows = rotate_back(grad_keys_own.reshape(head_shape), cosine_table, sine_table)
    grad_key_rows = grad_key_rows.astype(jnp.bfloat16).reshape(row_count, D)
    grad_joined = jnp.concatenate(
        [grad_queries, grad_key_rows, grad_values_own.astype(jnp.bfloat16).reshape(row_count, D)], 1
    )
    grad_projection = jnp.einsum(
        "rd,rk->dk", input_one, grad_joined, preferred_element_type=jnp.float32
    )
    grad_input_one = jnp.einsum(
        "rk,dk->rd", grad_joined, projection, preferred_element_type=jnp.float32
    )
    grad_time_pair = jnp.concatenate(
        [grad_keys[:, 0].reshape(item_count, D), value_gradients[:, 0].reshape(item_count, D)], 1
    )
    time_rows = jnp.dot(input_time.astype(jnp.float32).T, grad_time_pair, precision=BEST_PRECISION)
    grad_projection = grad_projection + jnp.concatenate(
        [jnp.zeros((D, D), jnp.float32), time_rows], 1
    )
    grad_input_time = jnp.einsum(
        "ik,dk->id", grad_time_pair, projection[:, D:].astype(jnp.float32), precision=BEST_PRECISION
    )
    grad_residual, gain_one = layer_back(grad_input_one, normed_one, inverse_one, gain_values[:, 0])
    grad_residual = (grad_residual + grad_after_self).astype(jnp.bfloat16)
    grad_embeds, gain_time = layer_back(
        grad_input_time, normed_time, inverse_time, gain_values[:, 0]
    )
    grad_in_weight = jnp.einsum(
        "rd,rc->dc", grad_residual, noised, preferred_element_type=jnp.float32
    )
    grad_table = jnp.dot(features.astype(jnp.float32).T, grad_embeds, precision=BEST_PRECISION)
    grad_gains = jnp.stack([gain_one + gain_time, gain_two, gain_three], 1)
    grad_ends = jnp.stack([grad_in_weight, grad_out_weight], 1)
    grad_cross = jnp.stack([grad_cross_query, grad_cross_out], 1)
    grad_squares = jnp.stack(
        [
            grad_projection[:, :D],
            grad_projection[:, D : 2 * D],
            grad_projection[:, 2 * D :],
            grad_attn_out,
        ],
        0,
    )
    grad_slots = jnp.take(to_blocks(grad_squares), assignment, axis=0)
    gate_pieces = grad_gate_up.reshape(D, 2, group_count, piece_width)
    group_grads = (
        lax.psum_scatter(
            grad_ends.astype(jnp.bfloat16), "dp", scatter_dimension=0, tiled=True
        ).astype(jnp.float32),
        lax.psum_scatter(
            grad_table.astype(jnp.bfloat16), "dp", scatter_dimension=0, tiled=True
        ).astype(jnp.float32),
        lax.psum_scatter(
            grad_slots.astype(jnp.bfloat16), "dp", scatter_dimension=0, tiled=True
        ).astype(jnp.float32),
        lax.psum_scatter(
            grad_cross.astype(jnp.bfloat16), "dp", scatter_dimension=0, tiled=True
        ).astype(jnp.float32),
        lax.psum_scatter(
            grad_textside.astype(jnp.bfloat16), "dp", scatter_dimension=0, tiled=True
        ).astype(jnp.float32),
        lax.psum_scatter(
            grad_gains.astype(jnp.bfloat16), "dp", scatter_dimension=0, tiled=True
        ).astype(jnp.float32),
        lax.psum_scatter(
            gate_pieces.astype(jnp.bfloat16), "dp", scatter_dimension=0, tiled=True
        ).astype(jnp.float32),
        lax.psum_scatter(
            grad_down.astype(jnp.bfloat16), "dp", scatter_dimension=0, tiled=True
        ).astype(jnp.float32),
    )
    placing = (jnp.arange(text_count_axis, dtype=jnp.int32) == text_index).astype(jnp.float32)
    spread_gate = group_grads[6][:, :, :, None, :] * placing[None, None, None, :, None]
    spread_gate = spread_gate.reshape(spread_gate.shape[0], 2 * FF)
    owned = (
        lax.psum_scatter(
            group_grads[0].astype(jnp.bfloat16), "text", scatter_dimension=0, tiled=True
        ).astype(jnp.float32),
        lax.psum_scatter(
            group_grads[1].astype(jnp.bfloat16), "text", scatter_dimension=0, tiled=True
        ).astype(jnp.float32),
        lax.psum_scatter(
            group_grads[2].astype(jnp.bfloat16), "text", scatter_dimension=0, tiled=True
        ).astype(jnp.float32),
        lax.psum_scatter(
            group_grads[3].astype(jnp.bfloat16), "text", scatter_dimension=0, tiled=True
        ).astype(jnp.float32),
        lax.psum_scatter(
            group_grads[4].astype(jnp.bfloat16), "text", scatter_dimension=0, tiled=True
        ).astype(jnp.float32),
        lax.psum_scatter(
            group_grads[5].astype(jnp.bfloat16), "text", scatter_dimension=0, tiled=True
        ).astype(jnp.float32),
        lax.psum_scatter(
            spread_gate.astype(jnp.bfloat16), "text", scatter_dimension=0, tiled=True
        ).astype(jnp.float32),
    )
    reduced = (owned[0], owned[1], owned[2], owned[3], owned[4], owned[6], group_grads[7], owned[5])
    square_sum = jnp.zeros((), jnp.float32)
    for member in reduced:
        square_sum = square_sum + jnp.sum(member * member)
    loss_part = jnp.sum(errors * errors) * mse_scale
    totals = lax.psum((square_sum, loss_part), ("dp", "text"))
    loss_total = totals[1] + CONTRAST_WEIGHT * contrast_value / items_total
    gradient_norm = jnp.sqrt(totals[0])
    masters = (
        end_weights,
        time_table,
        square_slots,
        cross_weights,
        key_value,
        gate_up,
        down_weight,
        norm_gains,
    )
    firsts = (
        first_ends,
        first_table,
        None,
        first_cross,
        first_key_value,
        first_gate_up,
        first_down,
        first_gains,
    )
    seconds = (
        second_ends,
        second_table,
        None,
        second_cross,
        second_key_value,
        second_gate_up,
        second_down,
        second_gains,
    )
    return finish(
        loss_total,
        gradient_norm,
        reduced,
        masters,
        firsts,
        seconds,
        (left_stats, right_stats, left_roots, right_roots),
    )


def swap(values, axis, bit=1):
    return lax.ppermute(values, axis, [(i, i ^ bit) for i in range(lax.axis_size(axis))])


def pick(values, position, axis=0):
    return lax.dynamic_index_in_dim(values, position, axis, keepdims=False)


def grow(values, axis):
    bit = 1
    while bit < lax.axis_size(axis):
        values = jnp.concatenate([values, swap(values, axis, bit)], 0)
        bit *= 2
    return values


def own_quarters(values, core, line):
    pair = jnp.concatenate([values, swap(values, "c")], 0)
    pieces = []
    for offset in range(4):
        target = line ^ offset
        piece = pick(pair, ((target // 2) ^ core) * 2 + target % 2)
        pieces.append(swap(piece, "z", offset) if offset else piece)
    return jnp.concatenate(pieces, 0)


def low_sum(*terms):
    total = terms[0].astype(jnp.float32)
    for term in terms[1:]:
        total = total + term.astype(jnp.float32)
    return total


def on_both(partial_sum):
    low = partial_sum.astype(jnp.bfloat16)
    return low_sum(low, swap(low, "c"))


def tdot(left, right):
    return lax.dot_general(left, right, (((0,), (0,)), ((), ())), preferred_element_type=jnp.float32)


def dot_back(left, right):
    return lax.dot_general(left, right, (((1,), (1,)), ((), ())), preferred_element_type=jnp.float32)


MESH_ID = pl.DeviceIdType.MESH
JOIN_TILE = 512


def anywhere(count):
    return [pl.BlockSpec(memory_space=pl.ANY)] * count


def coordinates():
    return tuple(lax.axis_index(axis) for axis in ("y", "x", "c", "z"))


def chip_peers(me):
    row, column, core, line = me
    beside = {
        "c": (row, column, 1 - core, line),
        "x": (row, 1 - column, core, line),
        "y": (1 - row, column, core, line),
    }
    for offset in (1, 2, 3):
        beside[offset] = (row, column, core, line ^ offset)
    return beside


def greet(peers):
    barrier = pltpu.get_barrier_semaphore()
    for peer in peers.values():
        pl.semaphore_signal(barrier, inc=1, device_id=peer, device_id_type=MESH_ID)
    pl.semaphore_wait(barrier, len(peers))


def send(source, target, send_sem, recv_sem, peer):
    return pltpu.make_async_remote_copy(
        src_ref=source,
        dst_ref=target,
        send_sem=send_sem,
        recv_sem=recv_sem,
        device_id=peer,
        device_id_type=MESH_ID,
    )


def gather_kernel(arrays, groups, *refs):
    count = len(arrays)
    inputs = sum(2 if kind == "cols" else 1 for kind, _, _ in arrays)
    sources, bufs = list(refs[:inputs]), refs[inputs : inputs + count]
    send_sem, recv_sem, core_send, core_recv, local_sem = refs[inputs + count :]
    me = coordinates()
    row, column, core, line = me
    plane = 2 * row + column
    peers = chip_peers(me)
    greet(peers)
    local, cross = [], []
    for index_value, (kind, _, _) in enumerate(arrays):
        spot = bufs[index_value].at[plane, 0 if kind == "one" else core, line]
        copy = pltpu.make_async_copy(sources.pop(0), spot, local_sem.at[index_value])
        copy.start()
        local.append(copy)
        cross.append(None)
        if kind == "cols":
            cross[-1] = send(
                sources.pop(0),
                spot,
                core_send.at[index_value],
                core_recv.at[index_value],
                peers["c"],
            )
            cross[-1].start()
    whole = slice(None)
    flat = [unit for group in groups for unit in group]
    ready = set()

    def move(number, slot, planes, lines, peer):
        array, _, rows, columns = flat[number]
        cores = {"cols": whole, "one": 0}.get(arrays[array][0], core)
        view = bufs[array].at[planes, cores, lines, rows, columns]
        return send(view, view, send_sem.at[number, slot], recv_sem.at[number, slot], peer)

    def line_copies(number):
        return [move(number, o - 1, plane, line, peers[o]) for o in (1, 2, 3)]

    def near_copy(number):
        axis = "y" if flat[number][1] else "x"
        return move(number, 3, plane, whole, peers[axis])

    def side_copy(number):
        axis = "x" if flat[number][1] else "y"
        return move(number, 4, plane, whole, peers[axis])

    def far_copy(number):
        color = flat[number][1]
        return move(number, 5, plane ^ (2 if color else 1), whole, peers["x" if color else "y"])

    def core_copy(number):
        array, _, rows, columns = flat[number]
        kind = arrays[array][0]
        if kind not in ("both", "half"):
            return None
        planes = whole if kind == "both" else pl.ds(2 * (1 - core), 2)
        view = bufs[array].at[planes, core, whole, rows, columns]
        return send(view, view, send_sem.at[number, 6], recv_sem.at[number, 6], peers["c"])

    def start_line(number):
        array = flat[number][0]
        if array not in ready:
            ready.add(array)
            local[array].wait()
            if cross[array] is not None:
                cross[array].wait()
        for copy in line_copies(number):
            copy.start()

    def start_near(number):
        for copy in line_copies(number):
            copy.wait_recv()
        near_copy(number).start()
        side_copy(number).start()

    def start_far(number):
        near_copy(number).wait_recv()
        far_copy(number).start()

    def close(number):
        side_copy(number).wait_recv()
        far_copy(number).wait_recv()
        last = core_copy(number)
        if last is not None:
            last.start()
        for copy in line_copies(number) + [near_copy(number), side_copy(number), far_copy(number)]:
            copy.wait_send()

    stages = (start_line, start_near, start_far, close)
    numbers, at = [], 0
    for group in groups:
        numbers.append(range(at, at + len(group)))
        at += len(group)
    for step in range(len(groups) + 3):
        for lag, stage in enumerate(stages):
            if 0 <= step - lag < len(groups):
                for number in numbers[step - lag]:
                    stage(number)
    for number in range(len(flat)):
        last = core_copy(number)
        if last is not None:
            last.wait()


def gather_weights(arrays, groups, sources, collective_id):
    units = sum(len(group) for group in groups)
    dma = pltpu.SemaphoreType.DMA
    return pl.pallas_call(
        partial(gather_kernel, arrays, groups),
        out_shape=[
            jax.ShapeDtypeStruct((4, 1 if kind == "one" else 2, 4) + shape, dtype)
            for kind, shape, dtype in arrays
        ],
        in_specs=anywhere(len(sources)),
        out_specs=anywhere(len(arrays)),
        scratch_shapes=[
            dma((units, 7)),
            dma((units, 7)),
            dma((len(arrays),)),
            dma((len(arrays),)),
            dma((len(arrays),)),
        ],
        compiler_params=pltpu.CompilerParams(collective_id=collective_id, has_side_effects=True),
    )(*sources)


def reduce_kernel(arrays, groups, *refs):
    count = len(arrays)
    flat = [unit for group in groups for unit in group]
    total = len(flat)
    sources = refs[:count]
    outputs = sum(2 if kind == "cols" else 1 for kind, _ in arrays)
    targets, at = [], count
    for kind, _ in arrays:
        width = 2 if kind == "cols" else 1
        targets.append(refs[at : at + width])
        at += width
    scratch = refs[at:]
    sides, onwards, mines, from_ons, from_lines, from_cores = (
        scratch[index_value * total : (index_value + 1) * total] for index_value in range(6)
    )
    send_sem, recv_sem, load_sem = scratch[6 * total :]
    me = coordinates()
    row, column, core, line = me
    plane = 2 * row + column
    peers = chip_peers(me)
    greet(peers)
    whole = slice(None)

    def source(number, planes):
        array, _, rows, columns = flat[number]
        return sources[array].at[planes, whole, whole, rows, columns]

    def first_copy(number, slot):
        bit, axis = (1, "x") if flat[number][1] else (2, "y")
        return send(
            source(number, plane ^ (3 if slot else bit)),
            sides[number].at[slot],
            send_sem.at[number, slot],
            recv_sem.at[number, slot],
            peers[axis],
        )

    def load_onward(number):
        off = 2 if flat[number][1] else 1
        return pltpu.make_async_copy(
            source(number, plane ^ off), onwards[number], load_sem.at[number, 0]
        )

    def load_mine(number):
        return pltpu.make_async_copy(source(number, plane), mines[number], load_sem.at[number, 1])

    def onward_copy(number):
        axis = "y" if flat[number][1] else "x"
        return send(
            onwards[number],
            from_ons[number],
            send_sem.at[number, 2],
            recv_sem.at[number, 2],
            peers[axis],
        )

    def line_copies(number):
        return [
            send(
                mines[number].at[whole, line ^ offset],
                from_lines[number].at[offset - 1],
                send_sem.at[number, 2 + offset],
                recv_sem.at[number, 2 + offset],
                peers[offset],
            )
            for offset in (1, 2, 3)
        ]

    def core_copy(number):
        return send(
            mines[number].at[1 - core, line],
            from_cores[number],
            send_sem.at[number, 6],
            recv_sem.at[number, 6],
            peers["c"],
        )

    def is_cols(number):
        return arrays[flat[number][0]][0] == "cols"

    def add_into(target, *terms):
        cores, lines, height, _ = target.shape

        def body(step, carry):
            side = step // (lines * (height // 16))
            rest = step % (lines * (height // 16))
            at_line = rest // (height // 16)
            rows = pl.ds(pl.multiple_of((rest % (height // 16)) * 16, 16), 16)
            value = target[side, at_line, rows].astype(jnp.float32)
            for term in terms:
                value = value + term[side, at_line, rows].astype(jnp.float32)
            target[side, at_line, rows] = value.astype(target.dtype)
            return carry

        lax.fori_loop(0, cores * lines * (height // 16), body, 0)

    def stage_one(number):
        first_copy(number, 1).start()
        first_copy(number, 0).start()
        load_onward(number).start()
        load_mine(number).start()

    def stage_two(number):
        first_copy(number, 1).wait_recv()
        load_onward(number).wait()
        add_into(onwards[number], sides[number].at[1])
        onward_copy(number).start()

    def stage_three(number):
        first_copy(number, 0).wait_recv()
        load_mine(number).wait()
        onward_copy(number).wait_recv()
        add_into(mines[number], sides[number].at[0], from_ons[number])
        for copy in line_copies(number):
            copy.start()

    def stage_four(number):
        for copy in line_copies(number):
            copy.wait_recv()
        array, _, rows, columns = flat[number]
        mine, pieces = mines[number], from_lines[number]
        for side in range(mine.shape[0]):
            value = mine[side, line].astype(jnp.float32)
            for offset in range(3):
                value = value + pieces[offset, side].astype(jnp.float32)
            mine[side, line] = value.astype(mine.dtype)
        if is_cols(number):
            core_copy(number).start()
            targets[array][0][rows, columns] = mine[core, line]
        else:
            targets[array][0][rows, columns] = mine[0, line]

    def stage_five(number):
        if is_cols(number):
            core_copy(number).wait()
            array, _, rows, columns = flat[number]
            targets[array][1][rows, columns] = from_cores[number][...]
        first_copy(number, 0).wait_send()
        first_copy(number, 1).wait_send()
        onward_copy(number).wait_send()
        for copy in line_copies(number):
            copy.wait_send()

    stages = (stage_one, stage_two, stage_three, stage_four, stage_five)
    numbers, at = [], 0
    for group in groups:
        numbers.append(range(at, at + len(group)))
        at += len(group)
    for step in range(len(groups) + 4):
        for lag, stage in enumerate(stages):
            if 0 <= step - lag < len(groups):
                for number in numbers[step - lag]:
                    stage(number)


def extent(sel, size):
    return size if isinstance(sel, slice) else sel.size


def reduce_gradients(arrays, groups, sources, collective_id):
    flat = [unit for group in groups for unit in group]
    vmem, dma, low = pltpu.VMEM, pltpu.SemaphoreType.DMA, jnp.bfloat16
    shapes = []
    for array, _, rows, columns in flat:
        kind, (height, width) = arrays[array]
        shapes.append((2 if kind == "cols" else 1, extent(rows, height), extent(columns, width)))
    scratch = [vmem((2, c, 4, h, w), low) for c, h, w in shapes]
    for _ in range(3):
        scratch += [vmem((c, 4, h, w), low) for c, h, w in shapes]
    scratch += [vmem((3, c, h, w), low) for c, h, w in shapes]
    scratch += [vmem((h, w) if c == 2 else (16, 128), low) for c, h, w in shapes]
    out_shape = []
    for kind, shape in arrays:
        out_shape += [jax.ShapeDtypeStruct(shape, low)] * (2 if kind == "cols" else 1)
    return pl.pallas_call(
        partial(reduce_kernel, arrays, groups),
        out_shape=out_shape,
        in_specs=anywhere(len(sources)),
        out_specs=[pl.BlockSpec(memory_space=pltpu.VMEM)] * len(out_shape),
        scratch_shapes=scratch
        + [dma((len(flat), 7)), dma((len(flat), 7)), dma((len(flat), 2))],
        compiler_params=pltpu.CompilerParams(
            collective_id=collective_id, has_side_effects=True, vmem_limit_bytes=60 * 2**20
        ),
    )(*sources)


def turned(values, cosine, sine):
    lane = lax.broadcasted_iota(jnp.int32, values.shape, 1)
    halfway = HD // 2
    partner = jnp.where(
        lane % HD < halfway,
        pltpu.roll(values, 128 - halfway, 1),
        pltpu.roll(values, halfway, 1),
    )
    return values * cosine + partner * sine


def join_kernel(rows, times, weights, cosine, sine, joined, joined_time):
    is_turned = pl.program_id(0) < 6

    def body(step, carry):
        at = pl.ds(pl.multiple_of(step * JOIN_TILE, JOIN_TILE), JOIN_TILE)
        values = jnp.dot(rows[at, :], weights[...], preferred_element_type=jnp.float32)

        @pl.when(is_turned)
        def turn():
            for side in (0, 128):
                joined[at, side : side + 128] = turned(
                    values[:, side : side + 128], cosine[at, :], sine[at, :]
                ).astype(joined.dtype)

        @pl.when(jnp.logical_not(is_turned))
        def keep():
            joined[at, :] = values.astype(joined.dtype)

        return carry

    lax.fori_loop(0, rows.shape[0] // JOIN_TILE, body, 0)
    joined_time[...] = jnp.dot(
        times[...], weights[...], preferred_element_type=jnp.float32
    ).astype(joined_time.dtype)


def join(rows, times, weights, cosine, sine):
    width = weights.shape[1]

    def fixed(array):
        return pl.BlockSpec(array.shape, lambda step: (0, 0))

    return pl.pallas_call(
        join_kernel,
        grid=(width // 256,),
        in_specs=[
            fixed(rows),
            fixed(times),
            pl.BlockSpec((D, 256), lambda step: (0, step)),
            fixed(cosine),
            fixed(sine),
        ],
        out_specs=[
            pl.BlockSpec((rows.shape[0], 256), lambda step: (0, step)),
            pl.BlockSpec((times.shape[0], 256), lambda step: (0, step)),
        ],
        out_shape=[
            jax.ShapeDtypeStruct((rows.shape[0], width), jnp.bfloat16),
            jax.ShapeDtypeStruct((times.shape[0], width), jnp.bfloat16),
        ],
        compiler_params=pltpu.CompilerParams(vmem_limit_bytes=48 * 2**20),
        cost_estimate=pl.CostEstimate(
            flops=2 * rows.shape[0] * D * width,
            bytes_accessed=2 * (rows.size + weights.size + rows.shape[0] * width),
            transcendentals=0,
        ),
    )(rows, times, weights, cosine, sine)


def head_lanes(shape, head):
    return lax.broadcasted_iota(jnp.int32, shape, 1) // HD == head


def attend_kernel(timed, queries, keys, values, first, second, mixed, logsum):
    tile = 256 if timed else 512

    def body(step, carry):
        at = pl.ds(pl.multiple_of(step * tile, tile), tile)
        rows = queries[at, :]
        total = jnp.zeros(rows.shape, jnp.float32)
        sums = jnp.zeros(rows.shape, jnp.float32)
        for head in range(2):
            own = head_lanes(rows.shape, head)
            query = jnp.where(own, rows, jnp.zeros_like(rows))
            scores = dot_back(query, keys[...]) * SCORE_SCALE
            if timed:
                extra = (
                    jnp.sum(
                        query.astype(jnp.float32) * first[0:1, :].astype(jnp.float32),
                        -1,
                        keepdims=True,
                    )
                    * SCORE_SCALE
                )
                peak = jnp.maximum(jnp.max(scores, -1, keepdims=True), extra)
            else:
                scores = scores + first[0:1, :]
                peak = jnp.max(scores, -1, keepdims=True)
            powers = jnp.exp(scores - peak)
            row_total = jnp.sum(powers, -1, keepdims=True)
            mixture = jnp.dot(
                powers.astype(jnp.bfloat16), values[...], preferred_element_type=jnp.float32
            )
            if timed:
                power = jnp.exp(extra - peak)
                row_total = row_total + power
                mixture = mixture + power * second[0:1, :].astype(jnp.float32)
            total = jnp.where(own, mixture / row_total, total)
            sums = jnp.where(own, peak + jnp.log(row_total), sums)
        mixed[at, :] = total.astype(mixed.dtype)
        logsum[at, :] = sums
        return carry

    lax.fori_loop(0, queries.shape[0] // tile, body, 0)


def lane_block(array, offset):
    return pl.BlockSpec((array.shape[0], 128), lambda pair: (0, pair + offset))


def attend(queries, keys, values, extras, offsets, timed):
    rows, count, pairs = queries.shape[0], keys.shape[0], HEADS // 4
    extra_specs = (
        [lane_block(extras[0], offsets[1]), lane_block(extras[1], offsets[2])]
        if timed
        else [pl.BlockSpec(extra.shape, lambda pair: (0, 0)) for extra in extras]
    )
    return pl.pallas_call(
        partial(attend_kernel, timed),
        grid=(pairs,),
        in_specs=[
            lane_block(queries, offsets[0]),
            lane_block(keys, offsets[1]),
            lane_block(values, offsets[2]),
        ]
        + extra_specs,
        out_specs=[pl.BlockSpec((rows, 128), lambda pair: (0, pair))] * 2,
        out_shape=[
            jax.ShapeDtypeStruct((rows, 128 * pairs), jnp.bfloat16),
            jax.ShapeDtypeStruct((rows, 128 * pairs), jnp.float32),
        ],
        compiler_params=pltpu.CompilerParams(vmem_limit_bytes=48 * 2**20),
        cost_estimate=pl.CostEstimate(
            flops=pairs * 2 * rows * count * 128 * 4,
            bytes_accessed=pairs * 128 * (rows * 10 + count * 4),
            transcendentals=pairs * 2 * rows * count,
        ),
    )(queries, keys, values, *extras)


def attend_back_kernel(timed, *refs):
    queries, keys, values, first, second, mixed, logsum, gradient = refs[:8]
    if timed:
        cosine, sine, out_q, out_k, out_v, out_first, out_second, sum_k, sum_v = refs[8:]
    else:
        out_q, out_k, out_v, sum_k, sum_v = refs[8:]
    sum_k[...] = jnp.zeros_like(sum_k)
    sum_v[...] = jnp.zeros_like(sum_v)
    if timed:
        out_first[...] = jnp.zeros_like(out_first)
        out_second[...] = jnp.zeros_like(out_second)

    tile = 256 if timed else 512

    def body(step, carry):
        at = pl.ds(pl.multiple_of(step * tile, tile), tile)
        rows, grad = queries[at, :], gradient[at, :]
        product = grad.astype(jnp.float32) * mixed[at, :].astype(jnp.float32)
        sums = logsum[at, :]
        sums_row = sums.T
        grad_query = jnp.zeros(rows.shape, jnp.float32)
        for head in range(2):
            own = head_lanes(rows.shape, head)
            query = jnp.where(own, rows, jnp.zeros_like(rows))
            grad_own = jnp.where(own, grad, jnp.zeros_like(grad))
            inner = jnp.sum(jnp.where(own, product, 0.0), -1, keepdims=True)
            inner_row = jnp.broadcast_to(inner, rows.shape).T[0:1, :]
            scores = dot_back(keys[...], query) * SCORE_SCALE
            if not timed:
                scores = scores + second[:, 0:1]
            attention = jnp.exp(scores - sums_row[head * HD : head * HD + 1, :])
            grad_attention = dot_back(values[...], grad_own)
            sum_v[...] += jnp.dot(
                attention.astype(jnp.bfloat16), grad_own, preferred_element_type=jnp.float32
            )
            grad_scores = (attention * (grad_attention - inner_row)).astype(jnp.bfloat16)
            sum_k[...] += jnp.dot(grad_scores, query, preferred_element_type=jnp.float32)
            key_own = jnp.where(
                head_lanes(keys.shape, head), keys[...], jnp.zeros(keys.shape, keys.dtype)
            )
            grad_query = grad_query + tdot(grad_scores, key_own)
            if timed:
                key_time = jnp.where(
                    own[0:1, :], first[0:1, :].astype(jnp.float32), jnp.zeros((1, 128), jnp.float32)
                )
                wide_query, wide_grad = query.astype(jnp.float32), grad_own.astype(jnp.float32)
                score = jnp.sum(wide_query * key_time, -1, keepdims=True) * SCORE_SCALE
                power = jnp.exp(score - sums[:, head * HD : head * HD + 1])
                back = jnp.sum(
                    wide_grad * second[0:1, :].astype(jnp.float32), -1, keepdims=True
                )
                grad_score = (power * (back - inner)).astype(jnp.bfloat16).astype(jnp.float32)
                grad_query = grad_query + grad_score * key_time
                out_first[0:1, :] += SCORE_SCALE * jnp.sum(
                    grad_score * wide_query, 0, keepdims=True
                )
                out_second[0:1, :] += jnp.sum(
                    power.astype(jnp.bfloat16).astype(jnp.float32) * wide_grad, 0, keepdims=True
                )
        grad_query = grad_query * SCORE_SCALE
        if timed:
            grad_query = turned(grad_query, cosine[at, :], -sine[at, :])
        out_q[at, :] = grad_query.astype(out_q.dtype)
        return carry

    lax.fori_loop(0, queries.shape[0] // tile, body, 0)
    grad_key = sum_k[...] * SCORE_SCALE
    if timed:
        grad_key = turned(grad_key, cosine[...], -sine[...])
    out_k[...] = grad_key.astype(out_k.dtype)
    out_v[...] = sum_v[...].astype(out_v.dtype)


def attend_back(queries, keys, values, extras, offsets, mixed, logsum, gradient, tables):
    timed = tables is not None
    rows, count, pairs = queries.shape[0], keys.shape[0], HEADS // 4
    extra_specs = (
        [lane_block(extras[0], offsets[1]), lane_block(extras[1], offsets[2])]
        if timed
        else [pl.BlockSpec(extra.shape, lambda pair: (0, 0)) for extra in extras]
    )
    low = jnp.bfloat16 if timed else jnp.float32

    def out(height, dtype):
        return (
            jax.ShapeDtypeStruct((height, 128 * pairs), dtype),
            pl.BlockSpec((height, 128), lambda pair: (0, pair)),
        )

    outs = [out(rows, jnp.bfloat16), out(count, low), out(count, low)]
    operands = [queries, keys, values, *extras, mixed, logsum, gradient]
    specs = (
        [
            lane_block(queries, offsets[0]),
            lane_block(keys, offsets[1]),
            lane_block(values, offsets[2]),
        ]
        + extra_specs
        + [lane_block(mixed, 0), lane_block(logsum, 0), lane_block(gradient, 0)]
    )
    if timed:
        outs += [out(8, jnp.float32), out(8, jnp.float32)]
        operands += list(tables)
        specs += [pl.BlockSpec(table.shape, lambda pair: (0, 0)) for table in tables]
    return pl.pallas_call(
        partial(attend_back_kernel, timed),
        grid=(pairs,),
        in_specs=specs,
        out_specs=[spec for _, spec in outs],
        out_shape=[shape for shape, _ in outs],
        scratch_shapes=[pltpu.VMEM((count, 128), jnp.float32)] * 2,
        compiler_params=pltpu.CompilerParams(vmem_limit_bytes=48 * 2**20),
        cost_estimate=pl.CostEstimate(
            flops=pairs * 2 * rows * count * 128 * 10,
            bytes_accessed=pairs * 128 * (rows * 16 + count * 8),
            transcendentals=pairs * 2 * rows * count,
        ),
    )(*operands)


def shifted(tile, is_shifted):
    wide = tile.astype(jnp.float32)
    return jnp.where(is_shifted, pltpu.roll(wide, BLK, 1), wide)


def assemble_kernel(joined_at, mix_at, pairs, joined, mix):
    step = pl.program_id(0)
    lane = lax.broadcasted_iota(jnp.int32, (BLK, 2 * BLK), 1)

    def fill(places, target, count):
        for pair in range(count):
            first = (step * count + pair) * 2
            left, right = places[first], places[first + 1]
            tile = jnp.where(
                lane < BLK,
                shifted(pairs[left // 2], left % 2 == 1),
                shifted(pairs[right // 2], right % 2 == 0),
            )
            target[:, pair * 2 * BLK : (pair + 1) * 2 * BLK] = tile.astype(target.dtype)

    fill(joined_at, joined, 6)
    fill(mix_at, mix, 2)


def assemble(pairs, joined_at, mix_at):
    half = D // 2
    return pl.pallas_call(
        assemble_kernel,
        grid_spec=pltpu.PrefetchScalarGridSpec(
            num_scalar_prefetch=2,
            grid=(8,),
            in_specs=[
                pl.BlockSpec(
                    pairs.shape, lambda step, *_: (0, 0, 0), pipeline_mode=pl.Buffered(1)
                )
            ],
            out_specs=[
                pl.BlockSpec((BLK, 3 * half), lambda step, *_: (step, 0)),
                pl.BlockSpec((BLK, half), lambda step, *_: (step // 2, step % 2)),
            ],
        ),
        out_shape=[
            jax.ShapeDtypeStruct((D, 3 * half), pairs.dtype),
            jax.ShapeDtypeStruct((half, D), pairs.dtype),
        ],
        compiler_params=pltpu.CompilerParams(vmem_limit_bytes=48 * 2**20),
        cost_estimate=pl.CostEstimate(
            flops=0, bytes_accessed=2 * pairs.size + 8 * half * D, transcendentals=0
        ),
    )(joined_at, mix_at, pairs)


SLOTS_STEP = 8


def collect_kernel(rows_at, columns_at, sides, joined, mix, target):
    step = pl.program_id(0)
    lane = lax.broadcasted_iota(jnp.int32, (BLK, 2 * BLK), 1)
    target[...] = jnp.zeros_like(target)
    for inner in range(SLOTS_STEP):
        slot, pair, right = step * SLOTS_STEP + inner, inner // 2, inner % 2
        code = sides[slot]
        rows = pl.ds(pl.multiple_of(rows_at[slot] * BLK, BLK), BLK)
        columns = pl.ds(pl.multiple_of(columns_at[slot] * 2 * BLK, 128), 2 * BLK)

        def put(source):
            tile = shifted(source[rows, columns], code % 2 != right).astype(target.dtype)
            own = lane // BLK == right
            target[pair] = jnp.where(own, tile, target[pair])

        @pl.when(code // 2 == 0)
        def from_joined():
            put(joined)

        @pl.when(code // 2 == 1)
        def from_mix():
            put(mix)


def collect(joined, mix, rows_at, columns_at, sides):
    steps = sides.shape[0] // SLOTS_STEP

    def resident(array):
        return pl.BlockSpec(array.shape, lambda step, *_: (0, 0), pipeline_mode=pl.Buffered(1))

    return pl.pallas_call(
        collect_kernel,
        grid_spec=pltpu.PrefetchScalarGridSpec(
            num_scalar_prefetch=3,
            grid=(steps,),
            in_specs=[resident(joined), resident(mix)],
            out_specs=pl.BlockSpec(
                (SLOTS_STEP // 2, BLK, 2 * BLK), lambda step, *_: (step, 0, 0)
            ),
        ),
        out_shape=jax.ShapeDtypeStruct((sides.shape[0] // 2, BLK, 2 * BLK), joined.dtype),
        compiler_params=pltpu.CompilerParams(vmem_limit_bytes=48 * 2**20),
        cost_estimate=pl.CostEstimate(
            flops=0,
            bytes_accessed=2 * (joined.size + mix.size) + 2 * sides.shape[0] * BLK * BLK,
            transcendentals=0,
        ),
    )(rows_at, columns_at, sides, joined, mix)


def item_per_chip(
    latents,
    noise_field,
    timesteps,
    text_tokens,
    text_lengths,
    negatives,
    assignment,
    end_weights,
    time_table,
    square_slots,
    cross_weights,
    key_value,
    gate_up,
    down_weight,
    norm_gains,
    first_ends,
    second_ends,
    first_table,
    second_table,
    first_cross,
    second_cross,
    first_key_value,
    second_key_value,
    first_gate_up,
    second_gate_up,
    first_down,
    second_down,
    first_gains,
    second_gains,
    left_stats,
    right_stats,
    left_roots,
    right_roots,
):
    bf16, f32 = jnp.bfloat16, jnp.float32
    row, column = lax.axis_index("y"), lax.axis_index("x")
    core, line = lax.axis_index("c"), lax.axis_index("z")
    plane = 2 * row + column
    item = 4 * plane + line
    quads = range(4)
    half = D // 2
    items_total = 16
    mse_scale = 1.0 / (items_total * FRAMES * DIN)

    pack = jnp.concatenate(
        [
            end_weights.reshape(4, D),
            time_table,
            jnp.pad(norm_gains.reshape(1, 144), ((0, 3), (0, D - 144))),
        ],
        0,
    ).astype(bf16)
    low_slots = square_slots.astype(bf16).reshape(4, 2, BLK, BLK)
    low_pairs = jnp.concatenate([low_slots[:, 0], low_slots[:, 1]], 2).reshape(4 * BLK, 2 * BLK)
    low_cross = cross_weights.astype(bf16)
    low_kv = key_value.astype(bf16)
    low_gate = gate_up.astype(bf16)
    low_down = down_weight.astype(bf16)

    def head_columns(array, which, side):
        return lax.dynamic_slice_in_dim(array, which * D + side * half, half, 1)

    def unit_columns(which, side):
        return jnp.concatenate(
            [
                lax.dynamic_slice_in_dim(
                    low_gate, which * FF + quadrant * 1536 + side * 768, 768, 1
                )
                for quadrant in quads
            ],
            1,
        )

    def kv_block(which, side):
        return head_columns(low_kv, which, side).reshape(16, 1152)

    def gathered(block):
        return lax.all_gather(block, ("y", "x", "z"), axis=0)

    feed_blocks = []
    for which in range(2):
        kept, received = unit_columns(which, core), swap(unit_columns(which, 1 - core), "c")
        feed_blocks.append(
            jnp.where(core == 0, jnp.stack([kept, received]), jnp.stack([received, kept]))
        )
    gate_weight, up_weight = (
        gathered(block).reshape(4, 4, 2, 48, FF // 2).transpose(0, 2, 1, 3, 4).reshape(D, FF // 2)
        for block in feed_blocks
    )
    down = gathered(low_down).reshape(FF // 2, D)
    arrays = (
        ("cols", (16, D), bf16),
        ("both", (4 * BLK, 2 * BLK), bf16),
        ("cols", (48, half), bf16),
        ("half", (48, D), bf16),
        ("cols", (16, 1152), bf16),
        ("cols", (16, 1152), bf16),
    )
    whole = slice(None)
    groups = [((0, 0, whole, whole), (5, 1, whole, whole))]
    groups += [
        ((1, 0, pl.ds(step * 96, 96), whole), (1, 1, pl.ds(384 + step * 96, 96), whole))
        for step in range(4)
    ]
    groups += [
        ((2, 0, whole, pl.ds(step * 384, 384)), (3, 1, whole, pl.ds(step * 768, 768)))
        for step in range(2)
    ]
    groups += [((4, 0, whole, whole),)]
    packs, all_pairs, cross_query, cross_out, keys_own, values_own = gather_weights(
        arrays,
        groups,
        (
            pack,
            pack,
            low_pairs,
            head_columns(low_cross[:, 0, :], 0, core),
            head_columns(low_cross[:, 0, :], 0, 1 - core),
            low_cross[:, 1, :],
            kv_block(0, core),
            kv_block(0, 1 - core),
            kv_block(1, core),
            kv_block(1, 1 - core),
        ),
        1,
    )
    packs = packs.reshape(32, 16, D)
    ends_full = packs[:, :4].reshape(D, 2, DIN)
    table_full = packs[:, 4:12].reshape(NTIME, D)
    gain_values = packs[:, 12, :144].reshape(D, 3).astype(f32)
    weight_in, weight_out = ends_full[:, 0, :], ends_full[:, 1, :]
    all_pairs = all_pairs.reshape(128, BLK, 2 * BLK)
    inverse_order = (
        jnp.zeros_like(assignment)
        .at[assignment]
        .set(jnp.arange(assignment.shape[0], dtype=jnp.int32))
    )

    def grid_blocks(matrix, rows, columns):
        return (matrix * 64 + rows * 8 + columns).reshape(-1)

    eight, four = jnp.arange(8, dtype=jnp.int32), jnp.arange(4, dtype=jnp.int32)
    joined_blocks = grid_blocks(
        jnp.arange(3, dtype=jnp.int32)[None, :, None],
        eight[:, None, None],
        (4 * core + four)[None, None, :],
    )
    out_blocks = grid_blocks(3, (4 * core + four)[:, None], eight[None, :])
    projection, weight_mix = assemble(
        all_pairs, inverse_order[joined_blocks], inverse_order[out_blocks]
    )
    cross_query = cross_query.reshape(D, half)
    cross_out = lax.dynamic_slice_in_dim(cross_out.reshape(D, D), core * half, half, 0)
    kv_own = jnp.concatenate(
        [keys_own.reshape(DT, half), values_own.reshape(DT, half)], 1
    )

    meta = jnp.concatenate([timesteps[:, None], text_lengths[:, None], negatives], 1)
    metas = meta
    for axis in ("c", "x", "y"):
        metas = grow(metas, axis)
    base = 4 * plane + 2 * core
    relative = jnp.arange(items_total, dtype=jnp.int32)
    metas = metas[(item ^ base) ^ relative]
    timestep, text_length = metas[0, 0], metas[0, 1]
    negative_rows = metas[:, 2:]
    frames = own_quarters(jnp.concatenate([latents, noise_field], 2), core, line)
    clean, noise = frames[:, :DIN], frames[:, DIN:]
    tokens = own_quarters(text_tokens, core, line)
    quarter = line ^ four
    frame_positions = (
        (quarter[:, None] * 256 + jnp.arange(256, dtype=jnp.int32)[None, :]).reshape(-1) + 1
    )
    token_slots = (
        quarter[:, None] * 32 + jnp.arange(32, dtype=jnp.int32)[None, :]
    ).reshape(-1)
    halfway = HD // 2
    frequency = jnp.exp(jnp.arange(halfway, dtype=f32) * (-2.0 * math.log(10000.0) / HD))
    turn = frame_positions.astype(f32)[:, None] * frequency[None, :]
    cosine_table = jnp.concatenate([jnp.cos(turn)] * 4, -1)
    sine_table = jnp.concatenate([-jnp.sin(turn), jnp.sin(turn)] * 2, -1)
    angle = (timestep.astype(f32) + 0.5) * (0.5 * math.pi / NTIME)
    signal, spread = jnp.cos(angle), jnp.sin(angle)
    noised = (signal * clean + spread * noise).astype(bf16)
    target = signal * noise - spread * clean

    residual = dot_back(noised, weight_in)
    normed_one, inverse_one = layer_stats(residual)
    input_one = (normed_one * gain_values[:, 0]).astype(bf16)
    features = time_features(timestep[None]).astype(bf16)
    embeds = jnp.dot(features, table_full, preferred_element_type=f32)
    normed_time, inverse_time = layer_stats(embeds)
    input_time = (normed_time * gain_values[:, 0]).astype(bf16)
    time_block = jnp.pad(input_time, ((0, 15), (0, 0)))
    joined, joined_time = join(input_one, time_block, projection, cosine_table, sine_table)
    pairs = half // 128
    self_offsets = (0, pairs, 2 * pairs)
    mixed_flat, logsum_self = attend(
        joined, joined, joined, (joined_time, joined_time), self_offsets, True
    )
    after_self = residual + on_both(jnp.dot(mixed_flat, weight_mix, preferred_element_type=f32))
    normed_two, inverse_two = layer_stats(after_self)
    input_two = (normed_two * gain_values[:, 1]).astype(bf16)
    cross_queries = jnp.dot(input_two, cross_query, preferred_element_type=f32).astype(bf16)
    projected = jnp.dot(tokens, kv_own, preferred_element_type=f32).astype(bf16)
    valid = token_slots < text_length
    cross_bias = jnp.where(valid, 0.0, MASK_VALUE).astype(f32)[None]
    text_biases = (
        jnp.broadcast_to(cross_bias, (8, 128)),
        jnp.broadcast_to(cross_bias.T, (128, 128)),
    )
    cross_offsets = (0, 0, pairs)
    cross_flat, logsum_cross = attend(
        cross_queries, projected, projected, text_biases, cross_offsets, False
    )
    after_cross = after_self + on_both(jnp.dot(cross_flat, cross_out, preferred_element_type=f32))
    normed_three, inverse_three = layer_stats(after_cross)
    input_three = (normed_three * gain_values[:, 2]).astype(bf16)
    gate_part = jnp.dot(input_three, gate_weight, preferred_element_type=f32)
    up_part = jnp.dot(input_three, up_weight, preferred_element_type=f32)
    sigmoid = jax.nn.sigmoid(gate_part)
    silu_value = gate_part * sigmoid
    hidden = (silu_value * up_part).astype(bf16)
    down_out = on_both(jnp.dot(hidden, down, preferred_element_type=f32))
    output_rows = after_cross + down_out
    output_low = output_rows.astype(bf16)
    predicted = jnp.dot(output_low, weight_out, preferred_element_type=f32)
    errors = predicted - target

    length_float = text_length.astype(f32)
    mask = valid.astype(f32)[:, None]
    text_half = jnp.sum(projected[:, :half].astype(f32) * mask, 0) / length_float
    text_rest = swap(text_half, "c")
    text_pool = jnp.where(
        core == 0,
        jnp.concatenate([text_half, text_rest]),
        jnp.concatenate([text_rest, text_half]),
    )
    pools = jnp.stack([jnp.sum(output_rows, 0) / FRAMES, text_pool], 0)[None]
    for axis in ("z", "x", "y"):
        pools = grow(pools, axis)
    inverse_pools = lax.rsqrt(jnp.sum(pools * pools, -1, keepdims=True) + POOL_EPS)
    units = pools * inverse_pools
    audio_units, text_units = units[:, 0], units[:, 1]
    similar = (
        lax.dot_general(
            audio_units, text_units, (((1,), (1,)), ((), ())), precision=BEST_PRECISION
        )
        / CONTRAST_TEMP
    )
    same = jnp.eye(items_total, dtype=f32)
    counts = same + jnp.sum(
        (negative_rows[:, None, :] == (item ^ relative)[None, :, None]).astype(f32), -1
    )
    peak = jnp.max(jnp.where(counts > 0, similar, -jnp.inf), -1, keepdims=True)
    powers = jnp.where(counts > 0, counts * jnp.exp(similar - peak), 0.0)
    totals_row = jnp.sum(powers, -1, keepdims=True)
    contrast_own = peak[0, 0] + jnp.log(totals_row[0, 0]) - similar[0, 0]
    grad_similar = (powers / totals_row - same) * (
        CONTRAST_WEIGHT / items_total / CONTRAST_TEMP
    )
    grad_audio_unit = jnp.sum(grad_similar[0][:, None] * text_units, 0)
    grad_text_unit = jnp.sum(grad_similar[:, 0][:, None] * audio_units, 0)

    def unit_back(gradient, unit, inverse):
        return inverse * (gradient - unit * jnp.sum(unit * gradient))

    grad_audio = unit_back(grad_audio_unit, audio_units[0], inverse_pools[0, 0])
    grad_text = unit_back(grad_text_unit, text_units[0], inverse_pools[0, 1])

    grad_predicted = (2.0 * mse_scale * errors).astype(bf16)
    grad_out_weight = tdot(output_low, grad_predicted)
    grad_output = dot_back(grad_predicted, weight_out) + grad_audio[None, :] / FRAMES
    grad_low = grad_output.astype(bf16)
    grad_down = tdot(hidden, grad_low).astype(bf16)
    grad_hidden = dot_back(grad_low, down)
    grad_gate = (grad_hidden * up_part * sigmoid * (1.0 + gate_part * (1.0 - sigmoid))).astype(bf16)
    grad_up = (grad_hidden * silu_value).astype(bf16)
    grad_gate_weight = tdot(input_three, grad_gate).astype(bf16)
    grad_up_weight = tdot(input_three, grad_up).astype(bf16)
    def scattered(gradient, width):
        total = lax.psum_scatter(
            gradient.reshape(4, -1, 4, width, gradient.shape[1]),
            ("y", "x"),
            scatter_dimension=0,
            tiled=True,
        )
        return lax.psum_scatter(total, "z", scatter_dimension=2, tiled=True)[0, :, 0]

    feed_sums = []
    for gradient in (grad_gate_weight, grad_up_weight):
        both_rows = scattered(gradient, 48)
        feed_sums.append((pick(both_rows, core), swap(pick(both_rows, 1 - core), "c")))
    gate_columns = []
    for mine, other in feed_sums:
        sides = (jnp.where(core == 0, mine, other), jnp.where(core == 0, other, mine))
        for quadrant in quads:
            for side in sides:
                gate_columns.append(side[:, quadrant * 768 : (quadrant + 1) * 768])
    grad_gate_up = jnp.concatenate(gate_columns, 1).astype(f32)
    grad_down = scattered(grad_down, 192)[0].astype(f32)
    grad_input_three = on_both(dot_back(grad_gate, gate_weight) + dot_back(grad_up, up_weight))
    grad_after_cross, gain_three = layer_back(
        grad_input_three, normed_three, inverse_three, gain_values[:, 2]
    )
    grad_after_cross = grad_after_cross + grad_output
    grad_cross_in = grad_after_cross.astype(bf16)
    cross_rows = tdot(cross_flat, grad_cross_in).astype(bf16).reshape(2, 2, 192, D)
    cross_kept = pick(cross_rows, core, 1)
    cross_received = swap(pick(cross_rows, 1 - core, 1), "c")
    cross_pair = jnp.stack([cross_kept, cross_received], 0)
    out_rows = jnp.where(core == 0, cross_pair, cross_pair[::-1]).reshape(4, 1, 4, 48, D)
    grad_mixed_cross = dot_back(grad_cross_in, cross_out).astype(bf16)
    grad_cq, grad_text_keys, grad_text_values = attend_back(
        cross_queries,
        projected,
        projected,
        text_biases,
        cross_offsets,
        cross_flat,
        logsum_cross,
        grad_mixed_cross,
        None,
    )
    grad_query_weight = tdot(input_two, grad_cq).astype(bf16).reshape(4, 2, 4, 48, half)
    grad_input_two = on_both(dot_back(grad_cq, cross_query))
    text_half_grad = lax.dynamic_slice_in_dim(grad_text, core * half, half, 0)
    grad_pair_keys = (
        grad_text_keys + mask * (text_half_grad[None, :] / length_float)
    ).astype(bf16)
    kv_sources = [
        tdot(tokens, gradient.astype(bf16)).astype(bf16).reshape(4, 2, 4, 16, 1152)
        for gradient in (grad_pair_keys, grad_text_values)
    ]
    grad_after_self, gain_two = layer_back(
        grad_input_two, normed_two, inverse_two, gain_values[:, 1]
    )
    grad_after_self = grad_after_self + grad_after_cross
    grad_self_in = grad_after_self.astype(bf16)
    grad_mix = tdot(mixed_flat, grad_self_in).astype(bf16)
    grad_mixed_self = dot_back(grad_self_in, weight_mix).astype(bf16)
    grad_queries, grad_keys, grad_values, grad_time_keys, grad_time_values = attend_back(
        joined,
        joined,
        joined,
        (joined_time, joined_time),
        self_offsets,
        mixed_flat,
        logsum_self,
        grad_mixed_self,
        (cosine_table, sine_table),
    )
    grad_joined = jnp.concatenate([grad_queries, grad_keys, grad_values], 1)
    grad_time_pair = jnp.concatenate([grad_time_keys[:1], grad_time_values[:1]], 1)
    time_row = jnp.concatenate([jnp.zeros((1, half), f32), grad_time_pair], 1)
    grad_projection = (
        tdot(input_one, grad_joined) + input_time.astype(f32).reshape(D, 1) * time_row
    ).astype(bf16)
    position = jnp.arange(256, dtype=jnp.int32)
    owner_core = core ^ (position // 128)
    block = assignment[
        (position // 32) % 4 * 64 + owner_core * 32 + (position // 8) % 4 * 8 + position % 8
    ]
    matrix, block_row, block_column = block // 64, (block // 8) % 8, block % 8
    is_out = matrix == 3
    side = jnp.where(is_out, block_row // 4, block_column // 4)
    code = jnp.where(side == core, 2 * is_out + block_column % 2, 4)
    collected = collect(
        grad_projection,
        grad_mix,
        jnp.where(is_out, block_row % 4, block_row),
        jnp.where(is_out, block_column // 2, matrix * 2 + (block_column % 4) // 2),
        code.astype(jnp.int32),
    ).reshape(2, 4, 1, 4, 4 * BLK, 2 * BLK)
    slot_sums = low_sum(collected[0], swap(collected[1], "c")).astype(bf16)

    partial_one = dot_back(grad_joined, projection)
    partial_time = jnp.dot(
        grad_time_pair, projection[:, half:].astype(f32).T, precision=BEST_PRECISION
    )
    grad_input_one = on_both(partial_one)
    grad_input_time = partial_time + swap(partial_time, "c")
    grad_residual, gain_one = layer_back(grad_input_one, normed_one, inverse_one, gain_values[:, 0])
    grad_residual = (grad_residual + grad_after_self).astype(bf16)
    grad_embeds, gain_time = layer_back(
        grad_input_time, normed_time, inverse_time, gain_values[:, 0]
    )
    grad_in_weight = tdot(grad_residual, noised)
    grad_table = features.astype(f32).reshape(NTIME, 1) * grad_embeds
    grad_gains = jnp.stack([gain_one + gain_time, gain_two, gain_three], 1)
    grad_ends = jnp.stack([grad_in_weight, grad_out_weight], 1)

    def own_rows(values, width):
        return pick(values.reshape(2, 2, 2, 4, -1, width), core, 2)

    small = jnp.concatenate(
        [
            own_rows(grad_ends.reshape(-1, D), D),
            own_rows(grad_table, D),
            jnp.pad(
                own_rows(grad_gains.reshape(32, 144), 144),
                ((0, 0), (0, 0), (0, 0), (0, 3), (0, D - 144)),
            ),
        ],
        3,
    )
    rest_arrays = (
        ("one", (4 * BLK, 2 * BLK)),
        ("cols", (48, half)),
        ("one", (48, D)),
        ("cols", (16, 1152)),
        ("cols", (16, 1152)),
        ("one", (16, D)),
    )
    rest_groups = [((3, 0, whole, whole), (4, 1, whole, whole))]
    rest_groups += [
        ((1, 0, whole, pl.ds(step * 384, 384)), (2, 1, whole, pl.ds(step * 768, 768)))
        for step in range(2)
    ]
    rest_groups += [
        ((0, 0, pl.ds(step * 96, 96), whole), (0, 1, pl.ds(384 + step * 96, 96), whole))
        for step in range(4)
    ]
    rest_groups += [((5, 0, whole, whole),)]
    rest_sums = reduce_gradients(
        rest_arrays,
        rest_groups,
        (
            slot_sums,
            grad_query_weight,
            out_rows,
            kv_sources[0],
            kv_sources[1],
            small.astype(bf16).reshape(4, 1, 4, 16, D),
        ),
        2,
    )
    slot_rows, query_mine, query_other, grad_cross_out, *kv_sums, small = (
        value.astype(f32) for value in rest_sums
    )
    slot_rows = slot_rows.reshape(4, BLK, 2 * BLK)
    grad_slots = jnp.stack([slot_rows[:, :, :BLK], slot_rows[:, :, BLK:]], 1).reshape(8, BLK, BLK)
    grad_cross_query = jnp.where(
        core == 0,
        jnp.concatenate([query_mine, query_other], 1),
        jnp.concatenate([query_other, query_mine], 1),
    )
    grad_cross = jnp.stack([grad_cross_query, grad_cross_out], 1)
    kv_columns = []
    for mine, other in (kv_sums[:2], kv_sums[2:]):
        mine, other = mine.reshape(24, half), other.reshape(24, half)
        kv_columns.append(jnp.where(core == 0, mine, other))
        kv_columns.append(jnp.where(core == 0, other, mine))
    grad_key_value = jnp.concatenate(kv_columns, 1)
    grad_ends = small[:4].reshape(48, 2, DIN)
    grad_table = small[4:12]
    grad_gains = small[12, :144].reshape(48, 3)

    reduced = (
        grad_ends,
        grad_table,
        grad_slots,
        grad_cross,
        grad_key_value,
        grad_gate_up,
        grad_down,
        grad_gains,
    )
    square_sum = jnp.zeros((), f32)
    for member in reduced:
        square_sum = square_sum + jnp.sum(member * member)
    loss_part = jnp.where(
        core == 0,
        jnp.sum(errors * errors) * mse_scale + contrast_own * (CONTRAST_WEIGHT / items_total),
        0.0,
    )
    loss_total, norm_square = all_sum(loss_part, square_sum)
    return finish(
        loss_total,
        jnp.sqrt(norm_square),
        reduced,
        (
            end_weights,
            time_table,
            square_slots,
            cross_weights,
            key_value,
            gate_up,
            down_weight,
            norm_gains,
        ),
        (
            first_ends,
            first_table,
            None,
            first_cross,
            first_key_value,
            first_gate_up,
            first_down,
            first_gains,
        ),
        (
            second_ends,
            second_table,
            None,
            second_cross,
            second_key_value,
            second_gate_up,
            second_down,
            second_gains,
        ),
        (left_stats, right_stats, left_roots, right_roots),
    )


def all_sum(*values):
    total = jnp.stack(values)
    for axis in ("c", "z", "x", "y"):
        bit = 1
        while bit < lax.axis_size(axis):
            total = total + swap(total, axis, bit)
            bit *= 2
    return total[0], total[1]


def finish(loss_total, gradient_norm, reduced, masters, firsts, seconds, statistics):
    factor = CLIP_NORM / jnp.maximum(gradient_norm, CLIP_NORM)
    results = [loss_total, gradient_norm]
    for index_value in (0, 1, 3, 4, 5, 6, 7):
        results.extend(
            adam_update(
                masters[index_value],
                firsts[index_value],
                seconds[index_value],
                factor * reduced[index_value],
                ADAM_RATES[index_value],
            )
        )
    clipped_slots = factor * reduced[2]
    left_new, right_new, slots_new = shampoo_update(masters[2], clipped_slots, *statistics)
    results.extend([clipped_slots, left_new, right_new, slots_new])
    return tuple(results)


def solution(mesh):
    lines = mesh.shape["text"]
    chips = mesh.devices.size // 2
    if mesh.shape["dp"] == 8 and lines == 4 and 2 * mesh.shape["dp"] == chips:
        mesh = Mesh(mesh.devices.reshape(2, 2, 2, lines), ("y", "x", "c", "z"))
        dp, text, body = ("y", "x", "c"), ("z",), item_per_chip
    else:
        dp, text, body = ("dp",), ("text",), shards
    own = dp + text
    in_specs = (
        P(dp, text, None),
        P(dp, text, None),
        P(dp),
        P(dp, text, None),
        P(dp),
        P(dp, None),
        P(),
    ) + (P(own),) * 26
    out_specs = (P(), P()) + (P(own),) * 25
    return jax.shard_map(body, mesh=mesh, in_specs=in_specs, out_specs=out_specs, check_vma=False)
```

```python
from functools import partial
import math

import jax
import jax.numpy as jnp
from jax import lax
from jax.experimental import pallas as pl
from jax.experimental.pallas import tpu as pltpu
from jax.sharding import Mesh, PartitionSpec as P

D = 1536
HEADS = 24
HD = 64
FF = 6144
DIN = 64
DT = 768
FRAMES = 1024
NTIME = 256
STEP = 10
BLK = 192


BEST_PRECISION = lax.Precision.HIGHEST
NORM_EPS = 1e-05
POOL_EPS = 1e-06
SCORE_SCALE = 0.125
CONTRAST_TEMP = 0.02
CONTRAST_WEIGHT = 0.1
CLIP_NORM = 0.005
BETA_FIRST = 0.9
BETA_SECOND = 0.999
ADAM_EPS = 1e-08
WEIGHT_DECAY = 0.01
ADAM_RATES = (0.02, 0.05, 0.0, 0.1, 0.02, 0.02, 0.02, 1.0)
STAT_DECAY = 0.999
SHAMPOO_RATE = 0.01
MASK_VALUE = -1000000000.0


def layer_stats(inputs):
    center = inputs - jnp.mean(inputs, -1, keepdims=True)
    inverse = lax.rsqrt(jnp.mean(center * center, -1, keepdims=True) + NORM_EPS)
    return (center * inverse, inverse)


def layer_back(grad_out, normed, inverse, gain_row):
    scaled = grad_out * gain_row
    grad_in = inverse * (
        scaled
        - jnp.mean(scaled, -1, keepdims=True)
        - normed * jnp.mean(scaled * normed, -1, keepdims=True)
    )
    return (grad_in, jnp.sum(grad_out * normed, 0))


def time_features(timesteps):
    halfway = NTIME // 2
    frequency = jnp.exp(jnp.arange(halfway, dtype=jnp.float32) * (math.log(64.0) / halfway))
    moment = (timesteps.astype(jnp.float32) + 0.5) / NTIME
    phase = 2.0 * math.pi * moment[:, None] * frequency[None, :]
    return jnp.concatenate([jnp.cos(phase), jnp.sin(phase)], 1)


def rope_tables(positions_count, offset):
    halfway = HD // 2
    frequency = jnp.exp(jnp.arange(halfway, dtype=jnp.float32) * (-2.0 * math.log(10000.0) / HD))
    positions = (jnp.arange(positions_count, dtype=jnp.int32) + offset).astype(jnp.float32)
    angles = positions[:, None] * frequency[None, :]
    return (jnp.concatenate([jnp.cos(angles)] * 2, -1), jnp.concatenate([jnp.sin(angles)] * 2, -1))


def rotate(values, cosine_table, sine_table):
    halfway = HD // 2
    turned = jnp.concatenate([-values[..., halfway:], values[..., :halfway]], -1)
    return values * cosine_table[:, None, :] + turned * sine_table[:, None, :]


def rotate_back(gradient, cosine_table, sine_table):
    halfway = HD // 2
    product = gradient * sine_table[:, None, :]
    return gradient * cosine_table[:, None, :] + jnp.concatenate(
        [product[..., halfway:], -product[..., :halfway]], -1
    )


def to_matrices(blocks):
    per_side = D // BLK
    return blocks.reshape(4, per_side, per_side, BLK, BLK).transpose(0, 1, 3, 2, 4).reshape(4, D, D)


def to_blocks(matrices):
    per_side = D // BLK
    return (
        matrices.reshape(4, per_side, BLK, per_side, BLK)
        .transpose(0, 1, 3, 2, 4)
        .reshape(4 * per_side * per_side, BLK, BLK)
    )


def normalize(vectors):
    return vectors * lax.rsqrt(jnp.sum(vectors * vectors, -1, keepdims=True) + POOL_EPS)


def contrast_loss(pooled_audio, pooled_text, negatives):
    audio_unit_vectors = normalize(pooled_audio)
    text_unit_vectors = normalize(pooled_text)
    positive_pairs = jnp.sum(audio_unit_vectors * text_unit_vectors, -1) / CONTRAST_TEMP
    negative_pairs = (
        jnp.einsum(
            "ux,uax->ua", audio_unit_vectors, text_unit_vectors[negatives], precision=BEST_PRECISION
        )
        / CONTRAST_TEMP
    )
    scores = jnp.concatenate([positive_pairs[:, None], negative_pairs], 1)
    peak_score = jnp.max(scores, -1, keepdims=True)
    logsum = peak_score[:, 0] + jnp.log(jnp.sum(jnp.exp(scores - peak_score), -1))
    return jnp.sum(logsum - positive_pairs)


def item_scores(one_query, one_key, one_bias):
    scores = jnp.einsum("fhd,khd->hfk", one_query, one_key, preferred_element_type=jnp.float32)
    return scores * SCORE_SCALE + one_bias


def attend_forward(queries, all_keys, values, key_bias):

    def single(pieces):
        one_query, one_key, one_value, one_bias = pieces
        scores = item_scores(one_query, one_key, one_bias)
        peak_score = jnp.max(scores, -1, keepdims=True)
        weights = jnp.exp(scores - peak_score)
        row_total = jnp.sum(weights, -1, keepdims=True)
        mixture = jnp.einsum(
            "hfk,khd->fhd",
            (weights / row_total).astype(jnp.bfloat16),
            one_value,
            preferred_element_type=jnp.float32,
        )
        return (mixture.astype(jnp.bfloat16), peak_score + jnp.log(row_total))

    return lax.map(single, (queries, all_keys, values, key_bias))


def attend_backward(queries, all_keys, values, key_bias, logsums, grad_mixture):

    def single(pieces):
        one_query, one_key, one_value, one_bias, one_logsum, grad_rows = pieces
        attention = jnp.exp(item_scores(one_query, one_key, one_bias) - one_logsum)
        grad_attention = jnp.einsum(
            "fhd,khd->hfk", grad_rows, one_value, preferred_element_type=jnp.float32
        )
        grad_value = jnp.einsum(
            "hfk,fhd->khd",
            attention.astype(jnp.bfloat16),
            grad_rows,
            preferred_element_type=jnp.float32,
        )
        grad_scores = attention * (
            grad_attention - jnp.sum(attention * grad_attention, -1, keepdims=True)
        )
        grad_scores = grad_scores.astype(jnp.bfloat16)
        grad_query = (
            jnp.einsum("hfk,khd->fhd", grad_scores, one_key, preferred_element_type=jnp.float32)
            * SCORE_SCALE
        )
        grad_key = (
            jnp.einsum("hfk,fhd->khd", grad_scores, one_query, preferred_element_type=jnp.float32)
            * SCORE_SCALE
        )
        return (grad_query, grad_key, grad_value)

    return lax.map(single, (queries, all_keys, values, key_bias, logsums, grad_mixture))


def feed_forward(rows_in, gate_matrix, down_matrix):
    width = down_matrix.shape[0]
    gate_values = jnp.dot(rows_in, gate_matrix, preferred_element_type=jnp.float32)
    gate_part = gate_values[:, :width]
    up_part = gate_values[:, width:]
    sigmoid = jax.nn.sigmoid(gate_part)
    silu_value = gate_part * sigmoid
    hidden = (silu_value * up_part).astype(jnp.bfloat16)
    partial_out = jnp.dot(hidden, down_matrix, preferred_element_type=jnp.float32)
    return (partial_out, (hidden, gate_part, up_part, sigmoid, silu_value))


def feed_back(rows_in, gate_matrix, down_matrix, kept, grad_low):
    hidden, gate_part, up_part, sigmoid, silu_value = kept
    grad_down = jnp.einsum("rf,rd->fd", hidden, grad_low, preferred_element_type=jnp.float32)
    grad_hidden = jnp.einsum("rd,fd->rf", grad_low, down_matrix, preferred_element_type=jnp.float32)
    grad_gate = grad_hidden * up_part * sigmoid * (1.0 + gate_part * (1.0 - sigmoid))
    grad_pair = jnp.concatenate([grad_gate, grad_hidden * silu_value], 1).astype(jnp.bfloat16)
    grad_gate_up = jnp.einsum("rd,rg->dg", rows_in, grad_pair, preferred_element_type=jnp.float32)
    grad_rows = jnp.einsum("rg,dg->rd", grad_pair, gate_matrix, preferred_element_type=jnp.float32)
    return (grad_rows, grad_gate_up, grad_down)


def adam_update(weight, first_moment, second_moment, gradient, rate):
    first_moment = BETA_FIRST * first_moment + (1.0 - BETA_FIRST) * gradient
    second_moment = BETA_SECOND * second_moment + (1.0 - BETA_SECOND) * gradient * gradient
    corrected = first_moment / (1.0 - BETA_FIRST**STEP)
    scaled = second_moment / (1.0 - BETA_SECOND**STEP)
    weight = weight - rate * (corrected / (jnp.sqrt(scaled) + ADAM_EPS) + WEIGHT_DECAY * weight)
    return (first_moment, second_moment, weight)


def shampoo_update(slots_now, gradient, rest, left_stat, right_stat, left_root, right_root):
    share_now = (1.0 - STAT_DECAY) * rest * rest
    left_stat = STAT_DECAY * left_stat + share_now * jnp.einsum(
        "sij,skj->sik", gradient, gradient, precision=lax.Precision.HIGH
    )
    right_stat = STAT_DECAY * right_stat + share_now * jnp.einsum(
        "sji,sjk->sik", gradient, gradient, precision=lax.Precision.HIGH
    )
    inner = jnp.einsum("sij,sjk->sik", gradient, right_root, precision=lax.Precision.HIGH)
    direction = jnp.einsum("sij,sjk->sik", left_root, inner, precision=lax.Precision.HIGH)
    return (
        left_stat,
        right_stat,
        slots_now - SHAMPOO_RATE * (rest * direction + WEIGHT_DECAY * slots_now),
    )


def shards(
    latents,
    noise_field,
    timesteps,
    text_tokens,
    text_lengths,
    negatives,
    assignment,
    end_weights,
    time_table,
    square_slots,
    cross_weights,
    key_value,
    gate_up,
    down_weight,
    norm_gains,
    first_ends,
    second_ends,
    first_table,
    second_table,
    first_cross,
    second_cross,
    first_key_value,
    second_key_value,
    first_gate_up,
    second_gate_up,
    first_down,
    second_down,
    first_gains,
    second_gains,
    left_stats,
    right_stats,
    left_roots,
    right_roots,
):
    text_index = lax.axis_index("text")
    group_index = lax.axis_index("dp")
    group_count = lax.axis_size("dp")
    text_count_axis = lax.axis_size("text")
    piece_width = FF // (group_count * text_count_axis)
    low_ends = end_weights.astype(jnp.bfloat16)
    low_table = time_table.astype(jnp.bfloat16)
    low_slots = square_slots.astype(jnp.bfloat16)
    low_cross = cross_weights.astype(jnp.bfloat16)
    low_pairs = key_value.astype(jnp.bfloat16)
    low_gains = norm_gains.astype(jnp.bfloat16)
    low_gate = gate_up.astype(jnp.bfloat16)
    low_down = down_weight.astype(jnp.bfloat16)
    group_set = (
        lax.all_gather(low_ends, "text", axis=0, tiled=True),
        lax.all_gather(low_table, "text", axis=0, tiled=True),
        lax.all_gather(low_slots, "text", axis=0, tiled=True),
        lax.all_gather(low_cross, "text", axis=0, tiled=True),
        lax.all_gather(low_pairs, "text", axis=0, tiled=True),
        lax.all_gather(low_gains, "text", axis=0, tiled=True),
        lax.all_gather(low_gate, "text", axis=0, tiled=True),
    )
    gate_group = group_set[6].reshape(
        group_set[6].shape[0], 2, group_count, text_count_axis, piece_width
    )
    gate_columns = lax.dynamic_index_in_dim(gate_group, text_index, 3, keepdims=False)
    full_set = (
        lax.all_gather(group_set[0], "dp", axis=0, tiled=True),
        lax.all_gather(group_set[1], "dp", axis=0, tiled=True),
        lax.all_gather(group_set[2], "dp", axis=0, tiled=True),
        lax.all_gather(group_set[3], "dp", axis=0, tiled=True),
        lax.all_gather(group_set[4], "dp", axis=0, tiled=True),
        lax.all_gather(group_set[5], "dp", axis=0, tiled=True),
        lax.all_gather(gate_columns, "dp", axis=0, tiled=True),
        lax.all_gather(low_down, "dp", axis=0, tiled=True),
    )
    ends_full, table_full, slots_full, cross_full, pairs_full, gains_full = full_set[:6]
    gate_full = full_set[6].reshape(D, 2 * group_count * piece_width)
    down_full = full_set[7]
    item_count = latents.shape[0]
    frames_dev = latents.shape[1]
    tokens_dev = text_tokens.shape[1]
    row_count = item_count * frames_dev
    items_total = item_count * group_count
    mse_scale = 1.0 / (items_total * FRAMES * DIN)
    weight_in = ends_full[:, 0, :]
    weight_out = ends_full[:, 1, :]
    gain_values = gains_full.astype(jnp.float32)
    inverse_order = (
        jnp.zeros_like(assignment)
        .at[assignment]
        .set(jnp.arange(assignment.shape[0], dtype=jnp.int32))
    )
    squares = to_matrices(slots_full[inverse_order])
    projection = jnp.concatenate([squares[0], squares[1], squares[2]], 1)
    cosine_table, sine_table = rope_tables(frames_dev, 1 + text_index * frames_dev)
    angles = (timesteps.astype(jnp.float32) + 0.5) * (0.5 * math.pi / NTIME)
    signal = jnp.cos(angles)[:, None, None]
    spread = jnp.sin(angles)[:, None, None]
    noised = (signal * latents + spread * noise_field).astype(jnp.bfloat16).reshape(row_count, DIN)
    residual = jnp.einsum("rc,dc->rd", noised, weight_in, preferred_element_type=jnp.float32)
    normed_one, inverse_one = layer_stats(residual)
    input_one = (normed_one * gain_values[:, 0]).astype(jnp.bfloat16)
    features = time_features(timesteps).astype(jnp.bfloat16)
    embeds = jnp.dot(features, table_full, preferred_element_type=jnp.float32)
    normed_time, inverse_time = layer_stats(embeds)
    input_time = (normed_time * gain_values[:, 0]).astype(jnp.bfloat16)
    joined_rows = jnp.dot(input_one, projection, preferred_element_type=jnp.float32)
    head_shape = (item_count, frames_dev, HEADS, HD)
    rot_queries = rotate(joined_rows[:, :D].reshape(head_shape), cosine_table, sine_table).astype(
        jnp.bfloat16
    )
    rot_keys = rotate(
        joined_rows[:, D : 2 * D].reshape(head_shape), cosine_table, sine_table
    ).astype(jnp.bfloat16)
    value_rows = joined_rows[:, 2 * D :].astype(jnp.bfloat16).reshape(item_count, frames_dev, D)
    time_pair = jnp.dot(input_time, projection[:, D:], preferred_element_type=jnp.float32).astype(
        jnp.bfloat16
    )
    keys_all, values_all = (
        lax.all_gather(rot_keys.reshape(item_count, frames_dev, D), "text", axis=1, tiled=True),
        lax.all_gather(value_rows, "text", axis=1, tiled=True),
    )
    key_count = keys_all.shape[1] + 1
    all_keys = jnp.concatenate([time_pair[:, None, :D], keys_all], 1).reshape(
        item_count, key_count, HEADS, HD
    )
    all_values = jnp.concatenate([time_pair[:, None, D:], values_all], 1).reshape(
        item_count, key_count, HEADS, HD
    )
    self_bias = jnp.zeros((item_count, key_count), jnp.float32)
    mixed_self, logsum_self = attend_forward(rot_queries, all_keys, all_values, self_bias)
    mixed_flat = mixed_self.reshape(row_count, D)
    after_self = residual + jnp.dot(mixed_flat, squares[3], preferred_element_type=jnp.float32)
    normed_two, inverse_two = layer_stats(after_self)
    input_two = (normed_two * gain_values[:, 1]).astype(jnp.bfloat16)
    cross_queries = jnp.dot(
        input_two, cross_full[:, 0, :], preferred_element_type=jnp.float32
    ).astype(jnp.bfloat16)
    cross_heads = cross_queries.reshape(head_shape)
    projected = jnp.dot(
        text_tokens.reshape(item_count * tokens_dev, DT),
        pairs_full,
        preferred_element_type=jnp.float32,
    )
    projected = projected.astype(jnp.bfloat16).reshape(item_count, tokens_dev, 2 * D)
    text_all = lax.all_gather(projected, "text", axis=1, tiled=True)
    text_count = text_all.shape[1]
    valid_keys = jnp.arange(text_count, dtype=jnp.int32)[None, :] < text_lengths[:, None]
    cross_bias = jnp.where(valid_keys, 0.0, MASK_VALUE).astype(jnp.float32)
    text_keys = text_all[:, :, :D].reshape(item_count, text_count, HEADS, HD)
    text_values = text_all[:, :, D:].reshape(item_count, text_count, HEADS, HD)
    mixed_cross, logsum_cross = attend_forward(cross_heads, text_keys, text_values, cross_bias)
    cross_flat = mixed_cross.reshape(row_count, D)
    after_cross = after_self + jnp.dot(
        cross_flat, cross_full[:, 1, :], preferred_element_type=jnp.float32
    )
    normed_three, inverse_three = layer_stats(after_cross)
    input_three = (normed_three * gain_values[:, 2]).astype(jnp.bfloat16)
    feed_rows = lax.all_gather(
        input_three.reshape(item_count, frames_dev, D), "text", axis=1, tiled=True
    ).reshape(-1, D)
    feed_out, feed_kept = feed_forward(feed_rows, gate_full, down_full)
    down_out = (
        lax.psum_scatter(
            feed_out.reshape(item_count, -1, D).astype(jnp.bfloat16),
            "text",
            scatter_dimension=1,
            tiled=True,
        )
        .astype(jnp.float32)
        .reshape(row_count, D)
    )
    output_rows = after_cross + down_out
    output_low = output_rows.astype(jnp.bfloat16)
    predicted = jnp.dot(output_low, weight_out, preferred_element_type=jnp.float32).reshape(
        latents.shape
    )
    errors = predicted - (signal * noise_field - spread * latents)
    lengths_float = text_lengths.astype(jnp.float32)
    own_valid = (text_index * tokens_dev + jnp.arange(tokens_dev, dtype=jnp.int32))[
        None, :
    ] < text_lengths[:, None]
    own_mask = own_valid.astype(jnp.float32)
    audio_part = jnp.sum(output_rows.reshape(item_count, frames_dev, D), 1)
    text_part = (
        jnp.sum(projected[:, :, :D].astype(jnp.float32) * own_mask[:, :, None], 1)
        / lengths_float[:, None]
    )
    pooled_set = (
        lax.all_gather(audio_part, ("dp", "text"), axis=0, tiled=True),
        lax.all_gather(text_part, ("dp", "text"), axis=0, tiled=True),
        lax.all_gather(negatives.astype(jnp.float32), ("dp", "text"), axis=0, tiled=True),
    )
    audio_pooled = (
        jnp.sum(pooled_set[0].reshape(group_count, text_count_axis, item_count, D), 1).reshape(
            -1, D
        )
        / FRAMES
    )
    text_pooled = jnp.sum(
        pooled_set[1].reshape(group_count, text_count_axis, item_count, D), 1
    ).reshape(-1, D)
    negative_rows = pooled_set[2].reshape(group_count, text_count_axis, item_count, -1)[:, 0]
    negative_rows = negative_rows.reshape(items_total, -1).astype(jnp.int32)
    contrast_value, contrast_back = jax.vjp(
        partial(contrast_loss, negatives=negative_rows), audio_pooled, text_pooled
    )
    grad_audio_all, grad_text_all = contrast_back(jnp.float32(CONTRAST_WEIGHT / items_total))
    grad_audio = lax.dynamic_slice_in_dim(grad_audio_all, group_index * item_count, item_count, 0)
    grad_text = lax.dynamic_slice_in_dim(grad_text_all, group_index * item_count, item_count, 0)
    grad_predicted = (2.0 * mse_scale * errors).astype(jnp.bfloat16).reshape(row_count, DIN)
    grad_out_weight = jnp.einsum(
        "rd,rc->dc", output_low, grad_predicted, preferred_element_type=jnp.float32
    )
    grad_output = jnp.einsum(
        "rc,dc->rd", grad_predicted, weight_out, preferred_element_type=jnp.float32
    )
    grad_output = (
        grad_output.reshape(item_count, frames_dev, D) + grad_audio[:, None, :] / FRAMES
    ).reshape(row_count, D)
    grad_down_in = grad_output.astype(jnp.bfloat16)
    grad_feed_rows = lax.all_gather(
        grad_down_in.reshape(item_count, frames_dev, D), "text", axis=1, tiled=True
    ).reshape(-1, D)
    grad_feed_in, grad_gate_up, grad_down = feed_back(
        feed_rows, gate_full, down_full, feed_kept, grad_feed_rows
    )
    grad_input_three = (
        lax.psum_scatter(
            grad_feed_in.reshape(item_count, -1, D).astype(jnp.bfloat16),
            "text",
            scatter_dimension=1,
            tiled=True,
        )
        .astype(jnp.float32)
        .reshape(row_count, D)
    )
    grad_after_cross, gain_three = layer_back(
        grad_input_three, normed_three, inverse_three, gain_values[:, 2]
    )
    grad_after_cross = grad_after_cross + grad_output
    grad_cross_in = grad_after_cross.astype(jnp.bfloat16)
    grad_cross_out = jnp.einsum(
        "rd,re->de", cross_flat, grad_cross_in, preferred_element_type=jnp.float32
    )
    grad_mixed_cross = jnp.einsum(
        "re,de->rd", grad_cross_in, cross_full[:, 1, :], preferred_element_type=jnp.float32
    )
    grad_mixed_cross = grad_mixed_cross.astype(jnp.bfloat16).reshape(head_shape)
    grad_cq, grad_text_keys, grad_text_values = attend_backward(
        cross_heads, text_keys, text_values, cross_bias, logsum_cross, grad_mixed_cross
    )
    grad_cq_low = grad_cq.reshape(row_count, D).astype(jnp.bfloat16)
    grad_cross_query = jnp.einsum(
        "rd,re->de", input_two, grad_cq_low, preferred_element_type=jnp.float32
    )
    grad_input_two = jnp.einsum(
        "re,de->rd", grad_cq_low, cross_full[:, 0, :], preferred_element_type=jnp.float32
    )
    grad_pairs = jnp.concatenate(
        [
            grad_text_keys.reshape(item_count, text_count, D),
            grad_text_values.reshape(item_count, text_count, D),
        ],
        2,
    )
    grad_own_pairs = lax.psum_scatter(
        grad_pairs.astype(jnp.bfloat16), "text", scatter_dimension=1, tiled=True
    ).astype(jnp.float32)
    pooled_grad = own_mask[:, :, None] * (grad_text[:, None, :] / lengths_float[:, None, None])
    grad_own_pairs = grad_own_pairs + jnp.concatenate([pooled_grad, jnp.zeros_like(pooled_grad)], 2)
    grad_own_pairs = grad_own_pairs.astype(jnp.bfloat16).reshape(item_count * tokens_dev, 2 * D)
    grad_textside = jnp.einsum(
        "tc,tk->ck",
        text_tokens.reshape(item_count * tokens_dev, DT),
        grad_own_pairs,
        preferred_element_type=jnp.float32,
    )
    grad_after_self, gain_two = layer_back(
        grad_input_two, normed_two, inverse_two, gain_values[:, 1]
    )
    grad_after_self = grad_after_self + grad_after_cross
    grad_self_in = grad_after_self.astype(jnp.bfloat16)
    grad_attn_out = jnp.einsum(
        "rd,re->de", mixed_flat, grad_self_in, preferred_element_type=jnp.float32
    )
    grad_mixed_self = jnp.einsum(
        "re,de->rd", grad_self_in, squares[3], preferred_element_type=jnp.float32
    )
    grad_mixed_self = grad_mixed_self.astype(jnp.bfloat16).reshape(head_shape)
    grad_rot_queries, grad_keys, value_gradients = attend_backward(
        rot_queries, all_keys, all_values, self_bias, logsum_self, grad_mixed_self
    )
    grad_keys_own, grad_values_own = (
        lax.psum_scatter(
            grad_keys[:, 1:].reshape(item_count, key_count - 1, D).astype(jnp.bfloat16),
            "text",
            scatter_dimension=1,
            tiled=True,
        ).astype(jnp.float32),
        lax.psum_scatter(
            value_gradients[:, 1:].reshape(item_count, key_count - 1, D).astype(jnp.bfloat16),
            "text",
            scatter_dimension=1,
            tiled=True,
        ).astype(jnp.float32),
    )
    grad_queries = (
        rotate_back(grad_rot_queries, cosine_table, sine_table)
        .astype(jnp.bfloat16)
        .reshape(row_count, D)
    )
    grad_key_rows = rotate_back(grad_keys_own.reshape(head_shape), cosine_table, sine_table)
    grad_key_rows = grad_key_rows.astype(jnp.bfloat16).reshape(row_count, D)
    grad_joined = jnp.concatenate(
        [grad_queries, grad_key_rows, grad_values_own.astype(jnp.bfloat16).reshape(row_count, D)], 1
    )
    grad_projection = jnp.einsum(
        "rd,rk->dk", input_one, grad_joined, preferred_element_type=jnp.float32
    )
    grad_input_one = jnp.einsum(
        "rk,dk->rd", grad_joined, projection, preferred_element_type=jnp.float32
    )
    grad_time_pair = jnp.concatenate(
        [grad_keys[:, 0].reshape(item_count, D), value_gradients[:, 0].reshape(item_count, D)], 1
    )
    time_rows = jnp.dot(input_time.astype(jnp.float32).T, grad_time_pair, precision=BEST_PRECISION)
    grad_projection = grad_projection + jnp.concatenate(
        [jnp.zeros((D, D), jnp.float32), time_rows], 1
    )
    grad_input_time = jnp.einsum(
        "ik,dk->id", grad_time_pair, projection[:, D:].astype(jnp.float32), precision=BEST_PRECISION
    )
    grad_residual, gain_one = layer_back(grad_input_one, normed_one, inverse_one, gain_values[:, 0])
    grad_residual = (grad_residual + grad_after_self).astype(jnp.bfloat16)
    grad_embeds, gain_time = layer_back(
        grad_input_time, normed_time, inverse_time, gain_values[:, 0]
    )
    grad_in_weight = jnp.einsum(
        "rd,rc->dc", grad_residual, noised, preferred_element_type=jnp.float32
    )
    grad_table = jnp.dot(features.astype(jnp.float32).T, grad_embeds, precision=BEST_PRECISION)
    grad_gains = jnp.stack([gain_one + gain_time, gain_two, gain_three], 1)
    grad_ends = jnp.stack([grad_in_weight, grad_out_weight], 1)
    grad_cross = jnp.stack([grad_cross_query, grad_cross_out], 1)
    grad_squares = jnp.stack(
        [
            grad_projection[:, :D],
            grad_projection[:, D : 2 * D],
            grad_projection[:, 2 * D :],
            grad_attn_out,
        ],
        0,
    )
    grad_slots = jnp.take(to_blocks(grad_squares), assignment, axis=0)
    gate_pieces = grad_gate_up.reshape(D, 2, group_count, piece_width)
    group_grads = (
        lax.psum_scatter(
            grad_ends.astype(jnp.bfloat16), "dp", scatter_dimension=0, tiled=True
        ).astype(jnp.float32),
        lax.psum_scatter(
            grad_table.astype(jnp.bfloat16), "dp", scatter_dimension=0, tiled=True
        ).astype(jnp.float32),
        lax.psum_scatter(
            grad_slots.astype(jnp.bfloat16), "dp", scatter_dimension=0, tiled=True
        ).astype(jnp.float32),
        lax.psum_scatter(
            grad_cross.astype(jnp.bfloat16), "dp", scatter_dimension=0, tiled=True
        ).astype(jnp.float32),
        lax.psum_scatter(
            grad_textside.astype(jnp.bfloat16), "dp", scatter_dimension=0, tiled=True
        ).astype(jnp.float32),
        lax.psum_scatter(
            grad_gains.astype(jnp.bfloat16), "dp", scatter_dimension=0, tiled=True
        ).astype(jnp.float32),
        lax.psum_scatter(
            gate_pieces.astype(jnp.bfloat16), "dp", scatter_dimension=0, tiled=True
        ).astype(jnp.float32),
        lax.psum_scatter(
            grad_down.astype(jnp.bfloat16), "dp", scatter_dimension=0, tiled=True
        ).astype(jnp.float32),
    )
    placing = (jnp.arange(text_count_axis, dtype=jnp.int32) == text_index).astype(jnp.float32)
    spread_gate = group_grads[6][:, :, :, None, :] * placing[None, None, None, :, None]
    spread_gate = spread_gate.reshape(spread_gate.shape[0], 2 * FF)
    owned = (
        lax.psum_scatter(
            group_grads[0].astype(jnp.bfloat16), "text", scatter_dimension=0, tiled=True
        ).astype(jnp.float32),
        lax.psum_scatter(
            group_grads[1].astype(jnp.bfloat16), "text", scatter_dimension=0, tiled=True
        ).astype(jnp.float32),
        lax.psum_scatter(
            group_grads[2].astype(jnp.bfloat16), "text", scatter_dimension=0, tiled=True
        ).astype(jnp.float32),
        lax.psum_scatter(
            group_grads[3].astype(jnp.bfloat16), "text", scatter_dimension=0, tiled=True
        ).astype(jnp.float32),
        lax.psum_scatter(
            group_grads[4].astype(jnp.bfloat16), "text", scatter_dimension=0, tiled=True
        ).astype(jnp.float32),
        lax.psum_scatter(
            group_grads[5].astype(jnp.bfloat16), "text", scatter_dimension=0, tiled=True
        ).astype(jnp.float32),
        lax.psum_scatter(
            spread_gate.astype(jnp.bfloat16), "text", scatter_dimension=0, tiled=True
        ).astype(jnp.float32),
    )
    reduced = (owned[0], owned[1], owned[2], owned[3], owned[4], owned[6], group_grads[7], owned[5])
    square_sum = jnp.zeros((), jnp.float32)
    for member in reduced:
        square_sum = square_sum + jnp.sum(member * member)
    loss_part = jnp.sum(errors * errors) * mse_scale
    totals = lax.psum((square_sum, loss_part), ("dp", "text"))
    loss_total = totals[1] + CONTRAST_WEIGHT * contrast_value / items_total
    gradient_norm = jnp.sqrt(totals[0])
    masters = (
        end_weights,
        time_table,
        square_slots,
        cross_weights,
        key_value,
        gate_up,
        down_weight,
        norm_gains,
    )
    firsts = (
        first_ends,
        first_table,
        None,
        first_cross,
        first_key_value,
        first_gate_up,
        first_down,
        first_gains,
    )
    seconds = (
        second_ends,
        second_table,
        None,
        second_cross,
        second_key_value,
        second_gate_up,
        second_down,
        second_gains,
    )
    return finish(
        loss_total,
        gradient_norm,
        reduced,
        masters,
        firsts,
        seconds,
        (left_stats, right_stats, left_roots, right_roots),
    )


def swap(values, axis, bit=1):
    return lax.ppermute(values, axis, [(i, i ^ bit) for i in range(lax.axis_size(axis))])


def pick(values, position, axis=0):
    return lax.dynamic_index_in_dim(values, position, axis, keepdims=False)


def low_sum(*terms):
    total = terms[0].astype(jnp.float32)
    for term in terms[1:]:
        total = total + term.astype(jnp.float32)
    return total


def on_both(partial_sum):
    low = partial_sum.astype(jnp.bfloat16)
    return low_sum(low, swap(low, "c"))


def tdot(left, right):
    return lax.dot_general(left, right, (((0,), (0,)), ((), ())), preferred_element_type=jnp.float32)


def dot_back(left, right):
    return lax.dot_general(left, right, (((1,), (1,)), ((), ())), preferred_element_type=jnp.float32)


MESH_ID = pl.DeviceIdType.MESH
JOIN_TILE = 512


def anywhere(count):
    return [pl.BlockSpec(memory_space=pl.ANY)] * count


def coordinates():
    return tuple(lax.axis_index(axis) for axis in ("y", "x", "c", "z"))


def chip_peers(me):
    row, column, core, line = me
    beside = {
        "c": (row, column, 1 - core, line),
        "x": (row, 1 - column, core, line),
        "y": (1 - row, column, core, line),
    }
    for offset in (1, 2, 3):
        beside[offset] = (row, column, core, line ^ offset)
    return beside


def greet(peers):
    barrier = pltpu.get_barrier_semaphore()
    for peer in peers.values():
        pl.semaphore_signal(barrier, inc=1, device_id=peer, device_id_type=MESH_ID)
    pl.semaphore_wait(barrier, len(peers))


def send(source, target, send_sem, recv_sem, peer):
    return pltpu.make_async_remote_copy(
        src_ref=source,
        dst_ref=target,
        send_sem=send_sem,
        recv_sem=recv_sem,
        device_id=peer,
        device_id_type=MESH_ID,
    )


def gather_kernel(arrays, groups, *refs):
    count = len(arrays)
    inputs = sum(2 if kind == "cols" else 1 for kind, _, _ in arrays)
    sources = list(refs[:inputs])
    send_sem, recv_sem, core_send, core_recv, local_sem, *item_sems = refs[inputs + 4 + count :]
    item_refs = refs[inputs : inputs + 2] + refs[inputs + 2 + count : inputs + 4 + count]
    bufs = refs[inputs + 2 : inputs + 2 + count]
    me = coordinates()
    row, column, core, line = me
    plane = 2 * row + column
    peers = chip_peers(me)
    others = {offset + 4: (row, column, 1 - core, line ^ offset) for offset in (1, 2, 3)}
    greet({**peers, **others})
    finish_items = move_items(me, item_refs, item_sems)
    local, cross = [], []
    for index_value, (kind, _, _) in enumerate(arrays):
        spot = bufs[index_value].at[plane, 0 if kind == "one" else core, line]
        copy = pltpu.make_async_copy(sources.pop(0), spot, local_sem.at[index_value])
        copy.start()
        local.append(copy)
        cross.append(None)
        if kind == "cols":
            cross[-1] = send(
                sources.pop(0),
                spot,
                core_send.at[index_value],
                core_recv.at[index_value],
                peers["c"],
            )
            cross[-1].start()
    whole = slice(None)
    flat = [unit for group in groups for unit in group]
    ready = set()

    def move(number, slot, planes, lines, peer):
        array, _, rows, columns = flat[number]
        cores = {"cols": whole, "one": 0}.get(arrays[array][0], core)
        view = bufs[array].at[planes, cores, lines, rows, columns]
        return send(view, view, send_sem.at[number, slot], recv_sem.at[number, slot], peer)

    def line_copies(number):
        return [move(number, o - 1, plane, line, peers[o]) for o in (1, 2, 3)]

    def near_copy(number):
        axis = "y" if flat[number][1] else "x"
        return move(number, 3, plane, whole, peers[axis])

    def side_copy(number):
        axis = "x" if flat[number][1] else "y"
        return move(number, 4, plane, whole, peers[axis])

    def far_copy(number):
        color = flat[number][1]
        return move(number, 5, plane ^ (2 if color else 1), whole, peers["x" if color else "y"])

    def core_copy(number):
        array, _, rows, columns = flat[number]
        kind = arrays[array][0]
        if kind not in ("both", "half"):
            return None
        planes = whole if kind == "both" else pl.ds(2 * (1 - core), 2)
        view = bufs[array].at[planes, core, whole, rows, columns]
        return send(view, view, send_sem.at[number, 6], recv_sem.at[number, 6], peers["c"])

    def start_line(number):
        array = flat[number][0]
        if array not in ready:
            ready.add(array)
            local[array].wait()
            if cross[array] is not None:
                cross[array].wait()
        for copy in line_copies(number):
            copy.start()

    def start_near(number):
        for copy in line_copies(number):
            copy.wait_recv()
        near_copy(number).start()
        side_copy(number).start()

    def start_far(number):
        near_copy(number).wait_recv()
        far_copy(number).start()

    def close(number):
        side_copy(number).wait_recv()
        far_copy(number).wait_recv()
        last = core_copy(number)
        if last is not None:
            last.start()
        for copy in line_copies(number) + [near_copy(number), side_copy(number), far_copy(number)]:
            copy.wait_send()

    stages = (start_line, start_near, start_far, close)
    numbers, at = [], 0
    for group in groups:
        numbers.append(range(at, at + len(group)))
        at += len(group)
    for step in range(len(groups) + 3):
        for lag, stage in enumerate(stages):
            if 0 <= step - lag < len(groups):
                for number in numbers[step - lag]:
                    stage(number)
    for number in range(len(flat)):
        last = core_copy(number)
        if last is not None:
            last.wait()
    finish_items()


def move_items(me, refs, sems):
    row, column, core, line = me
    send_sem, recv_sem, local_sem = sems

    def outgoing(kind, inner, side):
        return send(
            refs[kind].at[inner],
            refs[2 + kind].at[line],
            send_sem.at[kind, inner, side],
            recv_sem.at[kind, line],
            (row, column, side, 2 * core + inner),
        )

    def kept(kind, inner):
        return pltpu.make_async_copy(
            refs[kind].at[inner], refs[2 + kind].at[line], local_sem.at[kind]
        )

    def incoming(kind, origin):
        return send(
            refs[kind].at[0],
            refs[2 + kind].at[origin],
            send_sem.at[kind, 0, 0],
            recv_sem.at[kind, origin],
            (row, column, 1 - core, line),
        )

    def each_target(act, keep):
        for kind in range(2):
            for inner in range(2):
                for side in range(2):
                    own = (2 * core + inner == line) & (core == side)

                    @pl.when(own)
                    def stay():
                        keep(kind, inner)

                    @pl.when(jnp.logical_not(own))
                    def leave():
                        act(kind, inner, side)

    each_target(
        lambda kind, inner, side: outgoing(kind, inner, side).start(),
        lambda kind, inner: kept(kind, inner).start(),
    )

    def finish_items():
        each_target(
            lambda kind, inner, side: outgoing(kind, inner, side).wait_send(),
            lambda kind, inner: kept(kind, inner).wait(),
        )
        for kind in range(2):
            for origin in range(4):

                @pl.when(jnp.logical_not((line == origin) & (core == line // 2)))
                def arrive():
                    incoming(kind, origin).wait_recv()

    return finish_items


def gather_weights(arrays, groups, sources, items, collective_id):
    units = sum(len(group) for group in groups)
    dma = pltpu.SemaphoreType.DMA
    return pl.pallas_call(
        partial(gather_kernel, arrays, groups),
        out_shape=[
            jax.ShapeDtypeStruct((4, 1 if kind == "one" else 2, 4) + shape, dtype)
            for kind, shape, dtype in arrays
        ]
        + [jax.ShapeDtypeStruct((4,) + item.shape[1:], item.dtype) for item in items],
        in_specs=anywhere(len(sources) + 2),
        out_specs=anywhere(len(arrays) + 2),
        scratch_shapes=[
            dma((units, 7)),
            dma((units, 7)),
            dma((len(arrays),)),
            dma((len(arrays),)),
            dma((len(arrays),)),
            dma((2, 2, 2)),
            dma((2, 4)),
            dma((2,)),
        ],
        compiler_params=pltpu.CompilerParams(collective_id=collective_id, has_side_effects=True),
    )(*sources, *items)


def share_kernel(values, shared, send_sem, recv_sem):
    row, column, core, line = coordinates()
    own = 8 * row + 4 * column + line

    def peer(offset):
        return (row ^ (offset // 8), column ^ (offset // 4 % 2), core, line ^ (offset % 4))

    greet({offset: peer(offset) for offset in range(1, 16)})
    copies = [
        send(
            values, shared.at[own], send_sem.at[offset], recv_sem.at[offset], peer(offset)
        )
        for offset in range(1, 16)
    ]
    for copy in copies:
        copy.start()
    shared[own] = values[...]
    for copy in copies:
        copy.wait()


def share(values, collective_id):
    dma = pltpu.SemaphoreType.DMA
    return pl.pallas_call(
        share_kernel,
        out_shape=jax.ShapeDtypeStruct((16,) + values.shape, values.dtype),
        in_specs=[pl.BlockSpec(memory_space=pltpu.VMEM)],
        out_specs=pl.BlockSpec(memory_space=pltpu.VMEM),
        scratch_shapes=[dma((16,)), dma((16,))],
        compiler_params=pltpu.CompilerParams(collective_id=collective_id, has_side_effects=True),
    )(values)


FEED_TILE = 256
FEED_ROWS = 512


def chunks(size, body):
    for start in range(0, size, FEED_ROWS):
        body(pl.ds(start, FEED_ROWS))


def feed_kernel(rows, gate_tile, up_tile, gate, up, hidden):
    def body(at):
        gate_part = jnp.dot(rows[at, :], gate_tile[...], preferred_element_type=jnp.float32)
        up_part = jnp.dot(rows[at, :], up_tile[...], preferred_element_type=jnp.float32)
        gate[at, :] = gate_part.astype(gate.dtype)
        up[at, :] = up_part.astype(up.dtype)
        hidden[at, :] = (gate_part * jax.nn.sigmoid(gate_part) * up_part).astype(hidden.dtype)

    chunks(rows.shape[0], body)


def hidden_back_kernel(grad, down_tile, gate, up, hidden, grad_gate, grad_up, grad_down):
    def body(at):
        back = dot_back(grad[at, :], down_tile[...])
        gate_part = gate[at, :].astype(jnp.float32)
        sigmoid = jax.nn.sigmoid(gate_part)
        grad_gate[at, :] = (
            back * up[at, :].astype(jnp.float32) * sigmoid * (1.0 + gate_part * (1.0 - sigmoid))
        ).astype(grad_gate.dtype)
        grad_up[at, :] = (back * gate_part * sigmoid).astype(grad_up.dtype)

    chunks(grad.shape[0], body)

    def weight(at):
        grad_down[:, at] = tdot(hidden[...], grad[:, at]).astype(grad_down.dtype)

    chunks(grad.shape[1], weight)


def rows_back_kernel(
    turned_rows, grad_gate, grad_up, gate_tile, up_tile, gate_out, up_out, rows_out, total
):
    @pl.when(pl.program_id(0) == 0)
    def clear():
        total[...] = jnp.zeros_like(total)

    def body(at):
        gate_out[at, :] = jnp.dot(
            turned_rows[at, :], grad_gate[...], preferred_element_type=jnp.float32
        ).astype(gate_out.dtype)
        up_out[at, :] = jnp.dot(
            turned_rows[at, :], grad_up[...], preferred_element_type=jnp.float32
        ).astype(up_out.dtype)
        total[:, at] += dot_back(grad_gate[...], gate_tile[at, :]) + dot_back(
            grad_up[...], up_tile[at, :]
        )

    chunks(turned_rows.shape[0], body)

    @pl.when(pl.program_id(0) == pl.num_programs(0) - 1)
    def store():
        rows_out[...] = total[...].astype(rows_out.dtype)


def feed_call(kernel, operands, outputs, flops, scratch=()):
    units = FF // 2

    def spec(shape, kind):
        height, width = shape
        if kind == "columns":
            return pl.BlockSpec((height, FEED_TILE), lambda step: (0, step))
        if kind == "rows":
            return pl.BlockSpec((FEED_TILE, width), lambda step: (step, 0))
        return pl.BlockSpec(shape, lambda step: (0, 0))

    low = jnp.bfloat16
    moved = sum(value.size for value, _ in operands) + sum(h * w for (h, w), _ in outputs)
    return pl.pallas_call(
        kernel,
        grid=(units // FEED_TILE,),
        in_specs=[spec(value.shape, kind) for value, kind in operands],
        out_specs=[spec(shape, kind) for shape, kind in outputs],
        out_shape=[jax.ShapeDtypeStruct(shape, low) for shape, _ in outputs],
        scratch_shapes=list(scratch),
        compiler_params=pltpu.CompilerParams(vmem_limit_bytes=56 * 2**20),
        cost_estimate=pl.CostEstimate(flops=flops, bytes_accessed=2 * moved, transcendentals=0),
    )(*[value for value, _ in operands])


def feed(rows, gate_weight, up_weight):
    shape = (rows.shape[0], FF // 2)
    return feed_call(
        feed_kernel,
        [(rows, "whole"), (gate_weight, "columns"), (up_weight, "columns")],
        [(shape, "columns")] * 3,
        4 * rows.size * (FF // 2),
    )


def hidden_back(grad, down, gate, up, hidden):
    shape = hidden.shape
    return feed_call(
        hidden_back_kernel,
        [
            (grad, "whole"),
            (down, "rows"),
            (gate, "columns"),
            (up, "columns"),
            (hidden, "columns"),
        ],
        [(shape, "columns"), (shape, "columns"), (down.shape, "rows")],
        4 * grad.size * (FF // 2),
    )


def rows_back(rows, grad_gate, grad_up, gate_weight, up_weight):
    return feed_call(
        rows_back_kernel,
        [
            (rows.T, "whole"),
            (grad_gate, "columns"),
            (grad_up, "columns"),
            (gate_weight, "columns"),
            (up_weight, "columns"),
        ],
        [(gate_weight.shape, "columns"), (up_weight.shape, "columns"), (rows.shape, "whole")],
        8 * rows.size * (FF // 2),
        [pltpu.VMEM(rows.shape, jnp.float32)],
    )


def reduce_kernel(arrays, groups, *refs):
    count = len(arrays)
    flat = [unit for group in groups for unit in group]
    total = len(flat)
    sources = refs[:count]
    outputs = sum(2 if kind == "cols" else 1 for kind, _ in arrays)
    targets, at = [], count
    for kind, _ in arrays:
        width = 2 if kind == "cols" else 1
        targets.append(refs[at : at + width])
        at += width
    scratch = refs[at:]
    sides, onwards, mines, from_ons, from_lines, from_cores = (
        scratch[index_value * total : (index_value + 1) * total] for index_value in range(6)
    )
    send_sem, recv_sem, load_sem = scratch[6 * total :]
    me = coordinates()
    row, column, core, line = me
    plane = 2 * row + column
    peers = chip_peers(me)
    greet(peers)
    whole = slice(None)

    def source(number, planes):
        array, _, rows, columns = flat[number]
        return sources[array].at[planes, whole, whole, rows, columns]

    def first_copy(number, slot):
        bit, axis = (1, "x") if flat[number][1] else (2, "y")
        return send(
            source(number, plane ^ (3 if slot else bit)),
            sides[number].at[slot],
            send_sem.at[number, slot],
            recv_sem.at[number, slot],
            peers[axis],
        )

    def load_onward(number):
        off = 2 if flat[number][1] else 1
        return pltpu.make_async_copy(
            source(number, plane ^ off), onwards[number], load_sem.at[number, 0]
        )

    def load_mine(number):
        return pltpu.make_async_copy(source(number, plane), mines[number], load_sem.at[number, 1])

    def onward_copy(number):
        axis = "y" if flat[number][1] else "x"
        return send(
            onwards[number],
            from_ons[number],
            send_sem.at[number, 2],
            recv_sem.at[number, 2],
            peers[axis],
        )

    def line_copies(number):
        return [
            send(
                mines[number].at[whole, line ^ offset],
                from_lines[number].at[offset - 1],
                send_sem.at[number, 2 + offset],
                recv_sem.at[number, 2 + offset],
                peers[offset],
            )
            for offset in (1, 2, 3)
        ]

    def core_copy(number):
        return send(
            mines[number].at[1 - core, line],
            from_cores[number],
            send_sem.at[number, 6],
            recv_sem.at[number, 6],
            peers["c"],
        )

    def is_cols(number):
        return arrays[flat[number][0]][0] == "cols"

    def add_into(target, *terms):
        cores, lines, height, _ = target.shape

        def body(step, carry):
            side = step // (lines * (height // 16))
            rest = step % (lines * (height // 16))
            at_line = rest // (height // 16)
            rows = pl.ds(pl.multiple_of((rest % (height // 16)) * 16, 16), 16)
            value = target[side, at_line, rows].astype(jnp.float32)
            for term in terms:
                value = value + term[side, at_line, rows].astype(jnp.float32)
            target[side, at_line, rows] = value.astype(target.dtype)
            return carry

        lax.fori_loop(0, cores * lines * (height // 16), body, 0)

    def stage_one(number):
        first_copy(number, 1).start()
        first_copy(number, 0).start()
        load_onward(number).start()
        load_mine(number).start()

    def stage_two(number):
        first_copy(number, 1).wait_recv()
        load_onward(number).wait()
        add_into(onwards[number], sides[number].at[1])
        onward_copy(number).start()

    def stage_three(number):
        first_copy(number, 0).wait_recv()
        load_mine(number).wait()
        onward_copy(number).wait_recv()
        add_into(mines[number], sides[number].at[0], from_ons[number])
        for copy in line_copies(number):
            copy.start()

    def stage_four(number):
        for copy in line_copies(number):
            copy.wait_recv()
        array, _, rows, columns = flat[number]
        mine, pieces = mines[number], from_lines[number]
        for side in range(mine.shape[0]):
            value = mine[side, line].astype(jnp.float32)
            for offset in range(3):
                value = value + pieces[offset, side].astype(jnp.float32)
            mine[side, line] = value.astype(mine.dtype)
        if is_cols(number):
            core_copy(number).start()
            targets[array][0][rows, columns] = mine[core, line]
        else:
            targets[array][0][rows, columns] = mine[0, line]

    def stage_five(number):
        if is_cols(number):
            core_copy(number).wait()
            array, _, rows, columns = flat[number]
            targets[array][1][rows, columns] = from_cores[number][...]
        first_copy(number, 0).wait_send()
        first_copy(number, 1).wait_send()
        onward_copy(number).wait_send()
        for copy in line_copies(number):
            copy.wait_send()

    stages = (stage_one, stage_two, stage_three, stage_four, stage_five)
    numbers, at = [], 0
    for group in groups:
        numbers.append(range(at, at + len(group)))
        at += len(group)
    for step in range(len(groups) + 4):
        for lag, stage in enumerate(stages):
            if 0 <= step - lag < len(groups):
                for number in numbers[step - lag]:
                    stage(number)


def extent(sel, size):
    return size if isinstance(sel, slice) else sel.size


def reduce_gradients(arrays, groups, sources, collective_id):
    flat = [unit for group in groups for unit in group]
    vmem, dma, low = pltpu.VMEM, pltpu.SemaphoreType.DMA, jnp.bfloat16
    shapes = []
    for array, _, rows, columns in flat:
        kind, (height, width) = arrays[array]
        shapes.append((2 if kind == "cols" else 1, extent(rows, height), extent(columns, width)))
    scratch = [vmem((2, c, 4, h, w), low) for c, h, w in shapes]
    for _ in range(3):
        scratch += [vmem((c, 4, h, w), low) for c, h, w in shapes]
    scratch += [vmem((3, c, h, w), low) for c, h, w in shapes]
    scratch += [vmem((h, w) if c == 2 else (16, 128), low) for c, h, w in shapes]
    out_shape = []
    for kind, shape in arrays:
        out_shape += [jax.ShapeDtypeStruct(shape, low)] * (2 if kind == "cols" else 1)
    return pl.pallas_call(
        partial(reduce_kernel, arrays, groups),
        out_shape=out_shape,
        in_specs=anywhere(len(sources)),
        out_specs=[pl.BlockSpec(memory_space=pltpu.VMEM)] * len(out_shape),
        scratch_shapes=scratch
        + [dma((len(flat), 7)), dma((len(flat), 7)), dma((len(flat), 2))],
        compiler_params=pltpu.CompilerParams(
            collective_id=collective_id, has_side_effects=True, vmem_limit_bytes=60 * 2**20
        ),
    )(*sources)


def turned(values, cosine, sine):
    lane = lax.broadcasted_iota(jnp.int32, values.shape, 1)
    halfway = HD // 2
    partner = jnp.where(
        lane % HD < halfway,
        pltpu.roll(values, 128 - halfway, 1),
        pltpu.roll(values, halfway, 1),
    )
    return values * cosine + partner * sine


def join_kernel(rows, times, weights, cosine, sine, joined, joined_time):
    is_turned = pl.program_id(0) < 6

    def body(step, carry):
        at = pl.ds(pl.multiple_of(step * JOIN_TILE, JOIN_TILE), JOIN_TILE)
        values = jnp.dot(rows[at, :], weights[...], preferred_element_type=jnp.float32)

        @pl.when(is_turned)
        def turn():
            for side in (0, 128):
                joined[at, side : side + 128] = turned(
                    values[:, side : side + 128], cosine[at, :], sine[at, :]
                ).astype(joined.dtype)

        @pl.when(jnp.logical_not(is_turned))
        def keep():
            joined[at, :] = values.astype(joined.dtype)

        return carry

    lax.fori_loop(0, rows.shape[0] // JOIN_TILE, body, 0)
    joined_time[...] = jnp.dot(
        times[...], weights[...], preferred_element_type=jnp.float32
    ).astype(joined_time.dtype)


def join(rows, times, weights, cosine, sine):
    width = weights.shape[1]

    def fixed(array):
        return pl.BlockSpec(array.shape, lambda step: (0, 0))

    return pl.pallas_call(
        join_kernel,
        grid=(width // 256,),
        in_specs=[
            fixed(rows),
            fixed(times),
            pl.BlockSpec((D, 256), lambda step: (0, step)),
            fixed(cosine),
            fixed(sine),
        ],
        out_specs=[
            pl.BlockSpec((rows.shape[0], 256), lambda step: (0, step)),
            pl.BlockSpec((times.shape[0], 256), lambda step: (0, step)),
        ],
        out_shape=[
            jax.ShapeDtypeStruct((rows.shape[0], width), jnp.bfloat16),
            jax.ShapeDtypeStruct((times.shape[0], width), jnp.bfloat16),
        ],
        compiler_params=pltpu.CompilerParams(vmem_limit_bytes=48 * 2**20),
        cost_estimate=pl.CostEstimate(
            flops=2 * rows.shape[0] * D * width,
            bytes_accessed=2 * (rows.size + weights.size + rows.shape[0] * width),
            transcendentals=0,
        ),
    )(rows, times, weights, cosine, sine)


def head_lanes(shape, head):
    return lax.broadcasted_iota(jnp.int32, shape, 1) // HD == head


def attend_kernel(timed, queries, keys, values, first, second, mixed, logsum):
    tile = 256 if timed else 512

    def body(step, carry):
        at = pl.ds(pl.multiple_of(step * tile, tile), tile)
        rows = queries[at, :]
        total = jnp.zeros(rows.shape, jnp.float32)
        sums = jnp.zeros(rows.shape, jnp.float32)
        for head in range(2):
            own = head_lanes(rows.shape, head)
            query = jnp.where(own, rows, jnp.zeros_like(rows))
            scores = dot_back(query, keys[...]) * SCORE_SCALE
            if timed:
                extra = (
                    jnp.sum(
                        query.astype(jnp.float32) * first[0:1, :].astype(jnp.float32),
                        -1,
                        keepdims=True,
                    )
                    * SCORE_SCALE
                )
                peak = jnp.maximum(jnp.max(scores, -1, keepdims=True), extra)
            else:
                scores = scores + first[0:1, :]
                peak = jnp.max(scores, -1, keepdims=True)
            powers = jnp.exp(scores - peak)
            row_total = jnp.sum(powers, -1, keepdims=True)
            mixture = jnp.dot(
                powers.astype(jnp.bfloat16), values[...], preferred_element_type=jnp.float32
            )
            if timed:
                power = jnp.exp(extra - peak)
                row_total = row_total + power
                mixture = mixture + power * second[0:1, :].astype(jnp.float32)
            total = jnp.where(own, mixture / row_total, total)
            sums = jnp.where(own, peak + jnp.log(row_total), sums)
        mixed[at, :] = total.astype(mixed.dtype)
        logsum[at, :] = sums
        return carry

    lax.fori_loop(0, queries.shape[0] // tile, body, 0)


def lane_block(array, offset):
    return pl.BlockSpec((array.shape[0], 128), lambda pair: (0, pair + offset))


def attend(queries, keys, values, extras, offsets, timed):
    rows, count, pairs = queries.shape[0], keys.shape[0], HEADS // 4
    extra_specs = (
        [lane_block(extras[0], offsets[1]), lane_block(extras[1], offsets[2])]
        if timed
        else [pl.BlockSpec(extra.shape, lambda pair: (0, 0)) for extra in extras]
    )
    return pl.pallas_call(
        partial(attend_kernel, timed),
        grid=(pairs,),
        in_specs=[
            lane_block(queries, offsets[0]),
            lane_block(keys, offsets[1]),
            lane_block(values, offsets[2]),
        ]
        + extra_specs,
        out_specs=[pl.BlockSpec((rows, 128), lambda pair: (0, pair))] * 2,
        out_shape=[
            jax.ShapeDtypeStruct((rows, 128 * pairs), jnp.bfloat16),
            jax.ShapeDtypeStruct((rows, 128 * pairs), jnp.float32),
        ],
        compiler_params=pltpu.CompilerParams(vmem_limit_bytes=48 * 2**20),
        cost_estimate=pl.CostEstimate(
            flops=3 * pairs * 2 * rows * count * 128 * 4,
            bytes_accessed=pairs * 128 * (rows * 10 + count * 4),
            transcendentals=pairs * 2 * rows * count,
        ),
    )(queries, keys, values, *extras)


def attend_back_kernel(timed, *refs):
    queries, keys, values, first, second, mixed, logsum, gradient = refs[:8]
    if timed:
        cosine, sine, out_q, out_k, out_v, out_first, out_second, sum_k, sum_v = refs[8:]
    else:
        out_q, out_k, out_v, sum_k, sum_v = refs[8:]
    sum_k[...] = jnp.zeros_like(sum_k)
    sum_v[...] = jnp.zeros_like(sum_v)
    if timed:
        out_first[...] = jnp.zeros_like(out_first)
        out_second[...] = jnp.zeros_like(out_second)

    tile = 256 if timed else 512

    def body(step, carry):
        at = pl.ds(pl.multiple_of(step * tile, tile), tile)
        rows, grad = queries[at, :], gradient[at, :]
        product = grad.astype(jnp.float32) * mixed[at, :].astype(jnp.float32)
        sums = logsum[at, :]
        sums_row = sums.T
        grad_query = jnp.zeros(rows.shape, jnp.float32)
        for head in range(2):
            own = head_lanes(rows.shape, head)
            query = jnp.where(own, rows, jnp.zeros_like(rows))
            grad_own = jnp.where(own, grad, jnp.zeros_like(grad))
            inner = jnp.sum(jnp.where(own, product, 0.0), -1, keepdims=True)
            inner_row = jnp.broadcast_to(inner, rows.shape).T[0:1, :]
            scores = dot_back(keys[...], query) * SCORE_SCALE
            if not timed:
                scores = scores + second[:, 0:1]
            attention = jnp.exp(scores - sums_row[head * HD : head * HD + 1, :])
            grad_attention = dot_back(values[...], grad_own)
            sum_v[...] += jnp.dot(
                attention.astype(jnp.bfloat16), grad_own, preferred_element_type=jnp.float32
            )
            grad_scores = (attention * (grad_attention - inner_row)).astype(jnp.bfloat16)
            sum_k[...] += jnp.dot(grad_scores, query, preferred_element_type=jnp.float32)
            key_own = jnp.where(
                head_lanes(keys.shape, head), keys[...], jnp.zeros(keys.shape, keys.dtype)
            )
            grad_query = grad_query + tdot(grad_scores, key_own)
            if timed:
                key_time = jnp.where(
                    own[0:1, :], first[0:1, :].astype(jnp.float32), jnp.zeros((1, 128), jnp.float32)
                )
                wide_query, wide_grad = query.astype(jnp.float32), grad_own.astype(jnp.float32)
                score = jnp.sum(wide_query * key_time, -1, keepdims=True) * SCORE_SCALE
                power = jnp.exp(score - sums[:, head * HD : head * HD + 1])
                back = jnp.sum(
                    wide_grad * second[0:1, :].astype(jnp.float32), -1, keepdims=True
                )
                grad_score = (power * (back - inner)).astype(jnp.bfloat16).astype(jnp.float32)
                grad_query = grad_query + grad_score * key_time
                out_first[0:1, :] += SCORE_SCALE * jnp.sum(
                    grad_score * wide_query, 0, keepdims=True
                )
                out_second[0:1, :] += jnp.sum(
                    power.astype(jnp.bfloat16).astype(jnp.float32) * wide_grad, 0, keepdims=True
                )
        grad_query = grad_query * SCORE_SCALE
        if timed:
            grad_query = turned(grad_query, cosine[at, :], -sine[at, :])
        out_q[at, :] = grad_query.astype(out_q.dtype)
        return carry

    lax.fori_loop(0, queries.shape[0] // tile, body, 0)
    grad_key = sum_k[...] * SCORE_SCALE
    if timed:
        grad_key = turned(grad_key, cosine[...], -sine[...])
    out_k[...] = grad_key.astype(out_k.dtype)
    out_v[...] = sum_v[...].astype(out_v.dtype)


def attend_back(queries, keys, values, extras, offsets, mixed, logsum, gradient, tables):
    timed = tables is not None
    rows, count, pairs = queries.shape[0], keys.shape[0], HEADS // 4
    extra_specs = (
        [lane_block(extras[0], offsets[1]), lane_block(extras[1], offsets[2])]
        if timed
        else [pl.BlockSpec(extra.shape, lambda pair: (0, 0)) for extra in extras]
    )
    low = jnp.bfloat16 if timed else jnp.float32

    def out(height, dtype):
        return (
            jax.ShapeDtypeStruct((height, 128 * pairs), dtype),
            pl.BlockSpec((height, 128), lambda pair: (0, pair)),
        )

    outs = [out(rows, jnp.bfloat16), out(count, low), out(count, low)]
    operands = [queries, keys, values, *extras, mixed, logsum, gradient]
    specs = (
        [
            lane_block(queries, offsets[0]),
            lane_block(keys, offsets[1]),
            lane_block(values, offsets[2]),
        ]
        + extra_specs
        + [lane_block(mixed, 0), lane_block(logsum, 0), lane_block(gradient, 0)]
    )
    if timed:
        outs += [out(8, jnp.float32), out(8, jnp.float32)]
        operands += list(tables)
        specs += [pl.BlockSpec(table.shape, lambda pair: (0, 0)) for table in tables]
    return pl.pallas_call(
        partial(attend_back_kernel, timed),
        grid=(pairs,),
        in_specs=specs,
        out_specs=[spec for _, spec in outs],
        out_shape=[shape for shape, _ in outs],
        scratch_shapes=[pltpu.VMEM((count, 128), jnp.float32)] * 2,
        compiler_params=pltpu.CompilerParams(vmem_limit_bytes=48 * 2**20),
        cost_estimate=pl.CostEstimate(
            flops=3 * pairs * 2 * rows * count * 128 * 10,
            bytes_accessed=pairs * 128 * (rows * 16 + count * 8),
            transcendentals=pairs * 2 * rows * count,
        ),
    )(*operands)


def shifted(tile, is_shifted):
    wide = tile.astype(jnp.float32)
    return jnp.where(is_shifted, pltpu.roll(wide, BLK, 1), wide)


def assemble_kernel(joined_at, mix_at, pairs, joined, mix):
    step = pl.program_id(0)
    lane = lax.broadcasted_iota(jnp.int32, (BLK, 2 * BLK), 1)

    def fill(places, target, count):
        for pair in range(count):
            first = (step * count + pair) * 2
            left, right = places[first], places[first + 1]
            tile = jnp.where(
                lane < BLK,
                shifted(pairs[left // 2], left % 2 == 1),
                shifted(pairs[right // 2], right % 2 == 0),
            )
            target[:, pair * 2 * BLK : (pair + 1) * 2 * BLK] = tile.astype(target.dtype)

    fill(joined_at, joined, 6)
    fill(mix_at, mix, 2)


def assemble(pairs, joined_at, mix_at):
    half = D // 2
    return pl.pallas_call(
        assemble_kernel,
        grid_spec=pltpu.PrefetchScalarGridSpec(
            num_scalar_prefetch=2,
            grid=(8,),
            in_specs=[
                pl.BlockSpec(
                    pairs.shape, lambda step, *_: (0, 0, 0), pipeline_mode=pl.Buffered(1)
                )
            ],
            out_specs=[
                pl.BlockSpec((BLK, 3 * half), lambda step, *_: (step, 0)),
                pl.BlockSpec((BLK, half), lambda step, *_: (step // 2, step % 2)),
            ],
        ),
        out_shape=[
            jax.ShapeDtypeStruct((D, 3 * half), pairs.dtype),
            jax.ShapeDtypeStruct((half, D), pairs.dtype),
        ],
        compiler_params=pltpu.CompilerParams(vmem_limit_bytes=48 * 2**20),
        cost_estimate=pl.CostEstimate(
            flops=0, bytes_accessed=2 * pairs.size + 8 * half * D, transcendentals=0
        ),
    )(joined_at, mix_at, pairs)


SLOTS_STEP = 8


def collect_kernel(rows_at, columns_at, sides, joined, mix, near, far):
    step = pl.program_id(0)
    lane = lax.broadcasted_iota(jnp.int32, (BLK, 2 * BLK), 1)

    def fill(target):
        target[...] = jnp.zeros_like(target)
        for inner in range(SLOTS_STEP):
            slot, pair, right = step * SLOTS_STEP + inner, inner // 2, inner % 2
            code = sides[slot]
            rows = pl.ds(pl.multiple_of(rows_at[slot] * BLK, BLK), BLK)
            columns = pl.ds(pl.multiple_of(columns_at[slot] * 2 * BLK, 128), 2 * BLK)
            own = lane // BLK == right

            def put(source, is_shifted):
                tile = source[rows, columns]
                if is_shifted:
                    tile = pltpu.roll(tile.astype(jnp.float32), BLK, 1).astype(tile.dtype)
                target[pair] = jnp.where(own, tile, target[pair])

            for which, source in enumerate((joined, mix)):
                for side in range(2):
                    pl.when(code == 2 * which + side)(partial(put, source, side != right))

    near_steps = pl.num_programs(0) // 2
    pl.when(step < near_steps)(partial(fill, near))
    pl.when(step >= near_steps)(partial(fill, far))


def collect(joined, mix, rows_at, columns_at, sides):
    steps = sides.shape[0] // SLOTS_STEP
    block = (SLOTS_STEP // 2, BLK, 2 * BLK)

    def resident(array):
        return pl.BlockSpec(array.shape, lambda step, *_: (0, 0), pipeline_mode=pl.Buffered(1))

    return pl.pallas_call(
        collect_kernel,
        grid_spec=pltpu.PrefetchScalarGridSpec(
            num_scalar_prefetch=3,
            grid=(steps,),
            in_specs=[resident(joined), resident(mix)],
            out_specs=[
                pl.BlockSpec(block, lambda step, *_: (jnp.minimum(step, steps // 2 - 1), 0, 0)),
                pl.BlockSpec(block, lambda step, *_: (jnp.maximum(step - steps // 2, 0), 0, 0)),
            ],
        ),
        out_shape=[jax.ShapeDtypeStruct((sides.shape[0] // 4, BLK, 2 * BLK), joined.dtype)] * 2,
        compiler_params=pltpu.CompilerParams(vmem_limit_bytes=48 * 2**20),
        cost_estimate=pl.CostEstimate(
            flops=0,
            bytes_accessed=4 * (joined.size + mix.size) + 4 * sides.shape[0] * BLK * BLK,
            transcendentals=0,
        ),
    )(rows_at, columns_at, sides, joined, mix)


def item_per_chip(
    latents,
    noise_field,
    timesteps,
    text_tokens,
    text_lengths,
    negatives,
    assignment,
    end_weights,
    time_table,
    square_slots,
    cross_weights,
    key_value,
    gate_up,
    down_weight,
    norm_gains,
    first_ends,
    second_ends,
    first_table,
    second_table,
    first_cross,
    second_cross,
    first_key_value,
    second_key_value,
    first_gate_up,
    second_gate_up,
    first_down,
    second_down,
    first_gains,
    second_gains,
    left_stats,
    right_stats,
    left_roots,
    right_roots,
):
    bf16, f32 = jnp.bfloat16, jnp.float32
    row, column = lax.axis_index("y"), lax.axis_index("x")
    core, line = lax.axis_index("c"), lax.axis_index("z")
    plane = 2 * row + column
    item = 4 * plane + line
    quads = range(4)
    half = D // 2
    items_total = 16
    mse_scale = 1.0 / (items_total * FRAMES * DIN)

    meta = jnp.concatenate([timesteps, text_lengths, negatives.reshape(-1)])[None]
    pack = jnp.concatenate(
        [
            time_table,
            jnp.pad(norm_gains.T.reshape(1, 144), ((0, 0), (0, D - 144))),
            jnp.pad(meta.astype(f32), ((0, 6), (0, D - 34))),
        ],
        0,
    ).astype(bf16)
    low_ends = end_weights.reshape(48, 2 * DIN).astype(bf16)
    low_slots = square_slots.astype(bf16).reshape(4, 2, BLK, BLK)
    low_pairs = jnp.concatenate([low_slots[:, 0], low_slots[:, 1]], 2).reshape(4 * BLK, 2 * BLK)
    low_cross = cross_weights.astype(bf16)
    low_kv = key_value.astype(bf16)
    low_gate = gate_up.astype(bf16)
    low_down = down_weight.astype(bf16)

    def head_columns(array, which, side):
        return lax.dynamic_slice_in_dim(array, which * D + side * half, half, 1)

    def unit_columns(which, side):
        return jnp.concatenate(
            [
                lax.dynamic_slice_in_dim(
                    low_gate, which * FF + quadrant * 1536 + side * 768, 768, 1
                )
                for quadrant in quads
            ],
            1,
        )

    def kv_block(which, side):
        return head_columns(low_kv, which, side).reshape(16, 1152)

    def gathered(block):
        return lax.all_gather(block, ("y", "x", "z"), axis=0)

    feed_blocks = []
    for which in range(2):
        kept, received = unit_columns(which, core), swap(unit_columns(which, 1 - core), "c")
        feed_blocks.append(
            jnp.where(core == 0, jnp.stack([kept, received]), jnp.stack([received, kept]))
        )
    gate_weight, up_weight = (gathered(block).reshape(D, FF // 2) for block in feed_blocks)
    down = gathered(low_down).reshape(FF // 2, D)
    arrays = (
        ("cols", (16, D), bf16),
        ("both", (4 * BLK, 2 * BLK), bf16),
        ("cols", (48, half), bf16),
        ("half", (48, D), bf16),
        ("cols", (16, 1152), bf16),
        ("cols", (16, 1152), bf16),
        ("cols", (48, 2 * DIN), bf16),
    )
    whole = slice(None)
    groups = [((0, 0, whole, whole), (5, 1, whole, whole), (6, 1, whole, whole))]
    groups += [
        ((1, 0, pl.ds(step * 96, 96), whole), (1, 1, pl.ds(384 + step * 96, 96), whole))
        for step in range(4)
    ]
    groups += [
        ((2, 0, whole, pl.ds(step * 384, 384)), (3, 1, whole, pl.ds(step * 768, 768)))
        for step in range(2)
    ]
    groups += [((4, 0, whole, whole),)]
    (
        packs,
        all_pairs,
        cross_query,
        cross_out,
        keys_own,
        values_own,
        ends_full,
        frames,
        tokens,
    ) = gather_weights(
        arrays,
        groups,
        (
            pack,
            pack,
            low_pairs,
            head_columns(low_cross[:, 0, :], 0, core),
            head_columns(low_cross[:, 0, :], 0, 1 - core),
            low_cross[:, 1, :],
            kv_block(0, core),
            kv_block(0, 1 - core),
            kv_block(1, core),
            kv_block(1, 1 - core),
            low_ends,
            low_ends,
        ),
        (jnp.concatenate([latents, noise_field], 2), text_tokens),
        1,
    )
    packs = packs.reshape(32, 16, D)
    table_full = packs[:, :8].reshape(NTIME, D)
    gain_values = packs[:, 8, :144].reshape(32, 3, 48).transpose(1, 0, 2).reshape(3, D).astype(f32)
    ends_full = ends_full.reshape(D, 2 * DIN)
    weight_in, weight_out = ends_full[:, :DIN], ends_full[:, DIN:]
    all_pairs = all_pairs.reshape(128, BLK, 2 * BLK)
    inverse_order = (
        jnp.zeros_like(assignment)
        .at[assignment]
        .set(jnp.arange(assignment.shape[0], dtype=jnp.int32))
    )

    def grid_blocks(matrix, rows, columns):
        return (matrix * 64 + rows * 8 + columns).reshape(-1)

    eight, four = jnp.arange(8, dtype=jnp.int32), jnp.arange(4, dtype=jnp.int32)
    joined_blocks = grid_blocks(
        jnp.arange(3, dtype=jnp.int32)[None, :, None],
        eight[:, None, None],
        (4 * core + four)[None, None, :],
    )
    out_blocks = grid_blocks(3, (4 * core + four)[:, None], eight[None, :])
    projection, weight_mix = assemble(
        all_pairs, inverse_order[joined_blocks], inverse_order[out_blocks]
    )
    cross_query = cross_query.reshape(D, half)
    cross_out = lax.dynamic_slice_in_dim(cross_out.reshape(D, D), core * half, half, 0)
    kv_own = jnp.concatenate(
        [keys_own.reshape(DT, half), values_own.reshape(DT, half)], 1
    )

    metas = packs.reshape(8, 4, 16, D)[:, 0, 9, :34].astype(jnp.int32)
    timestep = pick(metas[:, :2].reshape(-1), item)
    text_length = pick(metas[:, 2:4].reshape(-1), item)
    negative_rows = metas[:, 4:].reshape(items_total, -1)
    frames = frames.reshape(FRAMES, 2 * DIN)
    clean, noise = frames[:, :DIN], frames[:, DIN:]
    tokens = tokens.reshape(-1, DT)
    frame_positions = jnp.arange(FRAMES, dtype=jnp.int32) + 1
    token_slots = jnp.arange(tokens.shape[0], dtype=jnp.int32)
    halfway = HD // 2
    frequency = jnp.exp(jnp.arange(halfway, dtype=f32) * (-2.0 * math.log(10000.0) / HD))
    turn = frame_positions.astype(f32)[:, None] * frequency[None, :]
    cosine_table = jnp.concatenate([jnp.cos(turn)] * 4, -1)
    sine_table = jnp.concatenate([-jnp.sin(turn), jnp.sin(turn)] * 2, -1)
    angle = (timestep.astype(f32) + 0.5) * (0.5 * math.pi / NTIME)
    signal, spread = jnp.cos(angle), jnp.sin(angle)
    noised = (signal * clean + spread * noise).astype(bf16)
    target = signal * noise - spread * clean

    residual = dot_back(noised, weight_in)
    normed_one, inverse_one = layer_stats(residual)
    input_one = (normed_one * gain_values[0]).astype(bf16)
    features = time_features(timestep[None]).astype(bf16)
    embeds = jnp.dot(features, table_full, preferred_element_type=f32)
    normed_time, inverse_time = layer_stats(embeds)
    input_time = (normed_time * gain_values[0]).astype(bf16)
    time_block = jnp.pad(input_time, ((0, 15), (0, 0)))
    joined, joined_time = join(input_one, time_block, projection, cosine_table, sine_table)
    pairs = half // 128
    self_offsets = (0, pairs, 2 * pairs)
    mixed_flat, logsum_self = attend(
        joined, joined, joined, (joined_time, joined_time), self_offsets, True
    )
    after_self = residual + on_both(jnp.dot(mixed_flat, weight_mix, preferred_element_type=f32))
    normed_two, inverse_two = layer_stats(after_self)
    input_two = (normed_two * gain_values[1]).astype(bf16)
    cross_queries = jnp.dot(input_two, cross_query, preferred_element_type=f32).astype(bf16)
    projected = jnp.dot(tokens, kv_own, preferred_element_type=f32).astype(bf16)
    valid = token_slots < text_length
    cross_bias = jnp.where(valid, 0.0, MASK_VALUE).astype(f32)[None]
    text_biases = (
        jnp.broadcast_to(cross_bias, (8, 128)),
        jnp.broadcast_to(cross_bias.T, (128, 128)),
    )
    cross_offsets = (0, 0, pairs)
    cross_flat, logsum_cross = attend(
        cross_queries, projected, projected, text_biases, cross_offsets, False
    )
    after_cross = after_self + on_both(jnp.dot(cross_flat, cross_out, preferred_element_type=f32))
    normed_three, inverse_three = layer_stats(after_cross)
    input_three = (normed_three * gain_values[2]).astype(bf16)
    feature = jnp.arange(D, dtype=jnp.int32)
    gathered_at = (feature // 384 * 4 + feature // 48 % 4) * 96 + feature // 192 % 2 * 48 + feature % 48
    reorder = (gathered_at[:, None] == feature[None, :]).astype(bf16)
    feed_rows = jnp.dot(input_three, reorder, preferred_element_type=f32).astype(bf16)
    gate_part, up_part, hidden = feed(feed_rows, gate_weight, up_weight)
    down_out = on_both(jnp.dot(hidden, down, preferred_element_type=f32))
    output_rows = after_cross + down_out
    output_low = output_rows.astype(bf16)
    predicted = jnp.dot(output_low, weight_out, preferred_element_type=f32)
    errors = predicted - target

    length_float = text_length.astype(f32)
    mask = valid.astype(f32)[:, None]
    text_half = jnp.sum(projected[:, :half].astype(f32) * mask, 0) / length_float
    text_rest = swap(text_half, "c")
    text_pool = jnp.where(
        core == 0,
        jnp.concatenate([text_half, text_rest]),
        jnp.concatenate([text_rest, text_half]),
    )
    pools = jnp.stack([jnp.sum(output_rows, 0) / FRAMES, text_pool], 0)
    pools = share(pools.reshape(8, D // 4), 3).reshape(items_total, 2, D)
    inverse_pools = lax.rsqrt(jnp.sum(pools * pools, -1, keepdims=True) + POOL_EPS)
    units = pools * inverse_pools
    audio_units, text_units = units[:, 0], units[:, 1]
    similar = (
        lax.dot_general(
            audio_units, text_units, (((1,), (1,)), ((), ())), precision=BEST_PRECISION
        )
        / CONTRAST_TEMP
    )
    same = jnp.eye(items_total, dtype=f32)
    counts = same + jnp.sum(
        (negative_rows[:, None, :] == jnp.arange(items_total, dtype=jnp.int32)[None, :, None]).astype(f32), -1
    )
    peak = jnp.max(jnp.where(counts > 0, similar, -jnp.inf), -1, keepdims=True)
    powers = jnp.where(counts > 0, counts * jnp.exp(similar - peak), 0.0)
    totals_row = jnp.sum(powers, -1, keepdims=True)
    contrast_own = pick(
        peak[:, 0] + jnp.log(totals_row[:, 0]) - jnp.sum(same * similar, -1), item
    )
    grad_similar = (powers / totals_row - same) * (
        CONTRAST_WEIGHT / items_total / CONTRAST_TEMP
    )
    grad_audio_unit = jnp.sum(pick(grad_similar, item)[:, None] * text_units, 0)
    grad_text_unit = jnp.sum(pick(grad_similar, item, 1)[:, None] * audio_units, 0)

    def unit_back(gradient, unit, inverse):
        return inverse * (gradient - unit * jnp.sum(unit * gradient))

    grad_audio = unit_back(grad_audio_unit, pick(audio_units, item), pick(inverse_pools, item)[0])
    grad_text = unit_back(grad_text_unit, pick(text_units, item), pick(inverse_pools, item)[1])

    grad_predicted = (2.0 * mse_scale * errors).astype(bf16)
    grad_out_weight = tdot(output_low, grad_predicted)
    grad_output = dot_back(grad_predicted, weight_out) + grad_audio[None, :] / FRAMES
    grad_low = grad_output.astype(bf16)
    grad_gate, grad_up, grad_down = hidden_back(grad_low, down, gate_part, up_part, hidden)
    grad_gate_weight, grad_up_weight, grad_feed_rows = rows_back(
        feed_rows, grad_gate, grad_up, gate_weight, up_weight
    )

    def over_plane(gradient, width):
        return lax.psum_scatter(
            gradient.reshape(4, 4, -1, width, gradient.shape[1]),
            ("y", "x"),
            scatter_dimension=0,
            tiled=True,
        )

    def over_line(total):
        return lax.psum_scatter(total, "z", scatter_dimension=1, tiled=True)[0, 0]

    totals = [
        over_plane(gradient, width)
        for gradient, width in ((grad_down, 192), (grad_gate_weight, 48), (grad_up_weight, 48))
    ]
    down_total, *gate_totals = [over_line(total) for total in totals]
    feed_sums = [
        (pick(both_rows, core), swap(pick(both_rows, 1 - core), "c")) for both_rows in gate_totals
    ]
    gate_columns = []
    for mine, other in feed_sums:
        sides = (jnp.where(core == 0, mine, other), jnp.where(core == 0, other, mine))
        for quadrant in quads:
            for side in sides:
                gate_columns.append(side[:, quadrant * 768 : (quadrant + 1) * 768])
    grad_gate_up = jnp.concatenate(gate_columns, 1).astype(f32)
    grad_down = down_total[0].astype(f32)
    grad_input_three = on_both(dot_back(grad_feed_rows, reorder))
    grad_after_cross, gain_three = layer_back(
        grad_input_three, normed_three, inverse_three, gain_values[2]
    )
    grad_after_cross = grad_after_cross + grad_output
    grad_cross_in = grad_after_cross.astype(bf16)
    cross_rows = tdot(cross_flat, grad_cross_in).astype(bf16).reshape(2, 2, 192, D)
    cross_kept = pick(cross_rows, core, 1)
    cross_received = swap(pick(cross_rows, 1 - core, 1), "c")
    cross_pair = jnp.stack([cross_kept, cross_received], 0)
    out_rows = jnp.where(core == 0, cross_pair, cross_pair[::-1]).reshape(4, 1, 4, 48, D)
    grad_mixed_cross = dot_back(grad_cross_in, cross_out).astype(bf16)
    grad_cq, grad_text_keys, grad_text_values = attend_back(
        cross_queries,
        projected,
        projected,
        text_biases,
        cross_offsets,
        cross_flat,
        logsum_cross,
        grad_mixed_cross,
        None,
    )
    grad_query_weight = tdot(input_two, grad_cq).astype(bf16).reshape(4, 2, 4, 48, half)
    grad_input_two = on_both(dot_back(grad_cq, cross_query))
    text_half_grad = lax.dynamic_slice_in_dim(grad_text, core * half, half, 0)
    grad_pair_keys = (
        grad_text_keys + mask * (text_half_grad[None, :] / length_float)
    ).astype(bf16)
    kv_sources = [
        tdot(tokens, gradient.astype(bf16)).astype(bf16).reshape(4, 2, 4, 16, 1152)
        for gradient in (grad_pair_keys, grad_text_values)
    ]
    grad_after_self, gain_two = layer_back(
        grad_input_two, normed_two, inverse_two, gain_values[1]
    )
    grad_after_self = grad_after_self + grad_after_cross
    grad_self_in = grad_after_self.astype(bf16)
    grad_mix = tdot(mixed_flat, grad_self_in).astype(bf16)
    grad_mixed_self = dot_back(grad_self_in, weight_mix).astype(bf16)
    grad_queries, grad_keys, grad_values, grad_time_keys, grad_time_values = attend_back(
        joined,
        joined,
        joined,
        (joined_time, joined_time),
        self_offsets,
        mixed_flat,
        logsum_self,
        grad_mixed_self,
        (cosine_table, sine_table),
    )
    grad_joined = jnp.concatenate([grad_queries, grad_keys, grad_values], 1)
    grad_time_pair = jnp.concatenate([grad_time_keys[:1], grad_time_values[:1]], 1)
    time_row = jnp.concatenate([jnp.zeros((1, half), f32), grad_time_pair], 1)
    grad_projection = (
        tdot(input_one, grad_joined) + input_time.astype(f32).reshape(D, 1) * time_row
    ).astype(bf16)
    position = jnp.arange(256, dtype=jnp.int32)
    owner_core = core ^ (position // 128)
    block = assignment[
        (position // 32) % 4 * 64 + owner_core * 32 + (position // 8) % 4 * 8 + position % 8
    ]
    matrix, block_row, block_column = block // 64, (block // 8) % 8, block % 8
    is_out = matrix == 3
    side = jnp.where(is_out, block_row // 4, block_column // 4)
    code = jnp.where(side == core, 2 * is_out + block_column % 2, 4)
    near_slots, far_slots = collect(
        grad_projection,
        grad_mix,
        jnp.where(is_out, block_row % 4, block_row),
        jnp.where(is_out, block_column // 2, matrix * 2 + (block_column % 4) // 2),
        code.astype(jnp.int32),
    )
    slot_sums = low_sum(near_slots, swap(far_slots, "c")).astype(bf16)
    slot_sums = slot_sums.reshape(4, 1, 4, 4 * BLK, 2 * BLK)

    partial_one = dot_back(grad_joined, projection)
    partial_time = jnp.dot(
        grad_time_pair, projection[:, half:].astype(f32).T, precision=BEST_PRECISION
    )
    grad_input_one = on_both(partial_one)
    grad_input_time = partial_time + swap(partial_time, "c")
    grad_residual, gain_one = layer_back(grad_input_one, normed_one, inverse_one, gain_values[0])
    grad_residual = (grad_residual + grad_after_self).astype(bf16)
    grad_embeds, gain_time = layer_back(
        grad_input_time, normed_time, inverse_time, gain_values[0]
    )
    grad_in_weight = tdot(grad_residual, noised)
    grad_table = features.astype(f32).reshape(NTIME, 1) * grad_embeds
    grad_gains = jnp.stack([gain_one + gain_time, gain_two, gain_three], 0)

    def own_rows(values):
        return pick(values.reshape((4, 2, 4) + values.shape[1:]), core, 1)

    small = jnp.concatenate(
        [
            own_rows(grad_table.reshape(32, 8, D)),
            jnp.pad(
                own_rows(grad_gains.reshape(3, 32, 48).transpose(1, 0, 2).reshape(32, 1, 144)),
                ((0, 0), (0, 0), (0, 7), (0, D - 144)),
            ),
        ],
        2,
    )
    grad_ends = own_rows(
        jnp.concatenate([grad_in_weight, grad_out_weight], 1).astype(bf16).reshape(32, 48, 2 * DIN)
    )
    rest_arrays = (
        ("one", (4 * BLK, 2 * BLK)),
        ("cols", (48, half)),
        ("one", (48, D)),
        ("cols", (16, 1152)),
        ("cols", (16, 1152)),
        ("one", (16, D)),
        ("one", (48, 2 * DIN)),
    )
    rest_groups = [((3, 0, whole, whole), (4, 1, whole, whole))]
    rest_groups += [
        ((1, 0, whole, pl.ds(step * 384, 384)), (2, 1, whole, pl.ds(step * 768, 768)))
        for step in range(2)
    ]
    rest_groups += [
        ((0, 0, pl.ds(step * 96, 96), whole), (0, 1, pl.ds(384 + step * 96, 96), whole))
        for step in range(4)
    ]
    rest_groups += [((5, 0, whole, whole), (6, 1, whole, whole))]
    rest_sums = reduce_gradients(
        rest_arrays,
        rest_groups,
        (
            slot_sums,
            grad_query_weight,
            out_rows,
            kv_sources[0],
            kv_sources[1],
            small.astype(bf16).reshape(4, 1, 4, 16, D),
            grad_ends.reshape(4, 1, 4, 48, 2 * DIN),
        ),
        2,
    )
    slot_rows, query_mine, query_other, grad_cross_out, *kv_sums, small, grad_ends = (
        value.astype(f32) for value in rest_sums
    )
    slot_rows = slot_rows.reshape(4, BLK, 2 * BLK)
    grad_slots = jnp.stack([slot_rows[:, :, :BLK], slot_rows[:, :, BLK:]], 1).reshape(8, BLK, BLK)
    grad_cross_query = jnp.where(
        core == 0,
        jnp.concatenate([query_mine, query_other], 1),
        jnp.concatenate([query_other, query_mine], 1),
    )
    grad_cross = jnp.stack([grad_cross_query, grad_cross_out], 1)
    kv_columns = []
    for mine, other in (kv_sums[:2], kv_sums[2:]):
        mine, other = mine.reshape(24, half), other.reshape(24, half)
        kv_columns.append(jnp.where(core == 0, mine, other))
        kv_columns.append(jnp.where(core == 0, other, mine))
    grad_key_value = jnp.concatenate(kv_columns, 1)
    grad_ends = grad_ends.reshape(48, 2, DIN)
    grad_table = small[:8]
    grad_gains = small[8, :144].reshape(3, 48).T

    reduced = (
        grad_ends,
        grad_table,
        grad_slots,
        grad_cross,
        grad_key_value,
        grad_gate_up,
        grad_down,
        grad_gains,
    )
    square_sum = jnp.zeros((), f32)
    for member in reduced:
        square_sum = square_sum + jnp.sum(member * member)
    loss_part = jnp.where(
        core == 0,
        jnp.sum(errors * errors) * mse_scale + contrast_own * (CONTRAST_WEIGHT / items_total),
        0.0,
    )
    loss_total, norm_square = all_sum(loss_part, square_sum)
    return finish(
        loss_total,
        jnp.sqrt(norm_square),
        reduced,
        (
            end_weights,
            time_table,
            square_slots,
            cross_weights,
            key_value,
            gate_up,
            down_weight,
            norm_gains,
        ),
        (
            first_ends,
            first_table,
            None,
            first_cross,
            first_key_value,
            first_gate_up,
            first_down,
            first_gains,
        ),
        (
            second_ends,
            second_table,
            None,
            second_cross,
            second_key_value,
            second_gate_up,
            second_down,
            second_gains,
        ),
        (left_stats, right_stats, left_roots, right_roots),
    )


def all_sum(*values):
    total = jnp.pad(jnp.stack(values)[None], ((0, 7), (0, 128 - len(values))))
    total = jnp.sum(share(total + swap(total, "c"), 4), 0)
    return total[0, 0], total[0, 1]


def finish(loss_total, gradient_norm, reduced, masters, firsts, seconds, statistics):
    factor = CLIP_NORM / jnp.maximum(gradient_norm, CLIP_NORM)
    results = [loss_total, gradient_norm]
    for index_value in (0, 1, 3, 4, 5, 6, 7):
        results.extend(
            adam_update(
                masters[index_value],
                firsts[index_value],
                seconds[index_value],
                factor * reduced[index_value],
                ADAM_RATES[index_value],
            )
        )
    slot_norm = jnp.sqrt(jnp.sum(reduced[2] * reduced[2]))
    slot_factor = CLIP_NORM / jnp.maximum(slot_norm, CLIP_NORM)
    left_new, right_new, slots_new = shampoo_update(
        masters[2], slot_factor * reduced[2], factor / slot_factor, *statistics
    )
    results.extend([factor * reduced[2], left_new, right_new, slots_new])
    return tuple(results)


def solution(mesh):
    lines = mesh.shape["text"]
    chips = mesh.devices.size // 2
    if mesh.shape["dp"] == 8 and lines == 4 and 2 * mesh.shape["dp"] == chips:
        mesh = Mesh(mesh.devices.reshape(2, 2, 2, lines), ("y", "x", "c", "z"))
        dp, text, body = ("y", "x", "c"), ("z",), item_per_chip
    else:
        dp, text, body = ("dp",), ("text",), shards
    own = dp + text
    in_specs = (
        P(dp, text, None),
        P(dp, text, None),
        P(dp),
        P(dp, text, None),
        P(dp),
        P(dp, None),
        P(),
    ) + (P(own),) * 26
    out_specs = (P(), P()) + (P(own),) * 25
    return jax.shard_map(body, mesh=mesh, in_specs=in_specs, out_specs=out_specs, check_vma=False)
```

```python
from functools import partial
import math

import jax
import jax.numpy as jnp
from jax import lax
from jax.experimental import pallas as pl
from jax.experimental.pallas import tpu as pltpu
from jax.sharding import Mesh, PartitionSpec as P

D = 1536
HEADS = 24
HD = 64
FF = 6144
DIN = 64
DT = 768
FRAMES = 1024
NTIME = 256
STEP = 10
BLK = 192


BEST_PRECISION = lax.Precision.HIGHEST
NORM_EPS = 1e-05
POOL_EPS = 1e-06
SCORE_SCALE = 0.125
CONTRAST_TEMP = 0.02
CONTRAST_WEIGHT = 0.1
CLIP_NORM = 0.005
BETA_FIRST = 0.9
BETA_SECOND = 0.999
ADAM_EPS = 1e-08
WEIGHT_DECAY = 0.01
ADAM_RATES = (0.02, 0.05, 0.0, 0.1, 0.02, 0.02, 0.02, 1.0)
STAT_DECAY = 0.999
SHAMPOO_RATE = 0.01
MASK_VALUE = -1000000000.0


def layer_stats(inputs):
    center = inputs - jnp.mean(inputs, -1, keepdims=True)
    inverse = lax.rsqrt(jnp.mean(center * center, -1, keepdims=True) + NORM_EPS)
    return (center * inverse, inverse)


def layer_back(grad_out, normed, inverse, gain_row):
    scaled = grad_out * gain_row
    grad_in = inverse * (
        scaled
        - jnp.mean(scaled, -1, keepdims=True)
        - normed * jnp.mean(scaled * normed, -1, keepdims=True)
    )
    return (grad_in, jnp.sum(grad_out * normed, 0))


def time_features(timesteps):
    halfway = NTIME // 2
    frequency = jnp.exp(jnp.arange(halfway, dtype=jnp.float32) * (math.log(64.0) / halfway))
    moment = (timesteps.astype(jnp.float32) + 0.5) / NTIME
    phase = 2.0 * math.pi * moment[:, None] * frequency[None, :]
    return jnp.concatenate([jnp.cos(phase), jnp.sin(phase)], 1)


def rope_tables(positions_count, offset):
    halfway = HD // 2
    frequency = jnp.exp(jnp.arange(halfway, dtype=jnp.float32) * (-2.0 * math.log(10000.0) / HD))
    positions = (jnp.arange(positions_count, dtype=jnp.int32) + offset).astype(jnp.float32)
    angles = positions[:, None] * frequency[None, :]
    return (jnp.concatenate([jnp.cos(angles)] * 2, -1), jnp.concatenate([jnp.sin(angles)] * 2, -1))


def rotate(values, cosine_table, sine_table):
    halfway = HD // 2
    turned = jnp.concatenate([-values[..., halfway:], values[..., :halfway]], -1)
    return values * cosine_table[:, None, :] + turned * sine_table[:, None, :]


def rotate_back(gradient, cosine_table, sine_table):
    halfway = HD // 2
    product = gradient * sine_table[:, None, :]
    return gradient * cosine_table[:, None, :] + jnp.concatenate(
        [product[..., halfway:], -product[..., :halfway]], -1
    )


def to_matrices(blocks):
    per_side = D // BLK
    return blocks.reshape(4, per_side, per_side, BLK, BLK).transpose(0, 1, 3, 2, 4).reshape(4, D, D)


def to_blocks(matrices):
    per_side = D // BLK
    return (
        matrices.reshape(4, per_side, BLK, per_side, BLK)
        .transpose(0, 1, 3, 2, 4)
        .reshape(4 * per_side * per_side, BLK, BLK)
    )


def normalize(vectors):
    return vectors * lax.rsqrt(jnp.sum(vectors * vectors, -1, keepdims=True) + POOL_EPS)


def contrast_loss(pooled_audio, pooled_text, negatives):
    audio_unit_vectors = normalize(pooled_audio)
    text_unit_vectors = normalize(pooled_text)
    positive_pairs = jnp.sum(audio_unit_vectors * text_unit_vectors, -1) / CONTRAST_TEMP
    negative_pairs = (
        jnp.einsum(
            "ux,uax->ua", audio_unit_vectors, text_unit_vectors[negatives], precision=BEST_PRECISION
        )
        / CONTRAST_TEMP
    )
    scores = jnp.concatenate([positive_pairs[:, None], negative_pairs], 1)
    peak_score = jnp.max(scores, -1, keepdims=True)
    logsum = peak_score[:, 0] + jnp.log(jnp.sum(jnp.exp(scores - peak_score), -1))
    return jnp.sum(logsum - positive_pairs)


def item_scores(one_query, one_key, one_bias):
    scores = jnp.einsum("fhd,khd->hfk", one_query, one_key, preferred_element_type=jnp.float32)
    return scores * SCORE_SCALE + one_bias


def attend_forward(queries, all_keys, values, key_bias):

    def single(pieces):
        one_query, one_key, one_value, one_bias = pieces
        scores = item_scores(one_query, one_key, one_bias)
        peak_score = jnp.max(scores, -1, keepdims=True)
        weights = jnp.exp(scores - peak_score)
        row_total = jnp.sum(weights, -1, keepdims=True)
        mixture = jnp.einsum(
            "hfk,khd->fhd",
            (weights / row_total).astype(jnp.bfloat16),
            one_value,
            preferred_element_type=jnp.float32,
        )
        return (mixture.astype(jnp.bfloat16), peak_score + jnp.log(row_total))

    return lax.map(single, (queries, all_keys, values, key_bias))


def attend_backward(queries, all_keys, values, key_bias, logsums, grad_mixture):

    def single(pieces):
        one_query, one_key, one_value, one_bias, one_logsum, grad_rows = pieces
        attention = jnp.exp(item_scores(one_query, one_key, one_bias) - one_logsum)
        grad_attention = jnp.einsum(
            "fhd,khd->hfk", grad_rows, one_value, preferred_element_type=jnp.float32
        )
        grad_value = jnp.einsum(
            "hfk,fhd->khd",
            attention.astype(jnp.bfloat16),
            grad_rows,
            preferred_element_type=jnp.float32,
        )
        grad_scores = attention * (
            grad_attention - jnp.sum(attention * grad_attention, -1, keepdims=True)
        )
        grad_scores = grad_scores.astype(jnp.bfloat16)
        grad_query = (
            jnp.einsum("hfk,khd->fhd", grad_scores, one_key, preferred_element_type=jnp.float32)
            * SCORE_SCALE
        )
        grad_key = (
            jnp.einsum("hfk,fhd->khd", grad_scores, one_query, preferred_element_type=jnp.float32)
            * SCORE_SCALE
        )
        return (grad_query, grad_key, grad_value)

    return lax.map(single, (queries, all_keys, values, key_bias, logsums, grad_mixture))


def feed_forward(rows_in, gate_matrix, down_matrix):
    width = down_matrix.shape[0]
    gate_values = jnp.dot(rows_in, gate_matrix, preferred_element_type=jnp.float32)
    gate_part = gate_values[:, :width]
    up_part = gate_values[:, width:]
    sigmoid = jax.nn.sigmoid(gate_part)
    silu_value = gate_part * sigmoid
    hidden = (silu_value * up_part).astype(jnp.bfloat16)
    partial_out = jnp.dot(hidden, down_matrix, preferred_element_type=jnp.float32)
    return (partial_out, (hidden, gate_part, up_part, sigmoid, silu_value))


def feed_back(rows_in, gate_matrix, down_matrix, kept, grad_low):
    hidden, gate_part, up_part, sigmoid, silu_value = kept
    grad_down = jnp.einsum("rf,rd->fd", hidden, grad_low, preferred_element_type=jnp.float32)
    grad_hidden = jnp.einsum("rd,fd->rf", grad_low, down_matrix, preferred_element_type=jnp.float32)
    grad_gate = grad_hidden * up_part * sigmoid * (1.0 + gate_part * (1.0 - sigmoid))
    grad_pair = jnp.concatenate([grad_gate, grad_hidden * silu_value], 1).astype(jnp.bfloat16)
    grad_gate_up = jnp.einsum("rd,rg->dg", rows_in, grad_pair, preferred_element_type=jnp.float32)
    grad_rows = jnp.einsum("rg,dg->rd", grad_pair, gate_matrix, preferred_element_type=jnp.float32)
    return (grad_rows, grad_gate_up, grad_down)


def adam_update(weight, first_moment, second_moment, gradient, rate):
    first_moment = BETA_FIRST * first_moment + (1.0 - BETA_FIRST) * gradient
    second_moment = BETA_SECOND * second_moment + (1.0 - BETA_SECOND) * gradient * gradient
    corrected = first_moment / (1.0 - BETA_FIRST**STEP)
    scaled = second_moment / (1.0 - BETA_SECOND**STEP)
    weight = weight - rate * (corrected / (jnp.sqrt(scaled) + ADAM_EPS) + WEIGHT_DECAY * weight)
    return (first_moment, second_moment, weight)


def shampoo_update(slots_now, gradient, left_stat, right_stat, left_root, right_root):
    left_stat = STAT_DECAY * left_stat + (1.0 - STAT_DECAY) * jnp.einsum(
        "sij,skj->sik", gradient, gradient, precision=BEST_PRECISION
    )
    right_stat = STAT_DECAY * right_stat + (1.0 - STAT_DECAY) * jnp.einsum(
        "sji,sjk->sik", gradient, gradient, precision=BEST_PRECISION
    )
    inner = jnp.einsum("sij,sjk->sik", gradient, right_root, precision=BEST_PRECISION)
    direction = jnp.einsum("sij,sjk->sik", left_root, inner, precision=BEST_PRECISION)
    return (
        left_stat,
        right_stat,
        slots_now - SHAMPOO_RATE * (direction + WEIGHT_DECAY * slots_now),
    )


def shards(
    latents,
    noise_field,
    timesteps,
    text_tokens,
    text_lengths,
    negatives,
    assignment,
    end_weights,
    time_table,
    square_slots,
    cross_weights,
    key_value,
    gate_up,
    down_weight,
    norm_gains,
    first_ends,
    second_ends,
    first_table,
    second_table,
    first_cross,
    second_cross,
    first_key_value,
    second_key_value,
    first_gate_up,
    second_gate_up,
    first_down,
    second_down,
    first_gains,
    second_gains,
    left_stats,
    right_stats,
    left_roots,
    right_roots,
):
    text_index = lax.axis_index("text")
    group_index = lax.axis_index("dp")
    group_count = lax.axis_size("dp")
    text_count_axis = lax.axis_size("text")
    piece_width = FF // (group_count * text_count_axis)
    low_ends = end_weights.astype(jnp.bfloat16)
    low_table = time_table.astype(jnp.bfloat16)
    low_slots = square_slots.astype(jnp.bfloat16)
    low_cross = cross_weights.astype(jnp.bfloat16)
    low_pairs = key_value.astype(jnp.bfloat16)
    low_gains = norm_gains.astype(jnp.bfloat16)
    low_gate = gate_up.astype(jnp.bfloat16)
    low_down = down_weight.astype(jnp.bfloat16)
    group_set = (
        lax.all_gather(low_ends, "text", axis=0, tiled=True),
        lax.all_gather(low_table, "text", axis=0, tiled=True),
        lax.all_gather(low_slots, "text", axis=0, tiled=True),
        lax.all_gather(low_cross, "text", axis=0, tiled=True),
        lax.all_gather(low_pairs, "text", axis=0, tiled=True),
        lax.all_gather(low_gains, "text", axis=0, tiled=True),
        lax.all_gather(low_gate, "text", axis=0, tiled=True),
    )
    gate_group = group_set[6].reshape(
        group_set[6].shape[0], 2, group_count, text_count_axis, piece_width
    )
    gate_columns = lax.dynamic_index_in_dim(gate_group, text_index, 3, keepdims=False)
    full_set = (
        lax.all_gather(group_set[0], "dp", axis=0, tiled=True),
        lax.all_gather(group_set[1], "dp", axis=0, tiled=True),
        lax.all_gather(group_set[2], "dp", axis=0, tiled=True),
        lax.all_gather(group_set[3], "dp", axis=0, tiled=True),
        lax.all_gather(group_set[4], "dp", axis=0, tiled=True),
        lax.all_gather(group_set[5], "dp", axis=0, tiled=True),
        lax.all_gather(gate_columns, "dp", axis=0, tiled=True),
        lax.all_gather(low_down, "dp", axis=0, tiled=True),
    )
    ends_full, table_full, slots_full, cross_full, pairs_full, gains_full = full_set[:6]
    gate_full = full_set[6].reshape(D, 2 * group_count * piece_width)
    down_full = full_set[7]
    item_count = latents.shape[0]
    frames_dev = latents.shape[1]
    tokens_dev = text_tokens.shape[1]
    row_count = item_count * frames_dev
    items_total = item_count * group_count
    mse_scale = 1.0 / (items_total * FRAMES * DIN)
    weight_in = ends_full[:, 0, :]
    weight_out = ends_full[:, 1, :]
    gain_values = gains_full.astype(jnp.float32)
    inverse_order = (
        jnp.zeros_like(assignment)
        .at[assignment]
        .set(jnp.arange(assignment.shape[0], dtype=jnp.int32))
    )
    squares = to_matrices(slots_full[inverse_order])
    projection = jnp.concatenate([squares[0], squares[1], squares[2]], 1)
    cosine_table, sine_table = rope_tables(frames_dev, 1 + text_index * frames_dev)
    angles = (timesteps.astype(jnp.float32) + 0.5) * (0.5 * math.pi / NTIME)
    signal = jnp.cos(angles)[:, None, None]
    spread = jnp.sin(angles)[:, None, None]
    noised = (signal * latents + spread * noise_field).astype(jnp.bfloat16).reshape(row_count, DIN)
    residual = jnp.einsum("rc,dc->rd", noised, weight_in, preferred_element_type=jnp.float32)
    normed_one, inverse_one = layer_stats(residual)
    input_one = (normed_one * gain_values[:, 0]).astype(jnp.bfloat16)
    features = time_features(timesteps).astype(jnp.bfloat16)
    embeds = jnp.dot(features, table_full, preferred_element_type=jnp.float32)
    normed_time, inverse_time = layer_stats(embeds)
    input_time = (normed_time * gain_values[:, 0]).astype(jnp.bfloat16)
    joined_rows = jnp.dot(input_one, projection, preferred_element_type=jnp.float32)
    head_shape = (item_count, frames_dev, HEADS, HD)
    rot_queries = rotate(joined_rows[:, :D].reshape(head_shape), cosine_table, sine_table).astype(
        jnp.bfloat16
    )
    rot_keys = rotate(
        joined_rows[:, D : 2 * D].reshape(head_shape), cosine_table, sine_table
    ).astype(jnp.bfloat16)
    value_rows = joined_rows[:, 2 * D :].astype(jnp.bfloat16).reshape(item_count, frames_dev, D)
    time_pair = jnp.dot(input_time, projection[:, D:], preferred_element_type=jnp.float32).astype(
        jnp.bfloat16
    )
    keys_all, values_all = (
        lax.all_gather(rot_keys.reshape(item_count, frames_dev, D), "text", axis=1, tiled=True),
        lax.all_gather(value_rows, "text", axis=1, tiled=True),
    )
    key_count = keys_all.shape[1] + 1
    all_keys = jnp.concatenate([time_pair[:, None, :D], keys_all], 1).reshape(
        item_count, key_count, HEADS, HD
    )
    all_values = jnp.concatenate([time_pair[:, None, D:], values_all], 1).reshape(
        item_count, key_count, HEADS, HD
    )
    self_bias = jnp.zeros((item_count, key_count), jnp.float32)
    mixed_self, logsum_self = attend_forward(rot_queries, all_keys, all_values, self_bias)
    mixed_flat = mixed_self.reshape(row_count, D)
    after_self = residual + jnp.dot(mixed_flat, squares[3], preferred_element_type=jnp.float32)
    normed_two, inverse_two = layer_stats(after_self)
    input_two = (normed_two * gain_values[:, 1]).astype(jnp.bfloat16)
    cross_queries = jnp.dot(
        input_two, cross_full[:, 0, :], preferred_element_type=jnp.float32
    ).astype(jnp.bfloat16)
    cross_heads = cross_queries.reshape(head_shape)
    projected = jnp.dot(
        text_tokens.reshape(item_count * tokens_dev, DT),
        pairs_full,
        preferred_element_type=jnp.float32,
    )
    projected = projected.astype(jnp.bfloat16).reshape(item_count, tokens_dev, 2 * D)
    text_all = lax.all_gather(projected, "text", axis=1, tiled=True)
    text_count = text_all.shape[1]
    valid_keys = jnp.arange(text_count, dtype=jnp.int32)[None, :] < text_lengths[:, None]
    cross_bias = jnp.where(valid_keys, 0.0, MASK_VALUE).astype(jnp.float32)
    text_keys = text_all[:, :, :D].reshape(item_count, text_count, HEADS, HD)
    text_values = text_all[:, :, D:].reshape(item_count, text_count, HEADS, HD)
    mixed_cross, logsum_cross = attend_forward(cross_heads, text_keys, text_values, cross_bias)
    cross_flat = mixed_cross.reshape(row_count, D)
    after_cross = after_self + jnp.dot(
        cross_flat, cross_full[:, 1, :], preferred_element_type=jnp.float32
    )
    normed_three, inverse_three = layer_stats(after_cross)
    input_three = (normed_three * gain_values[:, 2]).astype(jnp.bfloat16)
    feed_rows = lax.all_gather(
        input_three.reshape(item_count, frames_dev, D), "text", axis=1, tiled=True
    ).reshape(-1, D)
    feed_out, feed_kept = feed_forward(feed_rows, gate_full, down_full)
    down_out = (
        lax.psum_scatter(
            feed_out.reshape(item_count, -1, D).astype(jnp.bfloat16),
            "text",
            scatter_dimension=1,
            tiled=True,
        )
        .astype(jnp.float32)
        .reshape(row_count, D)
    )
    output_rows = after_cross + down_out
    output_low = output_rows.astype(jnp.bfloat16)
    predicted = jnp.dot(output_low, weight_out, preferred_element_type=jnp.float32).reshape(
        latents.shape
    )
    errors = predicted - (signal * noise_field - spread * latents)
    lengths_float = text_lengths.astype(jnp.float32)
    own_valid = (text_index * tokens_dev + jnp.arange(tokens_dev, dtype=jnp.int32))[
        None, :
    ] < text_lengths[:, None]
    own_mask = own_valid.astype(jnp.float32)
    audio_part = jnp.sum(output_rows.reshape(item_count, frames_dev, D), 1)
    text_part = (
        jnp.sum(projected[:, :, :D].astype(jnp.float32) * own_mask[:, :, None], 1)
        / lengths_float[:, None]
    )
    pooled_set = (
        lax.all_gather(audio_part, ("dp", "text"), axis=0, tiled=True),
        lax.all_gather(text_part, ("dp", "text"), axis=0, tiled=True),
        lax.all_gather(negatives.astype(jnp.float32), ("dp", "text"), axis=0, tiled=True),
    )
    audio_pooled = (
        jnp.sum(pooled_set[0].reshape(group_count, text_count_axis, item_count, D), 1).reshape(
            -1, D
        )
        / FRAMES
    )
    text_pooled = jnp.sum(
        pooled_set[1].reshape(group_count, text_count_axis, item_count, D), 1
    ).reshape(-1, D)
    negative_rows = pooled_set[2].reshape(group_count, text_count_axis, item_count, -1)[:, 0]
    negative_rows = negative_rows.reshape(items_total, -1).astype(jnp.int32)
    contrast_value, contrast_back = jax.vjp(
        partial(contrast_loss, negatives=negative_rows), audio_pooled, text_pooled
    )
    grad_audio_all, grad_text_all = contrast_back(jnp.float32(CONTRAST_WEIGHT / items_total))
    grad_audio = lax.dynamic_slice_in_dim(grad_audio_all, group_index * item_count, item_count, 0)
    grad_text = lax.dynamic_slice_in_dim(grad_text_all, group_index * item_count, item_count, 0)
    grad_predicted = (2.0 * mse_scale * errors).astype(jnp.bfloat16).reshape(row_count, DIN)
    grad_out_weight = jnp.einsum(
        "rd,rc->dc", output_low, grad_predicted, preferred_element_type=jnp.float32
    )
    grad_output = jnp.einsum(
        "rc,dc->rd", grad_predicted, weight_out, preferred_element_type=jnp.float32
    )
    grad_output = (
        grad_output.reshape(item_count, frames_dev, D) + grad_audio[:, None, :] / FRAMES
    ).reshape(row_count, D)
    grad_down_in = grad_output.astype(jnp.bfloat16)
    grad_feed_rows = lax.all_gather(
        grad_down_in.reshape(item_count, frames_dev, D), "text", axis=1, tiled=True
    ).reshape(-1, D)
    grad_feed_in, grad_gate_up, grad_down = feed_back(
        feed_rows, gate_full, down_full, feed_kept, grad_feed_rows
    )
    grad_input_three = (
        lax.psum_scatter(
            grad_feed_in.reshape(item_count, -1, D).astype(jnp.bfloat16),
            "text",
            scatter_dimension=1,
            tiled=True,
        )
        .astype(jnp.float32)
        .reshape(row_count, D)
    )
    grad_after_cross, gain_three = layer_back(
        grad_input_three, normed_three, inverse_three, gain_values[:, 2]
    )
    grad_after_cross = grad_after_cross + grad_output
    grad_cross_in = grad_after_cross.astype(jnp.bfloat16)
    grad_cross_out = jnp.einsum(
        "rd,re->de", cross_flat, grad_cross_in, preferred_element_type=jnp.float32
    )
    grad_mixed_cross = jnp.einsum(
        "re,de->rd", grad_cross_in, cross_full[:, 1, :], preferred_element_type=jnp.float32
    )
    grad_mixed_cross = grad_mixed_cross.astype(jnp.bfloat16).reshape(head_shape)
    grad_cq, grad_text_keys, grad_text_values = attend_backward(
        cross_heads, text_keys, text_values, cross_bias, logsum_cross, grad_mixed_cross
    )
    grad_cq_low = grad_cq.reshape(row_count, D).astype(jnp.bfloat16)
    grad_cross_query = jnp.einsum(
        "rd,re->de", input_two, grad_cq_low, preferred_element_type=jnp.float32
    )
    grad_input_two = jnp.einsum(
        "re,de->rd", grad_cq_low, cross_full[:, 0, :], preferred_element_type=jnp.float32
    )
    grad_pairs = jnp.concatenate(
        [
            grad_text_keys.reshape(item_count, text_count, D),
            grad_text_values.reshape(item_count, text_count, D),
        ],
        2,
    )
    grad_own_pairs = lax.psum_scatter(
        grad_pairs.astype(jnp.bfloat16), "text", scatter_dimension=1, tiled=True
    ).astype(jnp.float32)
    pooled_grad = own_mask[:, :, None] * (grad_text[:, None, :] / lengths_float[:, None, None])
    grad_own_pairs = grad_own_pairs + jnp.concatenate([pooled_grad, jnp.zeros_like(pooled_grad)], 2)
    grad_own_pairs = grad_own_pairs.astype(jnp.bfloat16).reshape(item_count * tokens_dev, 2 * D)
    grad_textside = jnp.einsum(
        "tc,tk->ck",
        text_tokens.reshape(item_count * tokens_dev, DT),
        grad_own_pairs,
        preferred_element_type=jnp.float32,
    )
    grad_after_self, gain_two = layer_back(
        grad_input_two, normed_two, inverse_two, gain_values[:, 1]
    )
    grad_after_self = grad_after_self + grad_after_cross
    grad_self_in = grad_after_self.astype(jnp.bfloat16)
    grad_attn_out = jnp.einsum(
        "rd,re->de", mixed_flat, grad_self_in, preferred_element_type=jnp.float32
    )
    grad_mixed_self = jnp.einsum(
        "re,de->rd", grad_self_in, squares[3], preferred_element_type=jnp.float32
    )
    grad_mixed_self = grad_mixed_self.astype(jnp.bfloat16).reshape(head_shape)
    grad_rot_queries, grad_keys, value_gradients = attend_backward(
        rot_queries, all_keys, all_values, self_bias, logsum_self, grad_mixed_self
    )
    grad_keys_own, grad_values_own = (
        lax.psum_scatter(
            grad_keys[:, 1:].reshape(item_count, key_count - 1, D).astype(jnp.bfloat16),
            "text",
            scatter_dimension=1,
            tiled=True,
        ).astype(jnp.float32),
        lax.psum_scatter(
            value_gradients[:, 1:].reshape(item_count, key_count - 1, D).astype(jnp.bfloat16),
            "text",
            scatter_dimension=1,
            tiled=True,
        ).astype(jnp.float32),
    )
    grad_queries = (
        rotate_back(grad_rot_queries, cosine_table, sine_table)
        .astype(jnp.bfloat16)
        .reshape(row_count, D)
    )
    grad_key_rows = rotate_back(grad_keys_own.reshape(head_shape), cosine_table, sine_table)
    grad_key_rows = grad_key_rows.astype(jnp.bfloat16).reshape(row_count, D)
    grad_joined = jnp.concatenate(
        [grad_queries, grad_key_rows, grad_values_own.astype(jnp.bfloat16).reshape(row_count, D)], 1
    )
    grad_projection = jnp.einsum(
        "rd,rk->dk", input_one, grad_joined, preferred_element_type=jnp.float32
    )
    grad_input_one = jnp.einsum(
        "rk,dk->rd", grad_joined, projection, preferred_element_type=jnp.float32
    )
    grad_time_pair = jnp.concatenate(
        [grad_keys[:, 0].reshape(item_count, D), value_gradients[:, 0].reshape(item_count, D)], 1
    )
    time_rows = jnp.dot(input_time.astype(jnp.float32).T, grad_time_pair, precision=BEST_PRECISION)
    grad_projection = grad_projection + jnp.concatenate(
        [jnp.zeros((D, D), jnp.float32), time_rows], 1
    )
    grad_input_time = jnp.einsum(
        "ik,dk->id", grad_time_pair, projection[:, D:].astype(jnp.float32), precision=BEST_PRECISION
    )
    grad_residual, gain_one = layer_back(grad_input_one, normed_one, inverse_one, gain_values[:, 0])
    grad_residual = (grad_residual + grad_after_self).astype(jnp.bfloat16)
    grad_embeds, gain_time = layer_back(
        grad_input_time, normed_time, inverse_time, gain_values[:, 0]
    )
    grad_in_weight = jnp.einsum(
        "rd,rc->dc", grad_residual, noised, preferred_element_type=jnp.float32
    )
    grad_table = jnp.dot(features.astype(jnp.float32).T, grad_embeds, precision=BEST_PRECISION)
    grad_gains = jnp.stack([gain_one + gain_time, gain_two, gain_three], 1)
    grad_ends = jnp.stack([grad_in_weight, grad_out_weight], 1)
    grad_cross = jnp.stack([grad_cross_query, grad_cross_out], 1)
    grad_squares = jnp.stack(
        [
            grad_projection[:, :D],
            grad_projection[:, D : 2 * D],
            grad_projection[:, 2 * D :],
            grad_attn_out,
        ],
        0,
    )
    grad_slots = jnp.take(to_blocks(grad_squares), assignment, axis=0)
    gate_pieces = grad_gate_up.reshape(D, 2, group_count, piece_width)
    group_grads = (
        lax.psum_scatter(
            grad_ends.astype(jnp.bfloat16), "dp", scatter_dimension=0, tiled=True
        ).astype(jnp.float32),
        lax.psum_scatter(
            grad_table.astype(jnp.bfloat16), "dp", scatter_dimension=0, tiled=True
        ).astype(jnp.float32),
        lax.psum_scatter(
            grad_slots.astype(jnp.bfloat16), "dp", scatter_dimension=0, tiled=True
        ).astype(jnp.float32),
        lax.psum_scatter(
            grad_cross.astype(jnp.bfloat16), "dp", scatter_dimension=0, tiled=True
        ).astype(jnp.float32),
        lax.psum_scatter(
            grad_textside.astype(jnp.bfloat16), "dp", scatter_dimension=0, tiled=True
        ).astype(jnp.float32),
        lax.psum_scatter(
            grad_gains.astype(jnp.bfloat16), "dp", scatter_dimension=0, tiled=True
        ).astype(jnp.float32),
        lax.psum_scatter(
            gate_pieces.astype(jnp.bfloat16), "dp", scatter_dimension=0, tiled=True
        ).astype(jnp.float32),
        lax.psum_scatter(
            grad_down.astype(jnp.bfloat16), "dp", scatter_dimension=0, tiled=True
        ).astype(jnp.float32),
    )
    placing = (jnp.arange(text_count_axis, dtype=jnp.int32) == text_index).astype(jnp.float32)
    spread_gate = group_grads[6][:, :, :, None, :] * placing[None, None, None, :, None]
    spread_gate = spread_gate.reshape(spread_gate.shape[0], 2 * FF)
    owned = (
        lax.psum_scatter(
            group_grads[0].astype(jnp.bfloat16), "text", scatter_dimension=0, tiled=True
        ).astype(jnp.float32),
        lax.psum_scatter(
            group_grads[1].astype(jnp.bfloat16), "text", scatter_dimension=0, tiled=True
        ).astype(jnp.float32),
        lax.psum_scatter(
            group_grads[2].astype(jnp.bfloat16), "text", scatter_dimension=0, tiled=True
        ).astype(jnp.float32),
        lax.psum_scatter(
            group_grads[3].astype(jnp.bfloat16), "text", scatter_dimension=0, tiled=True
        ).astype(jnp.float32),
        lax.psum_scatter(
            group_grads[4].astype(jnp.bfloat16), "text", scatter_dimension=0, tiled=True
        ).astype(jnp.float32),
        lax.psum_scatter(
            group_grads[5].astype(jnp.bfloat16), "text", scatter_dimension=0, tiled=True
        ).astype(jnp.float32),
        lax.psum_scatter(
            spread_gate.astype(jnp.bfloat16), "text", scatter_dimension=0, tiled=True
        ).astype(jnp.float32),
    )
    reduced = (owned[0], owned[1], owned[2], owned[3], owned[4], owned[6], group_grads[7], owned[5])
    square_sum = jnp.zeros((), jnp.float32)
    for member in reduced:
        square_sum = square_sum + jnp.sum(member * member)
    loss_part = jnp.sum(errors * errors) * mse_scale
    totals = lax.psum((square_sum, loss_part), ("dp", "text"))
    loss_total = totals[1] + CONTRAST_WEIGHT * contrast_value / items_total
    gradient_norm = jnp.sqrt(totals[0])
    masters = (
        end_weights,
        time_table,
        square_slots,
        cross_weights,
        key_value,
        gate_up,
        down_weight,
        norm_gains,
    )
    firsts = (
        first_ends,
        first_table,
        None,
        first_cross,
        first_key_value,
        first_gate_up,
        first_down,
        first_gains,
    )
    seconds = (
        second_ends,
        second_table,
        None,
        second_cross,
        second_key_value,
        second_gate_up,
        second_down,
        second_gains,
    )
    return finish(
        loss_total,
        gradient_norm,
        reduced,
        masters,
        firsts,
        seconds,
        (left_stats, right_stats, left_roots, right_roots),
    )


def swap(values, axis, bit=1):
    return lax.ppermute(values, axis, [(i, i ^ bit) for i in range(lax.axis_size(axis))])


def pick(values, position, axis=0):
    return lax.dynamic_index_in_dim(values, position, axis, keepdims=False)


def low_sum(*terms):
    total = terms[0].astype(jnp.float32)
    for term in terms[1:]:
        total = total + term.astype(jnp.float32)
    return total


def on_both(partial_sum):
    low = partial_sum.astype(jnp.bfloat16)
    return low_sum(low, swap(low, "c"))


def tdot(left, right):
    return lax.dot_general(left, right, (((0,), (0,)), ((), ())), preferred_element_type=jnp.float32)


def dot_back(left, right):
    return lax.dot_general(left, right, (((1,), (1,)), ((), ())), preferred_element_type=jnp.float32)


MESH_ID = pl.DeviceIdType.MESH
JOIN_TILE = 512


def anywhere(count):
    return [pl.BlockSpec(memory_space=pl.ANY)] * count


def coordinates():
    return tuple(lax.axis_index(axis) for axis in ("y", "x", "c", "z"))


def chip_peers(me):
    row, column, core, line = me
    beside = {
        "c": (row, column, 1 - core, line),
        "x": (row, 1 - column, core, line),
        "y": (1 - row, column, core, line),
    }
    for offset in (1, 2, 3):
        beside[offset] = (row, column, core, line ^ offset)
    return beside


def greet(peers):
    barrier = pltpu.get_barrier_semaphore()
    for peer in peers.values():
        pl.semaphore_signal(barrier, inc=1, device_id=peer, device_id_type=MESH_ID)
    pl.semaphore_wait(barrier, len(peers))


def send(source, target, send_sem, recv_sem, peer):
    return pltpu.make_async_remote_copy(
        src_ref=source,
        dst_ref=target,
        send_sem=send_sem,
        recv_sem=recv_sem,
        device_id=peer,
        device_id_type=MESH_ID,
    )


def gather_kernel(arrays, groups, *refs):
    count = len(arrays)
    inputs = sum(2 if kind == "cols" else 1 for kind, _, _ in arrays)
    sources = list(refs[:inputs])
    send_sem, recv_sem, core_send, core_recv, local_sem, *item_sems = refs[inputs + 4 + count :]
    item_refs = refs[inputs : inputs + 2] + refs[inputs + 2 + count : inputs + 4 + count]
    bufs = refs[inputs + 2 : inputs + 2 + count]
    me = coordinates()
    row, column, core, line = me
    plane = 2 * row + column
    peers = chip_peers(me)
    others = {offset + 4: (row, column, 1 - core, line ^ offset) for offset in (1, 2, 3)}
    greet({**peers, **others})
    finish_items = move_items(me, item_refs, item_sems)
    local, cross = [], []
    for index_value, (kind, _, _) in enumerate(arrays):
        spot = bufs[index_value].at[plane, 0 if kind == "one" else core, line]
        copy = pltpu.make_async_copy(sources.pop(0), spot, local_sem.at[index_value])
        copy.start()
        local.append(copy)
        cross.append(None)
        if kind == "cols":
            cross[-1] = send(
                sources.pop(0),
                spot,
                core_send.at[index_value],
                core_recv.at[index_value],
                peers["c"],
            )
            cross[-1].start()
    whole = slice(None)
    flat = [unit for group in groups for unit in group]
    ready = set()

    def move(number, slot, planes, lines, peer):
        array, _, rows, columns = flat[number]
        cores = {"cols": whole, "one": 0}.get(arrays[array][0], core)
        view = bufs[array].at[planes, cores, lines, rows, columns]
        return send(view, view, send_sem.at[number, slot], recv_sem.at[number, slot], peer)

    def line_copies(number):
        return [move(number, o - 1, plane, line, peers[o]) for o in (1, 2, 3)]

    def near_copy(number):
        axis = "y" if flat[number][1] else "x"
        return move(number, 3, plane, whole, peers[axis])

    def side_copy(number):
        axis = "x" if flat[number][1] else "y"
        return move(number, 4, plane, whole, peers[axis])

    def far_copy(number):
        color = flat[number][1]
        return move(number, 5, plane ^ (2 if color else 1), whole, peers["x" if color else "y"])

    def core_copy(number):
        array, _, rows, columns = flat[number]
        kind = arrays[array][0]
        if kind not in ("both", "half"):
            return None
        planes = whole if kind == "both" else pl.ds(2 * (1 - core), 2)
        view = bufs[array].at[planes, core, whole, rows, columns]
        return send(view, view, send_sem.at[number, 6], recv_sem.at[number, 6], peers["c"])

    def start_line(number):
        array = flat[number][0]
        if array not in ready:
            ready.add(array)
            local[array].wait()
            if cross[array] is not None:
                cross[array].wait()
        for copy in line_copies(number):
            copy.start()

    def start_near(number):
        for copy in line_copies(number):
            copy.wait_recv()
        near_copy(number).start()
        side_copy(number).start()

    def start_far(number):
        near_copy(number).wait_recv()
        far_copy(number).start()

    def close(number):
        side_copy(number).wait_recv()
        far_copy(number).wait_recv()
        last = core_copy(number)
        if last is not None:
            last.start()
        for copy in line_copies(number) + [near_copy(number), side_copy(number), far_copy(number)]:
            copy.wait_send()

    stages = (start_line, start_near, start_far, close)
    numbers, at = [], 0
    for group in groups:
        numbers.append(range(at, at + len(group)))
        at += len(group)
    for step in range(len(groups) + 3):
        for lag, stage in enumerate(stages):
            if 0 <= step - lag < len(groups):
                for number in numbers[step - lag]:
                    stage(number)
    for number in range(len(flat)):
        last = core_copy(number)
        if last is not None:
            last.wait()
    finish_items()


def move_items(me, refs, sems):
    row, column, core, line = me
    send_sem, recv_sem, local_sem = sems

    def outgoing(kind, inner, side):
        return send(
            refs[kind].at[inner],
            refs[2 + kind].at[line],
            send_sem.at[kind, inner, side],
            recv_sem.at[kind, line],
            (row, column, side, 2 * core + inner),
        )

    def kept(kind, inner):
        return pltpu.make_async_copy(
            refs[kind].at[inner], refs[2 + kind].at[line], local_sem.at[kind]
        )

    def incoming(kind, origin):
        return send(
            refs[kind].at[0],
            refs[2 + kind].at[origin],
            send_sem.at[kind, 0, 0],
            recv_sem.at[kind, origin],
            (row, column, 1 - core, line),
        )

    def each_target(act, keep):
        for kind in range(2):
            for inner in range(2):
                for side in range(2):
                    own = (2 * core + inner == line) & (core == side)

                    @pl.when(own)
                    def stay():
                        keep(kind, inner)

                    @pl.when(jnp.logical_not(own))
                    def leave():
                        act(kind, inner, side)

    each_target(
        lambda kind, inner, side: outgoing(kind, inner, side).start(),
        lambda kind, inner: kept(kind, inner).start(),
    )

    def finish_items():
        each_target(
            lambda kind, inner, side: outgoing(kind, inner, side).wait_send(),
            lambda kind, inner: kept(kind, inner).wait(),
        )
        for kind in range(2):
            for origin in range(4):

                @pl.when(jnp.logical_not((line == origin) & (core == line // 2)))
                def arrive():
                    incoming(kind, origin).wait_recv()

    return finish_items


def gather_weights(arrays, groups, sources, items, collective_id):
    units = sum(len(group) for group in groups)
    dma = pltpu.SemaphoreType.DMA
    return pl.pallas_call(
        partial(gather_kernel, arrays, groups),
        out_shape=[
            jax.ShapeDtypeStruct((4, 1 if kind == "one" else 2, 4) + shape, dtype)
            for kind, shape, dtype in arrays
        ]
        + [jax.ShapeDtypeStruct((4,) + item.shape[1:], item.dtype) for item in items],
        in_specs=anywhere(len(sources) + 2),
        out_specs=anywhere(len(arrays) + 2),
        scratch_shapes=[
            dma((units, 7)),
            dma((units, 7)),
            dma((len(arrays),)),
            dma((len(arrays),)),
            dma((len(arrays),)),
            dma((2, 2, 2)),
            dma((2, 4)),
            dma((2,)),
        ],
        compiler_params=pltpu.CompilerParams(collective_id=collective_id, has_side_effects=True),
    )(*sources, *items)


def share_kernel(values, shared, send_sem, recv_sem):
    row, column, core, line = coordinates()
    own = 8 * row + 4 * column + line

    def peer(offset):
        return (row ^ (offset // 8), column ^ (offset // 4 % 2), core, line ^ (offset % 4))

    greet({offset: peer(offset) for offset in range(1, 16)})
    copies = [
        send(
            values, shared.at[own], send_sem.at[offset], recv_sem.at[offset], peer(offset)
        )
        for offset in range(1, 16)
    ]
    for copy in copies:
        copy.start()
    shared[own] = values[...]
    for copy in copies:
        copy.wait()


def share(values, collective_id):
    dma = pltpu.SemaphoreType.DMA
    return pl.pallas_call(
        share_kernel,
        out_shape=jax.ShapeDtypeStruct((16,) + values.shape, values.dtype),
        in_specs=[pl.BlockSpec(memory_space=pltpu.VMEM)],
        out_specs=pl.BlockSpec(memory_space=pltpu.VMEM),
        scratch_shapes=[dma((16,)), dma((16,))],
        compiler_params=pltpu.CompilerParams(collective_id=collective_id, has_side_effects=True),
    )(values)


def total_kernel(count, loss, *refs):
    pieces, result = refs[:count], refs[count]
    own_part, core_part, shared, send_sem, recv_sem = refs[count + 1 :]
    row, column, core, line = coordinates()
    own = 8 * row + 4 * column + line

    def peer(offset):
        return (row ^ (offset // 8), column ^ (offset // 4 % 2), core, line ^ (offset % 4))

    peers = {offset: peer(offset) for offset in range(1, 16)}
    peers[0] = (row, column, 1 - core, line)
    greet(peers)
    squares = jnp.zeros((1, 1), jnp.float32)
    for piece in pieces:
        value = piece[...].astype(jnp.float32)
        value = jnp.sum(value * value, 0, keepdims=True)
        squares = squares + jnp.sum(value, 1, keepdims=True)
    lane = lax.broadcasted_iota(jnp.int32, (8, 128), 1)
    own_part[...] = jnp.where(lane == 0, loss[0:1, 0:1], jnp.where(lane == 1, squares, 0.0))
    across = send(own_part, core_part, send_sem.at[0], recv_sem.at[0], peers[0])
    across.start()
    across.wait()
    own_part[...] = own_part[...] + core_part[...]
    copies = [
        send(own_part, shared.at[own], send_sem.at[offset], recv_sem.at[offset], peers[offset])
        for offset in range(1, 16)
    ]
    for copy in copies:
        copy.start()
    shared[own] = own_part[...]
    for copy in copies:
        copy.wait()
    total = shared[0]
    for index_value in range(1, 16):
        total = total + shared[index_value]
    result[...] = total


def total_squares(loss, pieces, collective_id):
    vmem, dma = pltpu.VMEM, pltpu.SemaphoreType.DMA
    tile = (8, 128)
    return pl.pallas_call(
        partial(total_kernel, len(pieces)),
        out_shape=jax.ShapeDtypeStruct(tile, jnp.float32),
        in_specs=[pl.BlockSpec(memory_space=vmem)] * (len(pieces) + 1),
        out_specs=pl.BlockSpec(memory_space=vmem),
        scratch_shapes=[
            vmem(tile, jnp.float32),
            vmem(tile, jnp.float32),
            vmem((16,) + tile, jnp.float32),
            dma((16,)),
            dma((16,)),
        ],
        compiler_params=pltpu.CompilerParams(
            collective_id=collective_id, has_side_effects=True, vmem_limit_bytes=48 * 2**20
        ),
    )(jnp.broadcast_to(loss, tile), *pieces)


def exact_dot(left, right, dims):
    return lax.dot_general(
        left,
        right,
        (dims, ((), ())),
        precision=BEST_PRECISION,
        preferred_element_type=jnp.float32,
    )


def shampoo_kernel(factor, pair, slots, left, right, left_root, right_root, *outs):
    clipped, new_left, new_right, new_slots = outs
    both = pair[0].astype(jnp.float32) * factor[0, 0]
    for side in range(2):
        grad = (pltpu.roll(both, BLK, 1) if side else both)[:, :BLK]
        clipped[side] = grad
        new_left[side] = STAT_DECAY * left[side] + (1.0 - STAT_DECAY) * exact_dot(
            grad, grad, ((1,), (1,))
        )
        new_right[side] = STAT_DECAY * right[side] + (1.0 - STAT_DECAY) * exact_dot(
            grad, grad, ((0,), (0,))
        )
        inner = exact_dot(grad, right_root[side], ((1,), (0,)))
        direction = exact_dot(left_root[side], inner, ((1,), (0,)))
        new_slots[side] = slots[side] - SHAMPOO_RATE * (direction + WEIGHT_DECAY * slots[side])


def shampoo_pairs(factor, pairs, slots, *statistics):
    steps = pairs.shape[0]
    block = pl.BlockSpec((2, BLK, BLK), lambda step: (step, 0, 0))
    return pl.pallas_call(
        shampoo_kernel,
        grid=(steps,),
        in_specs=[
            pl.BlockSpec(memory_space=pltpu.SMEM),
            pl.BlockSpec((1, BLK, 2 * BLK), lambda step: (step, 0, 0)),
        ]
        + [block] * 5,
        out_specs=[block] * 4,
        out_shape=[jax.ShapeDtypeStruct(slots.shape, jnp.float32)] * 4,
        cost_estimate=pl.CostEstimate(
            flops=96 * steps * BLK**3, bytes_accessed=40 * slots.size, transcendentals=0
        ),
    )(factor.reshape(1, 1), pairs, slots, *statistics)


NORM_ROWS = 128


def norm_back_kernel(mine, other, normed, inverse, gain, rest, *outs):
    grad_low, gain_out = outs[-2:]
    total = mine[...].astype(jnp.float32) + other[...].astype(jnp.float32)
    row = normed[...]

    @pl.when(pl.program_id(0) == 0)
    def clear():
        gain_out[...] = jnp.zeros_like(gain_out)

    gain_out[0:1, :] += jnp.sum(total * row, 0, keepdims=True)
    scaled = total * gain[0:1, :]
    grad = scaled - jnp.mean(scaled, -1, keepdims=True)
    grad = inverse[...] * (grad - row * jnp.mean(scaled * row, -1, keepdims=True))
    grad = grad + rest[...]
    grad_low[...] = grad.astype(grad_low.dtype)
    if len(outs) == 3:
        outs[0][...] = grad


def norm_back(partial_sum, normed, inverse, gain, rest, keep):
    low = partial_sum.astype(jnp.bfloat16)
    rows, width = rest.shape

    def block(columns):
        return pl.BlockSpec((NORM_ROWS, columns), lambda step: (step, 0))

    fixed = pl.BlockSpec((8, width), lambda step: (0, 0))
    wide = [jax.ShapeDtypeStruct((rows, width), jnp.float32)] if keep else []
    outs = pl.pallas_call(
        norm_back_kernel,
        grid=(rows // NORM_ROWS,),
        in_specs=[block(width)] * 3 + [block(1), fixed, block(width)],
        out_specs=[block(width)] * (len(wide) + 1) + [fixed],
        out_shape=wide
        + [
            jax.ShapeDtypeStruct((rows, width), jnp.bfloat16),
            jax.ShapeDtypeStruct((8, width), jnp.float32),
        ],
        cost_estimate=pl.CostEstimate(
            flops=16 * rows * width, bytes_accessed=18 * rows * width, transcendentals=0
        ),
    )(low, swap(low, "c"), normed, inverse, jnp.broadcast_to(gain, (8, width)), rest)
    return (*outs[:-1], outs[-1][0])


FEED_TILE = 256
UP_LOW = 768
FEED_ROWS = 512


def chunks(size, body):
    for start in range(0, size, FEED_ROWS):
        body(pl.ds(start, FEED_ROWS))


def feed_kernel(rows, gate_tile, up_tile, gate, up, hidden):
    def body(at):
        gate_part = jnp.dot(rows[at, :], gate_tile[...], preferred_element_type=jnp.float32)
        up_part = jnp.dot(rows[at, :], up_tile[...], preferred_element_type=jnp.float32)
        gate[at, :] = gate_part.astype(gate.dtype)
        up[at, :] = up_part.astype(up.dtype)
        hidden[at, :] = (gate_part * jax.nn.sigmoid(gate_part) * up_part).astype(hidden.dtype)

    chunks(rows.shape[0], body)


def hidden_back_kernel(grad, down_tile, gate, up, hidden, grad_gate, grad_up, grad_down):
    def body(at):
        back = dot_back(grad[at, :], down_tile[...])
        gate_part = gate[at, :].astype(jnp.float32)
        sigmoid = jax.nn.sigmoid(gate_part)
        grad_gate[at, :] = (
            back * up[at, :].astype(jnp.float32) * sigmoid * (1.0 + gate_part * (1.0 - sigmoid))
        ).astype(grad_gate.dtype)
        grad_up[at, :] = (back * gate_part * sigmoid).astype(grad_up.dtype)

    chunks(grad.shape[0], body)

    def weight(at):
        grad_down[:, at] = tdot(hidden[...], grad[:, at]).astype(grad_down.dtype)

    chunks(grad.shape[1], weight)


def rows_back_kernel(
    turned_rows, grad_gate, grad_up, gate_tile, up_tile, gate_out, up_low, up_high, rows_out, total
):
    @pl.when(pl.program_id(0) == 0)
    def clear():
        total[...] = jnp.zeros_like(total)

    is_low = pl.program_id(0) < UP_LOW // FEED_TILE

    def body(at):
        gate_out[at, :] = jnp.dot(
            turned_rows[at, :], grad_gate[...], preferred_element_type=jnp.float32
        ).astype(gate_out.dtype)
        up_part = jnp.dot(
            turned_rows[at, :], grad_up[...], preferred_element_type=jnp.float32
        ).astype(up_low.dtype)

        @pl.when(is_low)
        def store_low():
            up_low[at, :] = up_part

        @pl.when(jnp.logical_not(is_low))
        def store_high():
            up_high[at, :] = up_part

        total[:, at] += dot_back(grad_gate[...], gate_tile[at, :]) + dot_back(
            grad_up[...], up_tile[at, :]
        )

    chunks(turned_rows.shape[0], body)

    @pl.when(pl.program_id(0) == pl.num_programs(0) - 1)
    def store():
        rows_out[...] = total[...].astype(rows_out.dtype)


def feed_call(kernel, operands, outputs, flops, scratch=()):
    units = FF // 2

    def spec(shape, kind):
        height, width = shape
        if kind == "columns":
            return pl.BlockSpec((height, FEED_TILE), lambda step: (0, step))
        if kind == "rows":
            return pl.BlockSpec((FEED_TILE, width), lambda step: (step, 0))
        if kind == "low":
            last = width // FEED_TILE - 1
            return pl.BlockSpec((height, FEED_TILE), lambda step: (0, jnp.minimum(step, last)))
        if kind == "high":
            first = (units - width) // FEED_TILE
            return pl.BlockSpec(
                (height, FEED_TILE), lambda step: (0, jnp.maximum(step - first, 0))
            )
        return pl.BlockSpec(shape, lambda step: (0, 0))

    low = jnp.bfloat16
    moved = sum(value.size for value, _ in operands) + sum(h * w for (h, w), _ in outputs)
    return pl.pallas_call(
        kernel,
        grid=(units // FEED_TILE,),
        in_specs=[spec(value.shape, kind) for value, kind in operands],
        out_specs=[spec(shape, kind) for shape, kind in outputs],
        out_shape=[jax.ShapeDtypeStruct(shape, low) for shape, _ in outputs],
        scratch_shapes=list(scratch),
        compiler_params=pltpu.CompilerParams(vmem_limit_bytes=56 * 2**20),
        cost_estimate=pl.CostEstimate(flops=flops, bytes_accessed=2 * moved, transcendentals=0),
    )(*[value for value, _ in operands])


def feed(rows, gate_weight, up_weight):
    shape = (rows.shape[0], FF // 2)
    return feed_call(
        feed_kernel,
        [(rows, "whole"), (gate_weight, "columns"), (up_weight, "columns")],
        [(shape, "columns")] * 3,
        4 * rows.size * (FF // 2),
    )


def hidden_back(grad, down, gate, up, hidden):
    shape = hidden.shape
    return feed_call(
        hidden_back_kernel,
        [
            (grad, "whole"),
            (down, "rows"),
            (gate, "columns"),
            (up, "columns"),
            (hidden, "columns"),
        ],
        [(shape, "columns"), (shape, "columns"), (down.shape, "rows")],
        4 * grad.size * (FF // 2),
    )


def rows_back(rows, grad_gate, grad_up, gate_weight, up_weight):
    return feed_call(
        rows_back_kernel,
        [
            (rows.T, "whole"),
            (grad_gate, "columns"),
            (grad_up, "columns"),
            (gate_weight, "columns"),
            (up_weight, "columns"),
        ],
        [
            (gate_weight.shape, "columns"),
            ((D, UP_LOW), "low"),
            ((D, FF // 2 - UP_LOW), "high"),
            (rows.shape, "whole"),
        ],
        8 * rows.size * (FF // 2),
        [pltpu.VMEM(rows.shape, jnp.float32)],
    )


def reduce_kernel(arrays, groups, *refs):
    count = len(arrays)
    flat = [unit for group in groups for unit in group]
    total = len(flat)
    sources = refs[:count]
    targets, scratch = refs[count : 2 * count], refs[2 * count :]
    sides, onwards, mines, from_ons, from_lines, from_cores = (
        scratch[index_value * total : (index_value + 1) * total] for index_value in range(6)
    )
    send_sem, recv_sem, load_sem = scratch[6 * total :]
    me = coordinates()
    row, column, core, line = me
    plane = 2 * row + column
    peers = chip_peers(me)
    greet(peers)
    whole = slice(None)

    def source(number, planes):
        array, _, rows, columns = flat[number]
        return sources[array].at[planes, whole, whole, rows, columns]

    def first_copy(number, slot):
        bit, axis = (1, "x") if flat[number][1] else (2, "y")
        return send(
            source(number, plane ^ (3 if slot else bit)),
            sides[number].at[slot],
            send_sem.at[number, slot],
            recv_sem.at[number, slot],
            peers[axis],
        )

    def load_onward(number):
        off = 2 if flat[number][1] else 1
        return pltpu.make_async_copy(
            source(number, plane ^ off), onwards[number], load_sem.at[number, 0]
        )

    def load_mine(number):
        return pltpu.make_async_copy(source(number, plane), mines[number], load_sem.at[number, 1])

    def onward_copy(number):
        axis = "y" if flat[number][1] else "x"
        return send(
            onwards[number],
            from_ons[number],
            send_sem.at[number, 2],
            recv_sem.at[number, 2],
            peers[axis],
        )

    def line_copies(number):
        return [
            send(
                mines[number].at[whole, line ^ offset],
                from_lines[number].at[offset - 1],
                send_sem.at[number, 2 + offset],
                recv_sem.at[number, 2 + offset],
                peers[offset],
            )
            for offset in (1, 2, 3)
        ]

    def core_copy(number):
        return send(
            mines[number].at[1 - core, line],
            from_cores[number],
            send_sem.at[number, 6],
            recv_sem.at[number, 6],
            peers["c"],
        )

    def side_columns(number, side):
        array, _, _, columns = flat[number]
        width = arrays[array][1][1]
        start = 0 if isinstance(columns, slice) else columns.start
        at = pl.multiple_of(side * width + start, 128)
        return pl.ds(at, extent(columns, width))

    def is_cols(number):
        return arrays[flat[number][0]][0] == "cols"

    def add_into(target, *terms):
        cores, lines, height, _ = target.shape

        def body(step, carry):
            side = step // (lines * (height // 16))
            rest = step % (lines * (height // 16))
            at_line = rest // (height // 16)
            rows = pl.ds(pl.multiple_of((rest % (height // 16)) * 16, 16), 16)
            value = target[side, at_line, rows].astype(jnp.float32)
            for term in terms:
                value = value + term[side, at_line, rows].astype(jnp.float32)
            target[side, at_line, rows] = value.astype(target.dtype)
            return carry

        lax.fori_loop(0, cores * lines * (height // 16), body, 0)

    def stage_one(number):
        first_copy(number, 1).start()
        first_copy(number, 0).start()
        load_onward(number).start()
        load_mine(number).start()

    def stage_two(number):
        first_copy(number, 1).wait_recv()
        load_onward(number).wait()
        add_into(onwards[number], sides[number].at[1])
        onward_copy(number).start()

    def stage_three(number):
        first_copy(number, 0).wait_recv()
        load_mine(number).wait()
        onward_copy(number).wait_recv()
        add_into(mines[number], sides[number].at[0], from_ons[number])
        for copy in line_copies(number):
            copy.start()

    def stage_four(number):
        for copy in line_copies(number):
            copy.wait_recv()
        array, _, rows, columns = flat[number]
        mine, pieces = mines[number], from_lines[number]
        for side in range(mine.shape[0]):
            value = mine[side, line].astype(jnp.float32)
            for offset in range(3):
                value = value + pieces[offset, side].astype(jnp.float32)
            mine[side, line] = value.astype(mine.dtype)
        if is_cols(number):
            core_copy(number).start()
            targets[array][rows, side_columns(number, core)] = mine[core, line]
        else:
            targets[array][rows, columns] = mine[0, line]

    def stage_five(number):
        if is_cols(number):
            core_copy(number).wait()
            array, _, rows, _ = flat[number]
            targets[array][rows, side_columns(number, 1 - core)] = from_cores[number][...]
        first_copy(number, 0).wait_send()
        first_copy(number, 1).wait_send()
        onward_copy(number).wait_send()
        for copy in line_copies(number):
            copy.wait_send()

    stages = (stage_one, stage_two, stage_three, stage_four, stage_five)
    numbers, at = [], 0
    for group in groups:
        numbers.append(range(at, at + len(group)))
        at += len(group)
    for step in range(len(groups) + 4):
        for lag, stage in enumerate(stages):
            if 0 <= step - lag < len(groups):
                for number in numbers[step - lag]:
                    stage(number)


def extent(sel, size):
    return size if isinstance(sel, slice) else sel.size


def reduce_gradients(arrays, groups, sources, collective_id):
    flat = [unit for group in groups for unit in group]
    vmem, dma, low = pltpu.VMEM, pltpu.SemaphoreType.DMA, jnp.bfloat16
    shapes = []
    for array, _, rows, columns in flat:
        kind, (height, width) = arrays[array]
        shapes.append((2 if kind == "cols" else 1, extent(rows, height), extent(columns, width)))
    scratch = [vmem((2, c, 4, h, w), low) for c, h, w in shapes]
    for _ in range(3):
        scratch += [vmem((c, 4, h, w), low) for c, h, w in shapes]
    scratch += [vmem((3, c, h, w), low) for c, h, w in shapes]
    scratch += [vmem((h, w) if c == 2 else (16, 128), low) for c, h, w in shapes]
    out_shape = [
        jax.ShapeDtypeStruct((height, width * (2 if kind == "cols" else 1)), low)
        for kind, (height, width) in arrays
    ]
    return pl.pallas_call(
        partial(reduce_kernel, arrays, groups),
        out_shape=out_shape,
        in_specs=anywhere(len(sources)),
        out_specs=[pl.BlockSpec(memory_space=pltpu.VMEM)] * len(out_shape),
        scratch_shapes=scratch
        + [dma((len(flat), 7)), dma((len(flat), 7)), dma((len(flat), 2))],
        compiler_params=pltpu.CompilerParams(
            collective_id=collective_id, has_side_effects=True, vmem_limit_bytes=60 * 2**20
        ),
    )(*sources)


def turned(values, cosine, sine):
    lane = lax.broadcasted_iota(jnp.int32, values.shape, 1)
    halfway = HD // 2
    partner = jnp.where(
        lane % HD < halfway,
        pltpu.roll(values, 128 - halfway, 1),
        pltpu.roll(values, halfway, 1),
    )
    return values * cosine + partner * sine


def join_kernel(rows, times, weights, cosine, sine, joined, joined_time):
    is_turned = pl.program_id(0) < 6

    def body(step, carry):
        at = pl.ds(pl.multiple_of(step * JOIN_TILE, JOIN_TILE), JOIN_TILE)
        values = jnp.dot(rows[at, :], weights[...], preferred_element_type=jnp.float32)

        @pl.when(is_turned)
        def turn():
            for side in (0, 128):
                joined[at, side : side + 128] = turned(
                    values[:, side : side + 128], cosine[at, :], sine[at, :]
                ).astype(joined.dtype)

        @pl.when(jnp.logical_not(is_turned))
        def keep():
            joined[at, :] = values.astype(joined.dtype)

        return carry

    lax.fori_loop(0, rows.shape[0] // JOIN_TILE, body, 0)
    joined_time[...] = jnp.dot(
        times[...], weights[...], preferred_element_type=jnp.float32
    ).astype(joined_time.dtype)


def join(rows, times, weights, cosine, sine):
    width = weights.shape[1]

    def fixed(array):
        return pl.BlockSpec(array.shape, lambda step: (0, 0))

    return pl.pallas_call(
        join_kernel,
        grid=(width // 256,),
        in_specs=[
            fixed(rows),
            fixed(times),
            pl.BlockSpec((D, 256), lambda step: (0, step)),
            fixed(cosine),
            fixed(sine),
        ],
        out_specs=[
            pl.BlockSpec((rows.shape[0], 256), lambda step: (0, step)),
            pl.BlockSpec((times.shape[0], 256), lambda step: (0, step)),
        ],
        out_shape=[
            jax.ShapeDtypeStruct((rows.shape[0], width), jnp.bfloat16),
            jax.ShapeDtypeStruct((times.shape[0], width), jnp.bfloat16),
        ],
        compiler_params=pltpu.CompilerParams(vmem_limit_bytes=48 * 2**20),
        cost_estimate=pl.CostEstimate(
            flops=2 * rows.shape[0] * D * width,
            bytes_accessed=2 * (rows.size + weights.size + rows.shape[0] * width),
            transcendentals=0,
        ),
    )(rows, times, weights, cosine, sine)


def head_lanes(shape, head):
    return lax.broadcasted_iota(jnp.int32, shape, 1) // HD == head


def attend_kernel(timed, queries, keys, values, first, second, mixed, logsum):
    tile = 256 if timed else 512

    def body(step, carry):
        at = pl.ds(pl.multiple_of(step * tile, tile), tile)
        rows = queries[at, :]
        total = jnp.zeros(rows.shape, jnp.float32)
        sums = jnp.zeros(rows.shape, jnp.float32)
        for head in range(2):
            own = head_lanes(rows.shape, head)
            query = jnp.where(own, rows, jnp.zeros_like(rows))
            scores = dot_back(query, keys[...]) * SCORE_SCALE
            if timed:
                extra = (
                    jnp.sum(
                        query.astype(jnp.float32) * first[0:1, :].astype(jnp.float32),
                        -1,
                        keepdims=True,
                    )
                    * SCORE_SCALE
                )
                peak = jnp.maximum(jnp.max(scores, -1, keepdims=True), extra)
            else:
                scores = scores + first[0:1, :]
                peak = jnp.max(scores, -1, keepdims=True)
            powers = jnp.exp(scores - peak)
            row_total = jnp.sum(powers, -1, keepdims=True)
            mixture = jnp.dot(
                powers.astype(jnp.bfloat16), values[...], preferred_element_type=jnp.float32
            )
            if timed:
                power = jnp.exp(extra - peak)
                row_total = row_total + power
                mixture = mixture + power * second[0:1, :].astype(jnp.float32)
            total = jnp.where(own, mixture / row_total, total)
            sums = jnp.where(own, peak + jnp.log(row_total), sums)
        mixed[at, :] = total.astype(mixed.dtype)
        logsum[at, :] = sums
        return carry

    lax.fori_loop(0, queries.shape[0] // tile, body, 0)


def lane_block(array, offset):
    return pl.BlockSpec((array.shape[0], 128), lambda pair: (0, pair + offset))


def attend(queries, keys, values, extras, offsets, timed):
    rows, count, pairs = queries.shape[0], keys.shape[0], HEADS // 4
    extra_specs = (
        [lane_block(extras[0], offsets[1]), lane_block(extras[1], offsets[2])]
        if timed
        else [pl.BlockSpec(extra.shape, lambda pair: (0, 0)) for extra in extras]
    )
    return pl.pallas_call(
        partial(attend_kernel, timed),
        grid=(pairs,),
        in_specs=[
            lane_block(queries, offsets[0]),
            lane_block(keys, offsets[1]),
            lane_block(values, offsets[2]),
        ]
        + extra_specs,
        out_specs=[pl.BlockSpec((rows, 128), lambda pair: (0, pair))] * 2,
        out_shape=[
            jax.ShapeDtypeStruct((rows, 128 * pairs), jnp.bfloat16),
            jax.ShapeDtypeStruct((rows, 128 * pairs), jnp.float32),
        ],
        compiler_params=pltpu.CompilerParams(vmem_limit_bytes=48 * 2**20),
        cost_estimate=pl.CostEstimate(
            flops=3 * pairs * 2 * rows * count * 128 * 4,
            bytes_accessed=pairs * 128 * (rows * 10 + count * 4),
            transcendentals=pairs * 2 * rows * count,
        ),
    )(queries, keys, values, *extras)


def attend_back_kernel(timed, *refs):
    queries, keys, values, first, second, mixed, logsum, gradient = refs[:8]
    if timed:
        cosine, sine, out_q, out_k, out_v, out_first, out_second, sum_k, sum_v = refs[8:]
    else:
        out_q, out_k, out_v, sum_k, sum_v = refs[8:]
    sum_k[...] = jnp.zeros_like(sum_k)
    sum_v[...] = jnp.zeros_like(sum_v)
    if timed:
        out_first[...] = jnp.zeros_like(out_first)
        out_second[...] = jnp.zeros_like(out_second)

    tile = 256 if timed else 512

    def body(step, carry):
        at = pl.ds(pl.multiple_of(step * tile, tile), tile)
        rows, grad = queries[at, :], gradient[at, :]
        product = grad.astype(jnp.float32) * mixed[at, :].astype(jnp.float32)
        sums = logsum[at, :]
        sums_row = sums.T
        grad_query = jnp.zeros(rows.shape, jnp.float32)
        for head in range(2):
            own = head_lanes(rows.shape, head)
            query = jnp.where(own, rows, jnp.zeros_like(rows))
            grad_own = jnp.where(own, grad, jnp.zeros_like(grad))
            inner = jnp.sum(jnp.where(own, product, 0.0), -1, keepdims=True)
            inner_row = jnp.broadcast_to(inner, rows.shape).T[0:1, :]
            scores = dot_back(keys[...], query) * SCORE_SCALE
            if not timed:
                scores = scores + second[:, 0:1]
            attention = jnp.exp(scores - sums_row[head * HD : head * HD + 1, :])
            grad_attention = dot_back(values[...], grad_own)
            sum_v[...] += jnp.dot(
                attention.astype(jnp.bfloat16), grad_own, preferred_element_type=jnp.float32
            )
            grad_scores = (attention * (grad_attention - inner_row)).astype(jnp.bfloat16)
            sum_k[...] += jnp.dot(grad_scores, query, preferred_element_type=jnp.float32)
            key_own = jnp.where(
                head_lanes(keys.shape, head), keys[...], jnp.zeros(keys.shape, keys.dtype)
            )
            grad_query = grad_query + tdot(grad_scores, key_own)
            if timed:
                key_time = jnp.where(
                    own[0:1, :], first[0:1, :].astype(jnp.float32), jnp.zeros((1, 128), jnp.float32)
                )
                wide_query, wide_grad = query.astype(jnp.float32), grad_own.astype(jnp.float32)
                score = jnp.sum(wide_query * key_time, -1, keepdims=True) * SCORE_SCALE
                power = jnp.exp(score - sums[:, head * HD : head * HD + 1])
                back = jnp.sum(
                    wide_grad * second[0:1, :].astype(jnp.float32), -1, keepdims=True
                )
                grad_score = (power * (back - inner)).astype(jnp.bfloat16).astype(jnp.float32)
                grad_query = grad_query + grad_score * key_time
                out_first[0:1, :] += SCORE_SCALE * jnp.sum(
                    grad_score * wide_query, 0, keepdims=True
                )
                out_second[0:1, :] += jnp.sum(
                    power.astype(jnp.bfloat16).astype(jnp.float32) * wide_grad, 0, keepdims=True
                )
        grad_query = grad_query * SCORE_SCALE
        if timed:
            grad_query = turned(grad_query, cosine[at, :], -sine[at, :])
        out_q[at, :] = grad_query.astype(out_q.dtype)
        return carry

    lax.fori_loop(0, queries.shape[0] // tile, body, 0)
    grad_key = sum_k[...] * SCORE_SCALE
    if timed:
        grad_key = turned(grad_key, cosine[...], -sine[...])
    out_k[...] = grad_key.astype(out_k.dtype)
    out_v[...] = sum_v[...].astype(out_v.dtype)


def attend_back(queries, keys, values, extras, offsets, mixed, logsum, gradient, tables):
    timed = tables is not None
    rows, count, pairs = queries.shape[0], keys.shape[0], HEADS // 4
    extra_specs = (
        [lane_block(extras[0], offsets[1]), lane_block(extras[1], offsets[2])]
        if timed
        else [pl.BlockSpec(extra.shape, lambda pair: (0, 0)) for extra in extras]
    )
    low = jnp.bfloat16 if timed else jnp.float32

    def out(height, dtype):
        return (
            jax.ShapeDtypeStruct((height, 128 * pairs), dtype),
            pl.BlockSpec((height, 128), lambda pair: (0, pair)),
        )

    outs = [out(rows, jnp.bfloat16), out(count, low), out(count, low)]
    operands = [queries, keys, values, *extras, mixed, logsum, gradient]
    specs = (
        [
            lane_block(queries, offsets[0]),
            lane_block(keys, offsets[1]),
            lane_block(values, offsets[2]),
        ]
        + extra_specs
        + [lane_block(mixed, 0), lane_block(logsum, 0), lane_block(gradient, 0)]
    )
    if timed:
        outs += [out(8, jnp.float32), out(8, jnp.float32)]
        operands += list(tables)
        specs += [pl.BlockSpec(table.shape, lambda pair: (0, 0)) for table in tables]
    return pl.pallas_call(
        partial(attend_back_kernel, timed),
        grid=(pairs,),
        in_specs=specs,
        out_specs=[spec for _, spec in outs],
        out_shape=[shape for shape, _ in outs],
        scratch_shapes=[pltpu.VMEM((count, 128), jnp.float32)] * 2,
        compiler_params=pltpu.CompilerParams(vmem_limit_bytes=48 * 2**20),
        cost_estimate=pl.CostEstimate(
            flops=3 * pairs * 2 * rows * count * 128 * 10,
            bytes_accessed=pairs * 128 * (rows * 16 + count * 8),
            transcendentals=pairs * 2 * rows * count,
        ),
    )(*operands)


def shifted(tile, is_shifted):
    wide = tile.astype(jnp.float32)
    return jnp.where(is_shifted, pltpu.roll(wide, BLK, 1), wide)


def assemble_kernel(joined_at, mix_at, pairs, joined, mix):
    step = pl.program_id(0)
    lane = lax.broadcasted_iota(jnp.int32, (BLK, 2 * BLK), 1)

    def fill(places, target, count):
        for pair in range(count):
            first = (step * count + pair) * 2
            left, right = places[first], places[first + 1]
            tile = jnp.where(
                lane < BLK,
                shifted(pairs[left // 2], left % 2 == 1),
                shifted(pairs[right // 2], right % 2 == 0),
            )
            target[:, pair * 2 * BLK : (pair + 1) * 2 * BLK] = tile.astype(target.dtype)

    fill(joined_at, joined, 6)
    fill(mix_at, mix, 2)


def assemble(pairs, joined_at, mix_at):
    half = D // 2
    return pl.pallas_call(
        assemble_kernel,
        grid_spec=pltpu.PrefetchScalarGridSpec(
            num_scalar_prefetch=2,
            grid=(8,),
            in_specs=[
                pl.BlockSpec(
                    pairs.shape, lambda step, *_: (0, 0, 0), pipeline_mode=pl.Buffered(1)
                )
            ],
            out_specs=[
                pl.BlockSpec((BLK, 3 * half), lambda step, *_: (step, 0)),
                pl.BlockSpec((BLK, half), lambda step, *_: (step // 2, step % 2)),
            ],
        ),
        out_shape=[
            jax.ShapeDtypeStruct((D, 3 * half), pairs.dtype),
            jax.ShapeDtypeStruct((half, D), pairs.dtype),
        ],
        compiler_params=pltpu.CompilerParams(vmem_limit_bytes=48 * 2**20),
        cost_estimate=pl.CostEstimate(
            flops=0, bytes_accessed=2 * pairs.size + 8 * half * D, transcendentals=0
        ),
    )(joined_at, mix_at, pairs)


SLOTS_STEP = 8


def collect_kernel(rows_at, columns_at, sides, joined, mix, near, far):
    step = pl.program_id(0)
    lane = lax.broadcasted_iota(jnp.int32, (BLK, 2 * BLK), 1)

    def fill(target):
        target[...] = jnp.zeros_like(target)
        for inner in range(SLOTS_STEP):
            slot, pair, right = step * SLOTS_STEP + inner, inner // 2, inner % 2
            code = sides[slot]
            rows = pl.ds(pl.multiple_of(rows_at[slot] * BLK, BLK), BLK)
            columns = pl.ds(pl.multiple_of(columns_at[slot] * 2 * BLK, 128), 2 * BLK)
            own = lane // BLK == right

            def put(source, is_shifted):
                tile = source[rows, columns]
                if is_shifted:
                    tile = pltpu.roll(tile.astype(jnp.float32), BLK, 1).astype(tile.dtype)
                target[pair] = jnp.where(own, tile, target[pair])

            for which, source in enumerate((joined, mix)):
                for side in range(2):
                    pl.when(code == 2 * which + side)(partial(put, source, side != right))

    near_steps = pl.num_programs(0) // 2
    pl.when(step < near_steps)(partial(fill, near))
    pl.when(step >= near_steps)(partial(fill, far))


def collect(joined, mix, rows_at, columns_at, sides):
    steps = sides.shape[0] // SLOTS_STEP
    block = (SLOTS_STEP // 2, BLK, 2 * BLK)

    def resident(array):
        return pl.BlockSpec(array.shape, lambda step, *_: (0, 0), pipeline_mode=pl.Buffered(1))

    return pl.pallas_call(
        collect_kernel,
        grid_spec=pltpu.PrefetchScalarGridSpec(
            num_scalar_prefetch=3,
            grid=(steps,),
            in_specs=[resident(joined), resident(mix)],
            out_specs=[
                pl.BlockSpec(block, lambda step, *_: (jnp.minimum(step, steps // 2 - 1), 0, 0)),
                pl.BlockSpec(block, lambda step, *_: (jnp.maximum(step - steps // 2, 0), 0, 0)),
            ],
        ),
        out_shape=[jax.ShapeDtypeStruct((sides.shape[0] // 4, BLK, 2 * BLK), joined.dtype)] * 2,
        compiler_params=pltpu.CompilerParams(vmem_limit_bytes=48 * 2**20),
        cost_estimate=pl.CostEstimate(
            flops=0,
            bytes_accessed=4 * (joined.size + mix.size) + 4 * sides.shape[0] * BLK * BLK,
            transcendentals=0,
        ),
    )(rows_at, columns_at, sides, joined, mix)


def item_per_chip(
    latents,
    noise_field,
    timesteps,
    text_tokens,
    text_lengths,
    negatives,
    assignment,
    end_weights,
    time_table,
    square_slots,
    cross_weights,
    key_value,
    gate_up,
    down_weight,
    norm_gains,
    first_ends,
    second_ends,
    first_table,
    second_table,
    first_cross,
    second_cross,
    first_key_value,
    second_key_value,
    first_gate_up,
    second_gate_up,
    first_down,
    second_down,
    first_gains,
    second_gains,
    left_stats,
    right_stats,
    left_roots,
    right_roots,
):
    bf16, f32 = jnp.bfloat16, jnp.float32
    row, column = lax.axis_index("y"), lax.axis_index("x")
    core, line = lax.axis_index("c"), lax.axis_index("z")
    plane = 2 * row + column
    item = 4 * plane + line
    quads = range(4)
    half = D // 2
    items_total = 16
    mse_scale = 1.0 / (items_total * FRAMES * DIN)

    meta = jnp.concatenate([timesteps, text_lengths, negatives.reshape(-1)])[None]
    pack = jnp.concatenate(
        [
            time_table,
            jnp.pad(norm_gains.T.reshape(1, 144), ((0, 0), (0, D - 144))),
            jnp.pad(meta.astype(f32), ((0, 6), (0, D - 34))),
        ],
        0,
    ).astype(bf16)
    low_ends = end_weights.reshape(48, 2 * DIN).astype(bf16)
    low_slots = square_slots.astype(bf16).reshape(4, 2, BLK, BLK)
    low_pairs = jnp.concatenate([low_slots[:, 0], low_slots[:, 1]], 2).reshape(4 * BLK, 2 * BLK)
    low_cross = cross_weights.astype(bf16)
    low_kv = key_value.astype(bf16)
    low_gate = gate_up.astype(bf16)
    low_down = down_weight.astype(bf16)

    def head_columns(array, which, side):
        return lax.dynamic_slice_in_dim(array, which * D + side * half, half, 1)

    def unit_columns(which, side):
        return jnp.concatenate(
            [
                lax.dynamic_slice_in_dim(
                    low_gate, which * FF + quadrant * 1536 + side * 768, 768, 1
                )
                for quadrant in quads
            ],
            1,
        )

    def kv_block(which, side):
        return head_columns(low_kv, which, side).reshape(16, 1152)

    def gathered(block):
        return lax.all_gather(block, ("y", "x", "z"), axis=0)

    feed_blocks = []
    for which in range(2):
        kept, received = unit_columns(which, core), swap(unit_columns(which, 1 - core), "c")
        feed_blocks.append(
            jnp.where(core == 0, jnp.stack([kept, received]), jnp.stack([received, kept]))
        )
    gate_weight, up_weight = (gathered(block).reshape(D, FF // 2) for block in feed_blocks)
    down = gathered(low_down).reshape(FF // 2, D)
    arrays = (
        ("both", (16, D), bf16),
        ("both", (4 * BLK, 2 * BLK), bf16),
        ("cols", (48, half), bf16),
        ("half", (48, D), bf16),
        ("cols", (16, 1152), bf16),
        ("cols", (16, 1152), bf16),
        ("both", (48, 2 * DIN), bf16),
    )
    whole = slice(None)
    groups = [((0, 0, whole, whole), (5, 1, whole, whole), (6, 1, whole, whole))]
    groups += [
        ((1, 0, pl.ds(step * 96, 96), whole), (1, 1, pl.ds(384 + step * 96, 96), whole))
        for step in range(4)
    ]
    groups += [
        ((2, 0, whole, pl.ds(step * 384, 384)), (3, 1, whole, pl.ds(step * 768, 768)))
        for step in range(2)
    ]
    groups += [((4, 0, whole, whole),)]
    (
        packs,
        all_pairs,
        cross_query,
        cross_out,
        keys_own,
        values_own,
        ends_full,
        frames,
        tokens,
    ) = gather_weights(
        arrays,
        groups,
        (
            pack,
            low_pairs,
            head_columns(low_cross[:, 0, :], 0, core),
            head_columns(low_cross[:, 0, :], 0, 1 - core),
            low_cross[:, 1, :],
            kv_block(0, core),
            kv_block(0, 1 - core),
            kv_block(1, core),
            kv_block(1, 1 - core),
            low_ends,
        ),
        (jnp.concatenate([latents, noise_field], 2), text_tokens),
        1,
    )
    packs = packs.reshape(32, 16, D)
    table_full = packs[:, :8].reshape(NTIME, D)
    gain_values = packs[:, 8, :144].reshape(32, 3, 48).transpose(1, 0, 2).reshape(3, D).astype(f32)
    ends_full = ends_full.reshape(D, 2 * DIN)
    weight_in, weight_out = ends_full[:, :DIN], ends_full[:, DIN:]
    all_pairs = all_pairs.reshape(128, BLK, 2 * BLK)
    inverse_order = (
        jnp.zeros_like(assignment)
        .at[assignment]
        .set(jnp.arange(assignment.shape[0], dtype=jnp.int32))
    )

    def grid_blocks(matrix, rows, columns):
        return (matrix * 64 + rows * 8 + columns).reshape(-1)

    eight, four = jnp.arange(8, dtype=jnp.int32), jnp.arange(4, dtype=jnp.int32)
    joined_blocks = grid_blocks(
        jnp.arange(3, dtype=jnp.int32)[None, :, None],
        eight[:, None, None],
        (4 * core + four)[None, None, :],
    )
    out_blocks = grid_blocks(3, (4 * core + four)[:, None], eight[None, :])
    projection, weight_mix = assemble(
        all_pairs, inverse_order[joined_blocks], inverse_order[out_blocks]
    )
    cross_query = cross_query.reshape(D, half)
    cross_out = lax.dynamic_slice_in_dim(cross_out.reshape(D, D), core * half, half, 0)
    kv_own = jnp.concatenate(
        [keys_own.reshape(DT, half), values_own.reshape(DT, half)], 1
    )

    metas = packs.reshape(8, 4, 16, D)[:, 0, 9, :34].astype(jnp.int32)
    timestep = pick(metas[:, :2].reshape(-1), item)
    text_length = pick(metas[:, 2:4].reshape(-1), item)
    negative_rows = metas[:, 4:].reshape(items_total, -1)
    frames = frames.reshape(FRAMES, 2 * DIN)
    clean, noise = frames[:, :DIN], frames[:, DIN:]
    tokens = tokens.reshape(-1, DT)
    frame_positions = jnp.arange(FRAMES, dtype=jnp.int32) + 1
    token_slots = jnp.arange(tokens.shape[0], dtype=jnp.int32)
    halfway = HD // 2
    frequency = jnp.exp(jnp.arange(halfway, dtype=f32) * (-2.0 * math.log(10000.0) / HD))
    turn = frame_positions.astype(f32)[:, None] * frequency[None, :]
    cosine_table = jnp.concatenate([jnp.cos(turn)] * 4, -1)
    sine_table = jnp.concatenate([-jnp.sin(turn), jnp.sin(turn)] * 2, -1)
    angle = (timestep.astype(f32) + 0.5) * (0.5 * math.pi / NTIME)
    signal, spread = jnp.cos(angle), jnp.sin(angle)
    noised = (signal * clean + spread * noise).astype(bf16)
    target = signal * noise - spread * clean

    residual = dot_back(noised, weight_in)
    normed_one, inverse_one = layer_stats(residual)
    input_one = (normed_one * gain_values[0]).astype(bf16)
    features = time_features(timestep[None]).astype(bf16)
    embeds = jnp.dot(features, table_full, preferred_element_type=f32)
    normed_time, inverse_time = layer_stats(embeds)
    input_time = (normed_time * gain_values[0]).astype(bf16)
    time_block = jnp.pad(input_time, ((0, 15), (0, 0)))
    joined, joined_time = join(input_one, time_block, projection, cosine_table, sine_table)
    pairs = half // 128
    self_offsets = (0, pairs, 2 * pairs)
    mixed_flat, logsum_self = attend(
        joined, joined, joined, (joined_time, joined_time), self_offsets, True
    )
    after_self = residual + on_both(jnp.dot(mixed_flat, weight_mix, preferred_element_type=f32))
    normed_two, inverse_two = layer_stats(after_self)
    input_two = (normed_two * gain_values[1]).astype(bf16)
    cross_queries = jnp.dot(input_two, cross_query, preferred_element_type=f32).astype(bf16)
    projected = jnp.dot(tokens, kv_own, preferred_element_type=f32).astype(bf16)
    valid = token_slots < text_length
    cross_bias = jnp.where(valid, 0.0, MASK_VALUE).astype(f32)[None]
    text_biases = (
        jnp.broadcast_to(cross_bias, (8, 128)),
        jnp.broadcast_to(cross_bias.T, (128, 128)),
    )
    cross_offsets = (0, 0, pairs)
    cross_flat, logsum_cross = attend(
        cross_queries, projected, projected, text_biases, cross_offsets, False
    )
    after_cross = after_self + on_both(jnp.dot(cross_flat, cross_out, preferred_element_type=f32))
    normed_three, inverse_three = layer_stats(after_cross)
    input_three = (normed_three * gain_values[2]).astype(bf16)
    feature = jnp.arange(D, dtype=jnp.int32)
    gathered_at = (feature // 384 * 4 + feature // 48 % 4) * 96 + feature // 192 % 2 * 48 + feature % 48
    reorder = (gathered_at[:, None] == feature[None, :]).astype(bf16)
    feed_rows = jnp.dot(input_three, reorder, preferred_element_type=f32).astype(bf16)
    gate_part, up_part, hidden = feed(feed_rows, gate_weight, up_weight)
    down_out = on_both(jnp.dot(hidden, down, preferred_element_type=f32))
    output_rows = after_cross + down_out
    output_low = output_rows.astype(bf16)
    predicted = jnp.dot(output_low, weight_out, preferred_element_type=f32)
    errors = predicted - target

    length_float = text_length.astype(f32)
    mask = valid.astype(f32)[:, None]
    text_half = jnp.sum(projected[:, :half].astype(f32) * mask, 0) / length_float
    text_rest = swap(text_half, "c")
    text_pool = jnp.where(
        core == 0,
        jnp.concatenate([text_half, text_rest]),
        jnp.concatenate([text_rest, text_half]),
    )
    pools = jnp.stack([jnp.sum(output_rows, 0) / FRAMES, text_pool], 0)
    pools = share(pools.reshape(8, D // 4), 3).reshape(items_total, 2, D)
    inverse_pools = lax.rsqrt(jnp.sum(pools * pools, -1, keepdims=True) + POOL_EPS)
    units = pools * inverse_pools
    audio_units, text_units = units[:, 0], units[:, 1]
    similar = (
        lax.dot_general(
            audio_units, text_units, (((1,), (1,)), ((), ())), precision=BEST_PRECISION
        )
        / CONTRAST_TEMP
    )
    same = jnp.eye(items_total, dtype=f32)
    counts = same + jnp.sum(
        (negative_rows[:, None, :] == jnp.arange(items_total, dtype=jnp.int32)[None, :, None]).astype(f32), -1
    )
    peak = jnp.max(jnp.where(counts > 0, similar, -jnp.inf), -1, keepdims=True)
    powers = jnp.where(counts > 0, counts * jnp.exp(similar - peak), 0.0)
    totals_row = jnp.sum(powers, -1, keepdims=True)
    contrast_own = pick(
        peak[:, 0] + jnp.log(totals_row[:, 0]) - jnp.sum(same * similar, -1), item
    )
    grad_similar = (powers / totals_row - same) * (
        CONTRAST_WEIGHT / items_total / CONTRAST_TEMP
    )
    grad_audio_unit = jnp.sum(pick(grad_similar, item)[:, None] * text_units, 0)
    grad_text_unit = jnp.sum(pick(grad_similar, item, 1)[:, None] * audio_units, 0)

    def unit_back(gradient, unit, inverse):
        return inverse * (gradient - unit * jnp.sum(unit * gradient))

    grad_audio = unit_back(grad_audio_unit, pick(audio_units, item), pick(inverse_pools, item)[0])
    grad_text = unit_back(grad_text_unit, pick(text_units, item), pick(inverse_pools, item)[1])

    grad_predicted = (2.0 * mse_scale * errors).astype(bf16)
    grad_out_weight = tdot(output_low, grad_predicted)
    grad_output = dot_back(grad_predicted, weight_out) + grad_audio[None, :] / FRAMES
    grad_low = grad_output.astype(bf16)
    grad_gate, grad_up, grad_down = hidden_back(grad_low, down, gate_part, up_part, hidden)
    grad_gate_weight, grad_up_low, grad_up_high, grad_feed_rows = rows_back(
        feed_rows, grad_gate, grad_up, gate_weight, up_weight
    )

    def over_plane(gradient, width):
        return lax.psum_scatter(
            gradient.reshape(4, 4, -1, width, gradient.shape[1]),
            ("y", "x"),
            scatter_dimension=0,
            tiled=True,
        )

    def over_line(total):
        return lax.psum_scatter(total, "z", scatter_dimension=1, tiled=True)[0, 0]

    down_total = over_plane(grad_down, 192)
    grad_after_cross, grad_cross_in, gain_three = norm_back(
        dot_back(grad_feed_rows, reorder),
        normed_three,
        inverse_three,
        gain_values[2],
        grad_output,
        True,
    )
    cross_rows = tdot(cross_flat, grad_cross_in).astype(bf16).reshape(2, 2, 192, D)
    cross_kept = pick(cross_rows, core, 1)
    cross_received = swap(pick(cross_rows, 1 - core, 1), "c")
    cross_pair = jnp.stack([cross_kept, cross_received], 0)
    out_rows = jnp.where(core == 0, cross_pair, cross_pair[::-1]).reshape(4, 1, 4, 48, D)
    grad_mixed_cross = dot_back(grad_cross_in, cross_out).astype(bf16)
    grad_cq, grad_text_keys, grad_text_values = attend_back(
        cross_queries,
        projected,
        projected,
        text_biases,
        cross_offsets,
        cross_flat,
        logsum_cross,
        grad_mixed_cross,
        None,
    )
    grad_query_weight = tdot(input_two, grad_cq).astype(bf16).reshape(4, 2, 4, 48, half)
    grad_input_two = on_both(dot_back(grad_cq, cross_query))
    text_half_grad = lax.dynamic_slice_in_dim(grad_text, core * half, half, 0)
    grad_pair_keys = (
        grad_text_keys + mask * (text_half_grad[None, :] / length_float)
    ).astype(bf16)
    kv_sources = [
        tdot(tokens, gradient.astype(bf16)).astype(bf16).reshape(4, 2, 4, 16, 1152)
        for gradient in (grad_pair_keys, grad_text_values)
    ]
    grad_after_self, gain_two = layer_back(
        grad_input_two, normed_two, inverse_two, gain_values[1]
    )
    grad_after_self = grad_after_self + grad_after_cross
    grad_self_in = grad_after_self.astype(bf16)
    grad_mix = tdot(mixed_flat, grad_self_in).astype(bf16)
    grad_mixed_self = dot_back(grad_self_in, weight_mix).astype(bf16)
    grad_queries, grad_keys, grad_values, grad_time_keys, grad_time_values = attend_back(
        joined,
        joined,
        joined,
        (joined_time, joined_time),
        self_offsets,
        mixed_flat,
        logsum_self,
        grad_mixed_self,
        (cosine_table, sine_table),
    )
    grad_gate_weight, down_total, _ = lax.optimization_barrier(
        (grad_gate_weight, down_total, grad_cross_in)
    )
    gate_total = over_plane(grad_gate_weight, 48)
    grad_up_high, gate_total, _ = lax.optimization_barrier(
        (grad_up_high, gate_total, grad_queries)
    )
    up_total = over_plane(grad_up_high, 48)
    gate_total, up_total = lax.optimization_barrier((gate_total, up_total))
    down_total, *gate_totals = [
        over_line(total) for total in (down_total, gate_total, up_total)
    ]
    feed_sums = [
        (pick(both_rows, core), swap(pick(both_rows, 1 - core), "c")) for both_rows in gate_totals
    ]
    grad_down_low = down_total[0]
    grad_joined = jnp.concatenate([grad_queries, grad_keys, grad_values], 1)
    grad_time_pair = jnp.concatenate([grad_time_keys[:1], grad_time_values[:1]], 1)
    time_row = jnp.concatenate([jnp.zeros((1, half), f32), grad_time_pair], 1)
    grad_projection = (
        tdot(input_one, grad_joined) + input_time.astype(f32).reshape(D, 1) * time_row
    ).astype(bf16)
    position = jnp.arange(256, dtype=jnp.int32)
    owner_core = core ^ (position // 128)
    block = assignment[
        (position // 32) % 4 * 64 + owner_core * 32 + (position // 8) % 4 * 8 + position % 8
    ]
    matrix, block_row, block_column = block // 64, (block // 8) % 8, block % 8
    is_out = matrix == 3
    side = jnp.where(is_out, block_row // 4, block_column // 4)
    code = jnp.where(side == core, 2 * is_out + block_column % 2, 4)
    near_slots, far_slots = collect(
        grad_projection,
        grad_mix,
        jnp.where(is_out, block_row % 4, block_row),
        jnp.where(is_out, block_column // 2, matrix * 2 + (block_column % 4) // 2),
        code.astype(jnp.int32),
    )
    slot_sums = low_sum(near_slots, swap(far_slots, "c")).astype(bf16)
    slot_sums, grad_down_low = lax.optimization_barrier((slot_sums, grad_down_low))
    slot_sums = slot_sums.reshape(4, 1, 4, 4 * BLK, 2 * BLK)

    partial_one = dot_back(grad_joined, projection)
    partial_time = jnp.dot(
        grad_time_pair, projection[:, half:].astype(f32).T, precision=BEST_PRECISION
    )
    grad_input_time = partial_time + swap(partial_time, "c")
    grad_residual, gain_one = layer_back(
        on_both(partial_one), normed_one, inverse_one, gain_values[0]
    )
    grad_residual = (grad_residual + grad_after_self).astype(bf16)
    grad_embeds, gain_time = layer_back(
        grad_input_time, normed_time, inverse_time, gain_values[0]
    )
    grad_in_weight = tdot(grad_residual, noised)
    grad_table = features.astype(f32).reshape(NTIME, 1) * grad_embeds
    grad_gains = jnp.stack([gain_one + gain_time, gain_two, gain_three], 0)

    def own_rows(values):
        return pick(values.reshape((4, 2, 4) + values.shape[1:]), core, 1)

    small = jnp.concatenate(
        [
            own_rows(grad_table.reshape(32, 8, D)),
            jnp.pad(
                own_rows(grad_gains.reshape(3, 32, 48).transpose(1, 0, 2).reshape(32, 1, 144)),
                ((0, 0), (0, 0), (0, 7), (0, D - 144)),
            ),
        ],
        2,
    )
    grad_ends = own_rows(
        jnp.concatenate([grad_in_weight, grad_out_weight], 1).astype(bf16).reshape(32, 48, 2 * DIN)
    )
    rest_arrays = (
        ("one", (4 * BLK, 2 * BLK)),
        ("cols", (48, half)),
        ("one", (48, D)),
        ("cols", (16, 1152)),
        ("cols", (16, 1152)),
        ("one", (16, D)),
        ("one", (48, 2 * DIN)),
        ("one", (96, UP_LOW)),
    )
    rest_groups = [
        ((7, 0, whole, pl.ds(0, UP_LOW // 2)), (7, 1, whole, pl.ds(UP_LOW // 2, UP_LOW // 2)))
    ]
    rest_groups += [((3, 0, whole, whole), (4, 1, whole, whole))]
    rest_groups += [
        ((1, 0, whole, pl.ds(step * 384, 384)), (2, 1, whole, pl.ds(step * 768, 768)))
        for step in range(2)
    ]
    rest_groups += [
        ((0, 0, pl.ds(step * 96, 96), whole), (0, 1, pl.ds(384 + step * 96, 96), whole))
        for step in range(4)
    ]
    rest_groups += [((5, 0, whole, whole), (6, 1, whole, whole))]
    rest_sums = reduce_gradients(
        rest_arrays,
        rest_groups,
        (
            slot_sums,
            grad_query_weight,
            out_rows,
            kv_sources[0],
            kv_sources[1],
            small.astype(bf16).reshape(4, 1, 4, 16, D),
            grad_ends.reshape(4, 1, 4, 48, 2 * DIN),
            grad_up_low.reshape(4, 1, 4, 96, UP_LOW),
        ),
        2,
    )
    grad_down = grad_down_low.astype(f32)
    up_sums = rest_sums[-1].reshape(2, 48, UP_LOW)
    slot_pairs = rest_sums[0].reshape(4, BLK, 2 * BLK)
    grad_cross_query, grad_cross_out, *kv_sums, small, grad_ends = (
        value.astype(f32) for value in rest_sums[1:-1]
    )
    gate_sides, (up_own, up_other) = feed_sums
    up_own = jnp.concatenate([pick(up_sums, core), up_own], 1)
    up_other = jnp.concatenate([swap(pick(up_sums, 1 - core), "c"), up_other], 1)
    gate_columns = []
    for mine, other in (gate_sides, (up_own, up_other)):
        sides = (jnp.where(core == 0, mine, other), jnp.where(core == 0, other, mine))
        for quadrant in quads:
            for side in sides:
                gate_columns.append(side[:, quadrant * 768 : (quadrant + 1) * 768])
    grad_gate_up = jnp.concatenate(gate_columns, 1).astype(f32)
    grad_cross = jnp.stack([grad_cross_query, grad_cross_out], 1)
    kv_columns = []
    for pair in kv_sums:
        kv_columns += [pair[:, :1152].reshape(24, half), pair[:, 1152:].reshape(24, half)]
    grad_key_value = jnp.concatenate(kv_columns, 1)
    grad_ends = grad_ends.reshape(48, 2, DIN)
    grad_table = small[:8]
    grad_gains = small[8, :144].reshape(3, 48).T

    reduced = (
        grad_ends,
        grad_table,
        slot_pairs,
        grad_cross,
        grad_key_value,
        grad_gate_up,
        grad_down,
        grad_gains,
    )
    loss_part = jnp.where(
        core == 0,
        jnp.sum(errors * errors) * mse_scale + contrast_own * (CONTRAST_WEIGHT / items_total),
        0.0,
    )
    totals = total_squares(
        loss_part, (*rest_sums[:-1], *gate_sides, up_own, up_other, grad_down_low), 4
    )
    loss_total, norm_square = totals[0, 0], totals[0, 1]
    return finish(
        loss_total,
        jnp.sqrt(norm_square),
        reduced,
        (
            end_weights,
            time_table,
            square_slots,
            cross_weights,
            key_value,
            gate_up,
            down_weight,
            norm_gains,
        ),
        (
            first_ends,
            first_table,
            None,
            first_cross,
            first_key_value,
            first_gate_up,
            first_down,
            first_gains,
        ),
        (
            second_ends,
            second_table,
            None,
            second_cross,
            second_key_value,
            second_gate_up,
            second_down,
            second_gains,
        ),
        (left_stats, right_stats, left_roots, right_roots),
    )


def finish(loss_total, gradient_norm, reduced, masters, firsts, seconds, statistics):
    factor = CLIP_NORM / jnp.maximum(gradient_norm, CLIP_NORM)
    results = [loss_total, gradient_norm]
    for index_value in (0, 1, 3, 4, 5, 6, 7):
        results.extend(
            adam_update(
                masters[index_value],
                firsts[index_value],
                seconds[index_value],
                factor * reduced[index_value],
                ADAM_RATES[index_value],
            )
        )
    if reduced[2].dtype == jnp.bfloat16:
        results.extend(shampoo_pairs(factor, reduced[2], masters[2], *statistics))
    else:
        clipped_slots = factor * reduced[2]
        results.append(clipped_slots)
        results.extend(shampoo_update(masters[2], clipped_slots, *statistics))
    return tuple(results)


def solution(mesh):
    lines = mesh.shape["text"]
    chips = mesh.devices.size // 2
    if mesh.shape["dp"] == 8 and lines == 4 and 2 * mesh.shape["dp"] == chips:
        mesh = Mesh(mesh.devices.reshape(2, 2, 2, lines), ("y", "x", "c", "z"))
        dp, text, body = ("y", "x", "c"), ("z",), item_per_chip
    else:
        dp, text, body = ("dp",), ("text",), shards
    own = dp + text
    in_specs = (
        P(dp, text, None),
        P(dp, text, None),
        P(dp),
        P(dp, text, None),
        P(dp),
        P(dp, None),
        P(),
    ) + (P(own),) * 26
    out_specs = (P(), P()) + (P(own),) * 25
    return jax.shard_map(body, mesh=mesh, in_specs=in_specs, out_specs=out_specs, check_vma=False)
```

```python
from functools import partial
import math

import jax
import jax.numpy as jnp
from jax import lax
from jax.experimental import pallas as pl
from jax.experimental.pallas import tpu as pltpu
from jax.sharding import Mesh, PartitionSpec as P

D = 1536
HEADS = 24
HD = 64
FF = 6144
DIN = 64
DT = 768
FRAMES = 1024
NTIME = 256
STEP = 10
BLK = 192


BEST_PRECISION = lax.Precision.HIGHEST
NORM_EPS = 1e-05
POOL_EPS = 1e-06
SCORE_SCALE = 0.125
CONTRAST_TEMP = 0.02
CONTRAST_WEIGHT = 0.1
CLIP_NORM = 0.005
BETA_FIRST = 0.9
BETA_SECOND = 0.999
ADAM_EPS = 1e-08
WEIGHT_DECAY = 0.01
ADAM_RATES = (0.02, 0.05, 0.0, 0.1, 0.02, 0.02, 0.02, 1.0)
STAT_DECAY = 0.999
SHAMPOO_RATE = 0.01
MASK_VALUE = -1000000000.0


def layer_stats(inputs):
    center = inputs - jnp.mean(inputs, -1, keepdims=True)
    inverse = lax.rsqrt(jnp.mean(center * center, -1, keepdims=True) + NORM_EPS)
    return (center * inverse, inverse)


def layer_back(grad_out, normed, inverse, gain_row):
    scaled = grad_out * gain_row
    grad_in = inverse * (
        scaled
        - jnp.mean(scaled, -1, keepdims=True)
        - normed * jnp.mean(scaled * normed, -1, keepdims=True)
    )
    return (grad_in, jnp.sum(grad_out * normed, 0))


def time_features(timesteps):
    halfway = NTIME // 2
    frequency = jnp.exp(jnp.arange(halfway, dtype=jnp.float32) * (math.log(64.0) / halfway))
    moment = (timesteps.astype(jnp.float32) + 0.5) / NTIME
    phase = 2.0 * math.pi * moment[:, None] * frequency[None, :]
    return jnp.concatenate([jnp.cos(phase), jnp.sin(phase)], 1)


def rope_tables(positions_count, offset):
    halfway = HD // 2
    frequency = jnp.exp(jnp.arange(halfway, dtype=jnp.float32) * (-2.0 * math.log(10000.0) / HD))
    positions = (jnp.arange(positions_count, dtype=jnp.int32) + offset).astype(jnp.float32)
    angles = positions[:, None] * frequency[None, :]
    return (jnp.concatenate([jnp.cos(angles)] * 2, -1), jnp.concatenate([jnp.sin(angles)] * 2, -1))


def rotate(values, cosine_table, sine_table):
    halfway = HD // 2
    turned = jnp.concatenate([-values[..., halfway:], values[..., :halfway]], -1)
    return values * cosine_table[:, None, :] + turned * sine_table[:, None, :]


def rotate_back(gradient, cosine_table, sine_table):
    halfway = HD // 2
    product = gradient * sine_table[:, None, :]
    return gradient * cosine_table[:, None, :] + jnp.concatenate(
        [product[..., halfway:], -product[..., :halfway]], -1
    )


def to_matrices(blocks):
    per_side = D // BLK
    return blocks.reshape(4, per_side, per_side, BLK, BLK).transpose(0, 1, 3, 2, 4).reshape(4, D, D)


def to_blocks(matrices):
    per_side = D // BLK
    return (
        matrices.reshape(4, per_side, BLK, per_side, BLK)
        .transpose(0, 1, 3, 2, 4)
        .reshape(4 * per_side * per_side, BLK, BLK)
    )


def normalize(vectors):
    return vectors * lax.rsqrt(jnp.sum(vectors * vectors, -1, keepdims=True) + POOL_EPS)


def contrast_loss(pooled_audio, pooled_text, negatives):
    audio_unit_vectors = normalize(pooled_audio)
    text_unit_vectors = normalize(pooled_text)
    positive_pairs = jnp.sum(audio_unit_vectors * text_unit_vectors, -1) / CONTRAST_TEMP
    negative_pairs = (
        jnp.einsum(
            "ux,uax->ua", audio_unit_vectors, text_unit_vectors[negatives], precision=BEST_PRECISION
        )
        / CONTRAST_TEMP
    )
    scores = jnp.concatenate([positive_pairs[:, None], negative_pairs], 1)
    peak_score = jnp.max(scores, -1, keepdims=True)
    logsum = peak_score[:, 0] + jnp.log(jnp.sum(jnp.exp(scores - peak_score), -1))
    return jnp.sum(logsum - positive_pairs)


def item_scores(one_query, one_key, one_bias):
    scores = jnp.einsum("fhd,khd->hfk", one_query, one_key, preferred_element_type=jnp.float32)
    return scores * SCORE_SCALE + one_bias


def attend_forward(queries, all_keys, values, key_bias):

    def single(pieces):
        one_query, one_key, one_value, one_bias = pieces
        scores = item_scores(one_query, one_key, one_bias)
        peak_score = jnp.max(scores, -1, keepdims=True)
        weights = jnp.exp(scores - peak_score)
        row_total = jnp.sum(weights, -1, keepdims=True)
        mixture = jnp.einsum(
            "hfk,khd->fhd",
            (weights / row_total).astype(jnp.bfloat16),
            one_value,
            preferred_element_type=jnp.float32,
        )
        return (mixture.astype(jnp.bfloat16), peak_score + jnp.log(row_total))

    return lax.map(single, (queries, all_keys, values, key_bias))


def attend_backward(queries, all_keys, values, key_bias, logsums, grad_mixture):

    def single(pieces):
        one_query, one_key, one_value, one_bias, one_logsum, grad_rows = pieces
        attention = jnp.exp(item_scores(one_query, one_key, one_bias) - one_logsum)
        grad_attention = jnp.einsum(
            "fhd,khd->hfk", grad_rows, one_value, preferred_element_type=jnp.float32
        )
        grad_value = jnp.einsum(
            "hfk,fhd->khd",
            attention.astype(jnp.bfloat16),
            grad_rows,
            preferred_element_type=jnp.float32,
        )
        grad_scores = attention * (
            grad_attention - jnp.sum(attention * grad_attention, -1, keepdims=True)
        )
        grad_scores = grad_scores.astype(jnp.bfloat16)
        grad_query = (
            jnp.einsum("hfk,khd->fhd", grad_scores, one_key, preferred_element_type=jnp.float32)
            * SCORE_SCALE
        )
        grad_key = (
            jnp.einsum("hfk,fhd->khd", grad_scores, one_query, preferred_element_type=jnp.float32)
            * SCORE_SCALE
        )
        return (grad_query, grad_key, grad_value)

    return lax.map(single, (queries, all_keys, values, key_bias, logsums, grad_mixture))


def feed_forward(rows_in, gate_matrix, down_matrix):
    width = down_matrix.shape[0]
    gate_values = jnp.dot(rows_in, gate_matrix, preferred_element_type=jnp.float32)
    gate_part = gate_values[:, :width]
    up_part = gate_values[:, width:]
    sigmoid = jax.nn.sigmoid(gate_part)
    silu_value = gate_part * sigmoid
    hidden = (silu_value * up_part).astype(jnp.bfloat16)
    partial_out = jnp.dot(hidden, down_matrix, preferred_element_type=jnp.float32)
    return (partial_out, (hidden, gate_part, up_part, sigmoid, silu_value))


def feed_back(rows_in, gate_matrix, down_matrix, kept, grad_low):
    hidden, gate_part, up_part, sigmoid, silu_value = kept
    grad_down = jnp.einsum("rf,rd->fd", hidden, grad_low, preferred_element_type=jnp.float32)
    grad_hidden = jnp.einsum("rd,fd->rf", grad_low, down_matrix, preferred_element_type=jnp.float32)
    grad_gate = grad_hidden * up_part * sigmoid * (1.0 + gate_part * (1.0 - sigmoid))
    grad_pair = jnp.concatenate([grad_gate, grad_hidden * silu_value], 1).astype(jnp.bfloat16)
    grad_gate_up = jnp.einsum("rd,rg->dg", rows_in, grad_pair, preferred_element_type=jnp.float32)
    grad_rows = jnp.einsum("rg,dg->rd", grad_pair, gate_matrix, preferred_element_type=jnp.float32)
    return (grad_rows, grad_gate_up, grad_down)


def adam_update(weight, first_moment, second_moment, gradient, rate):
    first_moment = BETA_FIRST * first_moment + (1.0 - BETA_FIRST) * gradient
    second_moment = BETA_SECOND * second_moment + (1.0 - BETA_SECOND) * gradient * gradient
    corrected = first_moment / (1.0 - BETA_FIRST**STEP)
    scaled = second_moment / (1.0 - BETA_SECOND**STEP)
    weight = weight - rate * (corrected / (jnp.sqrt(scaled) + ADAM_EPS) + WEIGHT_DECAY * weight)
    return (first_moment, second_moment, weight)


def shampoo_update(slots_now, gradient, left_stat, right_stat, left_root, right_root):
    left_stat = STAT_DECAY * left_stat + (1.0 - STAT_DECAY) * jnp.einsum(
        "sij,skj->sik", gradient, gradient, precision=BEST_PRECISION
    )
    right_stat = STAT_DECAY * right_stat + (1.0 - STAT_DECAY) * jnp.einsum(
        "sji,sjk->sik", gradient, gradient, precision=BEST_PRECISION
    )
    inner = jnp.einsum("sij,sjk->sik", gradient, right_root, precision=BEST_PRECISION)
    direction = jnp.einsum("sij,sjk->sik", left_root, inner, precision=BEST_PRECISION)
    return (
        left_stat,
        right_stat,
        slots_now - SHAMPOO_RATE * (direction + WEIGHT_DECAY * slots_now),
    )


def shards(
    latents,
    noise_field,
    timesteps,
    text_tokens,
    text_lengths,
    negatives,
    assignment,
    end_weights,
    time_table,
    square_slots,
    cross_weights,
    key_value,
    gate_up,
    down_weight,
    norm_gains,
    first_ends,
    second_ends,
    first_table,
    second_table,
    first_cross,
    second_cross,
    first_key_value,
    second_key_value,
    first_gate_up,
    second_gate_up,
    first_down,
    second_down,
    first_gains,
    second_gains,
    left_stats,
    right_stats,
    left_roots,
    right_roots,
):
    text_index = lax.axis_index("text")
    group_index = lax.axis_index("dp")
    group_count = lax.axis_size("dp")
    text_count_axis = lax.axis_size("text")
    piece_width = FF // (group_count * text_count_axis)
    low_ends = end_weights.astype(jnp.bfloat16)
    low_table = time_table.astype(jnp.bfloat16)
    low_slots = square_slots.astype(jnp.bfloat16)
    low_cross = cross_weights.astype(jnp.bfloat16)
    low_pairs = key_value.astype(jnp.bfloat16)
    low_gains = norm_gains.astype(jnp.bfloat16)
    low_gate = gate_up.astype(jnp.bfloat16)
    low_down = down_weight.astype(jnp.bfloat16)
    group_set = (
        lax.all_gather(low_ends, "text", axis=0, tiled=True),
        lax.all_gather(low_table, "text", axis=0, tiled=True),
        lax.all_gather(low_slots, "text", axis=0, tiled=True),
        lax.all_gather(low_cross, "text", axis=0, tiled=True),
        lax.all_gather(low_pairs, "text", axis=0, tiled=True),
        lax.all_gather(low_gains, "text", axis=0, tiled=True),
        lax.all_gather(low_gate, "text", axis=0, tiled=True),
    )
    gate_group = group_set[6].reshape(
        group_set[6].shape[0], 2, group_count, text_count_axis, piece_width
    )
    gate_columns = lax.dynamic_index_in_dim(gate_group, text_index, 3, keepdims=False)
    full_set = (
        lax.all_gather(group_set[0], "dp", axis=0, tiled=True),
        lax.all_gather(group_set[1], "dp", axis=0, tiled=True),
        lax.all_gather(group_set[2], "dp", axis=0, tiled=True),
        lax.all_gather(group_set[3], "dp", axis=0, tiled=True),
        lax.all_gather(group_set[4], "dp", axis=0, tiled=True),
        lax.all_gather(group_set[5], "dp", axis=0, tiled=True),
        lax.all_gather(gate_columns, "dp", axis=0, tiled=True),
        lax.all_gather(low_down, "dp", axis=0, tiled=True),
    )
    ends_full, table_full, slots_full, cross_full, pairs_full, gains_full = full_set[:6]
    gate_full = full_set[6].reshape(D, 2 * group_count * piece_width)
    down_full = full_set[7]
    item_count = latents.shape[0]
    frames_dev = latents.shape[1]
    tokens_dev = text_tokens.shape[1]
    row_count = item_count * frames_dev
    items_total = item_count * group_count
    mse_scale = 1.0 / (items_total * FRAMES * DIN)
    weight_in = ends_full[:, 0, :]
    weight_out = ends_full[:, 1, :]
    gain_values = gains_full.astype(jnp.float32)
    inverse_order = (
        jnp.zeros_like(assignment)
        .at[assignment]
        .set(jnp.arange(assignment.shape[0], dtype=jnp.int32))
    )
    squares = to_matrices(slots_full[inverse_order])
    projection = jnp.concatenate([squares[0], squares[1], squares[2]], 1)
    cosine_table, sine_table = rope_tables(frames_dev, 1 + text_index * frames_dev)
    angles = (timesteps.astype(jnp.float32) + 0.5) * (0.5 * math.pi / NTIME)
    signal = jnp.cos(angles)[:, None, None]
    spread = jnp.sin(angles)[:, None, None]
    noised = (signal * latents + spread * noise_field).astype(jnp.bfloat16).reshape(row_count, DIN)
    residual = jnp.einsum("rc,dc->rd", noised, weight_in, preferred_element_type=jnp.float32)
    normed_one, inverse_one = layer_stats(residual)
    input_one = (normed_one * gain_values[:, 0]).astype(jnp.bfloat16)
    features = time_features(timesteps).astype(jnp.bfloat16)
    embeds = jnp.dot(features, table_full, preferred_element_type=jnp.float32)
    normed_time, inverse_time = layer_stats(embeds)
    input_time = (normed_time * gain_values[:, 0]).astype(jnp.bfloat16)
    joined_rows = jnp.dot(input_one, projection, preferred_element_type=jnp.float32)
    head_shape = (item_count, frames_dev, HEADS, HD)
    rot_queries = rotate(joined_rows[:, :D].reshape(head_shape), cosine_table, sine_table).astype(
        jnp.bfloat16
    )
    rot_keys = rotate(
        joined_rows[:, D : 2 * D].reshape(head_shape), cosine_table, sine_table
    ).astype(jnp.bfloat16)
    value_rows = joined_rows[:, 2 * D :].astype(jnp.bfloat16).reshape(item_count, frames_dev, D)
    time_pair = jnp.dot(input_time, projection[:, D:], preferred_element_type=jnp.float32).astype(
        jnp.bfloat16
    )
    keys_all, values_all = (
        lax.all_gather(rot_keys.reshape(item_count, frames_dev, D), "text", axis=1, tiled=True),
        lax.all_gather(value_rows, "text", axis=1, tiled=True),
    )
    key_count = keys_all.shape[1] + 1
    all_keys = jnp.concatenate([time_pair[:, None, :D], keys_all], 1).reshape(
        item_count, key_count, HEADS, HD
    )
    all_values = jnp.concatenate([time_pair[:, None, D:], values_all], 1).reshape(
        item_count, key_count, HEADS, HD
    )
    self_bias = jnp.zeros((item_count, key_count), jnp.float32)
    mixed_self, logsum_self = attend_forward(rot_queries, all_keys, all_values, self_bias)
    mixed_flat = mixed_self.reshape(row_count, D)
    after_self = residual + jnp.dot(mixed_flat, squares[3], preferred_element_type=jnp.float32)
    normed_two, inverse_two = layer_stats(after_self)
    input_two = (normed_two * gain_values[:, 1]).astype(jnp.bfloat16)
    cross_queries = jnp.dot(
        input_two, cross_full[:, 0, :], preferred_element_type=jnp.float32
    ).astype(jnp.bfloat16)
    cross_heads = cross_queries.reshape(head_shape)
    projected = jnp.dot(
        text_tokens.reshape(item_count * tokens_dev, DT),
        pairs_full,
        preferred_element_type=jnp.float32,
    )
    projected = projected.astype(jnp.bfloat16).reshape(item_count, tokens_dev, 2 * D)
    text_all = lax.all_gather(projected, "text", axis=1, tiled=True)
    text_count = text_all.shape[1]
    valid_keys = jnp.arange(text_count, dtype=jnp.int32)[None, :] < text_lengths[:, None]
    cross_bias = jnp.where(valid_keys, 0.0, MASK_VALUE).astype(jnp.float32)
    text_keys = text_all[:, :, :D].reshape(item_count, text_count, HEADS, HD)
    text_values = text_all[:, :, D:].reshape(item_count, text_count, HEADS, HD)
    mixed_cross, logsum_cross = attend_forward(cross_heads, text_keys, text_values, cross_bias)
    cross_flat = mixed_cross.reshape(row_count, D)
    after_cross = after_self + jnp.dot(
        cross_flat, cross_full[:, 1, :], preferred_element_type=jnp.float32
    )
    normed_three, inverse_three = layer_stats(after_cross)
    input_three = (normed_three * gain_values[:, 2]).astype(jnp.bfloat16)
    feed_rows = lax.all_gather(
        input_three.reshape(item_count, frames_dev, D), "text", axis=1, tiled=True
    ).reshape(-1, D)
    feed_out, feed_kept = feed_forward(feed_rows, gate_full, down_full)
    down_out = (
        lax.psum_scatter(
            feed_out.reshape(item_count, -1, D).astype(jnp.bfloat16),
            "text",
            scatter_dimension=1,
            tiled=True,
        )
        .astype(jnp.float32)
        .reshape(row_count, D)
    )
    output_rows = after_cross + down_out
    output_low = output_rows.astype(jnp.bfloat16)
    predicted = jnp.dot(output_low, weight_out, preferred_element_type=jnp.float32).reshape(
        latents.shape
    )
    errors = predicted - (signal * noise_field - spread * latents)
    lengths_float = text_lengths.astype(jnp.float32)
    own_valid = (text_index * tokens_dev + jnp.arange(tokens_dev, dtype=jnp.int32))[
        None, :
    ] < text_lengths[:, None]
    own_mask = own_valid.astype(jnp.float32)
    audio_part = jnp.sum(output_rows.reshape(item_count, frames_dev, D), 1)
    text_part = (
        jnp.sum(projected[:, :, :D].astype(jnp.float32) * own_mask[:, :, None], 1)
        / lengths_float[:, None]
    )
    pooled_set = (
        lax.all_gather(audio_part, ("dp", "text"), axis=0, tiled=True),
        lax.all_gather(text_part, ("dp", "text"), axis=0, tiled=True),
        lax.all_gather(negatives.astype(jnp.float32), ("dp", "text"), axis=0, tiled=True),
    )
    audio_pooled = (
        jnp.sum(pooled_set[0].reshape(group_count, text_count_axis, item_count, D), 1).reshape(
            -1, D
        )
        / FRAMES
    )
    text_pooled = jnp.sum(
        pooled_set[1].reshape(group_count, text_count_axis, item_count, D), 1
    ).reshape(-1, D)
    negative_rows = pooled_set[2].reshape(group_count, text_count_axis, item_count, -1)[:, 0]
    negative_rows = negative_rows.reshape(items_total, -1).astype(jnp.int32)
    contrast_value, contrast_back = jax.vjp(
        partial(contrast_loss, negatives=negative_rows), audio_pooled, text_pooled
    )
    grad_audio_all, grad_text_all = contrast_back(jnp.float32(CONTRAST_WEIGHT / items_total))
    grad_audio = lax.dynamic_slice_in_dim(grad_audio_all, group_index * item_count, item_count, 0)
    grad_text = lax.dynamic_slice_in_dim(grad_text_all, group_index * item_count, item_count, 0)
    grad_predicted = (2.0 * mse_scale * errors).astype(jnp.bfloat16).reshape(row_count, DIN)
    grad_out_weight = jnp.einsum(
        "rd,rc->dc", output_low, grad_predicted, preferred_element_type=jnp.float32
    )
    grad_output = jnp.einsum(
        "rc,dc->rd", grad_predicted, weight_out, preferred_element_type=jnp.float32
    )
    grad_output = (
        grad_output.reshape(item_count, frames_dev, D) + grad_audio[:, None, :] / FRAMES
    ).reshape(row_count, D)
    grad_down_in = grad_output.astype(jnp.bfloat16)
    grad_feed_rows = lax.all_gather(
        grad_down_in.reshape(item_count, frames_dev, D), "text", axis=1, tiled=True
    ).reshape(-1, D)
    grad_feed_in, grad_gate_up, grad_down = feed_back(
        feed_rows, gate_full, down_full, feed_kept, grad_feed_rows
    )
    grad_input_three = (
        lax.psum_scatter(
            grad_feed_in.reshape(item_count, -1, D).astype(jnp.bfloat16),
            "text",
            scatter_dimension=1,
            tiled=True,
        )
        .astype(jnp.float32)
        .reshape(row_count, D)
    )
    grad_after_cross, gain_three = layer_back(
        grad_input_three, normed_three, inverse_three, gain_values[:, 2]
    )
    grad_after_cross = grad_after_cross + grad_output
    grad_cross_in = grad_after_cross.astype(jnp.bfloat16)
    grad_cross_out = jnp.einsum(
        "rd,re->de", cross_flat, grad_cross_in, preferred_element_type=jnp.float32
    )
    grad_mixed_cross = jnp.einsum(
        "re,de->rd", grad_cross_in, cross_full[:, 1, :], preferred_element_type=jnp.float32
    )
    grad_mixed_cross = grad_mixed_cross.astype(jnp.bfloat16).reshape(head_shape)
    grad_cq, grad_text_keys, grad_text_values = attend_backward(
        cross_heads, text_keys, text_values, cross_bias, logsum_cross, grad_mixed_cross
    )
    grad_cq_low = grad_cq.reshape(row_count, D).astype(jnp.bfloat16)
    grad_cross_query = jnp.einsum(
        "rd,re->de", input_two, grad_cq_low, preferred_element_type=jnp.float32
    )
    grad_input_two = jnp.einsum(
        "re,de->rd", grad_cq_low, cross_full[:, 0, :], preferred_element_type=jnp.float32
    )
    grad_pairs = jnp.concatenate(
        [
            grad_text_keys.reshape(item_count, text_count, D),
            grad_text_values.reshape(item_count, text_count, D),
        ],
        2,
    )
    grad_own_pairs = lax.psum_scatter(
        grad_pairs.astype(jnp.bfloat16), "text", scatter_dimension=1, tiled=True
    ).astype(jnp.float32)
    pooled_grad = own_mask[:, :, None] * (grad_text[:, None, :] / lengths_float[:, None, None])
    grad_own_pairs = grad_own_pairs + jnp.concatenate([pooled_grad, jnp.zeros_like(pooled_grad)], 2)
    grad_own_pairs = grad_own_pairs.astype(jnp.bfloat16).reshape(item_count * tokens_dev, 2 * D)
    grad_textside = jnp.einsum(
        "tc,tk->ck",
        text_tokens.reshape(item_count * tokens_dev, DT),
        grad_own_pairs,
        preferred_element_type=jnp.float32,
    )
    grad_after_self, gain_two = layer_back(
        grad_input_two, normed_two, inverse_two, gain_values[:, 1]
    )
    grad_after_self = grad_after_self + grad_after_cross
    grad_self_in = grad_after_self.astype(jnp.bfloat16)
    grad_attn_out = jnp.einsum(
        "rd,re->de", mixed_flat, grad_self_in, preferred_element_type=jnp.float32
    )
    grad_mixed_self = jnp.einsum(
        "re,de->rd", grad_self_in, squares[3], preferred_element_type=jnp.float32
    )
    grad_mixed_self = grad_mixed_self.astype(jnp.bfloat16).reshape(head_shape)
    grad_rot_queries, grad_keys, value_gradients = attend_backward(
        rot_queries, all_keys, all_values, self_bias, logsum_self, grad_mixed_self
    )
    grad_keys_own, grad_values_own = (
        lax.psum_scatter(
            grad_keys[:, 1:].reshape(item_count, key_count - 1, D).astype(jnp.bfloat16),
            "text",
            scatter_dimension=1,
            tiled=True,
        ).astype(jnp.float32),
        lax.psum_scatter(
            value_gradients[:, 1:].reshape(item_count, key_count - 1, D).astype(jnp.bfloat16),
            "text",
            scatter_dimension=1,
            tiled=True,
        ).astype(jnp.float32),
    )
    grad_queries = (
        rotate_back(grad_rot_queries, cosine_table, sine_table)
        .astype(jnp.bfloat16)
        .reshape(row_count, D)
    )
    grad_key_rows = rotate_back(grad_keys_own.reshape(head_shape), cosine_table, sine_table)
    grad_key_rows = grad_key_rows.astype(jnp.bfloat16).reshape(row_count, D)
    grad_joined = jnp.concatenate(
        [grad_queries, grad_key_rows, grad_values_own.astype(jnp.bfloat16).reshape(row_count, D)], 1
    )
    grad_projection = jnp.einsum(
        "rd,rk->dk", input_one, grad_joined, preferred_element_type=jnp.float32
    )
    grad_input_one = jnp.einsum(
        "rk,dk->rd", grad_joined, projection, preferred_element_type=jnp.float32
    )
    grad_time_pair = jnp.concatenate(
        [grad_keys[:, 0].reshape(item_count, D), value_gradients[:, 0].reshape(item_count, D)], 1
    )
    time_rows = jnp.dot(input_time.astype(jnp.float32).T, grad_time_pair, precision=BEST_PRECISION)
    grad_projection = grad_projection + jnp.concatenate(
        [jnp.zeros((D, D), jnp.float32), time_rows], 1
    )
    grad_input_time = jnp.einsum(
        "ik,dk->id", grad_time_pair, projection[:, D:].astype(jnp.float32), precision=BEST_PRECISION
    )
    grad_residual, gain_one = layer_back(grad_input_one, normed_one, inverse_one, gain_values[:, 0])
    grad_residual = (grad_residual + grad_after_self).astype(jnp.bfloat16)
    grad_embeds, gain_time = layer_back(
        grad_input_time, normed_time, inverse_time, gain_values[:, 0]
    )
    grad_in_weight = jnp.einsum(
        "rd,rc->dc", grad_residual, noised, preferred_element_type=jnp.float32
    )
    grad_table = jnp.dot(features.astype(jnp.float32).T, grad_embeds, precision=BEST_PRECISION)
    grad_gains = jnp.stack([gain_one + gain_time, gain_two, gain_three], 1)
    grad_ends = jnp.stack([grad_in_weight, grad_out_weight], 1)
    grad_cross = jnp.stack([grad_cross_query, grad_cross_out], 1)
    grad_squares = jnp.stack(
        [
            grad_projection[:, :D],
            grad_projection[:, D : 2 * D],
            grad_projection[:, 2 * D :],
            grad_attn_out,
        ],
        0,
    )
    grad_slots = jnp.take(to_blocks(grad_squares), assignment, axis=0)
    gate_pieces = grad_gate_up.reshape(D, 2, group_count, piece_width)
    group_grads = (
        lax.psum_scatter(
            grad_ends.astype(jnp.bfloat16), "dp", scatter_dimension=0, tiled=True
        ).astype(jnp.float32),
        lax.psum_scatter(
            grad_table.astype(jnp.bfloat16), "dp", scatter_dimension=0, tiled=True
        ).astype(jnp.float32),
        lax.psum_scatter(
            grad_slots.astype(jnp.bfloat16), "dp", scatter_dimension=0, tiled=True
        ).astype(jnp.float32),
        lax.psum_scatter(
            grad_cross.astype(jnp.bfloat16), "dp", scatter_dimension=0, tiled=True
        ).astype(jnp.float32),
        lax.psum_scatter(
            grad_textside.astype(jnp.bfloat16), "dp", scatter_dimension=0, tiled=True
        ).astype(jnp.float32),
        lax.psum_scatter(
            grad_gains.astype(jnp.bfloat16), "dp", scatter_dimension=0, tiled=True
        ).astype(jnp.float32),
        lax.psum_scatter(
            gate_pieces.astype(jnp.bfloat16), "dp", scatter_dimension=0, tiled=True
        ).astype(jnp.float32),
        lax.psum_scatter(
            grad_down.astype(jnp.bfloat16), "dp", scatter_dimension=0, tiled=True
        ).astype(jnp.float32),
    )
    placing = (jnp.arange(text_count_axis, dtype=jnp.int32) == text_index).astype(jnp.float32)
    spread_gate = group_grads[6][:, :, :, None, :] * placing[None, None, None, :, None]
    spread_gate = spread_gate.reshape(spread_gate.shape[0], 2 * FF)
    owned = (
        lax.psum_scatter(
            group_grads[0].astype(jnp.bfloat16), "text", scatter_dimension=0, tiled=True
        ).astype(jnp.float32),
        lax.psum_scatter(
            group_grads[1].astype(jnp.bfloat16), "text", scatter_dimension=0, tiled=True
        ).astype(jnp.float32),
        lax.psum_scatter(
            group_grads[2].astype(jnp.bfloat16), "text", scatter_dimension=0, tiled=True
        ).astype(jnp.float32),
        lax.psum_scatter(
            group_grads[3].astype(jnp.bfloat16), "text", scatter_dimension=0, tiled=True
        ).astype(jnp.float32),
        lax.psum_scatter(
            group_grads[4].astype(jnp.bfloat16), "text", scatter_dimension=0, tiled=True
        ).astype(jnp.float32),
        lax.psum_scatter(
            group_grads[5].astype(jnp.bfloat16), "text", scatter_dimension=0, tiled=True
        ).astype(jnp.float32),
        lax.psum_scatter(
            spread_gate.astype(jnp.bfloat16), "text", scatter_dimension=0, tiled=True
        ).astype(jnp.float32),
    )
    reduced = (owned[0], owned[1], owned[2], owned[3], owned[4], owned[6], group_grads[7], owned[5])
    square_sum = jnp.zeros((), jnp.float32)
    for member in reduced:
        square_sum = square_sum + jnp.sum(member * member)
    loss_part = jnp.sum(errors * errors) * mse_scale
    totals = lax.psum((square_sum, loss_part), ("dp", "text"))
    loss_total = totals[1] + CONTRAST_WEIGHT * contrast_value / items_total
    gradient_norm = jnp.sqrt(totals[0])
    masters = (
        end_weights,
        time_table,
        square_slots,
        cross_weights,
        key_value,
        gate_up,
        down_weight,
        norm_gains,
    )
    firsts = (
        first_ends,
        first_table,
        None,
        first_cross,
        first_key_value,
        first_gate_up,
        first_down,
        first_gains,
    )
    seconds = (
        second_ends,
        second_table,
        None,
        second_cross,
        second_key_value,
        second_gate_up,
        second_down,
        second_gains,
    )
    return finish(
        loss_total,
        gradient_norm,
        reduced,
        masters,
        firsts,
        seconds,
        (left_stats, right_stats, left_roots, right_roots),
    )


def swap(values, axis, bit=1):
    return lax.ppermute(values, axis, [(i, i ^ bit) for i in range(lax.axis_size(axis))])


def pick(values, position, axis=0):
    return lax.dynamic_index_in_dim(values, position, axis, keepdims=False)


def low_sum(*terms):
    total = terms[0].astype(jnp.float32)
    for term in terms[1:]:
        total = total + term.astype(jnp.float32)
    return total


def on_both(partial_sum):
    low = partial_sum.astype(jnp.bfloat16)
    return low_sum(low, swap(low, "c"))


def tdot(left, right):
    return lax.dot_general(left, right, (((0,), (0,)), ((), ())), preferred_element_type=jnp.float32)


def dot_back(left, right):
    return lax.dot_general(left, right, (((1,), (1,)), ((), ())), preferred_element_type=jnp.float32)


MESH_ID = pl.DeviceIdType.MESH
JOIN_TILE = 512


def anywhere(count):
    return [pl.BlockSpec(memory_space=pl.ANY)] * count


def coordinates():
    return tuple(lax.axis_index(axis) for axis in ("y", "x", "c", "z"))


def chip_peers(me):
    row, column, core, line = me
    beside = {
        "c": (row, column, 1 - core, line),
        "x": (row, 1 - column, core, line),
        "y": (1 - row, column, core, line),
    }
    for offset in (1, 2, 3):
        beside[offset] = (row, column, core, line ^ offset)
    return beside


def greet(peers):
    barrier = pltpu.get_barrier_semaphore()
    for peer in peers.values():
        pl.semaphore_signal(barrier, inc=1, device_id=peer, device_id_type=MESH_ID)
    pl.semaphore_wait(barrier, len(peers))


def send(source, target, send_sem, recv_sem, peer):
    return pltpu.make_async_remote_copy(
        src_ref=source,
        dst_ref=target,
        send_sem=send_sem,
        recv_sem=recv_sem,
        device_id=peer,
        device_id_type=MESH_ID,
    )


def gather_kernel(arrays, groups, *refs):
    count = len(arrays)
    inputs = sum(2 if kind == "cols" else 1 for kind, _, _ in arrays)
    sources = list(refs[:inputs])
    send_sem, recv_sem, core_send, core_recv, local_sem, *item_sems = refs[inputs + 4 + count :]
    item_refs = refs[inputs : inputs + 2] + refs[inputs + 2 + count : inputs + 4 + count]
    bufs = refs[inputs + 2 : inputs + 2 + count]
    me = coordinates()
    row, column, core, line = me
    plane = 2 * row + column
    peers = chip_peers(me)
    others = {offset + 4: (row, column, 1 - core, line ^ offset) for offset in (1, 2, 3)}
    greet({**peers, **others})
    finish_items = move_items(me, item_refs, item_sems)
    local, cross = [], []
    for index_value, (kind, _, _) in enumerate(arrays):
        spot = bufs[index_value].at[plane, 0 if kind == "one" else core, line]
        copy = pltpu.make_async_copy(sources.pop(0), spot, local_sem.at[index_value])
        copy.start()
        local.append(copy)
        cross.append(None)
        if kind == "cols":
            cross[-1] = send(
                sources.pop(0),
                spot,
                core_send.at[index_value],
                core_recv.at[index_value],
                peers["c"],
            )
            cross[-1].start()
    whole = slice(None)
    flat = [unit for group in groups for unit in group]
    ready = set()

    def move(number, slot, planes, lines, peer):
        array, _, rows, columns = flat[number]
        cores = {"cols": whole, "one": 0}.get(arrays[array][0], core)
        view = bufs[array].at[planes, cores, lines, rows, columns]
        return send(view, view, send_sem.at[number, slot], recv_sem.at[number, slot], peer)

    def line_copies(number):
        return [move(number, o - 1, plane, line, peers[o]) for o in (1, 2, 3)]

    def near_copy(number):
        axis = "y" if flat[number][1] else "x"
        return move(number, 3, plane, whole, peers[axis])

    def side_copy(number):
        axis = "x" if flat[number][1] else "y"
        return move(number, 4, plane, whole, peers[axis])

    def far_copy(number):
        color = flat[number][1]
        return move(number, 5, plane ^ (2 if color else 1), whole, peers["x" if color else "y"])

    def core_copy(number):
        array, _, rows, columns = flat[number]
        kind = arrays[array][0]
        if kind not in ("both", "half"):
            return None
        planes = whole if kind == "both" else pl.ds(2 * (1 - core), 2)
        view = bufs[array].at[planes, core, whole, rows, columns]
        return send(view, view, send_sem.at[number, 6], recv_sem.at[number, 6], peers["c"])

    def start_line(number):
        array = flat[number][0]
        if array not in ready:
            ready.add(array)
            local[array].wait()
            if cross[array] is not None:
                cross[array].wait()
        for copy in line_copies(number):
            copy.start()

    def start_near(number):
        for copy in line_copies(number):
            copy.wait_recv()
        near_copy(number).start()
        side_copy(number).start()

    def start_far(number):
        near_copy(number).wait_recv()
        far_copy(number).start()

    def close(number):
        side_copy(number).wait_recv()
        far_copy(number).wait_recv()
        last = core_copy(number)
        if last is not None:
            last.start()
        for copy in line_copies(number) + [near_copy(number), side_copy(number), far_copy(number)]:
            copy.wait_send()

    stages = (start_line, start_near, start_far, close)
    numbers, at = [], 0
    for group in groups:
        numbers.append(range(at, at + len(group)))
        at += len(group)
    for step in range(len(groups) + 3):
        for lag, stage in enumerate(stages):
            if 0 <= step - lag < len(groups):
                for number in numbers[step - lag]:
                    stage(number)
    for number in range(len(flat)):
        last = core_copy(number)
        if last is not None:
            last.wait()
    finish_items()


def move_items(me, refs, sems):
    row, column, core, line = me
    send_sem, recv_sem, local_sem = sems

    def outgoing(kind, inner, side):
        return send(
            refs[kind].at[inner],
            refs[2 + kind].at[line],
            send_sem.at[kind, inner, side],
            recv_sem.at[kind, line],
            (row, column, side, 2 * core + inner),
        )

    def kept(kind, inner):
        return pltpu.make_async_copy(
            refs[kind].at[inner], refs[2 + kind].at[line], local_sem.at[kind]
        )

    def incoming(kind, origin):
        return send(
            refs[kind].at[0],
            refs[2 + kind].at[origin],
            send_sem.at[kind, 0, 0],
            recv_sem.at[kind, origin],
            (row, column, 1 - core, line),
        )

    def each_target(act, keep):
        for kind in range(2):
            for inner in range(2):
                for side in range(2):
                    own = (2 * core + inner == line) & (core == side)

                    @pl.when(own)
                    def stay():
                        keep(kind, inner)

                    @pl.when(jnp.logical_not(own))
                    def leave():
                        act(kind, inner, side)

    each_target(
        lambda kind, inner, side: outgoing(kind, inner, side).start(),
        lambda kind, inner: kept(kind, inner).start(),
    )

    def finish_items():
        each_target(
            lambda kind, inner, side: outgoing(kind, inner, side).wait_send(),
            lambda kind, inner: kept(kind, inner).wait(),
        )
        for kind in range(2):
            for origin in range(4):

                @pl.when(jnp.logical_not((line == origin) & (core == line // 2)))
                def arrive():
                    incoming(kind, origin).wait_recv()

    return finish_items


def gather_weights(arrays, groups, sources, items, collective_id):
    units = sum(len(group) for group in groups)
    dma = pltpu.SemaphoreType.DMA
    return pl.pallas_call(
        partial(gather_kernel, arrays, groups),
        out_shape=[
            jax.ShapeDtypeStruct((4, 1 if kind == "one" else 2, 4) + shape, dtype)
            for kind, shape, dtype in arrays
        ]
        + [jax.ShapeDtypeStruct((4,) + item.shape[1:], item.dtype) for item in items],
        in_specs=anywhere(len(sources) + 2),
        out_specs=anywhere(len(arrays) + 2),
        scratch_shapes=[
            dma((units, 7)),
            dma((units, 7)),
            dma((len(arrays),)),
            dma((len(arrays),)),
            dma((len(arrays),)),
            dma((2, 2, 2)),
            dma((2, 4)),
            dma((2,)),
        ],
        compiler_params=pltpu.CompilerParams(collective_id=collective_id, has_side_effects=True),
    )(*sources, *items)


def share_kernel(values, shared, send_sem, recv_sem):
    row, column, core, line = coordinates()
    own = 8 * row + 4 * column + line

    def peer(offset):
        return (row ^ (offset // 8), column ^ (offset // 4 % 2), core, line ^ (offset % 4))

    greet({offset: peer(offset) for offset in range(1, 16)})
    copies = [
        send(
            values, shared.at[own], send_sem.at[offset], recv_sem.at[offset], peer(offset)
        )
        for offset in range(1, 16)
    ]
    for copy in copies:
        copy.start()
    shared[own] = values[...]
    for copy in copies:
        copy.wait()


def share(values, collective_id):
    dma = pltpu.SemaphoreType.DMA
    return pl.pallas_call(
        share_kernel,
        out_shape=jax.ShapeDtypeStruct((16,) + values.shape, values.dtype),
        in_specs=[pl.BlockSpec(memory_space=pltpu.VMEM)],
        out_specs=pl.BlockSpec(memory_space=pltpu.VMEM),
        scratch_shapes=[dma((16,)), dma((16,))],
        compiler_params=pltpu.CompilerParams(collective_id=collective_id, has_side_effects=True),
    )(values)


def total_kernel(count, loss, *refs):
    pieces, result = refs[:count], refs[count]
    own_part, core_part, shared, send_sem, recv_sem = refs[count + 1 :]
    row, column, core, line = coordinates()
    own = 8 * row + 4 * column + line

    def peer(offset):
        return (row ^ (offset // 8), column ^ (offset // 4 % 2), core, line ^ (offset % 4))

    peers = {offset: peer(offset) for offset in range(1, 16)}
    peers[0] = (row, column, 1 - core, line)
    greet(peers)
    squares = jnp.zeros((1, 1), jnp.float32)
    for piece in pieces:
        value = piece[...].astype(jnp.float32)
        value = jnp.sum(value * value, 0, keepdims=True)
        squares = squares + jnp.sum(value, 1, keepdims=True)
    lane = lax.broadcasted_iota(jnp.int32, (8, 128), 1)
    own_part[...] = jnp.where(lane == 0, loss[0:1, 0:1], jnp.where(lane == 1, squares, 0.0))
    across = send(own_part, core_part, send_sem.at[0], recv_sem.at[0], peers[0])
    across.start()
    across.wait()
    own_part[...] = own_part[...] + core_part[...]
    copies = [
        send(own_part, shared.at[own], send_sem.at[offset], recv_sem.at[offset], peers[offset])
        for offset in range(1, 16)
    ]
    for copy in copies:
        copy.start()
    shared[own] = own_part[...]
    for copy in copies:
        copy.wait()
    total = shared[0]
    for index_value in range(1, 16):
        total = total + shared[index_value]
    result[...] = total


def total_squares(loss, pieces, collective_id):
    vmem, dma = pltpu.VMEM, pltpu.SemaphoreType.DMA
    tile = (8, 128)
    return pl.pallas_call(
        partial(total_kernel, len(pieces)),
        out_shape=jax.ShapeDtypeStruct(tile, jnp.float32),
        in_specs=[pl.BlockSpec(memory_space=vmem)] * (len(pieces) + 1),
        out_specs=pl.BlockSpec(memory_space=vmem),
        scratch_shapes=[
            vmem(tile, jnp.float32),
            vmem(tile, jnp.float32),
            vmem((16,) + tile, jnp.float32),
            dma((16,)),
            dma((16,)),
        ],
        compiler_params=pltpu.CompilerParams(
            collective_id=collective_id, has_side_effects=True, vmem_limit_bytes=48 * 2**20
        ),
    )(jnp.broadcast_to(loss, tile), *pieces)


def exact_dot(left, right, dims):
    return lax.dot_general(
        left,
        right,
        (dims, ((), ())),
        precision=BEST_PRECISION,
        preferred_element_type=jnp.float32,
    )


def shampoo_kernel(factor, pair, slots, left, right, left_root, right_root, *outs):
    clipped, new_left, new_right, new_slots = outs
    both = pair[0].astype(jnp.float32) * factor[0, 0]
    for side in range(2):
        grad = (pltpu.roll(both, BLK, 1) if side else both)[:, :BLK]
        clipped[side] = grad
        new_left[side] = STAT_DECAY * left[side] + (1.0 - STAT_DECAY) * exact_dot(
            grad, grad, ((1,), (1,))
        )
        new_right[side] = STAT_DECAY * right[side] + (1.0 - STAT_DECAY) * exact_dot(
            grad, grad, ((0,), (0,))
        )
        inner = exact_dot(grad, right_root[side], ((1,), (0,)))
        direction = exact_dot(left_root[side], inner, ((1,), (0,)))
        new_slots[side] = slots[side] - SHAMPOO_RATE * (direction + WEIGHT_DECAY * slots[side])


def shampoo_pairs(factor, pairs, slots, *statistics):
    steps = pairs.shape[0]
    block = pl.BlockSpec((2, BLK, BLK), lambda step: (step, 0, 0))
    return pl.pallas_call(
        shampoo_kernel,
        grid=(steps,),
        in_specs=[
            pl.BlockSpec(memory_space=pltpu.SMEM),
            pl.BlockSpec((1, BLK, 2 * BLK), lambda step: (step, 0, 0)),
        ]
        + [block] * 5,
        out_specs=[block] * 4,
        out_shape=[jax.ShapeDtypeStruct(slots.shape, jnp.float32)] * 4,
        cost_estimate=pl.CostEstimate(
            flops=96 * steps * BLK**3, bytes_accessed=40 * slots.size, transcendentals=0
        ),
    )(factor.reshape(1, 1), pairs, slots, *statistics)


NORM_ROWS = 128


def norm_back_kernel(mine, other, normed, inverse, gain, rest, *outs):
    grad_low, gain_out = outs[-2:]
    total = mine[...].astype(jnp.float32) + other[...].astype(jnp.float32)
    row = normed[...]

    @pl.when(pl.program_id(0) == 0)
    def clear():
        gain_out[...] = jnp.zeros_like(gain_out)

    gain_out[0:1, :] += jnp.sum(total * row, 0, keepdims=True)
    scaled = total * gain[0:1, :]
    grad = scaled - jnp.mean(scaled, -1, keepdims=True)
    grad = inverse[...] * (grad - row * jnp.mean(scaled * row, -1, keepdims=True))
    grad = grad + rest[...]
    grad_low[...] = grad.astype(grad_low.dtype)
    if len(outs) == 3:
        outs[0][...] = grad


def norm_back(partial_sum, normed, inverse, gain, rest, keep):
    low = partial_sum.astype(jnp.bfloat16)
    rows, width = rest.shape

    def block(columns):
        return pl.BlockSpec((NORM_ROWS, columns), lambda step: (step, 0))

    fixed = pl.BlockSpec((8, width), lambda step: (0, 0))
    wide = [jax.ShapeDtypeStruct((rows, width), jnp.float32)] if keep else []
    outs = pl.pallas_call(
        norm_back_kernel,
        grid=(rows // NORM_ROWS,),
        in_specs=[block(width)] * 3 + [block(1), fixed, block(width)],
        out_specs=[block(width)] * (len(wide) + 1) + [fixed],
        out_shape=wide
        + [
            jax.ShapeDtypeStruct((rows, width), jnp.bfloat16),
            jax.ShapeDtypeStruct((8, width), jnp.float32),
        ],
        cost_estimate=pl.CostEstimate(
            flops=16 * rows * width, bytes_accessed=18 * rows * width, transcendentals=0
        ),
    )(low, swap(low, "c"), normed, inverse, jnp.broadcast_to(gain, (8, width)), rest)
    return (*outs[:-1], outs[-1][0])


FEED_TILE = 256
FEED_ROWS = 512


def chunks(size, body):
    for start in range(0, size, FEED_ROWS):
        body(pl.ds(start, FEED_ROWS))


def feed_kernel(rows, gate_tile, up_tile, gate, up, hidden):
    def body(at):
        gate_part = jnp.dot(rows[at, :], gate_tile[...], preferred_element_type=jnp.float32)
        up_part = jnp.dot(rows[at, :], up_tile[...], preferred_element_type=jnp.float32)
        gate[at, :] = gate_part.astype(gate.dtype)
        up[at, :] = up_part.astype(up.dtype)
        hidden[at, :] = (gate_part * jax.nn.sigmoid(gate_part) * up_part).astype(hidden.dtype)

    chunks(rows.shape[0], body)


def hidden_back_kernel(grad, down_tile, gate, up, hidden, grad_gate, grad_up, grad_down):
    def body(at):
        back = dot_back(grad[at, :], down_tile[...])
        gate_part = gate[at, :].astype(jnp.float32)
        sigmoid = jax.nn.sigmoid(gate_part)
        grad_gate[at, :] = (
            back * up[at, :].astype(jnp.float32) * sigmoid * (1.0 + gate_part * (1.0 - sigmoid))
        ).astype(grad_gate.dtype)
        grad_up[at, :] = (back * gate_part * sigmoid).astype(grad_up.dtype)

    chunks(grad.shape[0], body)

    def weight(at):
        grad_down[:, at] = tdot(hidden[...], grad[:, at]).astype(grad_down.dtype)

    chunks(grad.shape[1], weight)


def rows_back_kernel(
    turned_rows, grad_gate, grad_up, gate_tile, up_tile, gate_out, up_out, rows_out, total
):
    @pl.when(pl.program_id(0) == 0)
    def clear():
        total[...] = jnp.zeros_like(total)

    def body(at):
        gate_out[at, :] = jnp.dot(
            turned_rows[at, :], grad_gate[...], preferred_element_type=jnp.float32
        ).astype(gate_out.dtype)
        up_out[at, :] = jnp.dot(
            turned_rows[at, :], grad_up[...], preferred_element_type=jnp.float32
        ).astype(up_out.dtype)
        total[:, at] += dot_back(grad_gate[...], gate_tile[at, :]) + dot_back(
            grad_up[...], up_tile[at, :]
        )

    chunks(turned_rows.shape[0], body)

    @pl.when(pl.program_id(0) == pl.num_programs(0) - 1)
    def store():
        rows_out[...] = total[...].astype(rows_out.dtype)


def feed_call(kernel, operands, outputs, flops, scratch=()):
    units = FF // 2

    def spec(shape, kind):
        height, width = shape
        if kind == "columns":
            return pl.BlockSpec((height, FEED_TILE), lambda step: (0, step))
        if kind == "rows":
            return pl.BlockSpec((FEED_TILE, width), lambda step: (step, 0))
        return pl.BlockSpec(shape, lambda step: (0, 0))

    low = jnp.bfloat16
    moved = sum(value.size for value, _ in operands) + sum(h * w for (h, w), _ in outputs)
    return pl.pallas_call(
        kernel,
        grid=(units // FEED_TILE,),
        in_specs=[spec(value.shape, kind) for value, kind in operands],
        out_specs=[spec(shape, kind) for shape, kind in outputs],
        out_shape=[jax.ShapeDtypeStruct(shape, low) for shape, _ in outputs],
        scratch_shapes=list(scratch),
        compiler_params=pltpu.CompilerParams(vmem_limit_bytes=56 * 2**20),
        cost_estimate=pl.CostEstimate(flops=flops, bytes_accessed=2 * moved, transcendentals=0),
    )(*[value for value, _ in operands])


def feed(rows, gate_weight, up_weight):
    shape = (rows.shape[0], FF // 2)
    return feed_call(
        feed_kernel,
        [(rows, "whole"), (gate_weight, "columns"), (up_weight, "columns")],
        [(shape, "columns")] * 3,
        4 * rows.size * (FF // 2),
    )


def hidden_back(grad, down, gate, up, hidden):
    shape = hidden.shape
    return feed_call(
        hidden_back_kernel,
        [
            (grad, "whole"),
            (down, "rows"),
            (gate, "columns"),
            (up, "columns"),
            (hidden, "columns"),
        ],
        [(shape, "columns"), (shape, "columns"), (down.shape, "rows")],
        4 * grad.size * (FF // 2),
    )


def rows_back(rows, grad_gate, grad_up, gate_weight, up_weight):
    return feed_call(
        rows_back_kernel,
        [
            (rows.T, "whole"),
            (grad_gate, "columns"),
            (grad_up, "columns"),
            (gate_weight, "columns"),
            (up_weight, "columns"),
        ],
        [
            (gate_weight.shape, "columns"),
            (up_weight.shape, "columns"),
            (rows.shape, "whole"),
        ],
        8 * rows.size * (FF // 2),
        [pltpu.VMEM(rows.shape, jnp.float32)],
    )


def reduce_kernel(arrays, groups, *refs):
    count = len(arrays)
    flat = [unit for group in groups for unit in group]
    total = len(flat)
    sources = refs[:count]
    targets, scratch = refs[count : 2 * count], refs[2 * count :]
    sides, onwards, mines, from_ons, from_lines, from_cores = (
        scratch[index_value * total : (index_value + 1) * total] for index_value in range(6)
    )
    send_sem, recv_sem, load_sem = scratch[6 * total :]
    me = coordinates()
    row, column, core, line = me
    plane = 2 * row + column
    peers = chip_peers(me)
    greet(peers)
    whole = slice(None)

    def source(number, planes):
        array, _, rows, columns = flat[number]
        return sources[array].at[planes, whole, whole, rows, columns]

    def first_copy(number, slot):
        bit, axis = (1, "x") if flat[number][1] else (2, "y")
        return send(
            source(number, plane ^ (3 if slot else bit)),
            sides[number].at[slot],
            send_sem.at[number, slot],
            recv_sem.at[number, slot],
            peers[axis],
        )

    def load_onward(number):
        off = 2 if flat[number][1] else 1
        return pltpu.make_async_copy(
            source(number, plane ^ off), onwards[number], load_sem.at[number, 0]
        )

    def load_mine(number):
        return pltpu.make_async_copy(source(number, plane), mines[number], load_sem.at[number, 1])

    def onward_copy(number):
        axis = "y" if flat[number][1] else "x"
        return send(
            onwards[number],
            from_ons[number],
            send_sem.at[number, 2],
            recv_sem.at[number, 2],
            peers[axis],
        )

    def line_copies(number):
        return [
            send(
                mines[number].at[whole, line ^ offset],
                from_lines[number].at[offset - 1],
                send_sem.at[number, 2 + offset],
                recv_sem.at[number, 2 + offset],
                peers[offset],
            )
            for offset in (1, 2, 3)
        ]

    def core_copy(number):
        return send(
            mines[number].at[1 - core, line],
            from_cores[number],
            send_sem.at[number, 6],
            recv_sem.at[number, 6],
            peers["c"],
        )

    def side_columns(number, side):
        array, _, _, columns = flat[number]
        width = arrays[array][1][1]
        start = 0 if isinstance(columns, slice) else columns.start
        at = pl.multiple_of(side * width + start, 128)
        return pl.ds(at, extent(columns, width))

    def is_cols(number):
        return arrays[flat[number][0]][0] == "cols"

    def add_into(target, *terms):
        cores, lines, height, _ = target.shape

        def body(step, carry):
            side = step // (lines * (height // 16))
            rest = step % (lines * (height // 16))
            at_line = rest // (height // 16)
            rows = pl.ds(pl.multiple_of((rest % (height // 16)) * 16, 16), 16)
            value = target[side, at_line, rows].astype(jnp.float32)
            for term in terms:
                value = value + term[side, at_line, rows].astype(jnp.float32)
            target[side, at_line, rows] = value.astype(target.dtype)
            return carry

        lax.fori_loop(0, cores * lines * (height // 16), body, 0)

    def stage_one(number):
        first_copy(number, 1).start()
        first_copy(number, 0).start()
        load_onward(number).start()
        load_mine(number).start()

    def stage_two(number):
        first_copy(number, 1).wait_recv()
        load_onward(number).wait()
        add_into(onwards[number], sides[number].at[1])
        onward_copy(number).start()

    def stage_three(number):
        first_copy(number, 0).wait_recv()
        load_mine(number).wait()
        onward_copy(number).wait_recv()
        add_into(mines[number], sides[number].at[0], from_ons[number])
        for copy in line_copies(number):
            copy.start()

    def stage_four(number):
        for copy in line_copies(number):
            copy.wait_recv()
        array, _, rows, columns = flat[number]
        mine, pieces = mines[number], from_lines[number]
        for side in range(mine.shape[0]):
            value = mine[side, line].astype(jnp.float32)
            for offset in range(3):
                value = value + pieces[offset, side].astype(jnp.float32)
            mine[side, line] = value.astype(mine.dtype)
        if is_cols(number):
            core_copy(number).start()
            targets[array][rows, side_columns(number, core)] = mine[core, line]
        else:
            targets[array][rows, columns] = mine[0, line]

    def stage_five(number):
        if is_cols(number):
            core_copy(number).wait()
            array, _, rows, _ = flat[number]
            targets[array][rows, side_columns(number, 1 - core)] = from_cores[number][...]
        first_copy(number, 0).wait_send()
        first_copy(number, 1).wait_send()
        onward_copy(number).wait_send()
        for copy in line_copies(number):
            copy.wait_send()

    stages = (stage_one, stage_two, stage_three, stage_four, stage_five)
    numbers, at = [], 0
    for group in groups:
        numbers.append(range(at, at + len(group)))
        at += len(group)
    for step in range(len(groups) + 4):
        for lag, stage in enumerate(stages):
            if 0 <= step - lag < len(groups):
                for number in numbers[step - lag]:
                    stage(number)


def extent(sel, size):
    return size if isinstance(sel, slice) else sel.size


def reduce_gradients(arrays, groups, sources, collective_id):
    flat = [unit for group in groups for unit in group]
    vmem, dma, low = pltpu.VMEM, pltpu.SemaphoreType.DMA, jnp.bfloat16
    shapes = []
    for array, _, rows, columns in flat:
        kind, (height, width) = arrays[array]
        shapes.append((2 if kind == "cols" else 1, extent(rows, height), extent(columns, width)))
    scratch = [vmem((2, c, 4, h, w), low) for c, h, w in shapes]
    for _ in range(3):
        scratch += [vmem((c, 4, h, w), low) for c, h, w in shapes]
    scratch += [vmem((3, c, h, w), low) for c, h, w in shapes]
    scratch += [vmem((h, w) if c == 2 else (16, 128), low) for c, h, w in shapes]
    out_shape = [
        jax.ShapeDtypeStruct((height, width * (2 if kind == "cols" else 1)), low)
        for kind, (height, width) in arrays
    ]
    return pl.pallas_call(
        partial(reduce_kernel, arrays, groups),
        out_shape=out_shape,
        in_specs=anywhere(len(sources)),
        out_specs=[pl.BlockSpec(memory_space=pltpu.VMEM)] * len(out_shape),
        scratch_shapes=scratch
        + [dma((len(flat), 7)), dma((len(flat), 7)), dma((len(flat), 2))],
        compiler_params=pltpu.CompilerParams(
            collective_id=collective_id, has_side_effects=True, vmem_limit_bytes=60 * 2**20
        ),
    )(*sources)


def turned(values, cosine, sine):
    lane = lax.broadcasted_iota(jnp.int32, values.shape, 1)
    halfway = HD // 2
    partner = jnp.where(
        lane % HD < halfway,
        pltpu.roll(values, 128 - halfway, 1),
        pltpu.roll(values, halfway, 1),
    )
    return values * cosine + partner * sine


def join_kernel(rows, times, weights, cosine, sine, joined, joined_time):
    is_turned = pl.program_id(0) < 6

    def body(step, carry):
        at = pl.ds(pl.multiple_of(step * JOIN_TILE, JOIN_TILE), JOIN_TILE)
        values = jnp.dot(rows[at, :], weights[...], preferred_element_type=jnp.float32)

        @pl.when(is_turned)
        def turn():
            for side in (0, 128):
                joined[at, side : side + 128] = turned(
                    values[:, side : side + 128], cosine[at, :], sine[at, :]
                ).astype(joined.dtype)

        @pl.when(jnp.logical_not(is_turned))
        def keep():
            joined[at, :] = values.astype(joined.dtype)

        return carry

    lax.fori_loop(0, rows.shape[0] // JOIN_TILE, body, 0)
    joined_time[...] = jnp.dot(
        times[...], weights[...], preferred_element_type=jnp.float32
    ).astype(joined_time.dtype)


def join(rows, times, weights, cosine, sine):
    width = weights.shape[1]

    def fixed(array):
        return pl.BlockSpec(array.shape, lambda step: (0, 0))

    return pl.pallas_call(
        join_kernel,
        grid=(width // 256,),
        in_specs=[
            fixed(rows),
            fixed(times),
            pl.BlockSpec((D, 256), lambda step: (0, step)),
            fixed(cosine),
            fixed(sine),
        ],
        out_specs=[
            pl.BlockSpec((rows.shape[0], 256), lambda step: (0, step)),
            pl.BlockSpec((times.shape[0], 256), lambda step: (0, step)),
        ],
        out_shape=[
            jax.ShapeDtypeStruct((rows.shape[0], width), jnp.bfloat16),
            jax.ShapeDtypeStruct((times.shape[0], width), jnp.bfloat16),
        ],
        compiler_params=pltpu.CompilerParams(vmem_limit_bytes=48 * 2**20),
        cost_estimate=pl.CostEstimate(
            flops=2 * rows.shape[0] * D * width,
            bytes_accessed=2 * (rows.size + weights.size + rows.shape[0] * width),
            transcendentals=0,
        ),
    )(rows, times, weights, cosine, sine)


def head_lanes(shape, head):
    return lax.broadcasted_iota(jnp.int32, shape, 1) // HD == head


def attend_kernel(timed, queries, keys, values, first, second, mixed, logsum):
    tile = 512

    def body(step, carry):
        at = pl.ds(pl.multiple_of(step * tile, tile), tile)
        rows = queries[at, :]
        total = jnp.zeros(rows.shape, jnp.float32)
        sums = jnp.zeros(rows.shape, jnp.float32)
        for head in range(2):
            own = head_lanes(rows.shape, head)
            query = jnp.where(own, rows, jnp.zeros_like(rows))
            scores = dot_back(query, keys[...]) * SCORE_SCALE
            if timed:
                extra = (
                    jnp.sum(
                        query.astype(jnp.float32) * first[0:1, :].astype(jnp.float32),
                        -1,
                        keepdims=True,
                    )
                    * SCORE_SCALE
                )
                peak = jnp.maximum(jnp.max(scores, -1, keepdims=True), extra)
            else:
                scores = scores + first[0:1, :]
                peak = jnp.max(scores, -1, keepdims=True)
            powers = jnp.exp(scores - peak)
            row_total = jnp.sum(powers, -1, keepdims=True)
            mixture = jnp.dot(
                powers.astype(jnp.bfloat16), values[...], preferred_element_type=jnp.float32
            )
            if timed:
                power = jnp.exp(extra - peak)
                row_total = row_total + power
                mixture = mixture + power * second[0:1, :].astype(jnp.float32)
            total = jnp.where(own, mixture / row_total, total)
            sums = jnp.where(own, peak + jnp.log(row_total), sums)
        mixed[at, :] = total.astype(mixed.dtype)
        logsum[at, :] = sums
        return carry

    lax.fori_loop(0, queries.shape[0] // tile, body, 0)


def lane_block(array, offset):
    return pl.BlockSpec((array.shape[0], 128), lambda pair: (0, pair + offset))


def attend(queries, keys, values, extras, offsets, timed):
    rows, count, pairs = queries.shape[0], keys.shape[0], HEADS // 4
    extra_specs = (
        [lane_block(extras[0], offsets[1]), lane_block(extras[1], offsets[2])]
        if timed
        else [pl.BlockSpec(extra.shape, lambda pair: (0, 0)) for extra in extras]
    )
    return pl.pallas_call(
        partial(attend_kernel, timed),
        grid=(pairs,),
        in_specs=[
            lane_block(queries, offsets[0]),
            lane_block(keys, offsets[1]),
            lane_block(values, offsets[2]),
        ]
        + extra_specs,
        out_specs=[pl.BlockSpec((rows, 128), lambda pair: (0, pair))] * 2,
        out_shape=[
            jax.ShapeDtypeStruct((rows, 128 * pairs), jnp.bfloat16),
            jax.ShapeDtypeStruct((rows, 128 * pairs), jnp.float32),
        ],
        compiler_params=pltpu.CompilerParams(vmem_limit_bytes=48 * 2**20),
        cost_estimate=pl.CostEstimate(
            flops=3 * pairs * 2 * rows * count * 128 * 4,
            bytes_accessed=pairs * 128 * (rows * 10 + count * 4),
            transcendentals=pairs * 2 * rows * count,
        ),
    )(queries, keys, values, *extras)


def attend_back_kernel(timed, *refs):
    queries, keys, values, first, second, mixed, logsum, gradient = refs[:8]
    if timed:
        cosine, sine, out_q, out_k, out_v, out_first, out_second, sum_k, sum_v = refs[8:]
    else:
        out_q, out_k, out_v, sum_k, sum_v = refs[8:]
    sum_k[...] = jnp.zeros_like(sum_k)
    sum_v[...] = jnp.zeros_like(sum_v)
    if timed:
        out_first[...] = jnp.zeros_like(out_first)
        out_second[...] = jnp.zeros_like(out_second)

    tile = 512

    def body(step, carry):
        at = pl.ds(pl.multiple_of(step * tile, tile), tile)
        rows, grad = queries[at, :], gradient[at, :]
        product = grad.astype(jnp.float32) * mixed[at, :].astype(jnp.float32)
        sums = logsum[at, :]
        sums_row = sums.T
        grad_query = jnp.zeros(rows.shape, jnp.float32)
        for head in range(2):
            own = head_lanes(rows.shape, head)
            query = jnp.where(own, rows, jnp.zeros_like(rows))
            grad_own = jnp.where(own, grad, jnp.zeros_like(grad))
            inner = jnp.sum(jnp.where(own, product, 0.0), -1, keepdims=True)
            inner_row = jnp.broadcast_to(inner, rows.shape).T[0:1, :]
            scores = dot_back(keys[...], query) * SCORE_SCALE
            if not timed:
                scores = scores + second[:, 0:1]
            attention = jnp.exp(scores - sums_row[head * HD : head * HD + 1, :])
            grad_attention = dot_back(values[...], grad_own)
            sum_v[...] += jnp.dot(
                attention.astype(jnp.bfloat16), grad_own, preferred_element_type=jnp.float32
            )
            grad_scores = (attention * (grad_attention - inner_row)).astype(jnp.bfloat16)
            sum_k[...] += jnp.dot(grad_scores, query, preferred_element_type=jnp.float32)
            key_own = jnp.where(
                head_lanes(keys.shape, head), keys[...], jnp.zeros(keys.shape, keys.dtype)
            )
            grad_query = grad_query + tdot(grad_scores, key_own)
            if timed:
                key_time = jnp.where(
                    own[0:1, :], first[0:1, :].astype(jnp.float32), jnp.zeros((1, 128), jnp.float32)
                )
                wide_query, wide_grad = query.astype(jnp.float32), grad_own.astype(jnp.float32)
                score = jnp.sum(wide_query * key_time, -1, keepdims=True) * SCORE_SCALE
                power = jnp.exp(score - sums[:, head * HD : head * HD + 1])
                back = jnp.sum(
                    wide_grad * second[0:1, :].astype(jnp.float32), -1, keepdims=True
                )
                grad_score = (power * (back - inner)).astype(jnp.bfloat16).astype(jnp.float32)
                grad_query = grad_query + grad_score * key_time
                out_first[0:1, :] += SCORE_SCALE * jnp.sum(
                    grad_score * wide_query, 0, keepdims=True
                )
                out_second[0:1, :] += jnp.sum(
                    power.astype(jnp.bfloat16).astype(jnp.float32) * wide_grad, 0, keepdims=True
                )
        grad_query = grad_query * SCORE_SCALE
        if timed:
            grad_query = turned(grad_query, cosine[at, :], -sine[at, :])
        out_q[at, :] = grad_query.astype(out_q.dtype)
        return carry

    lax.fori_loop(0, queries.shape[0] // tile, body, 0)
    grad_key = sum_k[...] * SCORE_SCALE
    if timed:
        grad_key = turned(grad_key, cosine[...], -sine[...])
    out_k[...] = grad_key.astype(out_k.dtype)
    out_v[...] = sum_v[...].astype(out_v.dtype)


def attend_back(queries, keys, values, extras, offsets, mixed, logsum, gradient, tables):
    timed = tables is not None
    rows, count, pairs = queries.shape[0], keys.shape[0], HEADS // 4
    extra_specs = (
        [lane_block(extras[0], offsets[1]), lane_block(extras[1], offsets[2])]
        if timed
        else [pl.BlockSpec(extra.shape, lambda pair: (0, 0)) for extra in extras]
    )
    low = jnp.bfloat16 if timed else jnp.float32

    def out(height, dtype):
        return (
            jax.ShapeDtypeStruct((height, 128 * pairs), dtype),
            pl.BlockSpec((height, 128), lambda pair: (0, pair)),
        )

    outs = [out(rows, jnp.bfloat16), out(count, low), out(count, low)]
    operands = [queries, keys, values, *extras, mixed, logsum, gradient]
    specs = (
        [
            lane_block(queries, offsets[0]),
            lane_block(keys, offsets[1]),
            lane_block(values, offsets[2]),
        ]
        + extra_specs
        + [lane_block(mixed, 0), lane_block(logsum, 0), lane_block(gradient, 0)]
    )
    if timed:
        outs += [out(8, jnp.float32), out(8, jnp.float32)]
        operands += list(tables)
        specs += [pl.BlockSpec(table.shape, lambda pair: (0, 0)) for table in tables]
    return pl.pallas_call(
        partial(attend_back_kernel, timed),
        grid=(pairs,),
        in_specs=specs,
        out_specs=[spec for _, spec in outs],
        out_shape=[shape for shape, _ in outs],
        scratch_shapes=[pltpu.VMEM((count, 128), jnp.float32)] * 2,
        compiler_params=pltpu.CompilerParams(vmem_limit_bytes=48 * 2**20),
        cost_estimate=pl.CostEstimate(
            flops=3 * pairs * 2 * rows * count * 128 * 10,
            bytes_accessed=pairs * 128 * (rows * 16 + count * 8),
            transcendentals=pairs * 2 * rows * count,
        ),
    )(*operands)


def shifted(tile, is_shifted):
    wide = tile.astype(jnp.float32)
    return jnp.where(is_shifted, pltpu.roll(wide, BLK, 1), wide)


def assemble_kernel(joined_at, mix_at, pairs, joined, mix):
    step = pl.program_id(0)
    lane = lax.broadcasted_iota(jnp.int32, (BLK, 2 * BLK), 1)

    def fill(places, target, count):
        for pair in range(count):
            first = (step * count + pair) * 2
            left, right = places[first], places[first + 1]
            tile = jnp.where(
                lane < BLK,
                shifted(pairs[left // 2], left % 2 == 1),
                shifted(pairs[right // 2], right % 2 == 0),
            )
            target[:, pair * 2 * BLK : (pair + 1) * 2 * BLK] = tile.astype(target.dtype)

    fill(joined_at, joined, 6)
    fill(mix_at, mix, 2)


def assemble(pairs, joined_at, mix_at):
    half = D // 2
    return pl.pallas_call(
        assemble_kernel,
        grid_spec=pltpu.PrefetchScalarGridSpec(
            num_scalar_prefetch=2,
            grid=(8,),
            in_specs=[
                pl.BlockSpec(
                    pairs.shape, lambda step, *_: (0, 0, 0), pipeline_mode=pl.Buffered(1)
                )
            ],
            out_specs=[
                pl.BlockSpec((BLK, 3 * half), lambda step, *_: (step, 0)),
                pl.BlockSpec((BLK, half), lambda step, *_: (step // 2, step % 2)),
            ],
        ),
        out_shape=[
            jax.ShapeDtypeStruct((D, 3 * half), pairs.dtype),
            jax.ShapeDtypeStruct((half, D), pairs.dtype),
        ],
        compiler_params=pltpu.CompilerParams(vmem_limit_bytes=48 * 2**20),
        cost_estimate=pl.CostEstimate(
            flops=0, bytes_accessed=2 * pairs.size + 8 * half * D, transcendentals=0
        ),
    )(joined_at, mix_at, pairs)


SLOTS_STEP = 8


def collect_kernel(rows_at, columns_at, sides, joined, mix, near, far):
    step = pl.program_id(0)
    lane = lax.broadcasted_iota(jnp.int32, (BLK, 2 * BLK), 1)

    def fill(target):
        target[...] = jnp.zeros_like(target)
        for inner in range(SLOTS_STEP):
            slot, pair, right = step * SLOTS_STEP + inner, inner // 2, inner % 2
            code = sides[slot]
            rows = pl.ds(pl.multiple_of(rows_at[slot] * BLK, BLK), BLK)
            columns = pl.ds(pl.multiple_of(columns_at[slot] * 2 * BLK, 128), 2 * BLK)
            own = lane // BLK == right

            def put(source, is_shifted):
                tile = source[rows, columns]
                if is_shifted:
                    tile = pltpu.roll(tile.astype(jnp.float32), BLK, 1).astype(tile.dtype)
                target[pair] = jnp.where(own, tile, target[pair])

            for which, source in enumerate((joined, mix)):
                for side in range(2):
                    pl.when(code == 2 * which + side)(partial(put, source, side != right))

    near_steps = pl.num_programs(0) // 2
    pl.when(step < near_steps)(partial(fill, near))
    pl.when(step >= near_steps)(partial(fill, far))


def collect(joined, mix, rows_at, columns_at, sides):
    steps = sides.shape[0] // SLOTS_STEP
    block = (SLOTS_STEP // 2, BLK, 2 * BLK)

    def resident(array):
        return pl.BlockSpec(array.shape, lambda step, *_: (0, 0), pipeline_mode=pl.Buffered(1))

    return pl.pallas_call(
        collect_kernel,
        grid_spec=pltpu.PrefetchScalarGridSpec(
            num_scalar_prefetch=3,
            grid=(steps,),
            in_specs=[resident(joined), resident(mix)],
            out_specs=[
                pl.BlockSpec(block, lambda step, *_: (jnp.minimum(step, steps // 2 - 1), 0, 0)),
                pl.BlockSpec(block, lambda step, *_: (jnp.maximum(step - steps // 2, 0), 0, 0)),
            ],
        ),
        out_shape=[jax.ShapeDtypeStruct((sides.shape[0] // 4, BLK, 2 * BLK), joined.dtype)] * 2,
        compiler_params=pltpu.CompilerParams(vmem_limit_bytes=48 * 2**20),
        cost_estimate=pl.CostEstimate(
            flops=0,
            bytes_accessed=4 * (joined.size + mix.size) + 4 * sides.shape[0] * BLK * BLK,
            transcendentals=0,
        ),
    )(rows_at, columns_at, sides, joined, mix)


def item_per_chip(
    latents,
    noise_field,
    timesteps,
    text_tokens,
    text_lengths,
    negatives,
    assignment,
    end_weights,
    time_table,
    square_slots,
    cross_weights,
    key_value,
    gate_up,
    down_weight,
    norm_gains,
    first_ends,
    second_ends,
    first_table,
    second_table,
    first_cross,
    second_cross,
    first_key_value,
    second_key_value,
    first_gate_up,
    second_gate_up,
    first_down,
    second_down,
    first_gains,
    second_gains,
    left_stats,
    right_stats,
    left_roots,
    right_roots,
):
    bf16, f32 = jnp.bfloat16, jnp.float32
    row, column = lax.axis_index("y"), lax.axis_index("x")
    core, line = lax.axis_index("c"), lax.axis_index("z")
    plane = 2 * row + column
    item = 4 * plane + line
    quads = range(4)
    half = D // 2
    items_total = 16
    mse_scale = 1.0 / (items_total * FRAMES * DIN)

    meta = jnp.concatenate([timesteps, text_lengths, negatives.reshape(-1)])[None]
    pack = jnp.concatenate(
        [
            time_table,
            jnp.pad(norm_gains.T.reshape(1, 144), ((0, 0), (0, D - 144))),
            jnp.pad(meta.astype(f32), ((0, 6), (0, D - 34))),
        ],
        0,
    ).astype(bf16)
    low_ends = end_weights.reshape(48, 2 * DIN).astype(bf16)
    low_slots = square_slots.astype(bf16).reshape(4, 2, BLK, BLK)
    low_pairs = jnp.concatenate([low_slots[:, 0], low_slots[:, 1]], 2).reshape(4 * BLK, 2 * BLK)
    low_cross = cross_weights.astype(bf16)
    low_kv = key_value.astype(bf16)
    low_gate = gate_up.astype(bf16)
    low_down = down_weight.astype(bf16)

    def head_columns(array, which, side):
        return lax.dynamic_slice_in_dim(array, which * D + side * half, half, 1)

    def unit_columns(which, side):
        return jnp.concatenate(
            [
                lax.dynamic_slice_in_dim(
                    low_gate, which * FF + quadrant * 1536 + side * 768, 768, 1
                )
                for quadrant in quads
            ],
            1,
        )

    def kv_block(which, side):
        return head_columns(low_kv, which, side).reshape(16, 1152)

    def gathered(block):
        return lax.all_gather(block, ("y", "x", "z"), axis=0)

    feed_blocks = []
    for which in range(2):
        kept, received = unit_columns(which, core), swap(unit_columns(which, 1 - core), "c")
        feed_blocks.append(
            jnp.where(core == 0, jnp.stack([kept, received]), jnp.stack([received, kept]))
        )
    gate_weight, up_weight = (gathered(block).reshape(D, FF // 2) for block in feed_blocks)
    down = gathered(low_down).reshape(FF // 2, D)
    arrays = (
        ("both", (16, D), bf16),
        ("both", (4 * BLK, 2 * BLK), bf16),
        ("cols", (48, half), bf16),
        ("half", (48, D), bf16),
        ("cols", (16, 1152), bf16),
        ("cols", (16, 1152), bf16),
        ("both", (48, 2 * DIN), bf16),
    )
    whole = slice(None)
    groups = [((0, 0, whole, whole), (5, 1, whole, whole), (6, 1, whole, whole))]
    groups += [
        ((1, 0, pl.ds(step * 96, 96), whole), (1, 1, pl.ds(384 + step * 96, 96), whole))
        for step in range(4)
    ]
    groups += [
        ((2, 0, whole, pl.ds(step * 384, 384)), (3, 1, whole, pl.ds(step * 768, 768)))
        for step in range(2)
    ]
    groups += [((4, 0, whole, whole),)]
    (
        packs,
        all_pairs,
        cross_query,
        cross_out,
        keys_own,
        values_own,
        ends_full,
        frames,
        tokens,
    ) = gather_weights(
        arrays,
        groups,
        (
            pack,
            low_pairs,
            head_columns(low_cross[:, 0, :], 0, core),
            head_columns(low_cross[:, 0, :], 0, 1 - core),
            low_cross[:, 1, :],
            kv_block(0, core),
            kv_block(0, 1 - core),
            kv_block(1, core),
            kv_block(1, 1 - core),
            low_ends,
        ),
        (jnp.concatenate([latents, noise_field], 2), text_tokens),
        1,
    )
    packs = packs.reshape(32, 16, D)
    table_full = packs[:, :8].reshape(NTIME, D)
    gain_values = packs[:, 8, :144].reshape(32, 3, 48).transpose(1, 0, 2).reshape(3, D).astype(f32)
    ends_full = ends_full.reshape(D, 2 * DIN)
    weight_in, weight_out = ends_full[:, :DIN], ends_full[:, DIN:]
    all_pairs = all_pairs.reshape(128, BLK, 2 * BLK)
    inverse_order = (
        jnp.zeros_like(assignment)
        .at[assignment]
        .set(jnp.arange(assignment.shape[0], dtype=jnp.int32))
    )

    def grid_blocks(matrix, rows, columns):
        return (matrix * 64 + rows * 8 + columns).reshape(-1)

    eight, four = jnp.arange(8, dtype=jnp.int32), jnp.arange(4, dtype=jnp.int32)
    joined_blocks = grid_blocks(
        jnp.arange(3, dtype=jnp.int32)[None, :, None],
        eight[:, None, None],
        (4 * core + four)[None, None, :],
    )
    out_blocks = grid_blocks(3, (4 * core + four)[:, None], eight[None, :])
    projection, weight_mix = assemble(
        all_pairs, inverse_order[joined_blocks], inverse_order[out_blocks]
    )
    cross_query = cross_query.reshape(D, half)
    cross_out = lax.dynamic_slice_in_dim(cross_out.reshape(D, D), core * half, half, 0)
    kv_own = jnp.concatenate(
        [keys_own.reshape(DT, half), values_own.reshape(DT, half)], 1
    )

    metas = packs.reshape(8, 4, 16, D)[:, 0, 9, :34].astype(jnp.int32)
    timestep = pick(metas[:, :2].reshape(-1), item)
    text_length = pick(metas[:, 2:4].reshape(-1), item)
    negative_rows = metas[:, 4:].reshape(items_total, -1)
    frames = frames.reshape(FRAMES, 2 * DIN)
    clean, noise = frames[:, :DIN], frames[:, DIN:]
    tokens = tokens.reshape(-1, DT)
    frame_positions = jnp.arange(FRAMES, dtype=jnp.int32) + 1
    token_slots = jnp.arange(tokens.shape[0], dtype=jnp.int32)
    halfway = HD // 2
    frequency = jnp.exp(jnp.arange(halfway, dtype=f32) * (-2.0 * math.log(10000.0) / HD))
    turn = frame_positions.astype(f32)[:, None] * frequency[None, :]
    cosine_table = jnp.concatenate([jnp.cos(turn)] * 4, -1)
    sine_table = jnp.concatenate([-jnp.sin(turn), jnp.sin(turn)] * 2, -1)
    angle = (timestep.astype(f32) + 0.5) * (0.5 * math.pi / NTIME)
    signal, spread = jnp.cos(angle), jnp.sin(angle)
    noised = (signal * clean + spread * noise).astype(bf16)
    target = signal * noise - spread * clean

    residual = dot_back(noised, weight_in)
    normed_one, inverse_one = layer_stats(residual)
    input_one = (normed_one * gain_values[0]).astype(bf16)
    features = time_features(timestep[None]).astype(bf16)
    embeds = jnp.dot(features, table_full, preferred_element_type=f32)
    normed_time, inverse_time = layer_stats(embeds)
    input_time = (normed_time * gain_values[0]).astype(bf16)
    time_block = jnp.pad(input_time, ((0, 15), (0, 0)))
    joined, joined_time = join(input_one, time_block, projection, cosine_table, sine_table)
    pairs = half // 128
    self_offsets = (0, pairs, 2 * pairs)
    mixed_flat, logsum_self = attend(
        joined, joined, joined, (joined_time, joined_time), self_offsets, True
    )
    after_self = residual + on_both(jnp.dot(mixed_flat, weight_mix, preferred_element_type=f32))
    normed_two, inverse_two = layer_stats(after_self)
    input_two = (normed_two * gain_values[1]).astype(bf16)
    cross_queries = jnp.dot(input_two, cross_query, preferred_element_type=f32).astype(bf16)
    projected = jnp.dot(tokens, kv_own, preferred_element_type=f32).astype(bf16)
    valid = token_slots < text_length
    cross_bias = jnp.where(valid, 0.0, MASK_VALUE).astype(f32)[None]
    text_biases = (
        jnp.broadcast_to(cross_bias, (8, 128)),
        jnp.broadcast_to(cross_bias.T, (128, 128)),
    )
    cross_offsets = (0, 0, pairs)
    cross_flat, logsum_cross = attend(
        cross_queries, projected, projected, text_biases, cross_offsets, False
    )
    after_cross = after_self + on_both(jnp.dot(cross_flat, cross_out, preferred_element_type=f32))
    normed_three, inverse_three = layer_stats(after_cross)
    input_three = (normed_three * gain_values[2]).astype(bf16)
    feature = jnp.arange(D, dtype=jnp.int32)
    gathered_at = (feature // 384 * 4 + feature // 48 % 4) * 96 + feature // 192 % 2 * 48 + feature % 48
    reorder = (gathered_at[:, None] == feature[None, :]).astype(bf16)
    feed_rows = jnp.dot(input_three, reorder, preferred_element_type=f32).astype(bf16)
    gate_part, up_part, hidden = feed(feed_rows, gate_weight, up_weight)
    down_out = on_both(jnp.dot(hidden, down, preferred_element_type=f32))
    output_rows = after_cross + down_out
    output_low = output_rows.astype(bf16)
    predicted = jnp.dot(output_low, weight_out, preferred_element_type=f32)
    errors = predicted - target

    length_float = text_length.astype(f32)
    mask = valid.astype(f32)[:, None]
    text_half = jnp.sum(projected[:, :half].astype(f32) * mask, 0) / length_float
    text_rest = swap(text_half, "c")
    text_pool = jnp.where(
        core == 0,
        jnp.concatenate([text_half, text_rest]),
        jnp.concatenate([text_rest, text_half]),
    )
    pools = jnp.stack([jnp.sum(output_rows, 0) / FRAMES, text_pool], 0)
    pools = share(pools.reshape(8, D // 4), 3).reshape(items_total, 2, D)
    inverse_pools = lax.rsqrt(jnp.sum(pools * pools, -1, keepdims=True) + POOL_EPS)
    units = pools * inverse_pools
    audio_units, text_units = units[:, 0], units[:, 1]
    similar = (
        lax.dot_general(
            audio_units, text_units, (((1,), (1,)), ((), ())), precision=BEST_PRECISION
        )
        / CONTRAST_TEMP
    )
    same = jnp.eye(items_total, dtype=f32)
    counts = same + jnp.sum(
        (negative_rows[:, None, :] == jnp.arange(items_total, dtype=jnp.int32)[None, :, None]).astype(f32), -1
    )
    peak = jnp.max(jnp.where(counts > 0, similar, -jnp.inf), -1, keepdims=True)
    powers = jnp.where(counts > 0, counts * jnp.exp(similar - peak), 0.0)
    totals_row = jnp.sum(powers, -1, keepdims=True)
    contrast_own = pick(
        peak[:, 0] + jnp.log(totals_row[:, 0]) - jnp.sum(same * similar, -1), item
    )
    grad_similar = (powers / totals_row - same) * (
        CONTRAST_WEIGHT / items_total / CONTRAST_TEMP
    )
    grad_audio_unit = jnp.sum(pick(grad_similar, item)[:, None] * text_units, 0)
    grad_text_unit = jnp.sum(pick(grad_similar, item, 1)[:, None] * audio_units, 0)

    def unit_back(gradient, unit, inverse):
        return inverse * (gradient - unit * jnp.sum(unit * gradient))

    grad_audio = unit_back(grad_audio_unit, pick(audio_units, item), pick(inverse_pools, item)[0])
    grad_text = unit_back(grad_text_unit, pick(text_units, item), pick(inverse_pools, item)[1])

    grad_predicted = (2.0 * mse_scale * errors).astype(bf16)
    grad_out_weight = tdot(output_low, grad_predicted)
    grad_output = dot_back(grad_predicted, weight_out) + grad_audio[None, :] / FRAMES
    grad_low = grad_output.astype(bf16)
    grad_gate, grad_up, grad_down = hidden_back(grad_low, down, gate_part, up_part, hidden)
    grad_gate_weight, grad_up_weight, grad_feed_rows = rows_back(
        feed_rows, grad_gate, grad_up, gate_weight, up_weight
    )

    def over_plane(gradient, width):
        return lax.psum_scatter(
            gradient.reshape(4, 4, -1, width, gradient.shape[1]),
            ("y", "x"),
            scatter_dimension=0,
            tiled=True,
        )

    def over_line(total):
        return lax.psum_scatter(total, "z", scatter_dimension=1, tiled=True)[0, 0]

    down_total = over_plane(grad_down, 192)
    grad_after_cross, grad_cross_in, gain_three = norm_back(
        dot_back(grad_feed_rows, reorder),
        normed_three,
        inverse_three,
        gain_values[2],
        grad_output,
        True,
    )
    cross_rows = tdot(cross_flat, grad_cross_in).astype(bf16).reshape(2, 2, 192, D)
    cross_kept = pick(cross_rows, core, 1)
    cross_received = swap(pick(cross_rows, 1 - core, 1), "c")
    cross_pair = jnp.stack([cross_kept, cross_received], 0)
    out_rows = jnp.where(core == 0, cross_pair, cross_pair[::-1]).reshape(4, 1, 4, 48, D)
    grad_mixed_cross = dot_back(grad_cross_in, cross_out).astype(bf16)
    grad_cq, grad_text_keys, grad_text_values = attend_back(
        cross_queries,
        projected,
        projected,
        text_biases,
        cross_offsets,
        cross_flat,
        logsum_cross,
        grad_mixed_cross,
        None,
    )
    grad_query_weight = tdot(input_two, grad_cq).astype(bf16).reshape(4, 2, 4, 48, half)
    grad_input_two = on_both(dot_back(grad_cq, cross_query))
    text_half_grad = lax.dynamic_slice_in_dim(grad_text, core * half, half, 0)
    grad_pair_keys = (
        grad_text_keys + mask * (text_half_grad[None, :] / length_float)
    ).astype(bf16)
    kv_sources = [
        tdot(tokens, gradient.astype(bf16)).astype(bf16).reshape(4, 2, 4, 16, 1152)
        for gradient in (grad_pair_keys, grad_text_values)
    ]
    grad_after_self, gain_two = layer_back(
        grad_input_two, normed_two, inverse_two, gain_values[1]
    )
    grad_after_self = grad_after_self + grad_after_cross
    grad_self_in = grad_after_self.astype(bf16)
    grad_mix = tdot(mixed_flat, grad_self_in).astype(bf16)
    grad_mixed_self = dot_back(grad_self_in, weight_mix).astype(bf16)
    grad_queries, grad_keys, grad_values, grad_time_keys, grad_time_values = attend_back(
        joined,
        joined,
        joined,
        (joined_time, joined_time),
        self_offsets,
        mixed_flat,
        logsum_self,
        grad_mixed_self,
        (cosine_table, sine_table),
    )
    grad_joined = jnp.concatenate([grad_queries, grad_keys, grad_values], 1)
    grad_time_pair = jnp.concatenate([grad_time_keys[:1], grad_time_values[:1]], 1)
    time_row = jnp.concatenate([jnp.zeros((1, half), f32), grad_time_pair], 1)
    grad_projection = (
        tdot(input_one, grad_joined) + input_time.astype(f32).reshape(D, 1) * time_row
    ).astype(bf16)
    grad_gate_weight, down_total, _ = lax.optimization_barrier(
        (grad_gate_weight, down_total, grad_cq)
    )
    gate_total = over_plane(grad_gate_weight, 48)
    grad_up_weight, gate_total, _ = lax.optimization_barrier(
        (grad_up_weight, gate_total, grad_projection)
    )
    up_total = over_plane(grad_up_weight, 48)
    down_total = over_line(down_total)
    grad_down_low = down_total[0]
    position = jnp.arange(256, dtype=jnp.int32)
    owner_core = core ^ (position // 128)
    block = assignment[
        (position // 32) % 4 * 64 + owner_core * 32 + (position // 8) % 4 * 8 + position % 8
    ]
    matrix, block_row, block_column = block // 64, (block // 8) % 8, block % 8
    is_out = matrix == 3
    side = jnp.where(is_out, block_row // 4, block_column // 4)
    code = jnp.where(side == core, 2 * is_out + block_column % 2, 4)
    near_slots, far_slots = collect(
        grad_projection,
        grad_mix,
        jnp.where(is_out, block_row % 4, block_row),
        jnp.where(is_out, block_column // 2, matrix * 2 + (block_column % 4) // 2),
        code.astype(jnp.int32),
    )
    slot_sums = low_sum(near_slots, swap(far_slots, "c")).astype(bf16)
    slot_sums, grad_down_low = lax.optimization_barrier((slot_sums, grad_down_low))
    slot_sums = slot_sums.reshape(4, 1, 4, 4 * BLK, 2 * BLK)

    partial_one = dot_back(grad_joined, projection)
    partial_time = jnp.dot(
        grad_time_pair, projection[:, half:].astype(f32).T, precision=BEST_PRECISION
    )
    grad_input_time = partial_time + swap(partial_time, "c")
    grad_residual, gain_one = layer_back(
        on_both(partial_one), normed_one, inverse_one, gain_values[0]
    )
    grad_residual = (grad_residual + grad_after_self).astype(bf16)
    gate_total, up_total, grad_residual = lax.optimization_barrier(
        (gate_total, up_total, grad_residual)
    )
    feed_sums = []
    for total in (gate_total, up_total):
        both_rows = over_line(total)
        feed_sums.append((pick(both_rows, core), swap(pick(both_rows, 1 - core), "c")))
    grad_embeds, gain_time = layer_back(
        grad_input_time, normed_time, inverse_time, gain_values[0]
    )
    grad_in_weight = tdot(grad_residual, noised)
    grad_table = features.astype(f32).reshape(NTIME, 1) * grad_embeds
    grad_gains = jnp.stack([gain_one + gain_time, gain_two, gain_three], 0)

    def own_rows(values):
        return pick(values.reshape((4, 2, 4) + values.shape[1:]), core, 1)

    small = jnp.concatenate(
        [
            own_rows(grad_table.reshape(32, 8, D)),
            jnp.pad(
                own_rows(grad_gains.reshape(3, 32, 48).transpose(1, 0, 2).reshape(32, 1, 144)),
                ((0, 0), (0, 0), (0, 7), (0, D - 144)),
            ),
        ],
        2,
    )
    grad_ends = own_rows(
        jnp.concatenate([grad_in_weight, grad_out_weight], 1).astype(bf16).reshape(32, 48, 2 * DIN)
    )
    rest_arrays = (
        ("one", (4 * BLK, 2 * BLK)),
        ("cols", (48, half)),
        ("one", (48, D)),
        ("cols", (16, 1152)),
        ("cols", (16, 1152)),
        ("one", (16, D)),
        ("one", (48, 2 * DIN)),
    )
    rest_groups = [((3, 0, whole, whole), (4, 1, whole, whole))]
    rest_groups += [
        ((1, 0, whole, pl.ds(step * 384, 384)), (2, 1, whole, pl.ds(step * 768, 768)))
        for step in range(2)
    ]
    rest_groups += [
        ((0, 0, pl.ds(step * 96, 96), whole), (0, 1, pl.ds(384 + step * 96, 96), whole))
        for step in range(4)
    ]
    rest_groups += [((5, 0, whole, whole), (6, 1, whole, whole))]
    rest_sums = reduce_gradients(
        rest_arrays,
        rest_groups,
        (
            slot_sums,
            grad_query_weight,
            out_rows,
            kv_sources[0],
            kv_sources[1],
            small.astype(bf16).reshape(4, 1, 4, 16, D),
            grad_ends.reshape(4, 1, 4, 48, 2 * DIN),
        ),
        2,
    )
    grad_down = grad_down_low.astype(f32)
    slot_pairs = rest_sums[0].reshape(4, BLK, 2 * BLK)
    grad_cross_query, grad_cross_out, *kv_sums, small, grad_ends = (
        value.astype(f32) for value in rest_sums[1:]
    )
    gate_sides, (up_own, up_other) = feed_sums
    gate_columns = []
    for mine, other in (gate_sides, (up_own, up_other)):
        sides = (jnp.where(core == 0, mine, other), jnp.where(core == 0, other, mine))
        for quadrant in quads:
            for side in sides:
                gate_columns.append(side[:, quadrant * 768 : (quadrant + 1) * 768])
    grad_gate_up = jnp.concatenate(gate_columns, 1).astype(f32)
    grad_cross = jnp.stack([grad_cross_query, grad_cross_out], 1)
    kv_columns = []
    for pair in kv_sums:
        kv_columns += [pair[:, :1152].reshape(24, half), pair[:, 1152:].reshape(24, half)]
    grad_key_value = jnp.concatenate(kv_columns, 1)
    grad_ends = grad_ends.reshape(48, 2, DIN)
    grad_table = small[:8]
    grad_gains = small[8, :144].reshape(3, 48).T

    reduced = (
        grad_ends,
        grad_table,
        slot_pairs,
        grad_cross,
        grad_key_value,
        grad_gate_up,
        grad_down,
        grad_gains,
    )
    loss_part = jnp.where(
        core == 0,
        jnp.sum(errors * errors) * mse_scale + contrast_own * (CONTRAST_WEIGHT / items_total),
        0.0,
    )
    totals = total_squares(
        loss_part, (*rest_sums, *gate_sides, up_own, up_other, grad_down_low), 4
    )
    loss_total, norm_square = totals[0, 0], totals[0, 1]
    return finish(
        loss_total,
        jnp.sqrt(norm_square),
        reduced,
        (
            end_weights,
            time_table,
            square_slots,
            cross_weights,
            key_value,
            gate_up,
            down_weight,
            norm_gains,
        ),
        (
            first_ends,
            first_table,
            None,
            first_cross,
            first_key_value,
            first_gate_up,
            first_down,
            first_gains,
        ),
        (
            second_ends,
            second_table,
            None,
            second_cross,
            second_key_value,
            second_gate_up,
            second_down,
            second_gains,
        ),
        (left_stats, right_stats, left_roots, right_roots),
    )


def finish(loss_total, gradient_norm, reduced, masters, firsts, seconds, statistics):
    factor = CLIP_NORM / jnp.maximum(gradient_norm, CLIP_NORM)
    results = [loss_total, gradient_norm]
    for index_value in (0, 1, 3, 4, 5, 6, 7):
        results.extend(
            adam_update(
                masters[index_value],
                firsts[index_value],
                seconds[index_value],
                factor * reduced[index_value],
                ADAM_RATES[index_value],
            )
        )
    if reduced[2].dtype == jnp.bfloat16:
        results.extend(shampoo_pairs(factor, reduced[2], masters[2], *statistics))
    else:
        clipped_slots = factor * reduced[2]
        results.append(clipped_slots)
        results.extend(shampoo_update(masters[2], clipped_slots, *statistics))
    return tuple(results)


def solution(mesh):
    lines = mesh.shape["text"]
    chips = mesh.devices.size // 2
    if mesh.shape["dp"] == 8 and lines == 4 and 2 * mesh.shape["dp"] == chips:
        mesh = Mesh(mesh.devices.reshape(2, 2, 2, lines), ("y", "x", "c", "z"))
        dp, text, body = ("y", "x", "c"), ("z",), item_per_chip
    else:
        dp, text, body = ("dp",), ("text",), shards
    own = dp + text
    in_specs = (
        P(dp, text, None),
        P(dp, text, None),
        P(dp),
        P(dp, text, None),
        P(dp),
        P(dp, None),
        P(),
    ) + (P(own),) * 26
    out_specs = (P(), P()) + (P(own),) * 25
    return jax.shard_map(body, mesh=mesh, in_specs=in_specs, out_specs=out_specs, check_vma=False)
```
